32 devices in a mesh: blk: 16 (over z, x, core), rel: 2 (over y).
Axes of the slice: x: 2, y: 2, z: 4, core: 2. Of those that a mesh axis runs over, the one named last changes fastest.
Arguments:
- left_slab: float32 [65536, 400], P(('blk', 'rel')), may hold values from -1.3 to 1.3
- left_state: float32 [65536], P(('blk', 'rel')), may hold values from 1e-05 to 0.0001
- right_slab: float32 [65536, 400], P(('blk', 'rel')), may hold values from -1.3 to 1.3
- right_state: float32 [65536], P(('blk', 'rel')), may hold values from 1e-05 to 0.0001
- relations: float32 [32, 400], replicated, may hold values from 0.1 to 1.9
- relation_state: float32 [32], replicated, may hold values from 0.01 to 0.2
- src_index: int32 [2, 8192], P(None, ('blk', 'rel')), may hold values from 0 to 2047
- dst_index: int32 [2, 8192], P(None, ('blk', 'rel')), may hold values from 0 to 2047
- relation_id: int32 [2, 8192], P(None, ('blk', 'rel')), may hold values from 0 to 31
- neg_source: int32 [2, 32000], P(None, ('blk', 'rel')), may hold values from 0 to 2047
- neg_target: int32 [2, 32000], P(None, ('blk', 'rel')), may hold values from 0 to 2047
Outputs:
- left_out: float32 [65536, 400], P(('blk', 'rel'))
- right_out: float32 [65536, 400], P(('blk', 'rel'))
- relations_out: float32 [16, 32, 400], P('blk')
The draws below stay inside these ranges and needn't reach their ends.
All inputs are finite; a program needn't handle non-finite values.
Results may differ from the reference program's by a relative error of at most 0.00069.
Values sent between devices are 32-bit elements; how exact they have to be, the bound alone decides.
No kernel may reach another device: no remote copies, remote signals or barrier semaphores. Data moves between devices by JAX's collectives and lax.ppermute only.
A program may use at most 64 MiB of HBM per device.

```python
import math
import jax
import jax.numpy as jnp
from jax import lax

D = 400
ROWS = 2048
EDGES = 256
NEG = 1000
NREL = 32
ROUNDS = 2
ENT = 65536
EDGE_ALL = 8192
NEG_ALL = 32000
N_BLK = 16
N_REL = 2


def touch_ends(entries, stream_key, low, top_value):
    index_at = [jax.random.randint(jax.random.fold_in(stream_key, axis), (), 0, length) for axis, length in enumerate(entries.shape)]
    widest = entries.shape.index(max(entries.shape))
    neighbour = index_at[:widest] + [(index_at[widest] + 1) % entries.shape[widest]] + index_at[widest + 1:]
    return entries.at[tuple(index_at)].set(low).at[tuple(neighbour)].set(top_value)


def block_levels(stream_key, extent, cuts, low, top_value):
    def one(position, parts):
        steps = jax.random.uniform(jax.random.fold_in(jax.random.fold_in(stream_key, 6), position), (parts,), jnp.float32, low / len(cuts), top_value / len(cuts))
        return jnp.repeat(jnp.exp(steps), extent[position] // parts).reshape((-1,) + (1,) * (len(extent) - position - 1))

    gain = one(*cuts[0])
    for cut in cuts[1:]:
        gain = gain * one(*cut)
    return gain


def bell_draw(key, shape, deviation, limit, shards=(), held_as=jnp.bfloat16):
    entries = deviation * jax.random.normal(key, shape, jnp.float32)
    if shards:
        entries = entries * block_levels(key, shape, shards, -0.22, 0.18)
    return jnp.clip(entries, -limit, limit).astype(held_as)


def setup_inputs(seed: int = 0) -> dict:
    streams_of = jax.random.split(jax.random.key(seed), 12)
    return {
        "left_slab": bell_draw(streams_of[0], (ENT, D), 0.22, 1.3, ((0, 32),), jnp.float32),
        "left_state": jnp.clip(jnp.exp(math.log(0.0001) - 2.3025851 * jax.random.uniform(streams_of[1], (ENT,), jnp.float32) ** block_levels(streams_of[1], (ENT,), ((0, 32),), -0.2, 0.2)), 9.999999747378752e-06, 0.0001),
        "right_slab": bell_draw(streams_of[2], (ENT, D), 0.22, 1.3, ((0, 32),), jnp.float32),
        "right_state": jnp.clip(jnp.exp(math.log(0.0001) - 2.3025851 * jax.random.uniform(streams_of[3], (ENT,), jnp.float32) ** block_levels(streams_of[3], (ENT,), ((0, 32),), -0.2, 0.2)), 9.999999747378752e-06, 0.0001),
        "relations": jnp.clip(1.0 + 0.18 * jax.random.normal(streams_of[4], (NREL, D), jnp.float32), 0.1, 1.9),
        "relation_state": jnp.clip(jnp.exp(jax.random.uniform(streams_of[5], (NREL,), jnp.float32, math.log(0.01), math.log(0.2))), 0.01, 0.2),
        "src_index": touch_ends(jax.random.randint(streams_of[6], (ROUNDS, EDGE_ALL), 0, ROWS), jax.random.fold_in(streams_of[6], 1), 0, ROWS - 1).astype(jnp.int32),
        "dst_index": touch_ends(jax.random.randint(streams_of[7], (ROUNDS, EDGE_ALL), 0, ROWS), jax.random.fold_in(streams_of[7], 1), 0, ROWS - 1).astype(jnp.int32),
        "relation_id": touch_ends(jax.random.randint(streams_of[8], (ROUNDS, EDGE_ALL), 0, NREL), jax.random.fold_in(streams_of[8], 1), 0, NREL - 1).astype(jnp.int32),
        "neg_source": touch_ends(jax.random.randint(streams_of[9], (ROUNDS, NEG_ALL), 0, ROWS), jax.random.fold_in(streams_of[9], 1), 0, ROWS - 1).astype(jnp.int32),
        "neg_target": touch_ends(jax.random.randint(streams_of[10], (ROUNDS, NEG_ALL), 0, ROWS), jax.random.fold_in(streams_of[10], 1), 0, ROWS - 1).astype(jnp.int32),
    }


rate = 0.1

def adagrad_rows(slab, state, grad):
    new_state = state + lax.optimization_barrier(jnp.mean(grad * grad, axis=1))
    return (slab - rate * grad / jnp.sqrt(new_state)[:, None], new_state)

def train_block(left, lstate, right, rstate, relations, src, dst, rid, nsrc, ndst):
    rows = left.shape[0]
    table = (rid[:, None] == jnp.arange(relations.shape[0], dtype=jnp.int32)[None, :]).astype(jnp.float32)
    weight = jnp.dot(table, relations, precision=lax.Precision.HIGHEST)
    source = left[src]
    target = right[dst]
    pos = lax.optimization_barrier(jnp.sum(source * weight * target, axis=1))
    query = (source * weight).astype(jnp.bfloat16)
    probe = (weight * target).astype(jnp.bfloat16)
    negy = right[ndst].astype(jnp.bfloat16)
    negx = left[nsrc].astype(jnp.bfloat16)
    score_t = jnp.dot(query, negy.T, preferred_element_type=jnp.float32)
    score_s = jnp.dot(probe, negx.T, preferred_element_type=jnp.float32)
    count = score_t.shape[1]
    coef = -jax.nn.sigmoid(-pos)[:, None]
    grad_t = (jax.nn.sigmoid(score_t) / count).astype(jnp.bfloat16)
    grad_s = (jax.nn.sigmoid(score_s) / count).astype(jnp.bfloat16)
    gq = jnp.dot(grad_t, negy, preferred_element_type=jnp.float32)
    gy = jnp.dot(grad_t.T, query, preferred_element_type=jnp.float32)
    gp = jnp.dot(grad_s, negx, preferred_element_type=jnp.float32)
    gx = jnp.dot(grad_s.T, probe, preferred_element_type=jnp.float32)
    g_source = coef * weight * target + gq * weight
    g_target = coef * weight * source + gp * weight
    g_weight = coef * source * target + gq * source + gp * target
    grad_left = jax.ops.segment_sum(g_source, src, num_segments=rows) + jax.ops.segment_sum(gx, nsrc, num_segments=rows)
    grad_right = jax.ops.segment_sum(g_target, dst, num_segments=rows) + jax.ops.segment_sum(gy, ndst, num_segments=rows)
    rel_grad = jnp.dot(table.T, g_weight, precision=lax.Precision.HIGHEST)
    left, lstate = adagrad_rows(left, lstate, grad_left)
    right, rstate = adagrad_rows(right, rstate, grad_right)
    return (left, lstate, right, rstate, rel_grad)

def reference(left_slab, left_state, right_slab, right_state, relations, relation_state, src_index, dst_index, relation_id, neg_source, neg_target):
    blocks = N_BLK * N_REL
    left = left_slab.reshape(blocks, ROWS, D)
    lstate = left_state.reshape(blocks, ROWS)
    right = right_slab.reshape(N_BLK, N_REL, ROWS, D)
    rstate = right_state.reshape(N_BLK, N_REL, ROWS)
    rel_total = jnp.zeros((N_BLK, NREL, D), jnp.float32)
    for step in range(ROUNDS):
        right = jnp.roll(right, 1, axis=0).reshape(blocks, ROWS, D)
        rstate = jnp.roll(rstate, 1, axis=0).reshape(blocks, ROWS)
        src = src_index[step].reshape(blocks, EDGES)
        dst = dst_index[step].reshape(blocks, EDGES)
        rid = relation_id[step].reshape(blocks, EDGES)
        nsrc = neg_source[step].reshape(blocks, NEG)
        ndst = neg_target[step].reshape(blocks, NEG)

        def one(items):
            return train_block(items[0], items[1], items[2], items[3], relations, items[4], items[5], items[6], items[7], items[8])
        left, lstate, right, rstate, rel_grad = lax.map(one, (left, lstate, right, rstate, src, dst, rid, nsrc, ndst))
        rel_total = rel_total + lax.optimization_barrier(jnp.sum(rel_grad.reshape(N_BLK, N_REL, NREL, D), axis=1))
        right = right.reshape(N_BLK, N_REL, ROWS, D)
        rstate = rstate.reshape(N_BLK, N_REL, ROWS)
    new_rstate = relation_state[None, :] + lax.optimization_barrier(jnp.mean(rel_total * rel_total, axis=2))
    relations_out = relations[None] - rate * rel_total / jnp.sqrt(new_rstate)[:, :, None]
    return (left.reshape(ENT, D), right.reshape(ENT, D), relations_out)
```

```python
import functools

import jax
import jax.numpy as jnp
from jax import lax
from jax.experimental import pallas as pl
from jax.experimental.pallas import tpu as pltpu
from jax.sharding import PartitionSpec as P

rate = 0.1
F32 = jnp.float32
BF16 = jnp.bfloat16
LANES = 128
STRIPE = 16

NN = (((1,), (0,)), ((), ()))
NT = (((1,), (1,)), ((), ()))
TN = (((0,), (0,)), ((), ()))


def mul(a, b, dims):
    return lax.dot_general(a, b, dims, preferred_element_type=F32)


def split(x, parts):
    out = []
    for _ in range(parts):
        part = x.astype(BF16)
        out.append(part)
        x = x - part.astype(F32)
    return out


def row_onehot(idx, table):
    count, rows = table.shape
    col = jnp.broadcast_to(idx, (LANES, count)).T
    lane = lax.broadcasted_iota(jnp.int32, (count, LANES), 1)
    for t in range(rows // LANES):
        hit = col == lane + t * LANES
        table[:, t * LANES : (t + 1) * LANES] = jnp.where(hit, 1.0, 0.0).astype(BF16)


def row_counts(idx, rows):
    count = idx.shape[1]
    high = lax.broadcasted_iota(jnp.int32, (rows // LANES, count), 0)
    low = lax.broadcasted_iota(jnp.int32, (LANES, count), 0)
    high_hit = jnp.where(idx // LANES == high, 1.0, 0.0).astype(BF16)
    low_hit = jnp.where(idx % LANES == low, 1.0, 0.0).astype(BF16)
    return mul(high_hit, low_hit, NT)


def split_slab(pieces, parts):
    depth = parts.shape[0] // 3
    start = 0
    for piece in pieces:
        cut = slice(start, start + piece.shape[1])
        start = cut.stop

        def stripe(i, carry, piece=piece, cut=cut):
            at = pl.multiple_of(i * STRIPE, STRIPE)
            for k, part in enumerate(split(piece[pl.ds(at, STRIPE), :], 3)):
                parts[pl.ds(pl.multiple_of(k * depth + i * STRIPE, STRIPE), STRIPE), cut] = part
            return carry

        lax.fori_loop(0, depth // STRIPE, stripe, 0)


def gather(parts, table):
    depth = parts.shape[0] // 3
    out = mul(parts[...], table[...], NT)
    return out[:depth] + out[depth : 2 * depth] + out[2 * depth :]


def negatives(query, slab, counts, grad, number, wide):
    rows = slab.shape[1]
    query_rows = query.astype(F32).T.astype(BF16)
    total = jnp.zeros(query.shape, F32)
    for c in range(rows // wide):
        cut = slice(c * wide, (c + 1) * wide)
        part = slab[:, cut]
        times = jnp.concatenate(
            [counts[t : t + 1, :] for t in range(c * wide // LANES, (c + 1) * wide // LANES)], axis=1
        )
        score = mul(query_rows, part, NN)
        weight = (jax.nn.sigmoid(score) * (1.0 / number)).astype(BF16)
        grad[:, cut] = mul(query, weight, NN) * times
        often = (weight.astype(F32) * times).astype(BF16)
        total = total + mul(part, often, NT)
    return total


def within(pieces, cut):
    width = pieces[0].shape[1]
    piece = pieces[cut.start // width]
    return piece, slice(cut.start % width, cut.start % width + cut.stop - cut.start)


def adagrad(slab, state, grad, edge_grad, table, wide, out, new_state, send=None):
    depth, rows = grad.shape
    high, low = split(edge_grad, 2)
    for c in range(rows // wide):
        cut = slice(c * wide, (c + 1) * wide)
        hits = table[:, cut]
        g = grad[:, cut] + mul(high, hits, NN) + mul(low, hits, NN)
        new = state[:, cut] + jnp.sum(g * g, axis=0, keepdims=True) * (1.0 / depth)
        new_state[:, cut] = new
        old, old_cut = within(slab, cut)
        to, to_cut = within(out, cut)
        to[0:depth, to_cut] = old[0:depth, old_cut] - g * (rate / jnp.sqrt(new))
        if send is not None:
            send(c, cut)


def train(parity, step, last, kept, takes, gives, *refs):
    refs = list(refs)
    (left, lstate, rstate_in, relations, rel_in, src, dst, rid, nsrc, ndst) = refs[:10]
    right = refs[10 : 10 + takes]
    refs = refs[10 + takes + kept :]
    left_out, lstate_out, rel_out = refs[:3]
    right_out = refs[3 : 3 + gives]
    (lparts, rparts, lgrad, rgrad, oh_src, oh_dst, rstate, new_rstate, sems) = refs[3 + gives :]
    depth, rows = left.shape
    wide = 512
    number = float(nsrc.shape[1])
    lstate_out[...] = lstate[...]
    rel_out[...] = rel_in[...]

    @pl.when(lax.axis_index("blk") % 2 == parity)
    def _():
        here = slice(step, step + 1)
        row_onehot(src[here, :], oh_src)
        row_onehot(dst[here, :], oh_dst)
        kinds = lax.broadcasted_iota(jnp.int32, (relations.shape[0], rid.shape[1]), 0)
        kind = jnp.where(rid[here, :] == kinds, 1.0, 0.0).astype(BF16)
        count_l = row_counts(nsrc[here, :], rows)
        count_r = row_counts(ndst[here, :], rows)
        weight = sum(mul(part, kind, TN) for part in split(relations[...], 3))
        split_slab([left], lparts)
        source = gather(lparts, oh_src)
        query = (source * weight).astype(BF16)
        split_slab(right, rparts)
        if right[0].shape[0] > depth:
            width = right[0].shape[1]
            for i, piece in enumerate(right):
                rstate[:, i * width : (i + 1) * width] = piece[depth : depth + 1, :]
        else:
            rstate[...] = rstate_in[...]
        target = gather(rparts, oh_dst)
        probe = (weight * target).astype(BF16)
        pos = jnp.sum(source * weight * target, axis=0, keepdims=True)
        coef = -jax.nn.sigmoid(-pos)
        gq = negatives(query, rparts.at[0:depth], count_r, rgrad, number, wide)
        gp = negatives(probe, lparts.at[0:depth], count_l, lgrad, number, wide)
        g_source = coef * weight * target + gq * weight
        g_target = coef * weight * source + gp * weight
        g_weight = coef * source * target + gq * source + gp * target
        rel_out[...] = rel_in[...] + sum(mul(kind, part, NT) for part in split(g_weight, 2))
        if last:
            copies = []

            def sender(k, result, to):
                def send(c, cut):
                    copy = pltpu.make_async_copy(result.at[:, cut], to.at[:, cut], sems.at[k, c])
                    copy.start()
                    copies.append(copy)

                return send

            adagrad(right, rstate, rgrad, g_target, oh_dst, wide, [rgrad], new_rstate, sender(0, rgrad, right_out[0]))
            adagrad([left], lstate, lgrad, g_source, oh_src, wide, [lgrad], lstate_out, sender(1, lgrad, left_out))
            for copy in copies:
                copy.wait()
        else:
            adagrad(right, rstate, rgrad, g_target, oh_dst, wide, right_out, new_rstate)
            width = right_out[0].shape[1]
            for i, piece in enumerate(right_out):
                state = new_rstate[:, i * width : (i + 1) * width]
                piece[depth : depth + 8, :] = jnp.broadcast_to(state, (8, width))
            adagrad([left], lstate, lgrad, g_source, oh_src, wide, [left_out], lstate_out)


def trained(parity, step, gives, left, lstate, right, rstate, relations, rel, index, keep=()):
    depth, rows = left.shape
    edges = index[0].shape[1]
    last = gives == 0
    gives = max(gives, 1)
    vmem = pl.BlockSpec(memory_space=pltpu.VMEM)
    large = pl.BlockSpec(memory_space=pl.ANY) if last else vmem
    block = jax.ShapeDtypeStruct((depth if last else depth + 8, rows // gives), F32)
    left_out, lstate_out, rel_out, *right_out = pl.pallas_call(
        functools.partial(train, parity, step, last, len(keep), len(right), gives),
        out_shape=(
            jax.ShapeDtypeStruct((depth, rows), F32),
            jax.ShapeDtypeStruct((1, rows), F32),
            jax.ShapeDtypeStruct(relations.shape, F32),
            *[block] * gives,
        ),
        in_specs=[vmem] * (10 + len(right)) + [large] * len(keep),
        out_specs=(large, vmem, vmem, *[large] * gives),
        scratch_shapes=[
            pltpu.VMEM((3 * depth, rows), BF16),
            pltpu.VMEM((3 * depth, rows), BF16),
            pltpu.VMEM((depth, rows), F32),
            pltpu.VMEM((depth, rows), F32),
            pltpu.VMEM((edges, rows), BF16),
            pltpu.VMEM((edges, rows), BF16),
            pltpu.VMEM((1, rows), F32),
            pltpu.VMEM((1, rows), F32),
            pltpu.SemaphoreType.DMA((2, rows // 512)),
        ],
        input_output_aliases={10 + len(right) + i: 3 * i for i in range(len(keep))},
        compiler_params=pltpu.CompilerParams(vmem_limit_bytes=30 * 2**20),
        cost_estimate=pl.CostEstimate(flops=1_000_000, bytes_accessed=100_000, transcendentals=0),
        name="round%d_parity%d" % (step, parity),
    )(left, lstate, rstate, relations, rel, *index, *right, *keep)
    return left_out, lstate_out, right_out, rel_out


NEAR = 4


def local(
    left_slab, left_state, right_slab, right_state, relations, relation_state,
    src_index, dst_index, relation_id, neg_source, neg_target,
):
    peers = lax.axis_size("blk")
    inside = [(i, i + 1) for i in range(0, peers, 2)]
    across = [(i, (i + 1) % peers) for i in range(1, peers, 2)]
    index = (src_index, dst_index, relation_id, neg_source, neg_target)
    left = left_slab.T
    right = right_slab.T
    rows = left.shape[1]
    lstate = left_state.reshape(1, rows)
    right_far = lax.ppermute(right, "blk", across)
    right_near = lax.ppermute(right, "blk", inside)
    state_far = lax.ppermute(right_state, "blk", across).reshape(1, rows)
    state_near = lax.ppermute(right_state, "blk", inside).reshape(1, rows)
    rel = jnp.zeros(relations.shape, F32)
    left_a, lstate, far, rel = trained(1, 0, 1, left, lstate, [right_near], state_near, relations, rel, index)
    far, right_far = lax.optimization_barrier((far, right_far))
    far = [lax.ppermute(piece, "blk", across) for piece in far]
    left_a, lstate, near, rel = trained(
        0, 0, NEAR, left, lstate, [right_far], state_far, relations, rel, index, (left_a,)
    )
    near = [lax.ppermute(piece, "blk", inside) for piece in near]
    left_b, lstate, right_b, rel = trained(1, 1, 0, left_a, lstate, near, state_near, relations, rel, index)
    left_b, lstate, right_b, rel = trained(
        0, 1, 0, left_a, lstate, far, state_far, relations, rel, index, (left_b, *right_b)
    )
    rel = lax.psum(rel, "rel")
    new_rstate = relation_state + jnp.mean(rel * rel, axis=1)
    relations_out = relations - rate * rel / jnp.sqrt(new_rstate)[:, None]
    return (left_b.T, right_b[0].T, relations_out[None])


def solution(mesh):
    in_specs = (
        P(("blk", "rel"), None),
        P(("blk", "rel")),
        P(("blk", "rel"), None),
        P(("blk", "rel")),
        P(),
        P(),
        P(None, ("blk", "rel")),
        P(None, ("blk", "rel")),
        P(None, ("blk", "rel")),
        P(None, ("blk", "rel")),
        P(None, ("blk", "rel")),
    )
    out_specs = (P(("blk", "rel"), None), P(("blk", "rel"), None), P("blk", None, None))
    return jax.shard_map(local, mesh=mesh, in_specs=in_specs, out_specs=out_specs, check_vma=False)
```

```python
import functools

import jax
import jax.numpy as jnp
from jax import lax
from jax.experimental import pallas as pl
from jax.experimental.pallas import tpu as pltpu
from jax.sharding import PartitionSpec as P

rate = 0.1
F32 = jnp.float32
BF16 = jnp.bfloat16
LANES = 128
STEP = 256
NEAR = (4, 4)
FAR = (5, 2, 1)
VMEM_LIMIT = 30 * 2**20

NN = (((1,), (0,)), ((), ()))
NT = (((1,), (1,)), ((), ()))
TN = (((0,), (0,)), ((), ()))


def mul(a, b, dims):
    return lax.dot_general(a, b, dims, preferred_element_type=F32)


def split(x, parts):
    out = []
    for _ in range(parts):
        part = x.astype(BF16)
        out.append(part)
        x = x - part.astype(F32)
    return out


def lanes_at(i, size):
    return pl.ds(pl.multiple_of(i * size, size), size)


def row_onehot(idx, table):
    count, rows = table.shape
    col = jnp.broadcast_to(idx, (LANES, count)).T
    lane = lax.broadcasted_iota(jnp.int32, (count, LANES), 1)

    def tile(t, carry):
        hit = col == lane + t * LANES
        table[:, lanes_at(t, LANES)] = jnp.where(hit, 1.0, 0.0).astype(BF16)
        return carry

    lax.fori_loop(0, rows // LANES, tile, 0)


def row_counts(idx, rows):
    count = idx.shape[1]
    high = lax.broadcasted_iota(jnp.int32, (rows // LANES, count), 0)
    low = lax.broadcasted_iota(jnp.int32, (LANES, count), 0)
    high_hit = jnp.where(idx // LANES == high, 1.0, 0.0).astype(BF16)
    low_hit = jnp.where(idx % LANES == low, 1.0, 0.0).astype(BF16)
    return mul(high_hit, low_hit, NT)


def times_at(counts, i):
    tiles = STEP // LANES
    return jnp.concatenate([counts[pl.ds(i * tiles + t, 1), :] for t in range(tiles)], axis=1)


def half_rows(x):
    return (0.5 * x).T.astype(BF16)


def negatives(rows16, query, query_rows, times, number):
    half = 0.5 / number
    weight = (jnp.tanh(mul(query_rows, rows16, NN)) * half + half).astype(BF16)
    often = (weight.astype(F32) * times).astype(BF16)
    return mul(query, weight, NN) * times, mul(rows16, often, NT)


def prepare(step, left, relations, src, dst, rid, nsrc, ndst,
            weight, source, query, query_rows, left16, oh_src, oh_dst, count_l, count_r, kind):
    rows = left.shape[1]
    here = slice(step, step + 1)
    row_onehot(src[here, :], oh_src)
    row_onehot(dst[here, :], oh_dst)
    count_l[...] = row_counts(nsrc[here, :], rows)
    count_r[...] = row_counts(ndst[here, :], rows)
    kinds = lax.broadcasted_iota(jnp.int32, kind.shape, 0)
    kind[...] = jnp.where(rid[here, :] == kinds, 1.0, 0.0).astype(BF16)
    weight[...] = sum(mul(part, kind[...], TN) for part in split(relations[...], 3))
    source[...] = jnp.zeros_like(source)

    def part(i, carry):
        cut = lanes_at(i, STEP)
        parts = split(left[:, cut], 3)
        left16[:, cut] = parts[0]
        source[...] += sum(mul(p, oh_src[:, cut], NT) for p in parts)
        return carry

    lax.fori_loop(0, rows // STEP, part, 0)
    product = source[...] * weight[...]
    query[...] = product.astype(BF16)
    query_rows[...] = half_rows(product.astype(BF16).astype(F32))


def take_piece(number, start, piece, query, query_rows, oh_dst, count_r, target, gq, rgrad):
    depth = target.shape[0]
    if start == 0:
        target[...] = jnp.zeros_like(target)
        gq[...] = jnp.zeros_like(gq)

    def part(i, carry):
        cut = lanes_at(i, STEP)
        parts = split(piece[0:depth, cut], 3)
        hits = oh_dst[:, lanes_at(i + start // STEP, STEP)]
        target[...] += sum(mul(p, hits, NT) for p in parts)
        times = times_at(count_r, i + start // STEP)
        rgrad[:, cut], more = negatives(parts[0], query[...], query_rows[...], times, number)
        gq[...] += more
        return carry

    lax.fori_loop(0, piece.shape[1] // STEP, part, 0)


def join(number, weight, source, target, gq, left16, count_l, kind, rel_in, probe, probe_rows, gp, lgrad, to_src, to_dst, rel_out):
    rows = left16.shape[1]
    product = weight[...] * target[...]
    probe[...] = product.astype(BF16)
    probe_rows[...] = half_rows(product.astype(BF16).astype(F32))
    gp[...] = jnp.zeros_like(gp)

    def part(i, carry):
        cut = lanes_at(i, STEP)
        lgrad[:, cut], more = negatives(left16[:, cut], probe[...], probe_rows[...], times_at(count_l, i), number)
        gp[...] += more
        return carry

    lax.fori_loop(0, rows // STEP, part, 0)
    depth = weight.shape[0]
    w, s, t = weight[...], source[...], target[...]
    coef = -jax.nn.sigmoid(-jnp.sum(s * w * t, axis=0, keepdims=True))
    to_src[0:depth, :], to_src[depth:, :] = split(coef * w * t + gq[...] * w, 2)
    to_dst[0:depth, :], to_dst[depth:, :] = split(coef * w * s + gp[...] * w, 2)
    g_weight = coef * s * t + gq[...] * s + gp[...] * t
    rel_out[...] = rel_in[...] + sum(mul(kind[...], p, NT) for p in split(g_weight, 2))


def adagrad(slab, state, grad, edges, table, start, out, new_state, send=None):
    depth = grad.shape[0]

    def part(i, carry):
        cut = lanes_at(i, STEP)
        hits = table[:, lanes_at(i + start // STEP, STEP)]
        g = grad[:, cut] + mul(edges[0:depth, :], hits, NN) + mul(edges[depth:, :], hits, NN)
        new = state[:, cut] + jnp.sum(g * g, axis=0, keepdims=True) * (1.0 / depth)
        new_state[:, cut] = new
        out[0:depth, cut] = slab[0:depth, cut] - g * (rate * lax.rsqrt(new))
        if send is not None:
            send(i).start()
        return carry

    lax.fori_loop(0, grad.shape[1] // STEP, part, 0)


def sender(result, to, start, sems):
    def copy(i):
        here = lanes_at(i, STEP)
        there = lanes_at(i + start // STEP, STEP)
        return pltpu.make_async_copy(result.at[:, here], to.at[:, there], sems.at[i + start // STEP])

    return copy


def wait_all(copy, count):
    def one(i, carry):
        copy(i).wait()
        return carry

    lax.fori_loop(0, count, one, 0)


def finish_last(left, lstate, right, rstate, lgrad, rgrads, to_src, to_dst, oh_src, oh_dst, spare, left_out, right_out, sems):
    start = 0
    sent = []
    for piece, state, grad in zip(right, rstate, rgrads):
        copy = sender(grad, right_out, start, sems.at[0])
        adagrad(piece, state, grad, to_dst, oh_dst, start, grad, spare, copy)
        sent.append((copy, piece.shape[1] // STEP))
        start += piece.shape[1]
    copy = sender(lgrad, left_out, 0, sems.at[1])
    adagrad(left, lstate, lgrad, to_src, oh_src, 0, lgrad, spare, copy)
    sent.append((copy, left.shape[1] // STEP))
    for copy, count in sent:
        wait_all(copy, count)


def on_parity(parity):
    return pl.when(lax.axis_index("blk") % 2 == parity)


def pieces_of(rows, eighths):
    sizes = [rows // 8 * n for n in eighths]
    return [(sum(sizes[:i]), size) for i, size in enumerate(sizes)]


def train(parity, step, number, last, kept, takes, gives, *refs):
    refs = list(refs)
    (left, lstate, rstate_in, relations, rel_in, src, dst, rid, nsrc, ndst) = refs[:10]
    right = refs[10 : 10 + takes]
    refs = refs[10 + takes + kept :]
    left_out, lstate_out, rel_out = refs[:3]
    right_out = refs[3 : 3 + len(gives)]
    (weight, source, query, query_rows, left16, oh_src, oh_dst, count_l, count_r, kind,
     target, gq, rgrad, probe, probe_rows, gp, lgrad, to_src, to_dst, spare, sems) = refs[3 + len(gives) :]
    depth, rows = left.shape
    lstate_out[...] = lstate[...]
    rel_out[...] = rel_in[...]

    @on_parity(parity)
    def _():
        prepare(step, left, relations, src, dst, rid, nsrc, ndst,
                weight, source, query, query_rows, left16, oh_src, oh_dst, count_l, count_r, kind)
        grads = []
        at = 0
        for piece in right:
            grads.append(rgrad.at[:, at : at + piece.shape[1]])
            take_piece(number, at, piece, query, query_rows, oh_dst, count_r, target, gq, grads[-1])
            at += piece.shape[1]
        join(number, weight, source, target, gq, left16, count_l, kind, rel_in, probe, probe_rows, gp, lgrad, to_src, to_dst, rel_out)
        if last:
            states = [piece.at[depth : depth + 1] for piece in right]
            finish_last(left, lstate, right, states, lgrad, grads, to_src, to_dst, oh_src, oh_dst, spare, left_out, right_out[0], sems)
        else:
            for (at, size), out in zip(pieces_of(rows, gives), right_out):
                cut = slice(at, at + size)
                adagrad(right[0].at[:, cut], rstate_in.at[:, cut], rgrad.at[:, cut], to_dst, oh_dst, at, out, spare)
                out[depth : depth + 8, :] = jnp.broadcast_to(spare[:, 0:size], (8, size))
            adagrad(left, lstate, lgrad, to_src, oh_src, 0, left_out, lstate_out)


def shape(*dims, dtype=F32):
    return jax.ShapeDtypeStruct(dims, dtype)


def prepared_shapes(depth, rows, edges, kinds):
    return (
        shape(depth, edges), shape(depth, edges), shape(depth, edges, dtype=BF16), shape(edges, depth, dtype=BF16),
        shape(depth, rows, dtype=BF16), shape(edges, rows, dtype=BF16), shape(edges, rows, dtype=BF16),
        shape(rows // LANES, LANES), shape(rows // LANES, LANES), shape(kinds, edges, dtype=BF16),
    )


def scratch(shapes):
    return [pltpu.VMEM(s.shape, s.dtype) for s in shapes]


def call(kernel, name, operands, shapes, in_large=(), out_large=(), scratch_shapes=(), aliases=None):
    vmem = pl.BlockSpec(memory_space=pltpu.VMEM)
    large = pl.BlockSpec(memory_space=pl.ANY)
    return pl.pallas_call(
        kernel,
        out_shape=tuple(shapes),
        in_specs=[large if i in in_large else vmem for i in range(len(operands))],
        out_specs=tuple(large if i in out_large else vmem for i in range(len(shapes))),
        scratch_shapes=list(scratch_shapes),
        input_output_aliases=aliases or {},
        compiler_params=pltpu.CompilerParams(vmem_limit_bytes=VMEM_LIMIT),
        cost_estimate=pl.CostEstimate(flops=1_000_000, bytes_accessed=100_000, transcendentals=0),
        name=name,
    )(*operands)


def trained(parity, step, gives, left, lstate, right, rstate, relations, rel, index, keep=()):
    depth, rows = left.shape
    edges = index[0].shape[1]
    number = float(index[3].shape[1])
    last = not gives
    blocks = [shape(depth + 8, size) for _at, size in pieces_of(rows, gives)] or [shape(depth, rows)]
    edge = shape(depth, edges)
    edge16 = shape(depth, edges, dtype=BF16)
    pair16 = shape(2 * depth, edges, dtype=BF16)
    slab = shape(depth, rows)
    inner = [edge, edge, slab, edge16, shape(edges, depth, dtype=BF16), edge, slab, pair16, pair16, shape(1, rows)]
    left_out, lstate_out, rel_out, *right_out = call(
        functools.partial(train, parity, step, number, last, len(keep), len(right), gives or (8,)),
        "round%d_parity%d" % (step, parity),
        [left, lstate, rstate, relations, rel, *index, *right, *keep],
        [slab, shape(1, rows), shape(*relations.shape), *blocks],
        out_large=(0, 3) if last else (),
        scratch_shapes=[
            *scratch(prepared_shapes(depth, rows, edges, relations.shape[0])),
            *scratch(inner),
            pltpu.SemaphoreType.DMA((2, rows // STEP)),
        ],
        aliases={10 + len(right) + i: 0 for i in range(len(keep))},
    )
    return left_out, lstate_out, right_out, rel_out


def last_round(parity, step, left, lstate, far, relations, rel, index, keep):
    depth, rows = left.shape
    edges = index[0].shape[1]
    number = float(index[3].shape[1])
    edge = shape(depth, edges)
    pair16 = shape(2 * depth, edges, dtype=BF16)
    slab = shape(depth, rows)

    def run(body):
        def kernel(*refs):
            @on_parity(parity)
            def _():
                body(*refs)

        return kernel

    (weight, source, query, query_rows, left16, oh_src, oh_dst, count_l, count_r, kind) = call(
        run(functools.partial(prepare, step)), "last_prepare",
        [left, relations, *index], prepared_shapes(depth, rows, edges, relations.shape[0]),
    )
    target = gq = None
    rgrads = []
    at = 0
    for i, piece in enumerate(far):
        held = [] if i == 0 else [target, gq]

        def body(piece, query, query_rows, oh_dst, count_r, *rest, at=at, held=len(held)):
            take_piece(number, at, piece, query, query_rows, oh_dst, count_r, *rest[held:])

        target, gq, rgrad = call(
            run(body), "last_piece%d" % i,
            [piece, query, query_rows, oh_dst, count_r, *held],
            [edge, edge, shape(depth, piece.shape[1])],
            aliases={5 + k: k for k in range(len(held))},
        )
        rgrads.append(rgrad)
        at += piece.shape[1]

    def join_body(weight, source, target, gq, left16, count_l, kind, rel_in, lgrad, to_src, to_dst, rel_out, probe, probe_rows, gp):
        rel_out[...] = rel_in[...]

        @on_parity(parity)
        def _():
            join(number, weight, source, target, gq, left16, count_l, kind, rel_in,
                 probe, probe_rows, gp, lgrad, to_src, to_dst, rel_out)

    lgrad, to_src, to_dst, rel = call(
        join_body, "last_join",
        [weight, source, target, gq, left16, count_l, kind, rel],
        [slab, pair16, pair16, shape(*relations.shape)],
        scratch_shapes=scratch([shape(depth, edges, dtype=BF16), shape(edges, depth, dtype=BF16), edge]),
    )

    def update():
        count = len(far)

        def body(left, lstate, lgrad, to_src, to_dst, oh_src, oh_dst, *rest):
            pieces = rest[:count]
            grads = rest[count : 2 * count]
            left_out, right_out, spare, sems = rest[2 * count + 2 :]
            states = [piece.at[depth : depth + 1] for piece in pieces]
            finish_last(left, lstate, pieces, states, lgrad, grads, to_src, to_dst, oh_src, oh_dst, spare, left_out, right_out, sems)

        operands = [left, lstate, lgrad, to_src, to_dst, oh_src, oh_dst, *far, *rgrads, *keep]
        places = (len(operands) - 2, len(operands) - 1)
        return call(
            run(body), "last_update", operands, [slab, slab], in_large=places, out_large=(0, 1),
            scratch_shapes=[pltpu.VMEM((1, rows), F32), pltpu.SemaphoreType.DMA((2, rows // STEP))],
            aliases={places[0]: 0, places[1]: 1},
        )

    return rel, update


def local(
    left_slab, left_state, right_slab, right_state, relations, relation_state,
    src_index, dst_index, relation_id, neg_source, neg_target,
):
    peers = lax.axis_size("blk")
    inside = [(i, i + 1) for i in range(0, peers, 2)]
    swap = inside + [(i + 1, i) for i in range(0, peers, 2)]
    across = [(i, (i + 1) % peers) for i in range(1, peers, 2)]
    skip = [(i, (i + 2) % peers) for i in range(0, peers, 2)]
    index = (src_index, dst_index, relation_id, neg_source, neg_target)
    left = left_slab.T
    right = right_slab.T
    rows = left.shape[1]
    lstate = left_state.reshape(1, rows)
    right_far = lax.ppermute(right, "blk", across)
    right_near = lax.ppermute(right, "blk", inside)
    state_near = lax.ppermute(right_state, "blk", swap)
    state_far = lax.ppermute(state_near, "blk", skip).reshape(1, rows)
    state_near = state_near.reshape(1, rows)
    rel = jnp.zeros(relations.shape, F32)
    left_a, lstate, far, rel = trained(1, 0, FAR, left, lstate, [right_near], state_near, relations, rel, index)
    far = [lax.ppermute(piece, "blk", across) for piece in far]
    left_a, lstate, near, rel = trained(
        0, 0, NEAR, left, lstate, [right_far], state_far, relations, rel, index, (left_a,)
    )
    near = [lax.ppermute(piece, "blk", inside) for piece in near]
    left_b, lstate, right_b, rel = trained(1, 1, (), left_a, lstate, near, state_near, relations, rel, index)
    rel, update = last_round(0, 1, left_a, lstate, far, relations, rel, index, (left_b, *right_b))
    if lax.axis_size("rel") == 2:
        rel = rel + lax.ppermute(rel, "rel", [(0, 1), (1, 0)])
    else:
        rel = lax.psum(rel, "rel")
    left_b, right_b = update()
    new_rstate = relation_state + jnp.mean(rel * rel, axis=1)
    relations_out = relations - rate * rel / jnp.sqrt(new_rstate)[:, None]
    return (left_b.T, right_b.T, relations_out[None])


def solution(mesh):
    in_specs = (
        P(("blk", "rel"), None),
        P(("blk", "rel")),
        P(("blk", "rel"), None),
        P(("blk", "rel")),
        P(),
        P(),
        P(None, ("blk", "rel")),
        P(None, ("blk", "rel")),
        P(None, ("blk", "rel")),
        P(None, ("blk", "rel")),
        P(None, ("blk", "rel")),
    )
    out_specs = (P(("blk", "rel"), None), P(("blk", "rel"), None), P("blk", None, None))
    return jax.shard_map(local, mesh=mesh, in_specs=in_specs, out_specs=out_specs, check_vma=False)
```

```python
import functools

import jax
import jax.numpy as jnp
from jax import lax
from jax.experimental import pallas as pl
from jax.experimental.pallas import tpu as pltpu
from jax.sharding import PartitionSpec as P

rate = 0.1
F32 = jnp.float32
BF16 = jnp.bfloat16
LANES = 128
NEAR = (4, 4)
NEAR_FIRST = (4, 4)
FAR = (6, 1, 1)
VMEM_LIMIT = 30 * 2**20

NN = (((1,), (0,)), ((), ()))
NT = (((1,), (1,)), ((), ()))
TN = (((0,), (0,)), ((), ()))


def mul(a, b, dims):
    return lax.dot_general(a, b, dims, preferred_element_type=F32)


def split(x, parts):
    out = []
    for _ in range(parts):
        part = x.astype(BF16)
        out.append(part)
        x = x - part.astype(F32)
    return out


def lanes_at(i, size):
    return pl.ds(pl.multiple_of(i * size, size), size)


def step_of(rows):
    return 512 if rows % 512 == 0 else 256


def row_onehot(idx, table):
    count, rows = table.shape
    col = jnp.broadcast_to(idx, (LANES, count)).T
    lane = lax.broadcasted_iota(jnp.int32, (count, LANES), 1)

    def tile(t, carry):
        hit = col == lane + t * LANES
        table[:, lanes_at(t, LANES)] = jnp.where(hit, 1.0, 0.0).astype(BF16)
        return carry

    lax.fori_loop(0, rows // LANES, tile, 0)


def row_counts(idx, rows):
    count = idx.shape[1]
    high = lax.broadcasted_iota(jnp.int32, (rows // LANES, count), 0)
    low = lax.broadcasted_iota(jnp.int32, (LANES, count), 0)
    high_hit = jnp.where(idx // LANES == high, 1.0, 0.0).astype(BF16)
    low_hit = jnp.where(idx % LANES == low, 1.0, 0.0).astype(BF16)
    return mul(high_hit, low_hit, NT)


def times_at(counts, i, size):
    tiles = size // LANES
    return jnp.concatenate([counts[pl.ds(i * tiles + t, 1), :] for t in range(tiles)], axis=1)


def half_rows(x):
    return (0.5 * x).T.astype(BF16)


def negatives(rows16, query, query_rows, times, number):
    half = 0.5 / number
    weight = (jnp.tanh(mul(query_rows, rows16, NN)) * half + half).astype(BF16)
    often = (weight.astype(F32) * times).astype(BF16)
    return mul(query, weight, NN) * times, mul(rows16, often, NT)


def prepare(step, left, relations, src, dst, rid, nsrc, ndst,
            weight, source, query, query_rows, left16, oh_src, oh_dst, count_l, count_r, kind):
    rows = left.shape[1]
    here = slice(step, step + 1)
    row_onehot(src[here, :], oh_src)
    row_onehot(dst[here, :], oh_dst)
    count_l[...] = row_counts(nsrc[here, :], rows)
    count_r[...] = row_counts(ndst[here, :], rows)
    kinds = lax.broadcasted_iota(jnp.int32, kind.shape, 0)
    kind[...] = jnp.where(rid[here, :] == kinds, 1.0, 0.0).astype(BF16)
    weight[...] = sum(mul(part, kind[...], TN) for part in split(relations[...], 3))
    source[...] = jnp.zeros_like(source)

    size = step_of(rows)

    def part(i, carry):
        cut = lanes_at(i, size)
        parts = split(left[:, cut], 3)
        left16[:, cut] = parts[0]
        source[...] += sum(mul(p, oh_src[:, cut], NT) for p in parts)
        return carry

    lax.fori_loop(0, rows // size, part, 0)
    product = source[...] * weight[...]
    query[...] = product.astype(BF16)
    query_rows[...] = half_rows(product.astype(BF16).astype(F32))


def take_piece(number, start, piece, query, query_rows, oh_dst, count_r, target, gq, rgrad):
    depth = target.shape[0]
    if start == 0:
        target[...] = jnp.zeros_like(target)
        gq[...] = jnp.zeros_like(gq)

    size = step_of(piece.shape[1])

    def part(i, carry):
        cut = lanes_at(i, size)
        parts = split(piece[0:depth, cut], 3)
        hits = oh_dst[:, lanes_at(i + start // size, size)]
        target[...] += sum(mul(p, hits, NT) for p in parts)
        times = times_at(count_r, i + start // size, size)
        rgrad[:, cut], more = negatives(parts[0], query[...], query_rows[...], times, number)
        gq[...] += more
        return carry

    lax.fori_loop(0, piece.shape[1] // size, part, 0)


def join(number, weight, source, target, gq, left16, count_l, kind, rel_in, probe, probe_rows, gp, lgrad, to_src, to_dst, rel_out):
    rows = left16.shape[1]
    product = weight[...] * target[...]
    probe[...] = product.astype(BF16)
    probe_rows[...] = half_rows(product.astype(BF16).astype(F32))
    gp[...] = jnp.zeros_like(gp)

    size = step_of(rows)

    def part(i, carry):
        cut = lanes_at(i, size)
        lgrad[:, cut], more = negatives(left16[:, cut], probe[...], probe_rows[...], times_at(count_l, i, size), number)
        gp[...] += more
        return carry

    lax.fori_loop(0, rows // size, part, 0)
    depth = weight.shape[0]
    w, s, t = weight[...], source[...], target[...]
    coef = -jax.nn.sigmoid(-jnp.sum(s * w * t, axis=0, keepdims=True))
    to_src[0:depth, :], to_src[depth:, :] = split(coef * w * t + gq[...] * w, 2)
    to_dst[0:depth, :], to_dst[depth:, :] = split(coef * w * s + gp[...] * w, 2)
    g_weight = coef * s * t + gq[...] * s + gp[...] * t
    rel_out[...] = rel_in[...] + sum(mul(kind[...], p, NT) for p in split(g_weight, 2))


def adagrad(slab, state, grad, edges, table, start, out, new_state, send=None):
    depth = grad.shape[0]
    size = step_of(grad.shape[1])

    def part(i, carry):
        cut = lanes_at(i, size)
        hits = table[:, lanes_at(i + start // size, size)]
        g = grad[:, cut] + mul(edges[0:depth, :], hits, NN) + mul(edges[depth:, :], hits, NN)
        new = state[:, cut] + jnp.sum(g * g, axis=0, keepdims=True) * (1.0 / depth)
        new_state[:, cut] = new
        out[0:depth, cut] = slab[0:depth, cut] - g * (rate * lax.rsqrt(new))
        if send is not None:
            send(i).start()
        return carry

    lax.fori_loop(0, grad.shape[1] // size, part, 0)


def sender(result, to, start, sems):
    size = step_of(result.shape[1])

    def copy(i):
        here = lanes_at(i, size)
        there = lanes_at(i + start // size, size)
        return pltpu.make_async_copy(result.at[:, here], to.at[:, there], sems.at[i + start // size])

    return copy


def wait_all(copy, count):
    def one(i, carry):
        copy(i).wait()
        return carry

    lax.fori_loop(0, count, one, 0)


def finish_last(left, lstate, right, rstate, lgrad, rgrads, to_src, to_dst, oh_src, oh_dst, spare, left_out, right_out, sems):
    start = 0
    sent = []
    for piece, state, grad in zip(right, rstate, rgrads):
        copy = sender(grad, right_out, start, sems.at[0])
        adagrad(piece, state, grad, to_dst, oh_dst, start, grad, spare, copy)
        sent.append((copy, piece.shape[1] // step_of(piece.shape[1])))
        start += piece.shape[1]
    copy = sender(lgrad, left_out, 0, sems.at[1])
    adagrad(left, lstate, lgrad, to_src, oh_src, 0, lgrad, spare, copy)
    sent.append((copy, left.shape[1] // step_of(left.shape[1])))
    for copy, count in sent:
        wait_all(copy, count)


def on_parity(parity):
    return pl.when(lax.axis_index("blk") % 2 == parity)


def pieces_of(rows, eighths):
    sizes = [rows // 8 * n for n in eighths]
    return [(sum(sizes[:i]), size) for i, size in enumerate(sizes)]


def rows_of(pieces, at, size):
    found = []
    start = 0
    for piece in pieces:
        begin, end = max(at, start), min(at + size, start + piece.shape[1])
        if begin < end:
            found.append((piece.at[:, begin - start : end - start], begin, end - begin))
        start += piece.shape[1]
    return found


def train(parity, number, last, kept, takes, gives, *refs):
    refs = list(refs)
    (left, lstate, rstate_in, rel_in) = refs[:4]
    (weight, source, query, query_rows, left16, oh_src, oh_dst, count_l, count_r, kind) = refs[4:14]
    right = refs[14 : 14 + takes]
    refs = refs[14 + takes + kept :]
    left_out, lstate_out, rel_out = refs[:3]
    right_out = refs[3 : 3 + len(gives)]
    (target, gq, rgrad, probe, probe_rows, gp, lgrad, to_src, to_dst, spare, sems) = refs[3 + len(gives) :]
    depth, rows = left.shape
    lstate_out[...] = lstate[...]
    rel_out[...] = rel_in[...]

    @on_parity(parity)
    def _():
        grads = []
        at = 0
        for piece in right:
            grads.append(rgrad.at[:, at : at + piece.shape[1]])
            take_piece(number, at, piece, query, query_rows, oh_dst, count_r, target, gq, grads[-1])
            at += piece.shape[1]
        join(number, weight, source, target, gq, left16, count_l, kind, rel_in, probe, probe_rows, gp, lgrad, to_src, to_dst, rel_out)
        if last:
            states = [piece.at[depth : depth + 1] for piece in right]
            finish_last(left, lstate, right, states, lgrad, grads, to_src, to_dst, oh_src, oh_dst, spare, left_out, right_out[0], sems)
        else:
            for (at, size), out in zip(pieces_of(rows, gives), right_out):
                for old, begin, length in rows_of(right, at, size):
                    cut = slice(begin, begin + length)
                    here = slice(begin - at, begin - at + length)
                    adagrad(old, rstate_in.at[:, cut], rgrad.at[:, cut], to_dst, oh_dst, begin, out.at[:, here], spare.at[:, here])
                out[depth : depth + 8, :] = jnp.broadcast_to(spare[:, 0:size], (8, size))
            adagrad(left, lstate, lgrad, to_src, oh_src, 0, left_out, lstate_out)


def shape(*dims, dtype=F32):
    return jax.ShapeDtypeStruct(dims, dtype)


def prepared_shapes(depth, rows, edges, kinds):
    return (
        shape(depth, edges), shape(depth, edges), shape(depth, edges, dtype=BF16), shape(edges, depth, dtype=BF16),
        shape(depth, rows, dtype=BF16), shape(edges, rows, dtype=BF16), shape(edges, rows, dtype=BF16),
        shape(rows // LANES, LANES), shape(rows // LANES, LANES), shape(kinds, edges, dtype=BF16),
    )


def scratch(shapes):
    return [pltpu.VMEM(s.shape, s.dtype) for s in shapes]


def call(kernel, name, operands, shapes, in_large=(), out_large=(), scratch_shapes=(), aliases=None):
    vmem = pl.BlockSpec(memory_space=pltpu.VMEM)
    large = pl.BlockSpec(memory_space=pl.ANY)
    return pl.pallas_call(
        kernel,
        out_shape=tuple(shapes),
        in_specs=[large if i in in_large else vmem for i in range(len(operands))],
        out_specs=tuple(large if i in out_large else vmem for i in range(len(shapes))),
        scratch_shapes=list(scratch_shapes),
        input_output_aliases=aliases or {},
        compiler_params=pltpu.CompilerParams(vmem_limit_bytes=VMEM_LIMIT),
        cost_estimate=pl.CostEstimate(flops=1_000_000, bytes_accessed=100_000, transcendentals=0),
        name=name,
    )(*operands)


def prepared(step, left, relations, index):
    depth, rows = left.shape
    return call(
        functools.partial(prepare, step), "prepare%d" % step, [left, relations, *index],
        prepared_shapes(depth, rows, index[0].shape[1], relations.shape[0]),
    )


def trained(parity, name, number, gives, left, lstate, right, rstate, rel, ready, keep=()):
    depth, rows = left.shape
    edges = ready[0].shape[1]
    last = not gives
    blocks = [shape(depth + 8, size) for _at, size in pieces_of(rows, gives)] or [shape(depth, rows)]
    edge = shape(depth, edges)
    edge16 = shape(depth, edges, dtype=BF16)
    pair16 = shape(2 * depth, edges, dtype=BF16)
    slab = shape(depth, rows)
    inner = [edge, edge, slab, edge16, shape(edges, depth, dtype=BF16), edge, slab, pair16, pair16, shape(1, rows)]
    left_out, lstate_out, rel_out, *right_out = call(
        functools.partial(train, parity, number, last, len(keep), len(right), gives or (8,)),
        name,
        [left, lstate, rstate, rel, *ready, *right, *keep],
        [slab, shape(1, rows), shape(*rel.shape), *blocks],
        out_large=(0, 3) if last else (),
        scratch_shapes=[*scratch(inner), pltpu.SemaphoreType.DMA((2, rows // 256))],
        aliases={14 + len(right) + i: 0 for i in range(len(keep))},
    )
    return left_out, lstate_out, right_out, rel_out


def last_round(parity, number, left, lstate, far, rel, ready, keep):
    depth, rows = left.shape
    (weight, source, query, query_rows, left16, oh_src, oh_dst, count_l, count_r, kind) = ready
    edges = weight.shape[1]
    edge = shape(depth, edges)
    pair16 = shape(2 * depth, edges, dtype=BF16)
    slab = shape(depth, rows)

    def run(body):
        def kernel(*refs):
            @on_parity(parity)
            def _():
                body(*refs)

        return kernel

    target = gq = None
    rgrads = []
    at = 0
    for i, piece in enumerate(far):
        held = [] if i == 0 else [target, gq]

        def body(piece, query, query_rows, oh_dst, count_r, *rest, at=at, held=len(held)):
            take_piece(number, at, piece, query, query_rows, oh_dst, count_r, *rest[held:])

        target, gq, rgrad = call(
            run(body), "last_piece%d" % i,
            [piece, query, query_rows, oh_dst, count_r, *held],
            [edge, edge, shape(depth, piece.shape[1])],
            aliases={5 + k: k for k in range(len(held))},
        )
        rgrads.append(rgrad)
        at += piece.shape[1]

    def join_body(weight, source, target, gq, left16, count_l, kind, rel_in, lgrad, to_src, to_dst, rel_out, probe, probe_rows, gp):
        rel_out[...] = rel_in[...]

        @on_parity(parity)
        def _():
            join(number, weight, source, target, gq, left16, count_l, kind, rel_in,
                 probe, probe_rows, gp, lgrad, to_src, to_dst, rel_out)

    lgrad, to_src, to_dst, rel = call(
        join_body, "last_join",
        [weight, source, target, gq, left16, count_l, kind, rel],
        [slab, pair16, pair16, shape(*rel.shape)],
        scratch_shapes=scratch([shape(depth, edges, dtype=BF16), shape(edges, depth, dtype=BF16), edge]),
    )

    def update():
        count = len(far)

        def body(left, lstate, lgrad, to_src, to_dst, oh_src, oh_dst, *rest):
            pieces = rest[:count]
            grads = rest[count : 2 * count]
            left_out, right_out, spare, sems = rest[2 * count + 2 :]
            states = [piece.at[depth : depth + 1] for piece in pieces]
            finish_last(left, lstate, pieces, states, lgrad, grads, to_src, to_dst, oh_src, oh_dst, spare, left_out, right_out, sems)

        operands = [left, lstate, lgrad, to_src, to_dst, oh_src, oh_dst, *far, *rgrads, *keep]
        places = (len(operands) - 2, len(operands) - 1)
        return call(
            run(body), "last_update", operands, [slab, slab], in_large=places, out_large=(0, 1),
            scratch_shapes=[pltpu.VMEM((1, rows), F32), pltpu.SemaphoreType.DMA((2, rows // 256))],
            aliases={places[0]: 0, places[1]: 1},
        )

    return rel, update


def local(
    left_slab, left_state, right_slab, right_state, relations, relation_state,
    src_index, dst_index, relation_id, neg_source, neg_target,
):
    peers = lax.axis_size("blk")
    inside = [(i, i + 1) for i in range(0, peers, 2)]
    swap = inside + [(i + 1, i) for i in range(0, peers, 2)]
    across = [(i, (i + 1) % peers) for i in range(1, peers, 2)]
    skip = [(i, (i + 2) % peers) for i in range(0, peers, 2)]
    index = (src_index, dst_index, relation_id, neg_source, neg_target)
    left = left_slab.T
    right = right_slab.T
    rows = left.shape[1]
    lstate = left_state.reshape(1, rows)
    number = float(neg_source.shape[1])
    right_far = lax.ppermute(right, "blk", across)
    right_near = [lax.ppermute(right[:, at : at + size], "blk", inside) for at, size in pieces_of(rows, NEAR_FIRST)]
    state_near = lax.ppermute(right_state, "blk", swap)
    state_far = lax.ppermute(state_near, "blk", skip).reshape(1, rows)
    state_near = state_near.reshape(1, rows)
    rel = jnp.zeros(relations.shape, F32)
    ready = prepared(0, left, relations, index)
    left_a, lstate, far, rel = trained(1, "first_near", number, FAR, left, lstate, right_near, state_near, rel, ready)
    far = [lax.ppermute(piece, "blk", across) for piece in far]
    left_a, lstate, near, rel = trained(
        0, "first_far", number, NEAR, left, lstate, [right_far], state_far, rel, ready, (left_a,)
    )
    near = [lax.ppermute(piece, "blk", inside) for piece in near]
    ready = prepared(1, left_a, relations, index)
    left_b, lstate, right_b, rel = trained(1, "last_near", number, (), left_a, lstate, near, state_near, rel, ready)
    rel, update = last_round(0, number, left_a, lstate, far, rel, ready, (left_b, *right_b))
    if lax.axis_size("rel") == 2:
        rel = rel + lax.ppermute(rel, "rel", [(0, 1), (1, 0)])
    else:
        rel = lax.psum(rel, "rel")
    left_b, right_b = update()
    new_rstate = relation_state + jnp.mean(rel * rel, axis=1)
    relations_out = relations - rate * rel / jnp.sqrt(new_rstate)[:, None]
    return (left_b.T, right_b.T, relations_out[None])


def solution(mesh):
    in_specs = (
        P(("blk", "rel"), None),
        P(("blk", "rel")),
        P(("blk", "rel"), None),
        P(("blk", "rel")),
        P(),
        P(),
        P(None, ("blk", "rel")),
        P(None, ("blk", "rel")),
        P(None, ("blk", "rel")),
        P(None, ("blk", "rel")),
        P(None, ("blk", "rel")),
    )
    out_specs = (P(("blk", "rel"), None), P(("blk", "rel"), None), P("blk", None, None))
    return jax.shard_map(local, mesh=mesh, in_specs=in_specs, out_specs=out_specs, check_vma=False)
```

```python
import functools

import jax
import jax.numpy as jnp
from jax import lax
from jax.experimental import pallas as pl
from jax.experimental.pallas import tpu as pltpu
from jax.sharding import PartitionSpec as P

rate = 0.1
F32 = jnp.float32
BF16 = jnp.bfloat16
LANES = 128
NEAR = (4, 4)
STATE = 1
NEAR_FIRST = (4, 4)
FAR = (6, 1, 1)
VMEM_LIMIT = 30 * 2**20

NN = (((1,), (0,)), ((), ()))
NT = (((1,), (1,)), ((), ()))
TN = (((0,), (0,)), ((), ()))


def mul(a, b, dims):
    return lax.dot_general(a, b, dims, preferred_element_type=F32)


def split(x, parts):
    out = []
    for _ in range(parts):
        part = x.astype(BF16)
        out.append(part)
        x = x - part.astype(F32)
    return out


def lanes_at(i, size):
    if isinstance(i, int):
        return slice(i * size, (i + 1) * size)
    return pl.ds(pl.multiple_of(i * size, size), size)


def step_of(rows):
    return 512 if rows % 512 == 0 else 256


def each(count, body, fixed=False):
    if fixed:
        for i in range(count):
            body(i)
        return

    def one(i, carry):
        body(i)
        return carry

    lax.fori_loop(0, count, one, 0)


def row_onehot(idx, table):
    count, rows = table.shape
    col = jnp.broadcast_to(idx, (LANES, count)).T
    lane = lax.broadcasted_iota(jnp.int32, (count, LANES), 1)

    def tile(t):
        hit = col == lane + t * LANES
        table[:, lanes_at(t, LANES)] = jnp.where(hit, 1.0, 0.0).astype(BF16)

    each(rows // LANES, tile)


def row_counts(idx, rows):
    count = idx.shape[1]
    high = lax.broadcasted_iota(jnp.int32, (rows // LANES, count), 0)
    low = lax.broadcasted_iota(jnp.int32, (LANES, count), 0)
    high_hit = jnp.where(idx // LANES == high, 1.0, 0.0).astype(BF16)
    low_hit = jnp.where(idx % LANES == low, 1.0, 0.0).astype(BF16)
    return mul(high_hit, low_hit, NT)


def times_at(counts, i, size):
    tiles = size // LANES
    return jnp.concatenate([counts[pl.ds(i * tiles + t, 1), :] for t in range(tiles)], axis=1)


def half_rows(x):
    return (0.5 * x).T.astype(BF16)


def negatives(rows16, query, query_rows, times, number):
    half = 0.5 / number
    weight = (jnp.tanh(mul(query_rows, rows16, NN)) * half + half).astype(BF16)
    often = (weight.astype(F32) * times).astype(BF16)
    return mul(query, weight, NN) * times, mul(rows16, often, NT)


def prepare(step, left, relations, src, dst, rid, nsrc, ndst,
            weight, source, query, query_rows, left16, oh_src, oh_dst, count_l, count_r, kind):
    rows = left.shape[1]
    here = slice(step, step + 1)
    row_onehot(src[here, :], oh_src)
    row_onehot(dst[here, :], oh_dst)
    count_l[...] = row_counts(nsrc[here, :], rows)
    count_r[...] = row_counts(ndst[here, :], rows)
    kinds = lax.broadcasted_iota(jnp.int32, kind.shape, 0)
    kind[...] = jnp.where(rid[here, :] == kinds, 1.0, 0.0).astype(BF16)
    weight[...] = sum(mul(part, kind[...], TN) for part in split(relations[...], 3))
    source[...] = jnp.zeros_like(source)

    size = step_of(rows)

    def part(i):
        cut = lanes_at(i, size)
        parts = split(left[:, cut], 3)
        left16[:, cut] = parts[0]
        source[...] += sum(mul(p, oh_src[:, cut], NT) for p in parts)

    each(rows // size, part)
    product = source[...] * weight[...]
    query[...] = product.astype(BF16)
    query_rows[...] = half_rows(product.astype(BF16).astype(F32))


def take_piece(number, start, piece, query, query_rows, oh_dst, count_r, target, gq, rgrad, fixed=False):
    depth = target.shape[0]
    if start == 0:
        target[...] = jnp.zeros_like(target)
        gq[...] = jnp.zeros_like(gq)

    size = step_of(piece.shape[1])

    def part(i):
        cut = lanes_at(i, size)
        parts = split(piece[0:depth, cut], 3)
        hits = oh_dst[:, lanes_at(i + start // size, size)]
        target[...] += sum(mul(p, hits, NT) for p in parts)
        times = times_at(count_r, i + start // size, size)
        rgrad[:, cut], more = negatives(parts[0], query[...], query_rows[...], times, number)
        gq[...] += more

    each(piece.shape[1] // size, part, fixed)


def join(number, weight, source, target, gq, left16, count_l, kind, rel_in,
         probe, probe_rows, gp, lgrad, to_src, to_dst, rel_out, fixed=False):
    rows = left16.shape[1]
    product = weight[...] * target[...]
    probe[...] = product.astype(BF16)
    probe_rows[...] = half_rows(product.astype(BF16).astype(F32))
    gp[...] = jnp.zeros_like(gp)

    size = step_of(rows)

    def part(i):
        cut = lanes_at(i, size)
        lgrad[:, cut], more = negatives(left16[:, cut], probe[...], probe_rows[...], times_at(count_l, i, size), number)
        gp[...] += more

    each(rows // size, part, fixed)
    depth = weight.shape[0]
    w, s, t = weight[...], source[...], target[...]
    coef = -jax.nn.sigmoid(-jnp.sum(s * w * t, axis=0, keepdims=True))
    to_src[0:depth, :], to_src[depth:, :] = split(coef * w * t + gq[...] * w, 2)
    to_dst[0:depth, :], to_dst[depth:, :] = split(coef * w * s + gp[...] * w, 2)
    g_weight = coef * s * t + gq[...] * s + gp[...] * t
    rel_out[...] = rel_in[...] + sum(mul(kind[...], p, NT) for p in split(g_weight, 2))


def adagrad(slab, state, grad, edges, table, start, out, new_state, send=None, fixed=False):
    depth = grad.shape[0]
    size = step_of(grad.shape[1])

    def part(i):
        cut = lanes_at(i, size)
        hits = table[:, lanes_at(i + start // size, size)]
        g = grad[:, cut] + mul(edges[0:depth, :], hits, NN) + mul(edges[depth:, :], hits, NN)
        new = state[:, cut] + jnp.sum(g * g, axis=0, keepdims=True) * (1.0 / depth)
        new_state[:, cut] = new
        out[0:depth, cut] = slab[0:depth, cut] - g * (rate * lax.rsqrt(new))
        if send is not None:
            send(i).start()

    each(grad.shape[1] // size, part, fixed)


def sender(result, to, start, sems):
    size = step_of(result.shape[1])

    def copy(i):
        here = lanes_at(i, size)
        there = lanes_at(i + start // size, size)
        return pltpu.make_async_copy(result.at[:, here], to.at[:, there], sems.at[i + start // size])

    return copy


def update_and_send(pieces, state, grads, edges, table, new_state, to, sems, fixed=False):
    start = 0
    sent = []
    for piece, grad in zip(pieces, grads):
        rows = grad.shape[1]
        copy = sender(grad, to, start, sems)
        cut = slice(start, start + rows)
        adagrad(piece, state.at[:, cut], grad, edges, table, start, grad, new_state.at[:, cut], copy, fixed)
        sent.append((copy, rows // step_of(rows)))
        start += rows

    def wait():
        for copy, count in sent:
            each(count, lambda i, copy=copy: copy(i).wait(), fixed)

    return wait


def pack_state(state, piece, depth):
    size = state.shape[1] // 8
    for k in range(8):
        piece[depth + k : depth + k + 1, 0:size] = state[:, k * size : (k + 1) * size]


def unpack_state(piece, depth, state):
    size = state.shape[1] // 8
    for k in range(8):
        state[:, k * size : (k + 1) * size] = piece[depth + k : depth + k + 1, 0:size]


def on_parity(parity):
    return pl.when(lax.axis_index("blk") % 2 == parity)


def pieces_of(rows, eighths):
    sizes = [rows // 8 * n for n in eighths]
    return [(sum(sizes[:i]), size) for i, size in enumerate(sizes)]


def rows_of(pieces, at, size):
    found = []
    start = 0
    for piece in pieces:
        begin, end = max(at, start), min(at + size, start + piece.shape[1])
        if begin < end:
            found.append((piece.at[:, begin - start : end - start], begin, end - begin))
        start += piece.shape[1]
    return found


def train(parity, number, last, kept, takes, gives, *refs):
    refs = list(refs)
    (left, lstate, rstate_in, rel_in) = refs[:4]
    (weight, source, query, query_rows, left16, oh_src, oh_dst, count_l, count_r, kind) = refs[4:14]
    right = refs[14 : 14 + takes]
    refs = refs[14 + takes + kept :]
    left_out, lstate_out, rel_out = refs[:3]
    right_out = refs[3 : 3 + len(gives)]
    (target, gq, rgrad, probe, probe_rows, gp, lgrad, to_src, to_dst, rstate, spare, sems) = refs[3 + len(gives) :]
    depth, rows = left.shape
    lstate_out[...] = lstate[...]
    rel_out[...] = rel_in[...]

    @on_parity(parity)
    def _():
        grads = []
        at = 0
        for piece in right:
            grads.append(rgrad.at[:, at : at + piece.shape[1]])
            take_piece(number, at, piece, query, query_rows, oh_dst, count_r, target, gq, grads[-1])
            at += piece.shape[1]
        join(number, weight, source, target, gq, left16, count_l, kind, rel_in,
             probe, probe_rows, gp, lgrad, to_src, to_dst, rel_out)
        if last:
            unpack_state(right[STATE], depth, rstate)
            wait_right = update_and_send(right, rstate, grads, to_dst, oh_dst, spare, right_out[0], sems.at[0])
            wait_left = update_and_send([left], lstate, [lgrad], to_src, oh_src, spare, left_out, sems.at[1])
            wait_right()
            wait_left()
        else:
            for (at, size), out in zip(pieces_of(rows, gives), right_out):
                for old, begin, length in rows_of(right, at, size):
                    cut = slice(begin, begin + length)
                    here = slice(begin - at, begin - at + length)
                    adagrad(old, rstate_in.at[:, cut], rgrad.at[:, cut], to_dst, oh_dst, begin, out.at[:, here], spare.at[:, cut])
            pack_state(spare, right_out[STATE], depth)
            adagrad(left, lstate, lgrad, to_src, oh_src, 0, left_out, lstate_out)


def shape(*dims, dtype=F32):
    return jax.ShapeDtypeStruct(dims, dtype)


def prepared_shapes(depth, rows, edges, kinds):
    return (
        shape(depth, edges), shape(depth, edges), shape(depth, edges, dtype=BF16), shape(edges, depth, dtype=BF16),
        shape(depth, rows, dtype=BF16), shape(edges, rows, dtype=BF16), shape(edges, rows, dtype=BF16),
        shape(rows // LANES, LANES), shape(rows // LANES, LANES), shape(kinds, edges, dtype=BF16),
    )


def scratch(shapes):
    return [pltpu.VMEM(s.shape, s.dtype) for s in shapes]


def call(kernel, name, operands, shapes, in_large=(), out_large=(), scratch_shapes=(), aliases=None):
    vmem = pl.BlockSpec(memory_space=pltpu.VMEM)
    large = pl.BlockSpec(memory_space=pl.ANY)
    return pl.pallas_call(
        kernel,
        out_shape=tuple(shapes),
        in_specs=[large if i in in_large else vmem for i in range(len(operands))],
        out_specs=tuple(large if i in out_large else vmem for i in range(len(shapes))),
        scratch_shapes=list(scratch_shapes),
        input_output_aliases=aliases or {},
        compiler_params=pltpu.CompilerParams(vmem_limit_bytes=VMEM_LIMIT),
        cost_estimate=pl.CostEstimate(flops=1_000_000, bytes_accessed=100_000, transcendentals=0),
        name=name,
    )(*operands)


def prepared(step, left, relations, index):
    depth, rows = left.shape
    return call(
        functools.partial(prepare, step), "prepare%d" % step, [left, relations, *index],
        prepared_shapes(depth, rows, index[0].shape[1], relations.shape[0]),
    )


def trained(parity, name, number, gives, left, lstate, right, rstate, rel, ready, keep=()):
    depth, rows = left.shape
    edges = ready[0].shape[1]
    last = not gives
    blocks = [shape(depth, size) for _at, size in pieces_of(rows, gives or (8,))]
    if not last:
        blocks[STATE] = shape(depth + 8, blocks[STATE].shape[1])
    edge = shape(depth, edges)
    edge16 = shape(depth, edges, dtype=BF16)
    pair16 = shape(2 * depth, edges, dtype=BF16)
    slab = shape(depth, rows)
    inner = [edge, edge, slab, edge16, shape(edges, depth, dtype=BF16), edge, slab, pair16, pair16, shape(1, rows), shape(1, rows)]
    left_out, lstate_out, rel_out, *right_out = call(
        functools.partial(train, parity, number, last, len(keep), len(right), gives or (8,)),
        name,
        [left, lstate, rstate, rel, *ready, *right, *keep],
        [slab, shape(1, rows), shape(*rel.shape), *blocks],
        out_large=(0, 3) if last else (),
        scratch_shapes=[*scratch(inner), pltpu.SemaphoreType.DMA((2, rows // 256))],
        aliases={14 + len(right) + i: 0 for i in range(len(keep))},
    )
    return left_out, lstate_out, right_out, rel_out


def only_on(parity, body):
    def kernel(*refs):
        @on_parity(parity)
        def _():
            body(*refs)

    return kernel


def last_pieces(parity, number, far, ready, after):
    (_weight, _source, query, query_rows, _left16, _oh_src, oh_dst, _count_l, count_r, _kind) = ready
    depth, edges = query.shape
    target = gq = None
    rgrads = []
    at = 0
    for i, piece in enumerate(far):
        held = [after] if i == 0 else [target, gq]

        def body(piece, query, query_rows, oh_dst, count_r, *rest, at=at, held=len(held)):
            take_piece(number, at, piece, query, query_rows, oh_dst, count_r, *rest[held:], fixed=True)

        target, gq, rgrad = call(
            only_on(parity, body), "last_piece%d" % i,
            [piece, query, query_rows, oh_dst, count_r, *held],
            [shape(depth, edges), shape(depth, edges), shape(depth, piece.shape[1])],
            aliases={5: 0, 6: 1} if i else {},
        )
        rgrads.append(rgrad)
        at += piece.shape[1]
    return target, gq, rgrads


def last_join(parity, number, target, gq, rel, ready):
    (weight, source, _query, _query_rows, left16, _oh_src, _oh_dst, count_l, _count_r, kind) = ready
    depth, rows = left16.shape
    edges = weight.shape[1]
    pair16 = shape(2 * depth, edges, dtype=BF16)

    def body(weight, source, target, gq, left16, count_l, kind, rel_in, lgrad, to_src, to_dst, rel_out, probe, probe_rows, gp):
        rel_out[...] = rel_in[...]

        @on_parity(parity)
        def _():
            join(number, weight, source, target, gq, left16, count_l, kind, rel_in,
                 probe, probe_rows, gp, lgrad, to_src, to_dst, rel_out, fixed=True)

    return call(
        body, "last_join",
        [weight, source, target, gq, left16, count_l, kind, rel],
        [shape(depth, rows), pair16, pair16, shape(*rel.shape)],
        scratch_shapes=scratch([shape(depth, edges, dtype=BF16), shape(edges, depth, dtype=BF16), shape(depth, edges)]),
    )


def last_right(parity, far, rgrads, to_dst, oh_dst, keep):
    count = len(far)
    depth, rows = keep.shape

    def body(to_dst, oh_dst, *rest):
        pieces, grads = rest[:count], rest[count : 2 * count]
        out, state, spare, sems = rest[2 * count + 1 :]
        unpack_state(pieces[STATE], depth, state)
        update_and_send(pieces, state, grads, to_dst, oh_dst, spare, out, sems, fixed=True)()

    operands = [to_dst, oh_dst, *far, *rgrads, keep]
    place = len(operands) - 1
    return call(
        only_on(parity, body), "last_right", operands, [shape(depth, rows)], in_large=(place,), out_large=(0,),
        scratch_shapes=[*scratch([shape(1, rows), shape(1, rows)]), pltpu.SemaphoreType.DMA((rows // 256,))],
        aliases={place: 0},
    )[0]


def last_left(parity, left, lstate, lgrad, to_src, oh_src, relations, relation_state, rels, keep):
    depth, rows = left.shape
    kinds = relations.shape[0]

    def body(left, lstate, lgrad, to_src, oh_src, relations, relation_state, *rest):
        rels = rest[: len(rest) - 7]
        left_out, relations_out, new_relations, spare, sems, sem = rest[len(rest) - 6 :]
        grad = sum(ref[...] for ref in rels)
        first = lax.broadcasted_iota(jnp.int32, (kinds, kinds), 0)
        second = lax.broadcasted_iota(jnp.int32, (kinds, kinds), 1)
        old = jnp.sum(jnp.where(first == second, relation_state[...], 0.0), axis=1, keepdims=True)
        new = old + jnp.sum(grad * grad, axis=1, keepdims=True) * (1.0 / depth)
        new_relations[...] = relations[...] - grad * (rate * lax.rsqrt(new))
        copy = pltpu.make_async_copy(new_relations, relations_out, sem)
        copy.start()

        @on_parity(parity)
        def _():
            update_and_send([left], lstate, [lgrad], to_src, oh_src, spare, left_out, sems, fixed=True)()

        copy.wait()

    operands = [left, lstate, lgrad, to_src, oh_src, relations, relation_state, *rels, keep]
    place = len(operands) - 1
    return call(
        body, "last_left", operands, [shape(depth, rows), shape(*relations.shape)], in_large=(place,), out_large=(0, 1),
        scratch_shapes=[
            *scratch([shape(*relations.shape), shape(1, rows)]),
            pltpu.SemaphoreType.DMA((rows // 256,)),
            pltpu.SemaphoreType.DMA,
        ],
        aliases={place: 0},
    )


def local(
    left_slab, left_state, right_slab, right_state, relations, relation_state,
    src_index, dst_index, relation_id, neg_source, neg_target,
):
    peers = lax.axis_size("blk")
    inside = [(i, i + 1) for i in range(0, peers, 2)]
    swap = inside + [(i + 1, i) for i in range(0, peers, 2)]
    across = [(i, (i + 1) % peers) for i in range(1, peers, 2)]
    skip = [(i, (i + 2) % peers) for i in range(0, peers, 2)]
    index = (src_index, dst_index, relation_id, neg_source, neg_target)
    left = left_slab.T
    right = right_slab.T
    rows = left.shape[1]
    lstate = left_state.reshape(1, rows)
    number = float(neg_source.shape[1])
    right_far = lax.ppermute(right, "blk", across)
    right_near = [lax.ppermute(right[:, at : at + size], "blk", inside) for at, size in pieces_of(rows, NEAR_FIRST)]
    state_near = lax.ppermute(right_state, "blk", swap)
    state_far = lax.ppermute(state_near, "blk", skip).reshape(1, rows)
    state_near = state_near.reshape(1, rows)
    rel = jnp.zeros(relations.shape, F32)
    ready = prepared(0, left, relations, index)
    left_a, lstate, far, rel = trained(1, "first_near", number, FAR, left, lstate, right_near, state_near, rel, ready)
    far = [lax.ppermute(piece, "blk", across) for piece in far]
    left_a, lstate, near, rel = trained(
        0, "first_far", number, NEAR, left, lstate, [right_far], state_far, rel, ready, (left_a,)
    )
    near = [lax.ppermute(piece, "blk", inside) for piece in near]
    ready = prepared(1, left_a, relations, index)
    left_b, lstate, right_b, rel = trained(1, "last_near", number, (), left_a, lstate, near, state_near, rel, ready)
    target, gq, rgrads = last_pieces(0, number, far, ready, lstate)
    lgrad, to_src, to_dst, rel = last_join(0, number, target, gq, rel, ready)
    if lax.axis_size("rel") == 2:
        rels = [rel, lax.ppermute(rel, "rel", [(0, 1), (1, 0)])]
    else:
        rels = [lax.psum(rel, "rel")]
    right_b = last_right(0, far, rgrads, to_dst, ready[6], right_b[0])
    left_b, relations_out = last_left(
        0, left_a, lstate, lgrad, to_src, ready[5], relations, relation_state.reshape(1, -1), rels, left_b
    )
    return (left_b.T, right_b.T, relations_out[None])


def solution(mesh):
    in_specs = (
        P(("blk", "rel"), None),
        P(("blk", "rel")),
        P(("blk", "rel"), None),
        P(("blk", "rel")),
        P(),
        P(),
        P(None, ("blk", "rel")),
        P(None, ("blk", "rel")),
        P(None, ("blk", "rel")),
        P(None, ("blk", "rel")),
        P(None, ("blk", "rel")),
    )
    out_specs = (P(("blk", "rel"), None), P(("blk", "rel"), None), P("blk", None, None))
    return jax.shard_map(local, mesh=mesh, in_specs=in_specs, out_specs=out_specs, check_vma=False)
```

```python
import functools

import jax
import jax.numpy as jnp
from jax import lax
from jax.experimental import pallas as pl
from jax.experimental.pallas import tpu as pltpu
from jax.sharding import PartitionSpec as P

rate = 0.1
F32 = jnp.float32
BF16 = jnp.bfloat16
LANES = 128
NEAR = (4, 4)
STATE = 0
NEAR_FIRST = (4, 4)
FAR = (6, 1, 1)
VMEM_LIMIT = 30 * 2**20

NN = (((1,), (0,)), ((), ()))
NT = (((1,), (1,)), ((), ()))
TN = (((0,), (0,)), ((), ()))


def mul(a, b, dims):
    return lax.dot_general(a, b, dims, preferred_element_type=F32)


def split(x, parts):
    out = []
    for _ in range(parts):
        part = x.astype(BF16)
        out.append(part)
        x = x - part.astype(F32)
    return out


def lanes_at(i, size):
    if isinstance(i, int):
        return slice(i * size, (i + 1) * size)
    return pl.ds(pl.multiple_of(i * size, size), size)


def step_of(rows):
    return 512 if rows % 512 == 0 else 256


def each(count, body, fixed=False):
    if fixed:
        for i in range(count):
            body(i)
        return

    def one(i, carry):
        body(i)
        return carry

    lax.fori_loop(0, count, one, 0)


def row_onehot(idx, table):
    count, rows = table.shape
    col = jnp.broadcast_to(idx, (LANES, count)).T
    lane = lax.broadcasted_iota(jnp.int32, (count, LANES), 1)

    def tile(t):
        hit = col == lane + t * LANES
        table[:, lanes_at(t, LANES)] = jnp.where(hit, 1.0, 0.0).astype(BF16)

    each(rows // LANES, tile)


def row_counts(idx, rows):
    count = idx.shape[1]
    high = lax.broadcasted_iota(jnp.int32, (rows // LANES, count), 0)
    low = lax.broadcasted_iota(jnp.int32, (LANES, count), 0)
    high_hit = jnp.where(idx // LANES == high, 1.0, 0.0).astype(BF16)
    low_hit = jnp.where(idx % LANES == low, 1.0, 0.0).astype(BF16)
    return mul(high_hit, low_hit, NT)


def times_at(counts, i, size):
    tiles = size // LANES
    return jnp.concatenate([counts[pl.ds(i * tiles + t, 1), :] for t in range(tiles)], axis=1)


def half_rows(x):
    return (0.5 * x).T.astype(BF16)


def negative_weights(rows16, query_rows, number):
    half = 0.5 / number
    return (jnp.tanh(mul(query_rows, rows16, NN)) * half + half).astype(BF16)


def often(weight, times):
    return (weight.astype(F32) * times).astype(BF16)


def negatives(rows16, query, query_rows, times, number):
    weight = negative_weights(rows16, query_rows, number)
    return mul(query, weight, NN) * times, mul(rows16, often(weight, times), NT)


def prepare(step, left, relations, src, dst, rid, nsrc, ndst,
            weight, source, query, query_rows, left16, oh_src, oh_dst, count_l, count_r, kind):
    rows = left.shape[1]
    here = slice(step, step + 1)
    row_onehot(src[here, :], oh_src)
    row_onehot(dst[here, :], oh_dst)
    count_l[...] = row_counts(nsrc[here, :], rows)
    count_r[...] = row_counts(ndst[here, :], rows)
    kinds = lax.broadcasted_iota(jnp.int32, kind.shape, 0)
    kind[...] = jnp.where(rid[here, :] == kinds, 1.0, 0.0).astype(BF16)
    weight[...] = sum(mul(part, kind[...], TN) for part in split(relations[...], 3))
    source[...] = jnp.zeros_like(source)

    size = step_of(rows)

    def part(i):
        cut = lanes_at(i, size)
        parts = split(left[:, cut], 3)
        left16[:, cut] = parts[0]
        source[...] += sum(mul(p, oh_src[:, cut], NT) for p in parts)

    each(rows // size, part)
    product = source[...] * weight[...]
    query[...] = product.astype(BF16)
    query_rows[...] = half_rows(product.astype(BF16).astype(F32))


def take_piece(number, start, piece, query, query_rows, oh_dst, count_r, target, gq, rgrad, fixed=False):
    depth = target.shape[0]
    if start == 0:
        target[...] = jnp.zeros_like(target)
        gq[...] = jnp.zeros_like(gq)

    size = step_of(piece.shape[1])

    def part(i):
        cut = lanes_at(i, size)
        parts = split(piece[0:depth, cut], 3)
        hits = oh_dst[:, lanes_at(i + start // size, size)]
        target[...] += sum(mul(p, hits, NT) for p in parts)
        times = times_at(count_r, i + start // size, size)
        rgrad[:, cut], more = negatives(parts[0], query[...], query_rows[...], times, number)
        gq[...] += more

    each(piece.shape[1] // size, part, fixed)


def join(number, weight, source, target, gq, left16, count_l, kind, rel_in,
         probe, probe_rows, gp, lgrad, to_src, to_dst, rel_out, fixed=False):
    rows = left16.shape[1]
    product = weight[...] * target[...]
    probe[...] = product.astype(BF16)
    probe_rows[...] = half_rows(product.astype(BF16).astype(F32))
    gp[...] = jnp.zeros_like(gp)

    size = step_of(rows)

    def part(i):
        cut = lanes_at(i, size)
        lgrad[:, cut], more = negatives(left16[:, cut], probe[...], probe_rows[...], times_at(count_l, i, size), number)
        gp[...] += more

    each(rows // size, part, fixed)
    depth = weight.shape[0]
    w, s, t = weight[...], source[...], target[...]
    coef = -jax.nn.sigmoid(-jnp.sum(s * w * t, axis=0, keepdims=True))
    to_src[0:depth, :], to_src[depth:, :] = split(coef * w * t + gq[...] * w, 2)
    to_dst[0:depth, :], to_dst[depth:, :] = split(coef * w * s + gp[...] * w, 2)
    g_weight = coef * s * t + gq[...] * s + gp[...] * t
    rel_out[...] = rel_in[...] + sum(mul(kind[...], p, NT) for p in split(g_weight, 2))


def adagrad(slab, state, grad, edges, table, start, out, new_state, send=None, fixed=False, more=None):
    depth = grad.shape[0]
    size = step_of(grad.shape[1])

    def part(i):
        cut = lanes_at(i, size)
        hits = table[:, lanes_at(i + start // size, size)]
        g = grad[:, cut] + mul(edges[0:depth, :], hits, NN) + mul(edges[depth:, :], hits, NN)
        if more is not None:
            g = g + more(i, size)
        new = state[:, cut] + jnp.sum(g * g, axis=0, keepdims=True) * (1.0 / depth)
        new_state[:, cut] = new
        out[0:depth, cut] = slab[0:depth, cut] - g * (rate * lax.rsqrt(new))
        if send is not None:
            send(i).start()

    each(grad.shape[1] // size, part, fixed)


def sender(result, to, start, sems):
    size = step_of(result.shape[1])

    def copy(i):
        here = lanes_at(i, size)
        there = lanes_at(i + start // size, size)
        return pltpu.make_async_copy(result.at[:, here], to.at[:, there], sems.at[i + start // size])

    return copy


def update_and_send(pieces, state, grads, edges, table, new_state, to, sems, fixed=False, start=0, more=None):
    sent = []
    for piece, grad in zip(pieces, grads):
        rows = grad.shape[1]
        copy = sender(grad, to, start, sems)
        cut = slice(start, start + rows)
        adagrad(piece, state.at[:, cut], grad, edges, table, start, grad, new_state.at[:, cut], copy, fixed, more)
        sent.append((copy, rows // step_of(rows)))
        start += rows

    def wait():
        for copy, count in sent:
            each(count, lambda i, copy=copy: copy(i).wait(), fixed)

    return wait


def pack_state(state, piece, depth):
    size = state.shape[1] // 8
    for k in range(8):
        piece[depth + k : depth + k + 1, 0:size] = state[:, k * size : (k + 1) * size]


def unpack_state(piece, depth, state):
    size = state.shape[1] // 8
    for k in range(8):
        state[:, k * size : (k + 1) * size] = piece[depth + k : depth + k + 1, 0:size]


def on_parity(parity):
    return pl.when(lax.axis_index("blk") % 2 == parity)


def pieces_of(rows, eighths):
    sizes = [rows // 8 * n for n in eighths]
    return [(sum(sizes[:i]), size) for i, size in enumerate(sizes)]


def rows_of(pieces, at, size):
    found = []
    start = 0
    for piece in pieces:
        begin, end = max(at, start), min(at + size, start + piece.shape[1])
        if begin < end:
            found.append((piece.at[:, begin - start : end - start], begin, end - begin))
        start += piece.shape[1]
    return found


def train(parity, number, last, fixed, kept, takes, gives, *refs):
    refs = list(refs)
    (left, lstate, rstate_in, rel_in) = refs[:4]
    (weight, source, query, query_rows, left16, oh_src, oh_dst, count_l, count_r, kind) = refs[4:14]
    right = refs[14 : 14 + takes]
    refs = refs[14 + takes + kept :]
    left_out, lstate_out, rel_out = refs[:3]
    right_out = refs[3 : 3 + len(gives)]
    (target, gq, rgrad, probe, probe_rows, gp, lgrad, to_src, to_dst, rstate, spare, sems) = refs[3 + len(gives) :]
    depth, rows = left.shape
    lstate_out[...] = lstate[...]
    rel_out[...] = rel_in[...]

    @on_parity(parity)
    def _():
        grads = []
        at = 0
        for piece in right:
            grads.append(rgrad.at[:, at : at + piece.shape[1]])
            take_piece(number, at, piece, query, query_rows, oh_dst, count_r, target, gq, grads[-1], fixed)
            at += piece.shape[1]
        join(number, weight, source, target, gq, left16, count_l, kind, rel_in,
             probe, probe_rows, gp, lgrad, to_src, to_dst, rel_out, fixed)
        if last:
            unpack_state(right[STATE], depth, rstate)
            wait_right = update_and_send(right, rstate, grads, to_dst, oh_dst, spare, right_out[0], sems.at[0], fixed)
            wait_left = update_and_send([left], lstate, [lgrad], to_src, oh_src, spare, left_out, sems.at[1], fixed)
            wait_right()
            wait_left()
        else:
            for (at, size), out in zip(pieces_of(rows, gives), right_out):
                for old, begin, length in rows_of(right, at, size):
                    cut = slice(begin, begin + length)
                    here = slice(begin - at, begin - at + length)
                    adagrad(old, rstate_in.at[:, cut], rgrad.at[:, cut], to_dst, oh_dst, begin, out.at[:, here], spare.at[:, cut], None, fixed)
            pack_state(spare, right_out[STATE], depth)
            adagrad(left, lstate, lgrad, to_src, oh_src, 0, left_out, lstate_out, None, fixed)


def shape(*dims, dtype=F32):
    return jax.ShapeDtypeStruct(dims, dtype)


def prepared_shapes(depth, rows, edges, kinds):
    return (
        shape(depth, edges), shape(depth, edges), shape(depth, edges, dtype=BF16), shape(edges, depth, dtype=BF16),
        shape(depth, rows, dtype=BF16), shape(edges, rows, dtype=BF16), shape(edges, rows, dtype=BF16),
        shape(rows // LANES, LANES), shape(rows // LANES, LANES), shape(kinds, edges, dtype=BF16),
    )


def scratch(shapes):
    return [pltpu.VMEM(s.shape, s.dtype) for s in shapes]


def call(kernel, name, operands, shapes, in_large=(), out_large=(), scratch_shapes=(), aliases=None):
    vmem = pl.BlockSpec(memory_space=pltpu.VMEM)
    large = pl.BlockSpec(memory_space=pl.ANY)
    return pl.pallas_call(
        kernel,
        out_shape=tuple(shapes),
        in_specs=[large if i in in_large else vmem for i in range(len(operands))],
        out_specs=tuple(large if i in out_large else vmem for i in range(len(shapes))),
        scratch_shapes=list(scratch_shapes),
        input_output_aliases=aliases or {},
        compiler_params=pltpu.CompilerParams(vmem_limit_bytes=VMEM_LIMIT),
        cost_estimate=pl.CostEstimate(flops=1_000_000, bytes_accessed=100_000, transcendentals=0),
        name=name,
    )(*operands)


def prepared(step, left, relations, index):
    depth, rows = left.shape
    return call(
        functools.partial(prepare, step), "prepare%d" % step, [left, relations, *index],
        prepared_shapes(depth, rows, index[0].shape[1], relations.shape[0]),
    )


def trained(parity, name, number, fixed, gives, left, lstate, right, rstate, rel, ready, keep=()):
    depth, rows = left.shape
    edges = ready[0].shape[1]
    last = not gives
    blocks = [shape(depth, size) for _at, size in pieces_of(rows, gives or (8,))]
    if not last:
        blocks[STATE] = shape(depth + 8, blocks[STATE].shape[1])
    edge = shape(depth, edges)
    edge16 = shape(depth, edges, dtype=BF16)
    pair16 = shape(2 * depth, edges, dtype=BF16)
    slab = shape(depth, rows)
    inner = [edge, edge, slab, edge16, shape(edges, depth, dtype=BF16), edge, slab, pair16, pair16, shape(1, rows), shape(1, rows)]
    left_out, lstate_out, rel_out, *right_out = call(
        functools.partial(train, parity, number, last, fixed, len(keep), len(right), gives or (8,)),
        name,
        [left, lstate, rstate, rel, *ready, *right, *keep],
        [slab, shape(1, rows), shape(*rel.shape), *blocks],
        out_large=(0, 3) if last else (),
        scratch_shapes=[*scratch(inner), pltpu.SemaphoreType.DMA((2, rows // 256))],
        aliases={14 + len(right) + i: 0 for i in range(len(keep))},
    )
    return left_out, lstate_out, right_out, rel_out


def only_on(parity, body):
    def kernel(*refs):
        @on_parity(parity)
        def _():
            body(*refs)

    return kernel


def last_piece(parity, name, number, at, piece, ready, after, held=()):
    (_weight, _source, query, query_rows, _left16, _oh_src, oh_dst, _count_l, count_r, _kind) = ready
    depth, edges = query.shape

    def body(piece, query, query_rows, oh_dst, count_r, *rest):
        take_piece(number, at, piece, query, query_rows, oh_dst, count_r, *rest[len(held) + 1 :], fixed=True)

    operands = [piece, query, query_rows, oh_dst, count_r, *held, after]
    return call(
        only_on(parity, body), name, operands,
        [shape(depth, edges), shape(depth, edges), shape(depth, piece.shape[1])],
        in_large=(len(operands) - 1,), aliases={5: 0, 6: 1} if held else {},
    )


def early_edges(parity, number, step, bound, target, ready, dst):
    (weight, source, _query, _query_rows, left16, _oh_src, _oh_dst, count_l, _count_r, _kind) = ready
    depth, rows = left16.shape
    edges = weight.shape[1]

    def body(weight, source, target, left16, count_l, dst, lgrad, to_dst, gp, probe, probe_rows):
        w, s, t = weight[...], source[...], target[...]
        product = (w * t).astype(BF16)
        probe[...] = product
        probe_rows[...] = half_rows(product.astype(F32))
        gp[...] = jnp.zeros_like(gp)
        size = step_of(rows)
        for i in range(rows // size):
            cut = lanes_at(i, size)
            lgrad[:, cut], more = negatives(left16[:, cut], probe[...], probe_rows[...], times_at(count_l, i, size), number)
            gp[...] += more
        early = dst[step : step + 1, :] < bound
        gp[...] = jnp.where(early, gp[...], 0.0)
        coef = -jax.nn.sigmoid(-jnp.sum(s * w * t, axis=0, keepdims=True))
        to_dst[0:depth, :], to_dst[depth:, :] = split(jnp.where(early, coef * w * s + gp[...] * w, 0.0), 2)

    return call(
        only_on(parity, body), "early_edges", [weight, source, target, left16, count_l, dst],
        [shape(depth, rows), shape(2 * depth, edges, dtype=BF16), shape(depth, edges)],
        scratch_shapes=scratch([shape(depth, edges, dtype=BF16), shape(edges, depth, dtype=BF16)]),
    )


def early_right(parity, piece, rgrad, to_dst, oh_dst, keep):
    depth, rows = keep.shape

    def body(piece, rgrad, to_dst, oh_dst, _keep, out, state, spare, sems):
        unpack_state(piece, depth, state)
        update_and_send([piece], state, [rgrad], to_dst, oh_dst, spare, out, sems, fixed=True)()

    return call(
        only_on(parity, body), "early_right", [piece, rgrad, to_dst, oh_dst, keep], [shape(depth, rows), shape(1, rows)],
        in_large=(4,), out_large=(0,),
        scratch_shapes=[*scratch([shape(1, rows)]), pltpu.SemaphoreType.DMA((rows // 256,))],
        aliases={4: 0},
    )


def late_edges(parity, number, step, at, bound, piece, ready, dst, target, gq, gp, rel):
    (weight, source, query, query_rows, left16, _oh_src, oh_dst, count_l, count_r, kind) = ready
    depth, rows = left16.shape
    edges = weight.shape[1]
    pair16 = shape(2 * depth, edges, dtype=BF16)

    def body(piece, weight, source, query, query_rows, left16, oh_dst, count_l, count_r, kind, dst, held_t, held_q, held_p, rel_in,
             rgrad, to_src, to_dst, rel_out, probe, weights, target, gq, gp, probe_rows):
        rel_out[...] = rel_in[...]

        @on_parity(parity)
        def _():
            target[...] = held_t[...]
            gq[...] = held_q[...]
            take_piece(number, at, piece, query, query_rows, oh_dst, count_r, target, gq, rgrad, fixed=True)
            late = dst[step : step + 1, :] >= bound
            w, s, t = weight[...], source[...], target[...]
            product = jnp.where(late, w * t, 0.0).astype(BF16)
            probe[...] = product
            probe_rows[...] = half_rows(product.astype(F32))
            gp[...] = jnp.zeros_like(gp)
            size = step_of(rows)
            for i in range(rows // size):
                cut = lanes_at(i, size)
                rows16 = left16[:, cut]
                part = negative_weights(rows16, probe_rows[...], number)
                weights[:, cut] = part
                gp[...] += mul(rows16, often(part, times_at(count_l, i, size)), NT)
            all_gp = held_p[...] + jnp.where(late, gp[...], 0.0)
            coef = -jax.nn.sigmoid(-jnp.sum(s * w * t, axis=0, keepdims=True))
            g_weight = coef * s * t + gq[...] * s + all_gp * t
            rel_out[...] = rel_in[...] + sum(mul(kind[...], p, NT) for p in split(g_weight, 2))
            to_src[0:depth, :], to_src[depth:, :] = split(coef * w * t + gq[...] * w, 2)
            to_dst[0:depth, :], to_dst[depth:, :] = split(jnp.where(late, coef * w * s + all_gp * w, 0.0), 2)

    return call(
        body, "late_edges",
        [piece, weight, source, query, query_rows, left16, oh_dst, count_l, count_r, kind, dst, target, gq, gp, rel],
        [shape(depth, piece.shape[1]), pair16, pair16, shape(*rel.shape), shape(depth, edges, dtype=BF16), shape(edges, rows, dtype=BF16)],
        scratch_shapes=scratch([shape(depth, edges)] * 3 + [shape(edges, depth, dtype=BF16)]),
    )


def late_slabs(parity, at, left, lstate, lgrad, to_src, oh_src, probe, weights, count_l, far, state, rgrads, to_dst, oh_dst, keep_left, keep_right):
    depth, rows = left.shape
    count = len(far)

    def body(left, lstate, lgrad, to_src, oh_src, probe, weights, count_l, state, to_dst, oh_dst, *rest):
        pieces, grads = rest[:count], rest[count : 2 * count]
        left_out, right_out, spare, sems = rest[2 * count + 2 :]

        def more(i, size):
            return mul(probe[...], weights[:, lanes_at(i, size)], NN) * times_at(count_l, i, size)

        wait_left = update_and_send([left], lstate, [lgrad], to_src, oh_src, spare, left_out, sems.at[0], fixed=True, more=more)
        wait_right = update_and_send(pieces, state, grads, to_dst, oh_dst, spare, right_out, sems.at[1], fixed=True, start=at)
        wait_left()
        wait_right()

    operands = [left, lstate, lgrad, to_src, oh_src, probe, weights, count_l, state, to_dst, oh_dst, *far, *rgrads, keep_left, keep_right]
    places = (len(operands) - 2, len(operands) - 1)
    return call(
        only_on(parity, body), "late_slabs", operands, [shape(depth, rows), shape(depth, rows)], in_large=places, out_large=(0, 1),
        scratch_shapes=[*scratch([shape(1, rows)]), pltpu.SemaphoreType.DMA((2, rows // 256))],
        aliases={places[0]: 0, places[1]: 1},
    )


def relation_update(relations, relation_state, rels):
    kinds, depth = relations.shape

    def body(relations, relation_state, *rest):
        grad = sum(ref[...] for ref in rest[:-1])
        first = lax.broadcasted_iota(jnp.int32, (kinds, kinds), 0)
        second = lax.broadcasted_iota(jnp.int32, (kinds, kinds), 1)
        old = jnp.sum(jnp.where(first == second, relation_state[...], 0.0), axis=1, keepdims=True)
        new = old + jnp.sum(grad * grad, axis=1, keepdims=True) * (1.0 / depth)
        rest[-1][...] = relations[...] - grad * (rate * lax.rsqrt(new))

    return call(body, "relation_update", [relations, relation_state, *rels], [shape(kinds, depth)])[0]


def local(
    left_slab, left_state, right_slab, right_state, relations, relation_state,
    src_index, dst_index, relation_id, neg_source, neg_target,
):
    peers = lax.axis_size("blk")
    inside = [(i, i + 1) for i in range(0, peers, 2)]
    swap = inside + [(i + 1, i) for i in range(0, peers, 2)]
    across = [(i, (i + 1) % peers) for i in range(1, peers, 2)]
    skip = [(i, (i + 2) % peers) for i in range(0, peers, 2)]
    index = (src_index, dst_index, relation_id, neg_source, neg_target)
    left = left_slab.T
    right = right_slab.T
    rows = left.shape[1]
    lstate = left_state.reshape(1, rows)
    number = float(neg_source.shape[1])
    right_far = lax.ppermute(right, "blk", across)
    right_near = [lax.ppermute(right[:, at : at + size], "blk", inside) for at, size in pieces_of(rows, NEAR_FIRST)]
    state_near = lax.ppermute(right_state, "blk", swap)
    state_far = lax.ppermute(state_near, "blk", skip).reshape(1, rows)
    state_near = state_near.reshape(1, rows)
    rel = jnp.zeros(relations.shape, F32)
    ready = prepared(0, left, relations, index)
    left_a, lstate, far, rel = trained(1, "first_near", number, False, FAR, left, lstate, right_near, state_near, rel, ready)
    far = [lax.ppermute(piece, "blk", across) for piece in far]
    left_a, lstate, near, rel = trained(
        0, "first_far", number, True, NEAR, left, lstate, [right_far], state_far, rel, ready, (left_a,)
    )
    near = [lax.ppermute(piece, "blk", inside) for piece in near]
    ready = prepared(1, left_a, relations, index)
    first_lstate = lstate
    left_b, lstate, right_b, rel = trained(1, "last_near", number, True, (), left_a, lstate, near, state_near, rel, ready)
    cuts = pieces_of(rows, FAR)
    bound = cuts[1][0]
    target, gq, rgrad = last_piece(0, "last_piece0", number, 0, far[0], ready, lstate)
    rgrads = [rgrad]
    lgrad, to_dst, gp = early_edges(0, number, 1, bound, target, ready, dst_index)
    right_b, state = early_right(0, far[0], rgrad, to_dst, ready[6], right_b[0])
    for i in range(1, len(far) - 1):
        target, gq, rgrad = last_piece(0, "last_piece%d" % i, number, cuts[i][0], far[i], ready, right_b, (target, gq))
        rgrads.append(rgrad)
    rgrad, to_src, to_dst, rel, probe, weights = late_edges(
        0, number, 1, cuts[-1][0], bound, far[-1], ready, dst_index, target, gq, gp, rel
    )
    rgrads.append(rgrad)
    if lax.axis_size("rel") == 2:
        rels = [rel, lax.ppermute(rel, "rel", [(0, 1), (1, 0)])]
    else:
        rels = [lax.psum(rel, "rel")]
    left_b, right_b = late_slabs(
        0, bound, left_a, first_lstate, lgrad, to_src, ready[5], probe, weights, ready[7],
        far[1:], state, rgrads[1:], to_dst, ready[6], left_b, right_b,
    )
    relations_out = relation_update(relations, relation_state.reshape(1, -1), rels)
    return (left_b.T, right_b.T, relations_out[None])


def solution(mesh):
    in_specs = (
        P(("blk", "rel"), None),
        P(("blk", "rel")),
        P(("blk", "rel"), None),
        P(("blk", "rel")),
        P(),
        P(),
        P(None, ("blk", "rel")),
        P(None, ("blk", "rel")),
        P(None, ("blk", "rel")),
        P(None, ("blk", "rel")),
        P(None, ("blk", "rel")),
    )
    out_specs = (P(("blk", "rel"), None), P(("blk", "rel"), None), P("blk", None, None))
    return jax.shard_map(local, mesh=mesh, in_specs=in_specs, out_specs=out_specs, check_vma=False)
```

```python
import functools

import jax
import jax.numpy as jnp
from jax import lax
from jax.experimental import pallas as pl
from jax.experimental.pallas import tpu as pltpu
from jax.sharding import PartitionSpec as P

rate = 0.1
F32 = jnp.float32
BF16 = jnp.bfloat16
LANES = 128
NEAR = (4, 4)
STATE = 0
NEAR_FIRST = (4, 4)
FAR = (6, 1, 1)
VMEM_LIMIT = 30 * 2**20

NN = (((1,), (0,)), ((), ()))
NT = (((1,), (1,)), ((), ()))
TN = (((0,), (0,)), ((), ()))


def mul(a, b, dims):
    return lax.dot_general(a, b, dims, preferred_element_type=F32)


def split(x, parts):
    out = []
    for _ in range(parts):
        part = x.astype(BF16)
        out.append(part)
        x = x - part.astype(F32)
    return out


def mul_parts(parts, table, dims):
    along = dims[0][1][0]
    return mul(jnp.concatenate(parts, axis=1), jnp.concatenate([table] * len(parts), axis=along), dims)


def lanes_at(i, size):
    if isinstance(i, int):
        return slice(i * size, (i + 1) * size)
    return pl.ds(pl.multiple_of(i * size, size), size)


def step_of(rows):
    return 512 if rows % 512 == 0 else 256


def each(count, body, fixed=False):
    if fixed:
        for i in range(count):
            body(i)
        return

    def one(i, carry):
        body(i)
        return carry

    lax.fori_loop(0, count, one, 0)


def row_onehot(idx, table):
    count, rows = table.shape
    col = jnp.broadcast_to(idx, (LANES, count)).T
    lane = lax.broadcasted_iota(jnp.int32, (count, LANES), 1)

    def tile(t):
        hit = col == lane + t * LANES
        table[:, lanes_at(t, LANES)] = jnp.where(hit, 1.0, 0.0).astype(BF16)

    each(rows // LANES, tile)


def row_counts(idx, rows):
    count = idx.shape[1]
    high = lax.broadcasted_iota(jnp.int32, (rows // LANES, count), 0)
    low = lax.broadcasted_iota(jnp.int32, (LANES, count), 0)
    high_hit = jnp.where(idx // LANES == high, 1.0, 0.0).astype(BF16)
    low_hit = jnp.where(idx % LANES == low, 1.0, 0.0).astype(BF16)
    return mul(high_hit, low_hit, NT)


def times_at(counts, i, size):
    tiles = size // LANES
    return jnp.concatenate([counts[pl.ds(i * tiles + t, 1), :] for t in range(tiles)], axis=1)


def half_rows(x):
    return (0.5 * x).T.astype(BF16)


def negative_weights(rows16, query_rows, number):
    half = 0.5 / number
    return (jnp.tanh(mul(query_rows, rows16, NN)) * half + half).astype(BF16)


def often(weight, times):
    return (weight.astype(F32) * times).astype(BF16)


def negatives(rows16, query, query_rows, times, number):
    weight = negative_weights(rows16, query_rows, number)
    return mul(query, weight, NN) * times, mul(rows16, often(weight, times), NT)


def prepare(step, left, relations, src, dst, rid, nsrc, ndst,
            weight, source, query, query_rows, left16, oh_src, oh_dst, count_l, count_r, kind):
    rows = left.shape[1]
    here = slice(step, step + 1)
    row_onehot(src[here, :], oh_src)
    row_onehot(dst[here, :], oh_dst)
    count_l[...] = row_counts(nsrc[here, :], rows)
    count_r[...] = row_counts(ndst[here, :], rows)
    kinds = lax.broadcasted_iota(jnp.int32, kind.shape, 0)
    kind[...] = jnp.where(rid[here, :] == kinds, 1.0, 0.0).astype(BF16)
    weight[...] = sum(mul(part, kind[...], TN) for part in split(relations[...], 3))
    source[...] = jnp.zeros_like(source)

    size = step_of(rows)

    def part(i):
        cut = lanes_at(i, size)
        parts = split(left[:, cut], 3)
        left16[:, cut] = parts[0]
        source[...] += mul_parts(parts, oh_src[:, cut], NT)

    each(rows // size, part)
    product = source[...] * weight[...]
    query[...] = product.astype(BF16)
    query_rows[...] = half_rows(product.astype(BF16).astype(F32))


def take_piece(number, start, piece, query, query_rows, oh_dst, count_r, target, gq, rgrad, fixed=False):
    depth = target.shape[0]
    if start == 0:
        target[...] = jnp.zeros_like(target)
        gq[...] = jnp.zeros_like(gq)

    size = step_of(piece.shape[1])

    def part(i):
        cut = lanes_at(i, size)
        parts = split(piece[0:depth, cut], 3)
        hits = oh_dst[:, lanes_at(i + start // size, size)]
        target[...] += mul_parts(parts, hits, NT)
        times = times_at(count_r, i + start // size, size)
        rgrad[:, cut], more = negatives(parts[0], query[...], query_rows[...], times, number)
        gq[...] += more

    each(piece.shape[1] // size, part, fixed)


def join(number, weight, source, target, gq, left16, count_l, kind, rel_in,
         probe, probe_rows, gp, lgrad, to_src, to_dst, rel_out, fixed=False):
    rows = left16.shape[1]
    product = weight[...] * target[...]
    probe[...] = product.astype(BF16)
    probe_rows[...] = half_rows(product.astype(BF16).astype(F32))
    gp[...] = jnp.zeros_like(gp)

    size = step_of(rows)

    def part(i):
        cut = lanes_at(i, size)
        lgrad[:, cut], more = negatives(left16[:, cut], probe[...], probe_rows[...], times_at(count_l, i, size), number)
        gp[...] += more

    each(rows // size, part, fixed)
    depth = weight.shape[0]
    w, s, t = weight[...], source[...], target[...]
    coef = -jax.nn.sigmoid(-jnp.sum(s * w * t, axis=0, keepdims=True))
    to_src[0:depth, :], to_src[depth:, :] = split(coef * w * t + gq[...] * w, 2)
    to_dst[0:depth, :], to_dst[depth:, :] = split(coef * w * s + gp[...] * w, 2)
    g_weight = coef * s * t + gq[...] * s + gp[...] * t
    rel_out[...] = rel_in[...] + sum(mul(kind[...], p, NT) for p in split(g_weight, 2))


def adagrad(slab, state, grad, edges, table, start, out, new_state, send=None, fixed=False, more=None):
    depth = grad.shape[0]
    size = step_of(grad.shape[1])

    def part(i):
        cut = lanes_at(i, size)
        hits = table[:, lanes_at(i + start // size, size)]
        g = grad[:, cut] + mul_parts([edges[0:depth, :], edges[depth:, :]], hits, NN)
        if more is not None:
            g = g + more(i, size)
        new = state[:, cut] + jnp.sum(g * g, axis=0, keepdims=True) * (1.0 / depth)
        new_state[:, cut] = new
        out[0:depth, cut] = slab[0:depth, cut] - g * (rate * lax.rsqrt(new))
        if send is not None:
            send(i).start()

    each(grad.shape[1] // size, part, fixed)


def sender(result, to, start, sems):
    size = step_of(result.shape[1])

    def copy(i):
        here = lanes_at(i, size)
        there = lanes_at(i + start // size, size)
        return pltpu.make_async_copy(result.at[:, here], to.at[:, there], sems.at[i + start // size])

    return copy


def update_and_send(pieces, state, grads, edges, table, new_state, to, sems, fixed=False, start=0, more=None):
    sent = []
    for piece, grad in zip(pieces, grads):
        rows = grad.shape[1]
        copy = sender(grad, to, start, sems)
        cut = slice(start, start + rows)
        adagrad(piece, state.at[:, cut], grad, edges, table, start, grad, new_state.at[:, cut], copy, fixed, more)
        sent.append((copy, rows // step_of(rows)))
        start += rows

    def wait():
        for copy, count in sent:
            each(count, lambda i, copy=copy: copy(i).wait(), fixed)

    return wait


def pack_state(state, piece, depth):
    size = state.shape[1] // 8
    for k in range(8):
        piece[depth + k : depth + k + 1, 0:size] = state[:, k * size : (k + 1) * size]


def unpack_state(piece, depth, state):
    size = state.shape[1] // 8
    for k in range(8):
        state[:, k * size : (k + 1) * size] = piece[depth + k : depth + k + 1, 0:size]


def on_parity(parity):
    return pl.when(lax.axis_index("blk") % 2 == parity)


def pieces_of(rows, eighths):
    sizes = [rows // 8 * n for n in eighths]
    return [(sum(sizes[:i]), size) for i, size in enumerate(sizes)]


def rows_of(pieces, at, size):
    found = []
    start = 0
    for piece in pieces:
        begin, end = max(at, start), min(at + size, start + piece.shape[1])
        if begin < end:
            found.append((piece.at[:, begin - start : end - start], begin, end - begin))
        start += piece.shape[1]
    return found


def train(parity, number, last, fixed, kept, takes, gives, *refs):
    refs = list(refs)
    (left, lstate, rstate_in, rel_in) = refs[:4]
    (weight, source, query, query_rows, left16, oh_src, oh_dst, count_l, count_r, kind) = refs[4:14]
    right = refs[14 : 14 + takes]
    refs = refs[14 + takes + kept :]
    left_out, lstate_out, rel_out = refs[:3]
    right_out = refs[3 : 3 + len(gives)]
    (target, gq, rgrad, probe, probe_rows, gp, lgrad, to_src, to_dst, rstate, spare, sems) = refs[3 + len(gives) :]
    depth, rows = left.shape
    lstate_out[...] = lstate[...]
    rel_out[...] = rel_in[...]

    @on_parity(parity)
    def _():
        grads = []
        at = 0
        for piece in right:
            grads.append(rgrad.at[:, at : at + piece.shape[1]])
            take_piece(number, at, piece, query, query_rows, oh_dst, count_r, target, gq, grads[-1], fixed)
            at += piece.shape[1]
        join(number, weight, source, target, gq, left16, count_l, kind, rel_in,
             probe, probe_rows, gp, lgrad, to_src, to_dst, rel_out, fixed)
        if last:
            unpack_state(right[STATE], depth, rstate)
            wait_right = update_and_send(right, rstate, grads, to_dst, oh_dst, spare, right_out[0], sems.at[0], fixed)
            wait_left = update_and_send([left], lstate, [lgrad], to_src, oh_src, spare, left_out, sems.at[1], fixed)
            wait_right()
            wait_left()
        else:
            for (at, size), out in zip(pieces_of(rows, gives), right_out):
                for old, begin, length in rows_of(right, at, size):
                    cut = slice(begin, begin + length)
                    here = slice(begin - at, begin - at + length)
                    adagrad(old, rstate_in.at[:, cut], rgrad.at[:, cut], to_dst, oh_dst, begin, out.at[:, here], spare.at[:, cut], None, fixed)
            pack_state(spare, right_out[STATE], depth)
            adagrad(left, lstate, lgrad, to_src, oh_src, 0, left_out, lstate_out, None, fixed)


def shape(*dims, dtype=F32):
    return jax.ShapeDtypeStruct(dims, dtype)


def prepared_shapes(depth, rows, edges, kinds):
    return (
        shape(depth, edges), shape(depth, edges), shape(depth, edges, dtype=BF16), shape(edges, depth, dtype=BF16),
        shape(depth, rows, dtype=BF16), shape(edges, rows, dtype=BF16), shape(edges, rows, dtype=BF16),
        shape(rows // LANES, LANES), shape(rows // LANES, LANES), shape(kinds, edges, dtype=BF16),
    )


def scratch(shapes):
    return [pltpu.VMEM(s.shape, s.dtype) for s in shapes]


def call(kernel, name, operands, shapes, in_large=(), out_large=(), scratch_shapes=(), aliases=None):
    vmem = pl.BlockSpec(memory_space=pltpu.VMEM)
    large = pl.BlockSpec(memory_space=pl.ANY)
    return pl.pallas_call(
        kernel,
        out_shape=tuple(shapes),
        in_specs=[large if i in in_large else vmem for i in range(len(operands))],
        out_specs=tuple(large if i in out_large else vmem for i in range(len(shapes))),
        scratch_shapes=list(scratch_shapes),
        input_output_aliases=aliases or {},
        compiler_params=pltpu.CompilerParams(vmem_limit_bytes=VMEM_LIMIT),
        cost_estimate=pl.CostEstimate(flops=1_000_000, bytes_accessed=100_000, transcendentals=0),
        name=name,
    )(*operands)


def prepared(step, left, relations, index):
    depth, rows = left.shape
    return call(
        functools.partial(prepare, step), "prepare%d" % step, [left, relations, *index],
        prepared_shapes(depth, rows, index[0].shape[1], relations.shape[0]),
    )


def trained(parity, name, number, fixed, gives, left, lstate, right, rstate, rel, ready, keep=()):
    depth, rows = left.shape
    edges = ready[0].shape[1]
    last = not gives
    blocks = [shape(depth, size) for _at, size in pieces_of(rows, gives or (8,))]
    if not last:
        blocks[STATE] = shape(depth + 8, blocks[STATE].shape[1])
    edge = shape(depth, edges)
    edge16 = shape(depth, edges, dtype=BF16)
    pair16 = shape(2 * depth, edges, dtype=BF16)
    slab = shape(depth, rows)
    inner = [edge, edge, slab, edge16, shape(edges, depth, dtype=BF16), edge, slab, pair16, pair16, shape(1, rows), shape(1, rows)]
    left_out, lstate_out, rel_out, *right_out = call(
        functools.partial(train, parity, number, last, fixed, len(keep), len(right), gives or (8,)),
        name,
        [left, lstate, rstate, rel, *ready, *right, *keep],
        [slab, shape(1, rows), shape(*rel.shape), *blocks],
        out_large=(0, 3) if last else (),
        scratch_shapes=[*scratch(inner), pltpu.SemaphoreType.DMA((2, rows // 256))],
        aliases={14 + len(right) + i: 0 for i in range(len(keep))},
    )
    return left_out, lstate_out, right_out, rel_out


def only_on(parity, body):
    def kernel(*refs):
        @on_parity(parity)
        def _():
            body(*refs)

    return kernel


def last_piece(parity, name, number, at, piece, ready, after, held=()):
    (_weight, _source, query, query_rows, _left16, _oh_src, oh_dst, _count_l, count_r, _kind) = ready
    depth, edges = query.shape

    def body(piece, query, query_rows, oh_dst, count_r, *rest):
        take_piece(number, at, piece, query, query_rows, oh_dst, count_r, *rest[len(held) + 1 :], fixed=True)

    operands = [piece, query, query_rows, oh_dst, count_r, *held, after]
    return call(
        only_on(parity, body), name, operands,
        [shape(depth, edges), shape(depth, edges), shape(depth, piece.shape[1])],
        aliases={5: 0, 6: 1} if held else {},
    )


def early_edges(parity, number, step, bound, target, ready, dst):
    (weight, source, _query, _query_rows, left16, _oh_src, _oh_dst, count_l, _count_r, _kind) = ready
    depth, rows = left16.shape
    edges = weight.shape[1]

    def body(weight, source, target, left16, count_l, dst, lgrad, to_dst, gp, probe, probe_rows):
        w, s, t = weight[...], source[...], target[...]
        product = (w * t).astype(BF16)
        probe[...] = product
        probe_rows[...] = half_rows(product.astype(F32))
        gp[...] = jnp.zeros_like(gp)
        size = step_of(rows)
        for i in range(rows // size):
            cut = lanes_at(i, size)
            lgrad[:, cut], more = negatives(left16[:, cut], probe[...], probe_rows[...], times_at(count_l, i, size), number)
            gp[...] += more
        early = dst[step : step + 1, :] < bound
        gp[...] = jnp.where(early, gp[...], 0.0)
        coef = -jax.nn.sigmoid(-jnp.sum(s * w * t, axis=0, keepdims=True))
        to_dst[0:depth, :], to_dst[depth:, :] = split(jnp.where(early, coef * w * s + gp[...] * w, 0.0), 2)

    return call(
        only_on(parity, body), "early_edges", [weight, source, target, left16, count_l, dst],
        [shape(depth, rows), shape(2 * depth, edges, dtype=BF16), shape(depth, edges)],
        scratch_shapes=scratch([shape(depth, edges, dtype=BF16), shape(edges, depth, dtype=BF16)]),
    )


def early_right(parity, piece, rgrad, to_dst, oh_dst, keep):
    depth, rows = keep.shape

    def body(piece, rgrad, to_dst, oh_dst, _keep, out, state, spare, sems):
        unpack_state(piece, depth, state)
        update_and_send([piece], state, [rgrad], to_dst, oh_dst, spare, out, sems, fixed=True)()

    return call(
        only_on(parity, body), "early_right", [piece, rgrad, to_dst, oh_dst, keep], [shape(depth, rows), shape(1, rows)],
        in_large=(4,), out_large=(0,),
        scratch_shapes=[*scratch([shape(1, rows)]), pltpu.SemaphoreType.DMA((rows // 256,))],
        aliases={4: 0},
    )


def late_edges(parity, number, step, at, bound, piece, ready, dst, target, gq, gp, rel):
    (weight, source, query, query_rows, left16, _oh_src, oh_dst, count_l, count_r, kind) = ready
    depth, rows = left16.shape
    edges = weight.shape[1]
    pair16 = shape(2 * depth, edges, dtype=BF16)

    def body(piece, weight, source, query, query_rows, left16, oh_dst, count_l, count_r, kind, dst, held_t, held_q, held_p, rel_in,
             rgrad, to_src, to_dst, rel_out, probe, weights, target, gq, gp, probe_rows):
        rel_out[...] = rel_in[...]

        @on_parity(parity)
        def _():
            target[...] = held_t[...]
            gq[...] = held_q[...]
            take_piece(number, at, piece, query, query_rows, oh_dst, count_r, target, gq, rgrad, fixed=True)
            late = dst[step : step + 1, :] >= bound
            w, s, t = weight[...], source[...], target[...]
            product = jnp.where(late, w * t, 0.0).astype(BF16)
            probe[...] = product
            probe_rows[...] = half_rows(product.astype(F32))
            gp[...] = jnp.zeros_like(gp)
            size = step_of(rows)
            for i in range(rows // size):
                cut = lanes_at(i, size)
                rows16 = left16[:, cut]
                part = negative_weights(rows16, probe_rows[...], number)
                weights[:, cut] = part
                gp[...] += mul(rows16, often(part, times_at(count_l, i, size)), NT)
            all_gp = held_p[...] + jnp.where(late, gp[...], 0.0)
            coef = -jax.nn.sigmoid(-jnp.sum(s * w * t, axis=0, keepdims=True))
            g_weight = coef * s * t + gq[...] * s + all_gp * t
            rel_out[...] = rel_in[...] + sum(mul(kind[...], p, NT) for p in split(g_weight, 2))
            to_src[0:depth, :], to_src[depth:, :] = split(coef * w * t + gq[...] * w, 2)
            to_dst[0:depth, :], to_dst[depth:, :] = split(jnp.where(late, coef * w * s + all_gp * w, 0.0), 2)

    return call(
        body, "late_edges",
        [piece, weight, source, query, query_rows, left16, oh_dst, count_l, count_r, kind, dst, target, gq, gp, rel],
        [shape(depth, piece.shape[1]), pair16, pair16, shape(*rel.shape), shape(depth, edges, dtype=BF16), shape(edges, rows, dtype=BF16)],
        scratch_shapes=scratch([shape(depth, edges)] * 3 + [shape(edges, depth, dtype=BF16)]),
    )


def late_left(parity, left, lstate, lgrad, to_src, oh_src, probe, weights, count_l, keep):
    depth, rows = left.shape

    def body(left, lstate, lgrad, to_src, oh_src, probe, weights, count_l, _keep, out, spare, sems):
        def more(i, size):
            return mul(probe[...], weights[:, lanes_at(i, size)], NN) * times_at(count_l, i, size)

        update_and_send([left], lstate, [lgrad], to_src, oh_src, spare, out, sems, fixed=True, more=more)()

    operands = [left, lstate, lgrad, to_src, oh_src, probe, weights, count_l, keep]
    return call(
        only_on(parity, body), "late_left", operands, [shape(depth, rows)], in_large=(8,), out_large=(0,),
        scratch_shapes=[*scratch([shape(1, rows)]), pltpu.SemaphoreType.DMA((rows // 256,))],
        aliases={8: 0},
    )[0]


def late_right(parity, at, far, state, rgrads, to_dst, oh_dst, relations, relation_state, rels, keep):
    depth, rows = keep.shape
    kinds = relations.shape[0]
    count = len(far)

    def body(state, to_dst, oh_dst, relations, relation_state, *rest):
        pieces, grads, rels = rest[:count], rest[count : 2 * count], rest[2 * count : 2 * count + len_rels]
        out, relations_out, new_relations, spare, sems, sem = rest[2 * count + len_rels + 1 :]
        grad = sum(ref[...] for ref in rels)
        first = lax.broadcasted_iota(jnp.int32, (kinds, kinds), 0)
        second = lax.broadcasted_iota(jnp.int32, (kinds, kinds), 1)
        old = jnp.sum(jnp.where(first == second, relation_state[...], 0.0), axis=1, keepdims=True)
        new = old + jnp.sum(grad * grad, axis=1, keepdims=True) * (1.0 / depth)
        new_relations[...] = relations[...] - grad * (rate * lax.rsqrt(new))
        copy = pltpu.make_async_copy(new_relations, relations_out, sem)
        copy.start()

        @on_parity(parity)
        def _():
            update_and_send(pieces, state, grads, to_dst, oh_dst, spare, out, sems, fixed=True, start=at)()

        copy.wait()

    len_rels = len(rels)
    operands = [state, to_dst, oh_dst, relations, relation_state, *far, *rgrads, *rels, keep]
    place = len(operands) - 1
    return call(
        body, "late_right", operands, [shape(depth, rows), shape(kinds, depth)], in_large=(place,), out_large=(0, 1),
        scratch_shapes=[
            *scratch([shape(kinds, depth), shape(1, rows)]),
            pltpu.SemaphoreType.DMA((rows // 256,)),
            pltpu.SemaphoreType.DMA,
        ],
        aliases={place: 0},
    )


def local(
    left_slab, left_state, right_slab, right_state, relations, relation_state,
    src_index, dst_index, relation_id, neg_source, neg_target,
):
    peers = lax.axis_size("blk")
    inside = [(i, i + 1) for i in range(0, peers, 2)]
    swap = inside + [(i + 1, i) for i in range(0, peers, 2)]
    across = [(i, (i + 1) % peers) for i in range(1, peers, 2)]
    skip = [(i, (i + 2) % peers) for i in range(0, peers, 2)]
    index = (src_index, dst_index, relation_id, neg_source, neg_target)
    left = left_slab.T
    right = right_slab.T
    rows = left.shape[1]
    lstate = left_state.reshape(1, rows)
    number = float(neg_source.shape[1])
    right_far = lax.ppermute(right, "blk", across)
    right_near = [lax.ppermute(right[:, at : at + size], "blk", inside) for at, size in pieces_of(rows, NEAR_FIRST)]
    state_near = lax.ppermute(right_state, "blk", swap)
    state_far = lax.ppermute(state_near, "blk", skip).reshape(1, rows)
    state_near = state_near.reshape(1, rows)
    rel = jnp.zeros(relations.shape, F32)
    ready = prepared(0, left, relations, index)
    left_a, lstate, far, rel = trained(1, "first_near", number, False, FAR, left, lstate, right_near, state_near, rel, ready)
    far = [lax.ppermute(piece, "blk", across) for piece in far]
    left_a, lstate, near, rel = trained(
        0, "first_far", number, True, NEAR, left, lstate, [right_far], state_far, rel, ready, (left_a,)
    )
    near = [lax.ppermute(piece, "blk", inside) for piece in near]
    ready = prepared(1, left_a, relations, index)
    first_lstate = lstate
    left_b, lstate, right_b, rel = trained(1, "last_near", number, True, (), left_a, lstate, near, state_near, rel, ready)
    cuts = pieces_of(rows, FAR)
    bound = cuts[1][0]
    target, gq, rgrad = last_piece(0, "last_piece0", number, 0, far[0], ready, lstate)
    rgrads = [rgrad]
    lgrad, to_dst, gp = early_edges(0, number, 1, bound, target, ready, dst_index)
    right_b, state = early_right(0, far[0], rgrad, to_dst, ready[6], right_b[0])
    for i in range(1, len(far) - 1):
        target, gq, rgrad = last_piece(0, "last_piece%d" % i, number, cuts[i][0], far[i], ready, state, (target, gq))
        rgrads.append(rgrad)
    rgrad, to_src, to_dst, rel, probe, weights = late_edges(
        0, number, 1, cuts[-1][0], bound, far[-1], ready, dst_index, target, gq, gp, rel
    )
    rgrads.append(rgrad)
    if lax.axis_size("rel") == 2:
        rels = [rel, lax.ppermute(rel, "rel", [(0, 1), (1, 0)])]
    else:
        rels = [lax.psum(rel, "rel")]
    left_b = late_left(0, left_a, first_lstate, lgrad, to_src, ready[5], probe, weights, ready[7], left_b)
    right_b, relations_out = late_right(
        0, bound, far[1:], state, rgrads[1:], to_dst, ready[6], relations, relation_state.reshape(1, -1), rels, right_b
    )
    return (left_b.T, right_b.T, relations_out[None])


def solution(mesh):
    in_specs = (
        P(("blk", "rel"), None),
        P(("blk", "rel")),
        P(("blk", "rel"), None),
        P(("blk", "rel")),
        P(),
        P(),
        P(None, ("blk", "rel")),
        P(None, ("blk", "rel")),
        P(None, ("blk", "rel")),
        P(None, ("blk", "rel")),
        P(None, ("blk", "rel")),
    )
    out_specs = (P(("blk", "rel"), None), P(("blk", "rel"), None), P("blk", None, None))
    return jax.shard_map(local, mesh=mesh, in_specs=in_specs, out_specs=out_specs, check_vma=False)
```

```python
import functools

import jax
import jax.numpy as jnp
from jax import lax
from jax.experimental import pallas as pl
from jax.experimental.pallas import tpu as pltpu
from jax.sharding import PartitionSpec as P

rate = 0.1
F32 = jnp.float32
BF16 = jnp.bfloat16
LANES = 128
NEAR = (4, 4)
STATE = 0
NEAR_FIRST = (4, 4)
FAR = (5, 2, 1)
VMEM_LIMIT = 30 * 2**20

NN = (((1,), (0,)), ((), ()))
NT = (((1,), (1,)), ((), ()))
TN = (((0,), (0,)), ((), ()))


def mul(a, b, dims):
    return lax.dot_general(a, b, dims, preferred_element_type=F32)


def split(x, parts):
    out = []
    for _ in range(parts):
        part = x.astype(BF16)
        out.append(part)
        x = x - part.astype(F32)
    return out


def mul_parts(parts, table, dims):
    along = dims[0][1][0]
    return mul(jnp.concatenate(parts, axis=1), jnp.concatenate([table] * len(parts), axis=along), dims)


def lanes_at(i, size, start=0):
    if isinstance(i, int):
        return slice(start + i * size, start + (i + 1) * size)
    return pl.ds(pl.multiple_of(start + i * size, LANES), size)


def step_of(rows):
    return 512 if rows % 512 == 0 else 256


def each(count, body, fixed=False):
    if fixed:
        for i in range(count):
            body(i)
        return

    def one(i, carry):
        body(i)
        return carry

    lax.fori_loop(0, count, one, 0)


def row_onehot(idx, table):
    count, rows = table.shape
    col = jnp.broadcast_to(idx, (LANES, count)).T
    lane = lax.broadcasted_iota(jnp.int32, (count, LANES), 1)

    def tile(t):
        hit = col == lane + t * LANES
        table[:, lanes_at(t, LANES)] = jnp.where(hit, 1.0, 0.0).astype(BF16)

    each(rows // LANES, tile)


def row_counts(idx, rows):
    count = idx.shape[1]
    high = lax.broadcasted_iota(jnp.int32, (rows // LANES, count), 0)
    low = lax.broadcasted_iota(jnp.int32, (LANES, count), 0)
    high_hit = jnp.where(idx // LANES == high, 1.0, 0.0).astype(BF16)
    low_hit = jnp.where(idx % LANES == low, 1.0, 0.0).astype(BF16)
    return mul(high_hit, low_hit, NT)


def times_at(counts, i, size, start=0):
    first = (start + i * size) // LANES
    return jnp.concatenate([counts[pl.ds(first + t, 1), :] for t in range(size // LANES)], axis=1)


def half_rows(x):
    return (0.5 * x).T.astype(BF16)


def negative_weights(rows16, query_rows, number):
    half = 0.5 / number
    return (jnp.tanh(mul(query_rows, rows16, NN)) * half + half).astype(BF16)


def often(weight, times):
    return (weight.astype(F32) * times).astype(BF16)


def negatives(rows16, query, query_rows, times, number):
    weight = negative_weights(rows16, query_rows, number)
    return mul(query, weight, NN) * times, mul(rows16, often(weight, times), NT)


def prepare(step, left, relations, src, dst, rid, nsrc, ndst,
            weight, source, query, query_rows, left16, oh_src, oh_dst, count_l, count_r, kind):
    rows = left.shape[1]
    here = slice(step, step + 1)
    row_onehot(src[here, :], oh_src)
    row_onehot(dst[here, :], oh_dst)
    count_l[...] = row_counts(nsrc[here, :], rows)
    count_r[...] = row_counts(ndst[here, :], rows)
    kinds = lax.broadcasted_iota(jnp.int32, kind.shape, 0)
    kind[...] = jnp.where(rid[here, :] == kinds, 1.0, 0.0).astype(BF16)
    weight[...] = sum(mul(part, kind[...], TN) for part in split(relations[...], 3))
    source[...] = jnp.zeros_like(source)

    size = step_of(rows)

    def part(i):
        cut = lanes_at(i, size)
        parts = split(left[:, cut], 3)
        left16[:, cut] = parts[0]
        source[...] += mul_parts(parts, oh_src[:, cut], NT)

    each(rows // size, part)
    product = source[...] * weight[...]
    query[...] = product.astype(BF16)
    query_rows[...] = half_rows(product.astype(BF16).astype(F32))


def take_piece(number, start, piece, query, query_rows, oh_dst, count_r, target, gq, rgrad, fixed=False):
    depth = target.shape[0]
    if start == 0:
        target[...] = jnp.zeros_like(target)
        gq[...] = jnp.zeros_like(gq)

    size = step_of(piece.shape[1])

    def part(i):
        cut = lanes_at(i, size)
        parts = split(piece[0:depth, cut], 3)
        hits = oh_dst[:, lanes_at(i, size, start)]
        target[...] += mul_parts(parts, hits, NT)
        times = times_at(count_r, i, size, start)
        rgrad[:, cut], more = negatives(parts[0], query[...], query_rows[...], times, number)
        gq[...] += more

    each(piece.shape[1] // size, part, fixed)


def join(number, weight, source, target, gq, left16, count_l, kind, rel_in,
         probe, probe_rows, gp, lgrad, to_src, to_dst, rel_out, fixed=False):
    rows = left16.shape[1]
    product = weight[...] * target[...]
    probe[...] = product.astype(BF16)
    probe_rows[...] = half_rows(product.astype(BF16).astype(F32))
    gp[...] = jnp.zeros_like(gp)

    size = step_of(rows)

    def part(i):
        cut = lanes_at(i, size)
        lgrad[:, cut], more = negatives(left16[:, cut], probe[...], probe_rows[...], times_at(count_l, i, size), number)
        gp[...] += more

    each(rows // size, part, fixed)
    depth = weight.shape[0]
    w, s, t = weight[...], source[...], target[...]
    coef = -jax.nn.sigmoid(-jnp.sum(s * w * t, axis=0, keepdims=True))
    to_src[0:depth, :], to_src[depth:, :] = split(coef * w * t + gq[...] * w, 2)
    to_dst[0:depth, :], to_dst[depth:, :] = split(coef * w * s + gp[...] * w, 2)
    g_weight = coef * s * t + gq[...] * s + gp[...] * t
    rel_out[...] = rel_in[...] + sum(mul(kind[...], p, NT) for p in split(g_weight, 2))


def adagrad(slab, state, grad, edges, table, start, out, new_state, send=None, fixed=False, more=None):
    depth = grad.shape[0]
    size = step_of(grad.shape[1])

    def part(i):
        cut = lanes_at(i, size)
        hits = table[:, lanes_at(i, size, start)]
        g = grad[:, cut] + mul_parts([edges[0:depth, :], edges[depth:, :]], hits, NN)
        if more is not None:
            g = g + more(i, size)
        new = state[:, cut] + jnp.sum(g * g, axis=0, keepdims=True) * (1.0 / depth)
        new_state[:, cut] = new
        out[0:depth, cut] = slab[0:depth, cut] - g * (rate * lax.rsqrt(new))
        if send is not None:
            send(i).start()

    each(grad.shape[1] // size, part, fixed)


def sender(result, to, start, sems):
    size = step_of(result.shape[1])

    def copy(i):
        here = lanes_at(i, size)
        there = lanes_at(i, size, start)
        return pltpu.make_async_copy(result.at[:, here], to.at[:, there], sems.at[i + start // 256])

    return copy


def update_and_send(pieces, state, grads, edges, table, new_state, to, sems, fixed=False, start=0, more=None):
    sent = []
    for piece, grad in zip(pieces, grads):
        rows = grad.shape[1]
        copy = sender(grad, to, start, sems)
        cut = slice(start, start + rows)
        adagrad(piece, state.at[:, cut], grad, edges, table, start, grad, new_state.at[:, cut], copy, fixed, more)
        sent.append((copy, rows // step_of(rows)))
        start += rows

    def wait():
        for copy, count in sent:
            each(count, lambda i, copy=copy: copy(i).wait(), fixed)

    return wait


def pack_state(state, piece, depth):
    size = state.shape[1] // 8
    for k in range(8):
        piece[depth + k : depth + k + 1, 0:size] = state[:, k * size : (k + 1) * size]


def unpack_state(piece, depth, state):
    size = state.shape[1] // 8
    for k in range(8):
        state[:, k * size : (k + 1) * size] = piece[depth + k : depth + k + 1, 0:size]


def on_parity(parity):
    return pl.when(lax.axis_index("blk") % 2 == parity)


def pieces_of(rows, eighths):
    sizes = [rows // 8 * n for n in eighths]
    return [(sum(sizes[:i]), size) for i, size in enumerate(sizes)]


def rows_of(pieces, at, size):
    found = []
    start = 0
    for piece in pieces:
        begin, end = max(at, start), min(at + size, start + piece.shape[1])
        if begin < end:
            found.append((piece.at[:, begin - start : end - start], begin, end - begin))
        start += piece.shape[1]
    return found


def train(parity, number, last, fixed, kept, takes, gives, *refs):
    refs = list(refs)
    (left, lstate, rstate_in, rel_in) = refs[:4]
    (weight, source, query, query_rows, left16, oh_src, oh_dst, count_l, count_r, kind) = refs[4:14]
    right = refs[14 : 14 + takes]
    refs = refs[14 + takes + kept :]
    left_out, lstate_out, rel_out = refs[:3]
    right_out = refs[3 : 3 + len(gives)]
    (target, gq, rgrad, probe, probe_rows, gp, lgrad, to_src, to_dst, rstate, spare, sems) = refs[3 + len(gives) :]
    depth, rows = left.shape
    lstate_out[...] = lstate[...]
    rel_out[...] = rel_in[...]

    @on_parity(parity)
    def _():
        grads = []
        at = 0
        for piece in right:
            grads.append(rgrad.at[:, at : at + piece.shape[1]])
            take_piece(number, at, piece, query, query_rows, oh_dst, count_r, target, gq, grads[-1], fixed)
            at += piece.shape[1]
        join(number, weight, source, target, gq, left16, count_l, kind, rel_in,
             probe, probe_rows, gp, lgrad, to_src, to_dst, rel_out, fixed)
        if last:
            unpack_state(right[STATE], depth, rstate)
            wait_right = update_and_send(right, rstate, grads, to_dst, oh_dst, spare, right_out[0], sems.at[0], fixed)
            wait_left = update_and_send([left], lstate, [lgrad], to_src, oh_src, spare, left_out, sems.at[1], fixed)
            wait_right()
            wait_left()
        else:
            for (at, size), out in zip(pieces_of(rows, gives), right_out):
                for old, begin, length in rows_of(right, at, size):
                    cut = slice(begin, begin + length)
                    here = slice(begin - at, begin - at + length)
                    adagrad(old, rstate_in.at[:, cut], rgrad.at[:, cut], to_dst, oh_dst, begin, out.at[:, here], spare.at[:, cut], None, fixed)
            pack_state(spare, right_out[STATE], depth)
            adagrad(left, lstate, lgrad, to_src, oh_src, 0, left_out, lstate_out, None, fixed)


def shape(*dims, dtype=F32):
    return jax.ShapeDtypeStruct(dims, dtype)


def prepared_shapes(depth, rows, edges, kinds):
    return (
        shape(depth, edges), shape(depth, edges), shape(depth, edges, dtype=BF16), shape(edges, depth, dtype=BF16),
        shape(depth, rows, dtype=BF16), shape(edges, rows, dtype=BF16), shape(edges, rows, dtype=BF16),
        shape(rows // LANES, LANES), shape(rows // LANES, LANES), shape(kinds, edges, dtype=BF16),
    )


def scratch(shapes):
    return [pltpu.VMEM(s.shape, s.dtype) for s in shapes]


def call(kernel, name, operands, shapes, in_large=(), out_large=(), scratch_shapes=(), aliases=None):
    vmem = pl.BlockSpec(memory_space=pltpu.VMEM)
    large = pl.BlockSpec(memory_space=pl.ANY)
    return pl.pallas_call(
        kernel,
        out_shape=tuple(shapes),
        in_specs=[large if i in in_large else vmem for i in range(len(operands))],
        out_specs=tuple(large if i in out_large else vmem for i in range(len(shapes))),
        scratch_shapes=list(scratch_shapes),
        input_output_aliases=aliases or {},
        compiler_params=pltpu.CompilerParams(vmem_limit_bytes=VMEM_LIMIT),
        cost_estimate=pl.CostEstimate(flops=1_000_000, bytes_accessed=100_000, transcendentals=0),
        name=name,
    )(*operands)


def prepared(step, left, relations, index):
    depth, rows = left.shape
    return call(
        functools.partial(prepare, step), "prepare%d" % step, [left, relations, *index],
        prepared_shapes(depth, rows, index[0].shape[1], relations.shape[0]),
    )


def trained(parity, name, number, fixed, gives, left, lstate, right, rstate, rel, ready, keep=()):
    depth, rows = left.shape
    edges = ready[0].shape[1]
    last = not gives
    blocks = [shape(depth, size) for _at, size in pieces_of(rows, gives or (8,))]
    if not last:
        blocks[STATE] = shape(depth + 8, blocks[STATE].shape[1])
    edge = shape(depth, edges)
    edge16 = shape(depth, edges, dtype=BF16)
    pair16 = shape(2 * depth, edges, dtype=BF16)
    slab = shape(depth, rows)
    inner = [edge, edge, slab, edge16, shape(edges, depth, dtype=BF16), edge, slab, pair16, pair16, shape(1, rows), shape(1, rows)]
    left_out, lstate_out, rel_out, *right_out = call(
        functools.partial(train, parity, number, last, fixed, len(keep), len(right), gives or (8,)),
        name,
        [left, lstate, rstate, rel, *ready, *right, *keep],
        [slab, shape(1, rows), shape(*rel.shape), *blocks],
        out_large=(0, 3) if last else (),
        scratch_shapes=[*scratch(inner), pltpu.SemaphoreType.DMA((2, rows // 256))],
        aliases={14 + len(right) + i: 0 for i in range(len(keep))},
    )
    return left_out, lstate_out, right_out, rel_out


def only_on(parity, body):
    def kernel(*refs):
        @on_parity(parity)
        def _():
            body(*refs)

    return kernel


def last_piece(parity, name, number, at, piece, ready, after, held=()):
    (_weight, _source, query, query_rows, _left16, _oh_src, oh_dst, _count_l, count_r, _kind) = ready
    depth, edges = query.shape

    def body(piece, query, query_rows, oh_dst, count_r, *rest):
        take_piece(number, at, piece, query, query_rows, oh_dst, count_r, *rest[len(held) + 1 :], fixed=True)

    operands = [piece, query, query_rows, oh_dst, count_r, *held, after]
    return call(
        only_on(parity, body), name, operands,
        [shape(depth, edges), shape(depth, edges), shape(depth, piece.shape[1])],
        aliases={5: 0, 6: 1} if held else {},
    )


def source_scores(number, probe, probe_rows, left16, count_l, gp, weights=None):
    rows = left16.shape[1]
    size = step_of(rows)
    gp[...] = jnp.zeros_like(gp)
    for i in range(rows // size):
        cut = lanes_at(i, size)
        rows16 = left16[:, cut]
        part = negative_weights(rows16, probe_rows[...], number)
        if weights is not None:
            weights[:, cut] = part
        gp[...] += mul(rows16, often(part, times_at(count_l, i, size)), NT)


def early_edges(parity, name, number, step, low, high, target, ready, dst):
    (weight, source, _query, _query_rows, left16, _oh_src, _oh_dst, count_l, _count_r, _kind) = ready
    depth = left16.shape[0]
    edges = weight.shape[1]

    def body(weight, source, target, left16, count_l, dst, to_dst, gp, probe, probe_rows):
        w, s, t = weight[...], source[...], target[...]
        product = (w * t).astype(BF16)
        probe[...] = product
        probe_rows[...] = half_rows(product.astype(F32))
        source_scores(number, probe, probe_rows, left16, count_l, gp)
        at = dst[step : step + 1, :]
        here = jnp.logical_and(at >= low, at < high)
        coef = -jax.nn.sigmoid(-jnp.sum(s * w * t, axis=0, keepdims=True))
        to_dst[0:depth, :], to_dst[depth:, :] = split(jnp.where(here, coef * w * s + gp[...] * w, 0.0), 2)

    return call(
        only_on(parity, body), name, [weight, source, target, left16, count_l, dst],
        [shape(2 * depth, edges, dtype=BF16)],
        scratch_shapes=scratch([shape(depth, edges), shape(depth, edges, dtype=BF16), shape(edges, depth, dtype=BF16)]),
    )[0]


def early_right(parity, name, at, piece, state, rgrad, to_dst, oh_dst, keep):
    depth, rows = keep.shape

    def body(piece, rgrad, to_dst, oh_dst, *rest):
        out, new_state, spare, sems = rest[-4:]
        if state is None:
            unpack_state(piece, depth, new_state)
        else:
            new_state[...] = rest[0][...]
        update_and_send([piece], new_state, [rgrad], to_dst, oh_dst, spare, out, sems, fixed=True, start=at)()

    operands = [piece, rgrad, to_dst, oh_dst, *([] if state is None else [state]), keep]
    place = len(operands) - 1
    return call(
        only_on(parity, body), name, operands, [shape(depth, rows), shape(1, rows)],
        in_large=(place,), out_large=(0,),
        scratch_shapes=[*scratch([shape(1, rows)]), pltpu.SemaphoreType.DMA((rows // 256,))],
        aliases={place: 0},
    )


def late_edges(parity, number, step, at, piece, ready, dst, target, gq, rel, after):
    (weight, source, query, query_rows, left16, _oh_src, oh_dst, count_l, count_r, kind) = ready
    depth, rows = left16.shape
    edges = weight.shape[1]
    pair16 = shape(2 * depth, edges, dtype=BF16)

    def body(piece, weight, source, query, query_rows, left16, oh_dst, count_l, count_r, kind, dst, held_t, held_q, rel_in,
             _after, rgrad, to_src, to_dst, rel_out, probe, weights, gp, probe_rows):
        rel_out[...] = rel_in[...]

        @on_parity(parity)
        def _():
            size = piece.shape[1]
            parts = split(piece[...], 3)
            w, s = weight[...], source[...]
            t = held_t[...] + mul_parts(parts, oh_dst[:, at : at + size], NT)
            product = (w * t).astype(BF16)
            probe[...] = product
            probe_rows[...] = half_rows(product.astype(F32))
            source_scores(number, probe, probe_rows, left16, count_l, gp, weights)
            rgrad[...], more = negatives(parts[0], query[...], query_rows[...], times_at(count_r, 0, size, at), number)
            q = held_q[...] + more
            p = gp[...]
            coef = -jax.nn.sigmoid(-jnp.sum(s * w * t, axis=0, keepdims=True))
            g_weight = coef * s * t + q * s + p * t
            rel_out[...] = rel_in[...] + sum(mul(kind[...], part, NT) for part in split(g_weight, 2))
            to_src[0:depth, :], to_src[depth:, :] = split(coef * w * t + q * w, 2)
            here = dst[step : step + 1, :] >= at
            to_dst[0:depth, :], to_dst[depth:, :] = split(jnp.where(here, coef * w * s + p * w, 0.0), 2)

    return call(
        body, "late_edges",
        [piece, weight, source, query, query_rows, left16, oh_dst, count_l, count_r, kind, dst, target, gq, rel, after],
        [shape(depth, piece.shape[1]), pair16, pair16, shape(*rel.shape), shape(depth, edges, dtype=BF16), shape(edges, rows, dtype=BF16)],
        scratch_shapes=scratch([shape(depth, edges), shape(edges, depth, dtype=BF16)]),
    )


def late_slabs(parity, at, left, lstate, to_src, oh_src, probe, weights, count_l, piece, state, rgrad, to_dst, oh_dst, keep_left, keep_right):
    depth, rows = left.shape
    sizes = [512] * (rows // 512 - 1) + [256] * 2

    def body(left, lstate, to_src, oh_src, probe, weights, count_l, piece, state, rgrad, to_dst, oh_dst,
             _keep_left, _keep_right, left_out, right_out, result, spare, sems):
        wait = update_and_send([piece], state, [rgrad], to_dst, oh_dst, spare, right_out, sems.at[1], fixed=True, start=at)
        copies = []
        start = 0
        for i, size in enumerate(sizes):
            cut = slice(start, start + size)
            g = mul(probe[...], weights[:, cut], NN) * times_at(count_l, 0, size, start)
            g = g + mul_parts([to_src[0:depth, :], to_src[depth:, :]], oh_src[:, cut], NN)
            new = lstate[:, cut] + jnp.sum(g * g, axis=0, keepdims=True) * (1.0 / depth)
            result[:, cut] = left[:, cut] - g * (rate * lax.rsqrt(new))
            copies.append(pltpu.make_async_copy(result.at[:, cut], left_out.at[:, cut], sems.at[0, i]))
            copies[-1].start()
            start += size
        wait()
        for copy in copies:
            copy.wait()

    operands = [left, lstate, to_src, oh_src, probe, weights, count_l, piece, state, rgrad, to_dst, oh_dst, keep_left, keep_right]
    return call(
        only_on(parity, body), "late_slabs", operands, [shape(depth, rows), shape(depth, rows)], in_large=(12, 13), out_large=(0, 1),
        scratch_shapes=[*scratch([shape(depth, rows), shape(1, rows)]), pltpu.SemaphoreType.DMA((2, rows // 256))],
        aliases={12: 0, 13: 1},
    )


def relation_update(relations, relation_state, rels):
    kinds, depth = relations.shape

    def body(relations, relation_state, *rest):
        grad = sum(ref[...] for ref in rest[:-1])
        first = lax.broadcasted_iota(jnp.int32, (kinds, kinds), 0)
        second = lax.broadcasted_iota(jnp.int32, (kinds, kinds), 1)
        old = jnp.sum(jnp.where(first == second, relation_state[...], 0.0), axis=1, keepdims=True)
        new = old + jnp.sum(grad * grad, axis=1, keepdims=True) * (1.0 / depth)
        rest[-1][...] = relations[...] - grad * (rate * lax.rsqrt(new))

    return call(body, "relation_update", [relations, relation_state, *rels], [shape(kinds, depth)])[0]


def local(
    left_slab, left_state, right_slab, right_state, relations, relation_state,
    src_index, dst_index, relation_id, neg_source, neg_target,
):
    peers = lax.axis_size("blk")
    inside = [(i, i + 1) for i in range(0, peers, 2)]
    swap = inside + [(i + 1, i) for i in range(0, peers, 2)]
    across = [(i, (i + 1) % peers) for i in range(1, peers, 2)]
    skip = [(i, (i + 2) % peers) for i in range(0, peers, 2)]
    index = (src_index, dst_index, relation_id, neg_source, neg_target)
    left = left_slab.T
    right = right_slab.T
    rows = left.shape[1]
    lstate = left_state.reshape(1, rows)
    number = float(neg_source.shape[1])
    right_far = lax.ppermute(right, "blk", across)
    right_near = [lax.ppermute(right[:, at : at + size], "blk", inside) for at, size in pieces_of(rows, NEAR_FIRST)]
    state_near = lax.ppermute(right_state, "blk", swap)
    state_far = lax.ppermute(state_near, "blk", skip).reshape(1, rows)
    state_near = state_near.reshape(1, rows)
    rel = jnp.zeros(relations.shape, F32)
    ready = prepared(0, left, relations, index)
    left_a, lstate, far, rel = trained(1, "first_near", number, False, FAR, left, lstate, right_near, state_near, rel, ready)
    far = [lax.ppermute(piece, "blk", across) for piece in far]
    left_a, lstate, near, rel = trained(
        0, "first_far", number, True, NEAR, left, lstate, [right_far], state_far, rel, ready, (left_a,)
    )
    near = [lax.ppermute(piece, "blk", inside) for piece in near]
    ready = prepared(1, left_a, relations, index)
    first_lstate = lstate
    left_b, lstate, right_b, rel = trained(1, "last_near", number, True, (), left_a, lstate, near, state_near, rel, ready)
    cuts = pieces_of(rows, FAR)
    right_b, = right_b
    held = ()
    state = None
    for i, (at, size) in enumerate(cuts[:-1]):
        after = lstate if state is None else state
        target, gq, rgrad = last_piece(0, "last_piece%d" % i, number, at, far[i], ready, after, held)
        held = (target, gq)
        to_dst = early_edges(0, "early_edges%d" % i, number, 1, at, at + size, target, ready, dst_index)
        right_b, state = early_right(0, "early_right%d" % i, at, far[i], state, rgrad, to_dst, ready[6], right_b)
    at = cuts[-1][0]
    rgrad, to_src, to_dst, rel, probe, weights = late_edges(0, number, 1, at, far[-1], ready, dst_index, target, gq, rel, state)
    if lax.axis_size("rel") == 2:
        rels = [rel, lax.ppermute(rel, "rel", [(0, 1), (1, 0)])]
    else:
        rels = [lax.psum(rel, "rel")]
    left_b, right_b = late_slabs(
        0, at, left_a, first_lstate, to_src, ready[5], probe, weights, ready[7],
        far[-1], state, rgrad, to_dst, ready[6], left_b, right_b,
    )
    relations_out = relation_update(relations, relation_state.reshape(1, -1), rels)
    return (left_b.T, right_b.T, relations_out[None])


def solution(mesh):
    in_specs = (
        P(("blk", "rel"), None),
        P(("blk", "rel")),
        P(("blk", "rel"), None),
        P(("blk", "rel")),
        P(),
        P(),
        P(None, ("blk", "rel")),
        P(None, ("blk", "rel")),
        P(None, ("blk", "rel")),
        P(None, ("blk", "rel")),
        P(None, ("blk", "rel")),
    )
    out_specs = (P(("blk", "rel"), None), P(("blk", "rel"), None), P("blk", None, None))
    return jax.shard_map(local, mesh=mesh, in_specs=in_specs, out_specs=out_specs, check_vma=False)
```

```python
import functools

import jax
import jax.numpy as jnp
from jax import lax
from jax.experimental import pallas as pl
from jax.experimental.pallas import tpu as pltpu
from jax.sharding import PartitionSpec as P

rate = 0.1
F32 = jnp.float32
BF16 = jnp.bfloat16
LANES = 128
NEAR = (4, 4)
STATE = 0
NEAR_FIRST = (4, 4)
FAR = (5, 2, 1)
VMEM_LIMIT = 30 * 2**20

NN = (((1,), (0,)), ((), ()))
NT = (((1,), (1,)), ((), ()))
TN = (((0,), (0,)), ((), ()))


def mul(a, b, dims):
    return lax.dot_general(a, b, dims, preferred_element_type=F32)


def split(x, parts):
    out = []
    for _ in range(parts):
        part = x.astype(BF16)
        out.append(part)
        x = x - part.astype(F32)
    return out


def mul_parts(parts, table, dims):
    along = dims[0][1][0]
    return mul(jnp.concatenate(parts, axis=1), jnp.concatenate([table] * len(parts), axis=along), dims)


def lanes_at(i, size, start=0):
    if isinstance(i, int):
        return slice(start + i * size, start + (i + 1) * size)
    return pl.ds(pl.multiple_of(start + i * size, LANES), size)


def step_of(rows, fixed=True):
    return 512 if rows % 512 == 0 and not fixed else 256


def each(count, body, fixed=False):
    if fixed:
        for i in range(count):
            body(i)
        return

    def one(i, carry):
        body(i)
        return carry

    lax.fori_loop(0, count, one, 0)


def row_onehot(idx, table):
    count, rows = table.shape
    col = jnp.broadcast_to(idx, (LANES, count)).T
    lane = lax.broadcasted_iota(jnp.int32, (count, LANES), 1)

    def tile(t):
        hit = col == lane + t * LANES
        table[:, lanes_at(t, LANES)] = jnp.where(hit, 1.0, 0.0).astype(BF16)

    each(rows // LANES, tile)


def row_counts(idx, rows):
    count = idx.shape[1]
    high = lax.broadcasted_iota(jnp.int32, (rows // LANES, count), 0)
    low = lax.broadcasted_iota(jnp.int32, (LANES, count), 0)
    high_hit = jnp.where(idx // LANES == high, 1.0, 0.0).astype(BF16)
    low_hit = jnp.where(idx % LANES == low, 1.0, 0.0).astype(BF16)
    return mul(high_hit, low_hit, NT)


def times_at(counts, i, size, start=0):
    first = (start + i * size) // LANES
    return jnp.concatenate([counts[pl.ds(first + t, 1), :] for t in range(size // LANES)], axis=1)


def half_rows(x):
    return (0.5 * x).T.astype(BF16)


def negative_weights(rows16, query_rows, number):
    half = 0.5 / number
    return (jnp.tanh(mul(query_rows, rows16, NN)) * half + half).astype(BF16)


def often(weight, times):
    return (weight.astype(F32) * times).astype(BF16)


def negatives(rows16, query, query_rows, times, number):
    weight = negative_weights(rows16, query_rows, number)
    return mul(query, weight, NN) * times, mul(rows16, often(weight, times), NT)


def prepare(step, left, relations, src, dst, rid, nsrc, ndst,
            weight, source, query, query_rows, left16, oh_src, oh_dst, count_l, count_r, kind):
    rows = left.shape[1]
    here = slice(step, step + 1)
    row_onehot(src[here, :], oh_src)
    row_onehot(dst[here, :], oh_dst)
    count_l[...] = row_counts(nsrc[here, :], rows)
    count_r[...] = row_counts(ndst[here, :], rows)
    kinds = lax.broadcasted_iota(jnp.int32, kind.shape, 0)
    kind[...] = jnp.where(rid[here, :] == kinds, 1.0, 0.0).astype(BF16)
    weight[...] = sum(mul(part, kind[...], TN) for part in split(relations[...], 3))
    source[...] = jnp.zeros_like(source)

    size = step_of(rows, fixed=False)

    def part(i):
        cut = lanes_at(i, size)
        parts = split(left[:, cut], 3)
        left16[:, cut] = parts[0]
        source[...] += mul_parts(parts, oh_src[:, cut], NT)

    each(rows // size, part)
    product = source[...] * weight[...]
    query[...] = product.astype(BF16)
    query_rows[...] = half_rows(product.astype(BF16).astype(F32))


def take_piece(number, start, piece, query, query_rows, oh_dst, count_r, target, gq, rgrad, fixed=False):
    depth = target.shape[0]
    if start == 0:
        target[...] = jnp.zeros_like(target)
        gq[...] = jnp.zeros_like(gq)

    size = step_of(piece.shape[1], fixed)

    def part(i):
        cut = lanes_at(i, size)
        parts = split(piece[0:depth, cut], 3)
        hits = oh_dst[:, lanes_at(i, size, start)]
        target[...] += mul_parts(parts, hits, NT)
        times = times_at(count_r, i, size, start)
        rgrad[:, cut], more = negatives(parts[0], query[...], query_rows[...], times, number)
        gq[...] += more

    each(piece.shape[1] // size, part, fixed)


def join(number, weight, source, target, gq, left16, count_l, kind, rel_in,
         probe, probe_rows, gp, lgrad, to_src, to_dst, rel_out, fixed=False):
    rows = left16.shape[1]
    product = weight[...] * target[...]
    probe[...] = product.astype(BF16)
    probe_rows[...] = half_rows(product.astype(BF16).astype(F32))
    gp[...] = jnp.zeros_like(gp)

    size = step_of(rows, fixed)

    def part(i):
        cut = lanes_at(i, size)
        lgrad[:, cut], more = negatives(left16[:, cut], probe[...], probe_rows[...], times_at(count_l, i, size), number)
        gp[...] += more

    each(rows // size, part, fixed)
    depth = weight.shape[0]
    w, s, t = weight[...], source[...], target[...]
    coef = -jax.nn.sigmoid(-jnp.sum(s * w * t, axis=0, keepdims=True))
    to_src[0:depth, :], to_src[depth:, :] = split(coef * w * t + gq[...] * w, 2)
    to_dst[0:depth, :], to_dst[depth:, :] = split(coef * w * s + gp[...] * w, 2)
    g_weight = coef * s * t + gq[...] * s + gp[...] * t
    rel_out[...] = rel_in[...] + sum(mul(kind[...], p, NT) for p in split(g_weight, 2))


def adagrad(slab, state, grad, edges, table, start, out, new_state, send=None, fixed=False, more=None):
    depth = grad.shape[0]
    size = step_of(grad.shape[1], fixed)

    def part(i):
        cut = lanes_at(i, size)
        hits = table[:, lanes_at(i, size, start)]
        g = grad[:, cut] + mul_parts([edges[0:depth, :], edges[depth:, :]], hits, NN)
        if more is not None:
            g = g + more(i, size)
        new = state[:, cut] + jnp.sum(g * g, axis=0, keepdims=True) * (1.0 / depth)
        new_state[:, cut] = new
        out[0:depth, cut] = slab[0:depth, cut] - g * (rate * lax.rsqrt(new))
        if send is not None:
            send(i).start()

    each(grad.shape[1] // size, part, fixed)


def sender(result, to, start, sems, fixed):
    size = step_of(result.shape[1], fixed)

    def copy(i):
        here = lanes_at(i, size)
        there = lanes_at(i, size, start)
        return pltpu.make_async_copy(result.at[:, here], to.at[:, there], sems.at[i + start // 256])

    return copy


def update_and_send(pieces, state, grads, edges, table, new_state, to, sems, fixed=False, start=0, more=None):
    sent = []
    for piece, grad in zip(pieces, grads):
        rows = grad.shape[1]
        copy = sender(grad, to, start, sems, fixed)
        cut = slice(start, start + rows)
        adagrad(piece, state.at[:, cut], grad, edges, table, start, grad, new_state.at[:, cut], copy, fixed, more)
        sent.append((copy, rows // step_of(rows, fixed)))
        start += rows

    def wait():
        for copy, count in sent:
            each(count, lambda i, copy=copy: copy(i).wait(), fixed)

    return wait


def pack_state(state, piece, depth):
    size = state.shape[1] // 8
    for k in range(8):
        piece[depth + k : depth + k + 1, 0:size] = state[:, k * size : (k + 1) * size]


def unpack_state(piece, depth, state):
    size = state.shape[1] // 8
    for k in range(8):
        state[:, k * size : (k + 1) * size] = piece[depth + k : depth + k + 1, 0:size]


def on_parity(parity):
    return pl.when(lax.axis_index("blk") % 2 == parity)


def pieces_of(rows, eighths):
    sizes = [rows // 8 * n for n in eighths]
    return [(sum(sizes[:i]), size) for i, size in enumerate(sizes)]


def rows_of(pieces, at, size):
    found = []
    start = 0
    for piece in pieces:
        begin, end = max(at, start), min(at + size, start + piece.shape[1])
        if begin < end:
            found.append((piece.at[:, begin - start : end - start], begin, end - begin))
        start += piece.shape[1]
    return found


def train(parity, number, last, fixed, kept, takes, gives, *refs):
    refs = list(refs)
    (left, lstate, rstate_in, rel_in) = refs[:4]
    (weight, source, query, query_rows, left16, oh_src, oh_dst, count_l, count_r, kind) = refs[4:14]
    right = refs[14 : 14 + takes]
    refs = refs[14 + takes + kept :]
    left_out, lstate_out, rel_out = refs[:3]
    right_out = refs[3 : 3 + len(gives)]
    (target, gq, rgrad, probe, probe_rows, gp, lgrad, to_src, to_dst, rstate, spare, sems) = refs[3 + len(gives) :]
    depth, rows = left.shape
    lstate_out[...] = lstate[...]
    rel_out[...] = rel_in[...]

    @on_parity(parity)
    def _():
        grads = []
        at = 0
        for piece in right:
            grads.append(rgrad.at[:, at : at + piece.shape[1]])
            take_piece(number, at, piece, query, query_rows, oh_dst, count_r, target, gq, grads[-1], fixed)
            at += piece.shape[1]
        join(number, weight, source, target, gq, left16, count_l, kind, rel_in,
             probe, probe_rows, gp, lgrad, to_src, to_dst, rel_out, fixed)
        if last:
            unpack_state(right[STATE], depth, rstate)
            wait_right = update_and_send(right, rstate, grads, to_dst, oh_dst, spare, right_out[0], sems.at[0], fixed)
            wait_left = update_and_send([left], lstate, [lgrad], to_src, oh_src, spare, left_out, sems.at[1], fixed)
            wait_right()
            wait_left()
        else:
            for (at, size), out in zip(pieces_of(rows, gives), right_out):
                for old, begin, length in rows_of(right, at, size):
                    cut = slice(begin, begin + length)
                    here = slice(begin - at, begin - at + length)
                    adagrad(old, rstate_in.at[:, cut], rgrad.at[:, cut], to_dst, oh_dst, begin, out.at[:, here], spare.at[:, cut], None, fixed)
            pack_state(spare, right_out[STATE], depth)
            adagrad(left, lstate, lgrad, to_src, oh_src, 0, left_out, lstate_out, None, fixed)


def shape(*dims, dtype=F32):
    return jax.ShapeDtypeStruct(dims, dtype)


def prepared_shapes(depth, rows, edges, kinds):
    return (
        shape(depth, edges), shape(depth, edges), shape(depth, edges, dtype=BF16), shape(edges, depth, dtype=BF16),
        shape(depth, rows, dtype=BF16), shape(edges, rows, dtype=BF16), shape(edges, rows, dtype=BF16),
        shape(rows // LANES, LANES), shape(rows // LANES, LANES), shape(kinds, edges, dtype=BF16),
    )


def scratch(shapes):
    return [pltpu.VMEM(s.shape, s.dtype) for s in shapes]


def call(kernel, name, operands, shapes, in_large=(), out_large=(), scratch_shapes=(), aliases=None):
    vmem = pl.BlockSpec(memory_space=pltpu.VMEM)
    large = pl.BlockSpec(memory_space=pl.ANY)
    return pl.pallas_call(
        kernel,
        out_shape=tuple(shapes),
        in_specs=[large if i in in_large else vmem for i in range(len(operands))],
        out_specs=tuple(large if i in out_large else vmem for i in range(len(shapes))),
        scratch_shapes=list(scratch_shapes),
        input_output_aliases=aliases or {},
        compiler_params=pltpu.CompilerParams(vmem_limit_bytes=VMEM_LIMIT),
        cost_estimate=pl.CostEstimate(flops=1_000_000, bytes_accessed=100_000, transcendentals=0),
        name=name,
    )(*operands)


def prepared(step, left, relations, index):
    depth, rows = left.shape
    return call(
        functools.partial(prepare, step), "prepare%d" % step, [left, relations, *index],
        prepared_shapes(depth, rows, index[0].shape[1], relations.shape[0]),
    )


def trained(parity, name, number, fixed, gives, left, lstate, right, rstate, rel, ready, keep=()):
    depth, rows = left.shape
    edges = ready[0].shape[1]
    last = not gives
    blocks = [shape(depth, size) for _at, size in pieces_of(rows, gives or (8,))]
    if not last:
        blocks[STATE] = shape(depth + 8, blocks[STATE].shape[1])
    edge = shape(depth, edges)
    edge16 = shape(depth, edges, dtype=BF16)
    pair16 = shape(2 * depth, edges, dtype=BF16)
    slab = shape(depth, rows)
    inner = [edge, edge, slab, edge16, shape(edges, depth, dtype=BF16), edge, slab, pair16, pair16, shape(1, rows), shape(1, rows)]
    left_out, lstate_out, rel_out, *right_out = call(
        functools.partial(train, parity, number, last, fixed, len(keep), len(right), gives or (8,)),
        name,
        [left, lstate, rstate, rel, *ready, *right, *keep],
        [slab, shape(1, rows), shape(*rel.shape), *blocks],
        out_large=(0, 3) if last else (),
        scratch_shapes=[*scratch(inner), pltpu.SemaphoreType.DMA((2, rows // 256))],
        aliases={14 + len(right) + i: 0 for i in range(len(keep))},
    )
    return left_out, lstate_out, right_out, rel_out


def only_on(parity, body):
    def kernel(*refs):
        @on_parity(parity)
        def _():
            body(*refs)

    return kernel


def last_piece(parity, name, number, at, piece, ready, after, held=()):
    (_weight, _source, query, query_rows, _left16, _oh_src, oh_dst, _count_l, count_r, _kind) = ready
    depth, edges = query.shape

    def body(piece, query, query_rows, oh_dst, count_r, *rest):
        take_piece(number, at, piece, query, query_rows, oh_dst, count_r, *rest[len(held) + 1 :], fixed=True)

    operands = [piece, query, query_rows, oh_dst, count_r, *held, after]
    return call(
        only_on(parity, body), name, operands,
        [shape(depth, edges), shape(depth, edges), shape(depth, piece.shape[1])],
        aliases={5: 0, 6: 1} if held else {},
    )


def source_scores(number, probe, probe_rows, left16, count_l, gp, weights=None):
    rows = left16.shape[1]
    size = step_of(rows)
    gp[...] = jnp.zeros_like(gp)
    for i in range(rows // size):
        cut = lanes_at(i, size)
        rows16 = left16[:, cut]
        part = negative_weights(rows16, probe_rows[...], number)
        if weights is not None:
            weights[:, cut] = part
        gp[...] += mul(rows16, often(part, times_at(count_l, i, size)), NT)


def early_edges(parity, name, number, step, low, high, target, ready, dst):
    (weight, source, _query, _query_rows, left16, _oh_src, _oh_dst, count_l, _count_r, _kind) = ready
    depth = left16.shape[0]
    edges = weight.shape[1]

    def body(weight, source, target, left16, count_l, dst, to_dst, gp, probe, probe_rows):
        w, s, t = weight[...], source[...], target[...]
        product = (w * t).astype(BF16)
        probe[...] = product
        probe_rows[...] = half_rows(product.astype(F32))
        source_scores(number, probe, probe_rows, left16, count_l, gp)
        at = dst[step : step + 1, :]
        here = jnp.logical_and(at >= low, at < high)
        coef = -jax.nn.sigmoid(-jnp.sum(s * w * t, axis=0, keepdims=True))
        to_dst[0:depth, :], to_dst[depth:, :] = split(jnp.where(here, coef * w * s + gp[...] * w, 0.0), 2)

    return call(
        only_on(parity, body), name, [weight, source, target, left16, count_l, dst],
        [shape(2 * depth, edges, dtype=BF16)],
        scratch_shapes=scratch([shape(depth, edges), shape(depth, edges, dtype=BF16), shape(edges, depth, dtype=BF16)]),
    )[0]


def early_right(parity, name, at, piece, state, rgrad, to_dst, oh_dst, keep):
    depth, rows = keep.shape

    def body(piece, rgrad, to_dst, oh_dst, *rest):
        out, new_state, spare, sems = rest[-4:]
        if state is None:
            unpack_state(piece, depth, new_state)
        else:
            new_state[...] = rest[0][...]
        update_and_send([piece], new_state, [rgrad], to_dst, oh_dst, spare, out, sems, fixed=True, start=at)()

    operands = [piece, rgrad, to_dst, oh_dst, *([] if state is None else [state]), keep]
    place = len(operands) - 1
    return call(
        only_on(parity, body), name, operands, [shape(depth, rows), shape(1, rows)],
        in_large=(place,), out_large=(0,),
        scratch_shapes=[*scratch([shape(1, rows)]), pltpu.SemaphoreType.DMA((rows // 256,))],
        aliases={place: 0},
    )


def late_edges(parity, number, step, at, piece, ready, dst, target, gq, rel, after):
    (weight, source, query, query_rows, left16, _oh_src, oh_dst, count_l, count_r, kind) = ready
    depth, rows = left16.shape
    edges = weight.shape[1]
    pair16 = shape(2 * depth, edges, dtype=BF16)

    def body(piece, weight, source, query, query_rows, left16, oh_dst, count_l, count_r, kind, dst, held_t, held_q, rel_in,
             _after, rgrad, to_src, to_dst, rel_out, probe, weights, gp, probe_rows):
        rel_out[...] = rel_in[...]

        @on_parity(parity)
        def _():
            size = piece.shape[1]
            parts = split(piece[...], 3)
            w, s = weight[...], source[...]
            t = held_t[...] + mul_parts(parts, oh_dst[:, at : at + size], NT)
            product = (w * t).astype(BF16)
            probe[...] = product
            probe_rows[...] = half_rows(product.astype(F32))
            source_scores(number, probe, probe_rows, left16, count_l, gp, weights)
            rgrad[...], more = negatives(parts[0], query[...], query_rows[...], times_at(count_r, 0, size, at), number)
            q = held_q[...] + more
            p = gp[...]
            coef = -jax.nn.sigmoid(-jnp.sum(s * w * t, axis=0, keepdims=True))
            g_weight = coef * s * t + q * s + p * t
            rel_out[...] = rel_in[...] + sum(mul(kind[...], part, NT) for part in split(g_weight, 2))
            to_src[0:depth, :], to_src[depth:, :] = split(coef * w * t + q * w, 2)
            here = dst[step : step + 1, :] >= at
            to_dst[0:depth, :], to_dst[depth:, :] = split(jnp.where(here, coef * w * s + p * w, 0.0), 2)

    return call(
        body, "late_edges",
        [piece, weight, source, query, query_rows, left16, oh_dst, count_l, count_r, kind, dst, target, gq, rel, after],
        [shape(depth, piece.shape[1]), pair16, pair16, shape(*rel.shape), shape(depth, edges, dtype=BF16), shape(edges, rows, dtype=BF16)],
        scratch_shapes=scratch([shape(depth, edges), shape(edges, depth, dtype=BF16)]),
    )


def left_rows(cut, left, lstate, to_src, oh_src, probe, weights, count_l):
    depth = left.shape[0]
    size = cut.stop - cut.start
    g = mul(probe[...], weights[:, cut], NN) * times_at(count_l, 0, size, cut.start)
    g = g + mul_parts([to_src[0:depth, :], to_src[depth:, :]], oh_src[:, cut], NN)
    new = lstate[:, cut] + jnp.sum(g * g, axis=0, keepdims=True) * (1.0 / depth)
    return left[:, cut] - g * (rate * lax.rsqrt(new))


def first_along_rel():
    return lax.axis_index("rel") < lax.axis_size("rel") // 2


def ahead_left(parity, left, lstate, to_src, oh_src, probe, weights, count_l, rel):
    depth, rows = left.shape

    def body(left, lstate, to_src, oh_src, probe, weights, count_l, _rel, result, _rel_out):
        @pl.when(first_along_rel())
        def _():
            for i in range(rows // 512):
                cut = slice(i * 256, (i + 1) * 256)
                result[:, cut] = left_rows(cut, left, lstate, to_src, oh_src, probe, weights, count_l)

    return call(
        only_on(parity, body), "ahead_left", [left, lstate, to_src, oh_src, probe, weights, count_l, rel],
        [shape(depth, rows // 2), shape(*rel.shape)], aliases={7: 1},
    )


def late_slabs(parity, at, left, lstate, to_src, oh_src, probe, weights, count_l, ahead,
               piece, state, rgrad, to_dst, oh_dst, keep_left, keep_right):
    depth, rows = left.shape

    def body(left, lstate, to_src, oh_src, probe, weights, count_l, ahead, piece, state, rgrad, to_dst, oh_dst,
             _keep_left, _keep_right, left_out, right_out, result, spare, sems):
        def made_ahead():
            return pltpu.make_async_copy(ahead, left_out.at[:, 0 : rows // 2], sems.at[0, 0])

        def copy(i):
            cut = slice(i * 256, (i + 1) * 256)
            return pltpu.make_async_copy(result.at[:, cut], left_out.at[:, cut], sems.at[0, i])

        def make(i):
            cut = slice(i * 256, (i + 1) * 256)
            result[:, cut] = left_rows(cut, left, lstate, to_src, oh_src, probe, weights, count_l)
            copy(i).start()

        count = rows // 256

        @pl.when(first_along_rel())
        def _():
            made_ahead().start()

        @pl.when(jnp.logical_not(first_along_rel()))
        def _():
            for i in range(count // 2):
                make(i)

        wait = update_and_send([piece], state, [rgrad], to_dst, oh_dst, spare, right_out, sems.at[1], fixed=True, start=at)
        for i in range(count // 2, count):
            make(i)
        wait()

        @pl.when(first_along_rel())
        def _():
            made_ahead().wait()

        @pl.when(jnp.logical_not(first_along_rel()))
        def _():
            for i in range(count // 2):
                copy(i).wait()

        for i in range(count // 2, count):
            copy(i).wait()

    operands = [left, lstate, to_src, oh_src, probe, weights, count_l, ahead, piece, state, rgrad, to_dst, oh_dst, keep_left, keep_right]
    return call(
        only_on(parity, body), "late_slabs", operands, [shape(depth, rows), shape(depth, rows)], in_large=(13, 14), out_large=(0, 1),
        scratch_shapes=[*scratch([shape(depth, rows), shape(1, rows)]), pltpu.SemaphoreType.DMA((2, rows // 256))],
        aliases={13: 0, 14: 1},
    )


def relation_update(relations, relation_state, rels):
    kinds, depth = relations.shape

    def body(relations, relation_state, *rest):
        grad = sum(ref[...] for ref in rest[:-1])
        first = lax.broadcasted_iota(jnp.int32, (kinds, kinds), 0)
        second = lax.broadcasted_iota(jnp.int32, (kinds, kinds), 1)
        old = jnp.sum(jnp.where(first == second, relation_state[...], 0.0), axis=1, keepdims=True)
        new = old + jnp.sum(grad * grad, axis=1, keepdims=True) * (1.0 / depth)
        rest[-1][...] = relations[...] - grad * (rate * lax.rsqrt(new))

    return call(body, "relation_update", [relations, relation_state, *rels], [shape(kinds, depth)])[0]


def local(
    left_slab, left_state, right_slab, right_state, relations, relation_state,
    src_index, dst_index, relation_id, neg_source, neg_target,
):
    peers = lax.axis_size("blk")
    inside = [(i, i + 1) for i in range(0, peers, 2)]
    swap = inside + [(i + 1, i) for i in range(0, peers, 2)]
    across = [(i, (i + 1) % peers) for i in range(1, peers, 2)]
    skip = [(i, (i + 2) % peers) for i in range(0, peers, 2)]
    index = (src_index, dst_index, relation_id, neg_source, neg_target)
    left = left_slab.T
    right = right_slab.T
    rows = left.shape[1]
    lstate = left_state.reshape(1, rows)
    number = float(neg_source.shape[1])
    right_far = lax.ppermute(right, "blk", across)
    right_near = [lax.ppermute(right[:, at : at + size], "blk", inside) for at, size in pieces_of(rows, NEAR_FIRST)]
    state_near = lax.ppermute(right_state, "blk", swap)
    state_far = lax.ppermute(state_near, "blk", skip).reshape(1, rows)
    state_near = state_near.reshape(1, rows)
    rel = jnp.zeros(relations.shape, F32)
    ready = prepared(0, left, relations, index)
    left_a, lstate, far, rel = trained(1, "first_near", number, False, FAR, left, lstate, right_near, state_near, rel, ready)
    far = [lax.ppermute(piece, "blk", across) for piece in far]
    left_a, lstate, near, rel = trained(
        0, "first_far", number, True, NEAR, left, lstate, [right_far], state_far, rel, ready, (left_a,)
    )
    near = [lax.ppermute(piece, "blk", inside) for piece in near]
    ready = prepared(1, left_a, relations, index)
    first_lstate = lstate
    left_b, lstate, right_b, rel = trained(1, "last_near", number, True, (), left_a, lstate, near, state_near, rel, ready)
    cuts = pieces_of(rows, FAR)
    right_b, = right_b
    held = ()
    state = None
    for i, (at, size) in enumerate(cuts[:-1]):
        after = lstate if state is None else state
        target, gq, rgrad = last_piece(0, "last_piece%d" % i, number, at, far[i], ready, after, held)
        held = (target, gq)
        to_dst = early_edges(0, "early_edges%d" % i, number, 1, at, at + size, target, ready, dst_index)
        right_b, state = early_right(0, "early_right%d" % i, at, far[i], state, rgrad, to_dst, ready[6], right_b)
    at = cuts[-1][0]
    rgrad, to_src, to_dst, rel, probe, weights = late_edges(0, number, 1, at, far[-1], ready, dst_index, target, gq, rel, state)
    ahead, rel = ahead_left(0, left_a, first_lstate, to_src, ready[5], probe, weights, ready[7], rel)
    if lax.axis_size("rel") == 2:
        rels = [rel, lax.ppermute(rel, "rel", [(0, 1), (1, 0)])]
    else:
        rels = [lax.psum(rel, "rel")]
    left_b, right_b = late_slabs(
        0, at, left_a, first_lstate, to_src, ready[5], probe, weights, ready[7], ahead,
        far[-1], state, rgrad, to_dst, ready[6], left_b, right_b,
    )
    relations_out = relation_update(relations, relation_state.reshape(1, -1), rels)
    return (left_b.T, right_b.T, relations_out[None])


def solution(mesh):
    in_specs = (
        P(("blk", "rel"), None),
        P(("blk", "rel")),
        P(("blk", "rel"), None),
        P(("blk", "rel")),
        P(),
        P(),
        P(None, ("blk", "rel")),
        P(None, ("blk", "rel")),
        P(None, ("blk", "rel")),
        P(None, ("blk", "rel")),
        P(None, ("blk", "rel")),
    )
    out_specs = (P(("blk", "rel"), None), P(("blk", "rel"), None), P("blk", None, None))
    return jax.shard_map(local, mesh=mesh, in_specs=in_specs, out_specs=out_specs, check_vma=False)
```

```python
import functools

import jax
import jax.numpy as jnp
from jax import lax
from jax.experimental import pallas as pl
from jax.experimental.pallas import tpu as pltpu
from jax.sharding import PartitionSpec as P

rate = 0.1
F32 = jnp.float32
BF16 = jnp.bfloat16
LANES = 128
NEAR = (4, 4)
STATE = 0
NEAR_FIRST = (4, 4)
FAR = (5, 2, 1)
VMEM_LIMIT = 30 * 2**20

NN = (((1,), (0,)), ((), ()))
NT = (((1,), (1,)), ((), ()))
TN = (((0,), (0,)), ((), ()))


def mul(a, b, dims):
    return lax.dot_general(a, b, dims, preferred_element_type=F32)


def split(x, parts):
    out = []
    for _ in range(parts):
        part = x.astype(BF16)
        out.append(part)
        x = x - part.astype(F32)
    return out


def mul_parts(parts, table, dims):
    along = dims[0][1][0]
    return mul(jnp.concatenate(parts, axis=1), jnp.concatenate([table] * len(parts), axis=along), dims)


def lanes_at(i, size, start=0):
    if isinstance(i, int):
        return slice(start + i * size, start + (i + 1) * size)
    return pl.ds(pl.multiple_of(start + i * size, LANES), size)


def step_of(rows, most=512):
    return next(size for size in (1024, 512, 256) if size <= most and rows % size == 0)


def each(count, body, fixed=False):
    if fixed:
        for i in range(count):
            body(i)
        return

    def one(i, carry):
        body(i)
        return carry

    lax.fori_loop(0, count, one, 0)


def row_onehot(idx, table):
    count, rows = table.shape
    col = jnp.broadcast_to(idx, (LANES, count)).T
    lane = lax.broadcasted_iota(jnp.int32, (count, LANES), 1)

    def tile(t):
        hit = col == lane + t * LANES
        table[:, lanes_at(t, LANES)] = jnp.where(hit, 1.0, 0.0).astype(BF16)

    each(rows // LANES, tile)


def row_counts(idx, rows):
    count = idx.shape[1]
    high = lax.broadcasted_iota(jnp.int32, (rows // LANES, count), 0)
    low = lax.broadcasted_iota(jnp.int32, (LANES, count), 0)
    high_hit = jnp.where(idx // LANES == high, 1.0, 0.0).astype(BF16)
    low_hit = jnp.where(idx % LANES == low, 1.0, 0.0).astype(BF16)
    return mul(high_hit, low_hit, NT)


def times_at(counts, i, size, start=0):
    first = (start + i * size) // LANES
    return jnp.concatenate([counts[pl.ds(first + t, 1), :] for t in range(size // LANES)], axis=1)


def half_rows(x):
    return (0.5 * x).T.astype(BF16)


def negative_weights(rows16, query_rows, number):
    half = 0.5 / number
    return (jnp.tanh(mul(query_rows, rows16, NN)) * half + half).astype(BF16)


def often(weight, times):
    return (weight.astype(F32) * times).astype(BF16)


def negatives(rows16, query, query_rows, times, number):
    weight = negative_weights(rows16, query_rows, number)
    return mul(query, weight, NN) * times, mul(rows16, often(weight, times), NT)


def prepare(step, left, relations, src, dst, rid, nsrc, ndst,
            weight, source, query, query_rows, left16, oh_src, oh_dst, count_l, count_r, kind):
    rows = left.shape[1]
    here = slice(step, step + 1)
    row_onehot(src[here, :], oh_src)
    row_onehot(dst[here, :], oh_dst)
    count_l[...] = row_counts(nsrc[here, :], rows)
    count_r[...] = row_counts(ndst[here, :], rows)
    kinds = lax.broadcasted_iota(jnp.int32, kind.shape, 0)
    kind[...] = jnp.where(rid[here, :] == kinds, 1.0, 0.0).astype(BF16)
    weight[...] = sum(mul(part, kind[...], TN) for part in split(relations[...], 3))
    source[...] = jnp.zeros_like(source)

    size = step_of(rows)

    def part(i):
        cut = lanes_at(i, size)
        parts = split(left[:, cut], 3)
        left16[:, cut] = parts[0]
        source[...] += mul_parts(parts, oh_src[:, cut], NT)

    each(rows // size, part)
    product = source[...] * weight[...]
    query[...] = product.astype(BF16)
    query_rows[...] = half_rows(product.astype(BF16).astype(F32))


def take_piece(number, start, piece, query, query_rows, oh_dst, count_r, target, gq, rgrad, fixed=False):
    depth = target.shape[0]
    if start == 0:
        target[...] = jnp.zeros_like(target)
        gq[...] = jnp.zeros_like(gq)

    size = step_of(piece.shape[1], 256 if fixed else 512)

    def part(i):
        cut = lanes_at(i, size)
        parts = split(piece[0:depth, cut], 3)
        hits = oh_dst[:, lanes_at(i, size, start)]
        target[...] += mul_parts(parts, hits, NT)
        times = times_at(count_r, i, size, start)
        rgrad[:, cut], more = negatives(parts[0], query[...], query_rows[...], times, number)
        gq[...] += more

    each(piece.shape[1] // size, part, fixed)


def join(number, weight, source, target, gq, left16, count_l, kind, rel_in,
         probe, probe_rows, gp, lgrad, to_src, to_dst, rel_out, fixed=False):
    rows = left16.shape[1]
    product = weight[...] * target[...]
    probe[...] = product.astype(BF16)
    probe_rows[...] = half_rows(product.astype(BF16).astype(F32))
    gp[...] = jnp.zeros_like(gp)

    size = step_of(rows)

    def part(i):
        cut = lanes_at(i, size)
        lgrad[:, cut], more = negatives(left16[:, cut], probe[...], probe_rows[...], times_at(count_l, i, size), number)
        gp[...] += more

    each(rows // size, part, fixed)
    depth = weight.shape[0]
    w, s, t = weight[...], source[...], target[...]
    coef = -jax.nn.sigmoid(-jnp.sum(s * w * t, axis=0, keepdims=True))
    to_src[0:depth, :], to_src[depth:, :] = split(coef * w * t + gq[...] * w, 2)
    to_dst[0:depth, :], to_dst[depth:, :] = split(coef * w * s + gp[...] * w, 2)
    g_weight = coef * s * t + gq[...] * s + gp[...] * t
    rel_out[...] = rel_in[...] + sum(mul(kind[...], p, NT) for p in split(g_weight, 2))


def adagrad(slab, state, grad, edges, table, start, out, new_state, send=None, fixed=False, more=None):
    depth = grad.shape[0]
    size = step_of(grad.shape[1])

    def part(i):
        cut = lanes_at(i, size)
        hits = table[:, lanes_at(i, size, start)]
        g = grad[:, cut] + mul_parts([edges[0:depth, :], edges[depth:, :]], hits, NN)
        if more is not None:
            g = g + more(i, size)
        new = state[:, cut] + jnp.sum(g * g, axis=0, keepdims=True) * (1.0 / depth)
        new_state[:, cut] = new
        out[0:depth, cut] = slab[0:depth, cut] - g * (rate * lax.rsqrt(new))
        if send is not None:
            send(i).start()

    each(grad.shape[1] // size, part, fixed)


def sender(result, to, start, sems):
    size = step_of(result.shape[1])

    def copy(i):
        here = lanes_at(i, size)
        there = lanes_at(i, size, start)
        return pltpu.make_async_copy(result.at[:, here], to.at[:, there], sems.at[i + start // 256])

    return copy


def update_and_send(pieces, state, grads, edges, table, new_state, to, sems, fixed=False, start=0, more=None):
    sent = []
    for piece, grad in zip(pieces, grads):
        rows = grad.shape[1]
        copy = sender(grad, to, start, sems)
        cut = slice(start, start + rows)
        adagrad(piece, state.at[:, cut], grad, edges, table, start, grad, new_state.at[:, cut], copy, fixed, more)
        sent.append((copy, rows // step_of(rows)))
        start += rows

    def wait():
        for copy, count in sent:
            each(count, lambda i, copy=copy: copy(i).wait(), fixed)

    return wait


def pack_state(state, piece, depth):
    size = state.shape[1] // 8
    for k in range(8):
        piece[depth + k : depth + k + 1, 0:size] = state[:, k * size : (k + 1) * size]


def unpack_state(piece, depth, state):
    size = state.shape[1] // 8
    for k in range(8):
        state[:, k * size : (k + 1) * size] = piece[depth + k : depth + k + 1, 0:size]


def on_parity(parity):
    return pl.when(lax.axis_index("blk") % 2 == parity)


def pieces_of(rows, eighths):
    sizes = [rows // 8 * n for n in eighths]
    return [(sum(sizes[:i]), size) for i, size in enumerate(sizes)]


def rows_of(pieces, at, size):
    found = []
    start = 0
    for piece in pieces:
        begin, end = max(at, start), min(at + size, start + piece.shape[1])
        if begin < end:
            found.append((piece.at[:, begin - start : end - start], begin, end - begin))
        start += piece.shape[1]
    return found


def train(parity, number, last, fixed, kept, takes, gives, *refs):
    refs = list(refs)
    (left, lstate, rstate_in, rel_in) = refs[:4]
    (weight, source, query, query_rows, left16, oh_src, oh_dst, count_l, count_r, kind) = refs[4:14]
    right = refs[14 : 14 + takes]
    refs = refs[14 + takes + kept :]
    left_out, lstate_out, rel_out = refs[:3]
    right_out = refs[3 : 3 + len(gives)]
    (target, gq, rgrad, probe, probe_rows, gp, lgrad, to_src, to_dst, rstate, spare, sems) = refs[3 + len(gives) :]
    depth, rows = left.shape
    lstate_out[...] = lstate[...]
    rel_out[...] = rel_in[...]

    @on_parity(parity)
    def _():
        grads = []
        at = 0
        for piece in right:
            grads.append(rgrad.at[:, at : at + piece.shape[1]])
            take_piece(number, at, piece, query, query_rows, oh_dst, count_r, target, gq, grads[-1], fixed)
            at += piece.shape[1]
        join(number, weight, source, target, gq, left16, count_l, kind, rel_in,
             probe, probe_rows, gp, lgrad, to_src, to_dst, rel_out, fixed)
        if last:
            unpack_state(right[STATE], depth, rstate)
            wait_right = update_and_send(right, rstate, grads, to_dst, oh_dst, spare, right_out[0], sems.at[0], fixed)
            wait_left = update_and_send([left], lstate, [lgrad], to_src, oh_src, spare, left_out, sems.at[1], fixed)
            wait_right()
            wait_left()
        else:
            for (at, size), out in zip(pieces_of(rows, gives), right_out):
                for old, begin, length in rows_of(right, at, size):
                    cut = slice(begin, begin + length)
                    here = slice(begin - at, begin - at + length)
                    adagrad(old, rstate_in.at[:, cut], rgrad.at[:, cut], to_dst, oh_dst, begin, out.at[:, here], spare.at[:, cut], None, fixed)
            pack_state(spare, right_out[STATE], depth)
            adagrad(left, lstate, lgrad, to_src, oh_src, 0, left_out, lstate_out, None, fixed)


def shape(*dims, dtype=F32):
    return jax.ShapeDtypeStruct(dims, dtype)


def prepared_shapes(depth, rows, edges, kinds):
    return (
        shape(depth, edges), shape(depth, edges), shape(depth, edges, dtype=BF16), shape(edges, depth, dtype=BF16),
        shape(depth, rows, dtype=BF16), shape(edges, rows, dtype=BF16), shape(edges, rows, dtype=BF16),
        shape(rows // LANES, LANES), shape(rows // LANES, LANES), shape(kinds, edges, dtype=BF16),
    )


def scratch(shapes):
    return [pltpu.VMEM(s.shape, s.dtype) for s in shapes]


def call(kernel, name, operands, shapes, in_large=(), out_large=(), scratch_shapes=(), aliases=None):
    vmem = pl.BlockSpec(memory_space=pltpu.VMEM)
    large = pl.BlockSpec(memory_space=pl.ANY)
    return pl.pallas_call(
        kernel,
        out_shape=tuple(shapes),
        in_specs=[large if i in in_large else vmem for i in range(len(operands))],
        out_specs=tuple(large if i in out_large else vmem for i in range(len(shapes))),
        scratch_shapes=list(scratch_shapes),
        input_output_aliases=aliases or {},
        compiler_params=pltpu.CompilerParams(vmem_limit_bytes=VMEM_LIMIT),
        cost_estimate=pl.CostEstimate(flops=1_000_000, bytes_accessed=100_000, transcendentals=0),
        name=name,
    )(*operands)


def prepared(step, left, relations, index):
    depth, rows = left.shape
    return call(
        functools.partial(prepare, step), "prepare%d" % step, [left, relations, *index],
        prepared_shapes(depth, rows, index[0].shape[1], relations.shape[0]),
    )


def trained(parity, name, number, fixed, gives, left, lstate, right, rstate, rel, ready, keep=()):
    depth, rows = left.shape
    edges = ready[0].shape[1]
    last = not gives
    blocks = [shape(depth, size) for _at, size in pieces_of(rows, gives or (8,))]
    if not last:
        blocks[STATE] = shape(depth + 8, blocks[STATE].shape[1])
    edge = shape(depth, edges)
    edge16 = shape(depth, edges, dtype=BF16)
    pair16 = shape(2 * depth, edges, dtype=BF16)
    slab = shape(depth, rows)
    inner = [edge, edge, slab, edge16, shape(edges, depth, dtype=BF16), edge, slab, pair16, pair16, shape(1, rows), shape(1, rows)]
    left_out, lstate_out, rel_out, *right_out = call(
        functools.partial(train, parity, number, last, fixed, len(keep), len(right), gives or (8,)),
        name,
        [left, lstate, rstate, rel, *ready, *right, *keep],
        [slab, shape(1, rows), shape(*rel.shape), *blocks],
        out_large=(0, 3) if last else (),
        scratch_shapes=[*scratch(inner), pltpu.SemaphoreType.DMA((2, rows // 256))],
        aliases={14 + len(right) + i: 0 for i in range(len(keep))},
    )
    return left_out, lstate_out, right_out, rel_out


def only_on(parity, body):
    def kernel(*refs):
        @on_parity(parity)
        def _():
            body(*refs)

    return kernel


def last_piece(parity, name, number, at, piece, ready, after, held=()):
    (_weight, _source, query, query_rows, _left16, _oh_src, oh_dst, _count_l, count_r, _kind) = ready
    depth, edges = query.shape

    def body(piece, query, query_rows, oh_dst, count_r, *rest):
        take_piece(number, at, piece, query, query_rows, oh_dst, count_r, *rest[len(held) + 1 :], fixed=True)

    operands = [piece, query, query_rows, oh_dst, count_r, *held, after]
    return call(
        only_on(parity, body), name, operands,
        [shape(depth, edges), shape(depth, edges), shape(depth, piece.shape[1])],
        aliases={5: 0, 6: 1} if held else {},
    )


def source_scores(number, probe, probe_rows, left16, count_l, gp, weights=None):
    rows = left16.shape[1]
    size = step_of(rows, 1024)
    gp[...] = jnp.zeros_like(gp)
    for i in range(rows // size):
        cut = lanes_at(i, size)
        rows16 = left16[:, cut]
        part = negative_weights(rows16, probe_rows[...], number)
        if weights is not None:
            weights[:, cut] = part
        gp[...] += mul(rows16, often(part, times_at(count_l, i, size)), NT)


def early_edges(parity, name, number, step, low, high, target, ready, dst):
    (weight, source, _query, _query_rows, left16, _oh_src, _oh_dst, count_l, _count_r, _kind) = ready
    depth = left16.shape[0]
    edges = weight.shape[1]

    def body(weight, source, target, left16, count_l, dst, to_dst, gp, probe, probe_rows):
        w, s, t = weight[...], source[...], target[...]
        product = (w * t).astype(BF16)
        probe[...] = product
        probe_rows[...] = half_rows(product.astype(F32))
        source_scores(number, probe, probe_rows, left16, count_l, gp)
        at = dst[step : step + 1, :]
        here = jnp.logical_and(at >= low, at < high)
        coef = -jax.nn.sigmoid(-jnp.sum(s * w * t, axis=0, keepdims=True))
        to_dst[0:depth, :], to_dst[depth:, :] = split(jnp.where(here, coef * w * s + gp[...] * w, 0.0), 2)

    return call(
        only_on(parity, body), name, [weight, source, target, left16, count_l, dst],
        [shape(2 * depth, edges, dtype=BF16)],
        scratch_shapes=scratch([shape(depth, edges), shape(depth, edges, dtype=BF16), shape(edges, depth, dtype=BF16)]),
    )[0]


def early_right(parity, name, at, piece, state, rgrad, to_dst, oh_dst, keep):
    depth, rows = keep.shape

    def body(piece, rgrad, to_dst, oh_dst, *rest):
        out, new_state, spare, sems = rest[-4:]
        if state is None:
            unpack_state(piece, depth, new_state)
        else:
            new_state[...] = rest[0][...]
        update_and_send([piece], new_state, [rgrad], to_dst, oh_dst, spare, out, sems, fixed=True, start=at)()

    operands = [piece, rgrad, to_dst, oh_dst, *([] if state is None else [state]), keep]
    place = len(operands) - 1
    return call(
        only_on(parity, body), name, operands, [shape(depth, rows), shape(1, rows)],
        in_large=(place,), out_large=(0,),
        scratch_shapes=[*scratch([shape(1, rows)]), pltpu.SemaphoreType.DMA((rows // 256,))],
        aliases={place: 0},
    )


def late_edges(parity, number, step, at, piece, ready, dst, target, gq, rel, after):
    (weight, source, query, query_rows, left16, _oh_src, oh_dst, count_l, count_r, kind) = ready
    depth, rows = left16.shape
    edges = weight.shape[1]
    pair16 = shape(2 * depth, edges, dtype=BF16)

    def body(piece, weight, source, query, query_rows, left16, oh_dst, count_l, count_r, kind, dst, held_t, held_q, rel_in,
             _after, rgrad, to_src, to_dst, rel_out, probe, weights, gp, probe_rows):
        rel_out[...] = rel_in[...]

        @on_parity(parity)
        def _():
            size = piece.shape[1]
            parts = split(piece[...], 3)
            w, s = weight[...], source[...]
            t = held_t[...] + mul_parts(parts, oh_dst[:, at : at + size], NT)
            product = (w * t).astype(BF16)
            probe[...] = product
            probe_rows[...] = half_rows(product.astype(F32))
            source_scores(number, probe, probe_rows, left16, count_l, gp, weights)
            rgrad[...], more = negatives(parts[0], query[...], query_rows[...], times_at(count_r, 0, size, at), number)
            q = held_q[...] + more
            p = gp[...]
            coef = -jax.nn.sigmoid(-jnp.sum(s * w * t, axis=0, keepdims=True))
            g_weight = coef * s * t + q * s + p * t
            rel_out[...] = rel_in[...] + sum(mul(kind[...], part, NT) for part in split(g_weight, 2))
            to_src[0:depth, :], to_src[depth:, :] = split(coef * w * t + q * w, 2)
            here = dst[step : step + 1, :] >= at
            to_dst[0:depth, :], to_dst[depth:, :] = split(jnp.where(here, coef * w * s + p * w, 0.0), 2)

    return call(
        body, "late_edges",
        [piece, weight, source, query, query_rows, left16, oh_dst, count_l, count_r, kind, dst, target, gq, rel, after],
        [shape(depth, piece.shape[1]), pair16, pair16, shape(*rel.shape), shape(depth, edges, dtype=BF16), shape(edges, rows, dtype=BF16)],
        scratch_shapes=scratch([shape(depth, edges), shape(edges, depth, dtype=BF16)]),
    )


def left_rows(cut, left, lstate, to_src, oh_src, probe, weights, count_l):
    depth = left.shape[0]
    size = cut.stop - cut.start
    g = mul(probe[...], weights[:, cut], NN) * times_at(count_l, 0, size, cut.start)
    g = g + mul_parts([to_src[0:depth, :], to_src[depth:, :]], oh_src[:, cut], NN)
    new = lstate[:, cut] + jnp.sum(g * g, axis=0, keepdims=True) * (1.0 / depth)
    return left[:, cut] - g * (rate * lax.rsqrt(new))


def first_along_rel():
    return lax.axis_index("rel") < lax.axis_size("rel") // 2


def ahead_left(parity, left, lstate, to_src, oh_src, probe, weights, count_l, rel):
    depth, rows = left.shape

    def body(left, lstate, to_src, oh_src, probe, weights, count_l, _rel, result, _rel_out):
        @pl.when(first_along_rel())
        def _():
            for i in range(rows // 512):
                cut = slice(i * 256, (i + 1) * 256)
                result[:, cut] = left_rows(cut, left, lstate, to_src, oh_src, probe, weights, count_l)

    return call(
        only_on(parity, body), "ahead_left", [left, lstate, to_src, oh_src, probe, weights, count_l, rel],
        [shape(depth, rows // 2), shape(*rel.shape)], aliases={7: 1},
    )


def late_slabs(parity, at, left, lstate, to_src, oh_src, probe, weights, count_l, ahead,
               piece, state, rgrad, to_dst, oh_dst, keep_left, keep_right):
    depth, rows = left.shape

    def body(left, lstate, to_src, oh_src, probe, weights, count_l, ahead, piece, state, rgrad, to_dst, oh_dst,
             _keep_left, _keep_right, left_out, right_out, result, spare, sems):
        def made_ahead():
            return pltpu.make_async_copy(ahead, left_out.at[:, 0 : rows // 2], sems.at[0, 0])

        def copy(i):
            cut = slice(i * 256, (i + 1) * 256)
            return pltpu.make_async_copy(result.at[:, cut], left_out.at[:, cut], sems.at[0, i])

        def make(i):
            cut = slice(i * 256, (i + 1) * 256)
            result[:, cut] = left_rows(cut, left, lstate, to_src, oh_src, probe, weights, count_l)
            copy(i).start()

        count = rows // 256

        @pl.when(first_along_rel())
        def _():
            made_ahead().start()

        @pl.when(jnp.logical_not(first_along_rel()))
        def _():
            for i in range(count // 2):
                make(i)

        wait = update_and_send([piece], state, [rgrad], to_dst, oh_dst, spare, right_out, sems.at[1], fixed=True, start=at)
        for i in range(count // 2, count):
            make(i)
        wait()

        @pl.when(first_along_rel())
        def _():
            made_ahead().wait()

        @pl.when(jnp.logical_not(first_along_rel()))
        def _():
            for i in range(count // 2):
                copy(i).wait()

        for i in range(count // 2, count):
            copy(i).wait()

    operands = [left, lstate, to_src, oh_src, probe, weights, count_l, ahead, piece, state, rgrad, to_dst, oh_dst, keep_left, keep_right]
    return call(
        only_on(parity, body), "late_slabs", operands, [shape(depth, rows), shape(depth, rows)], in_large=(13, 14), out_large=(0, 1),
        scratch_shapes=[*scratch([shape(depth, rows), shape(1, rows)]), pltpu.SemaphoreType.DMA((2, rows // 256))],
        aliases={13: 0, 14: 1},
    )


def relation_update(relations, relation_state, rels):
    kinds, depth = relations.shape

    def body(relations, relation_state, *rest):
        grad = sum(ref[...] for ref in rest[:-1])
        first = lax.broadcasted_iota(jnp.int32, (kinds, kinds), 0)
        second = lax.broadcasted_iota(jnp.int32, (kinds, kinds), 1)
        old = jnp.sum(jnp.where(first == second, relation_state[...], 0.0), axis=1, keepdims=True)
        new = old + jnp.sum(grad * grad, axis=1, keepdims=True) * (1.0 / depth)
        rest[-1][...] = relations[...] - grad * (rate * lax.rsqrt(new))

    return call(body, "relation_update", [relations, relation_state, *rels], [shape(kinds, depth)])[0]


def local(
    left_slab, left_state, right_slab, right_state, relations, relation_state,
    src_index, dst_index, relation_id, neg_source, neg_target,
):
    peers = lax.axis_size("blk")
    inside = [(i, i + 1) for i in range(0, peers, 2)]
    swap = inside + [(i + 1, i) for i in range(0, peers, 2)]
    across = [(i, (i + 1) % peers) for i in range(1, peers, 2)]
    skip = [(i, (i + 2) % peers) for i in range(0, peers, 2)]
    index = (src_index, dst_index, relation_id, neg_source, neg_target)
    left = left_slab.T
    right = right_slab.T
    rows = left.shape[1]
    lstate = left_state.reshape(1, rows)
    number = float(neg_source.shape[1])
    right_far = lax.ppermute(right, "blk", across)
    right_near = [lax.ppermute(right[:, at : at + size], "blk", inside) for at, size in pieces_of(rows, NEAR_FIRST)]
    state_near = lax.ppermute(right_state, "blk", swap)
    state_far = lax.ppermute(state_near, "blk", skip).reshape(1, rows)
    state_near = state_near.reshape(1, rows)
    rel = jnp.zeros(relations.shape, F32)
    ready = prepared(0, left, relations, index)
    left_a, lstate, far, rel = trained(1, "first_near", number, False, FAR, left, lstate, right_near, state_near, rel, ready)
    far = [lax.ppermute(piece, "blk", across) for piece in far]
    left_a, lstate, near, rel = trained(
        0, "first_far", number, True, NEAR, left, lstate, [right_far], state_far, rel, ready, (left_a,)
    )
    near = [lax.ppermute(piece, "blk", inside) for piece in near]
    ready = prepared(1, left_a, relations, index)
    first_lstate = lstate
    left_b, lstate, right_b, rel = trained(1, "last_near", number, False, (), left_a, lstate, near, state_near, rel, ready)
    cuts = pieces_of(rows, FAR)
    right_b, = right_b
    held = ()
    state = None
    for i, (at, size) in enumerate(cuts[:-1]):
        after = lstate if state is None else state
        target, gq, rgrad = last_piece(0, "last_piece%d" % i, number, at, far[i], ready, after, held)
        held = (target, gq)
        to_dst = early_edges(0, "early_edges%d" % i, number, 1, at, at + size, target, ready, dst_index)
        right_b, state = early_right(0, "early_right%d" % i, at, far[i], state, rgrad, to_dst, ready[6], right_b)
    at = cuts[-1][0]
    rgrad, to_src, to_dst, rel, probe, weights = late_edges(0, number, 1, at, far[-1], ready, dst_index, target, gq, rel, state)
    ahead, rel = ahead_left(0, left_a, first_lstate, to_src, ready[5], probe, weights, ready[7], rel)
    if lax.axis_size("rel") == 2:
        rels = [rel, lax.ppermute(rel, "rel", [(0, 1), (1, 0)])]
    else:
        rels = [lax.psum(rel, "rel")]
    left_b, right_b = late_slabs(
        0, at, left_a, first_lstate, to_src, ready[5], probe, weights, ready[7], ahead,
        far[-1], state, rgrad, to_dst, ready[6], left_b, right_b,
    )
    relations_out = relation_update(relations, relation_state.reshape(1, -1), rels)
    return (left_b.T, right_b.T, relations_out[None])


def solution(mesh):
    in_specs = (
        P(("blk", "rel"), None),
        P(("blk", "rel")),
        P(("blk", "rel"), None),
        P(("blk", "rel")),
        P(),
        P(),
        P(None, ("blk", "rel")),
        P(None, ("blk", "rel")),
        P(None, ("blk", "rel")),
        P(None, ("blk", "rel")),
        P(None, ("blk", "rel")),
    )
    out_specs = (P(("blk", "rel"), None), P(("blk", "rel"), None), P("blk", None, None))
    return jax.shard_map(local, mesh=mesh, in_specs=in_specs, out_specs=out_specs, check_vma=False)
```

```python
import functools

import jax
import jax.numpy as jnp
from jax import lax
from jax.experimental import pallas as pl
from jax.experimental.pallas import tpu as pltpu
from jax.sharding import PartitionSpec as P

rate = 0.1
F32 = jnp.float32
BF16 = jnp.bfloat16
LANES = 128
NEAR = (4, 4)
STATE = 0
NEAR_FIRST = (4, 4)
FAR = (5, 2, 1)
VMEM_LIMIT = 30 * 2**20

NN = (((1,), (0,)), ((), ()))
NT = (((1,), (1,)), ((), ()))
TN = (((0,), (0,)), ((), ()))


def mul(a, b, dims):
    return lax.dot_general(a, b, dims, preferred_element_type=F32)


def split(x, parts):
    out = []
    for _ in range(parts):
        part = x.astype(BF16)
        out.append(part)
        x = x - part.astype(F32)
    return out


def mul_parts(parts, table, dims):
    along = dims[0][1][0]
    return mul(jnp.concatenate(parts, axis=1), jnp.concatenate([table] * len(parts), axis=along), dims)


def lanes_at(i, size, start=0):
    if isinstance(i, int):
        return slice(start + i * size, start + (i + 1) * size)
    return pl.ds(pl.multiple_of(start + i * size, LANES), size)


def step_of(rows, most=512):
    return next(size for size in (1024, 512, 256) if size <= most and rows % size == 0)


def each(count, body, fixed=False):
    if fixed:
        for i in range(count):
            body(i)
        return

    def one(i, carry):
        body(i)
        return carry

    lax.fori_loop(0, count, one, 0)


def row_onehot(idx, table):
    count, rows = table.shape
    col = jnp.broadcast_to(idx, (LANES, count)).T
    lane = lax.broadcasted_iota(jnp.int32, (count, LANES), 1)

    def tile(t):
        hit = col == lane + t * LANES
        table[:, lanes_at(t, LANES)] = jnp.where(hit, 1.0, 0.0).astype(BF16)

    each(rows // LANES, tile)


def row_counts(idx, rows):
    count = idx.shape[1]
    high = lax.broadcasted_iota(jnp.int32, (rows // LANES, count), 0)
    low = lax.broadcasted_iota(jnp.int32, (LANES, count), 0)
    high_hit = jnp.where(idx // LANES == high, 1.0, 0.0).astype(BF16)
    low_hit = jnp.where(idx % LANES == low, 1.0, 0.0).astype(BF16)
    return mul(high_hit, low_hit, NT)


def times_at(counts, i, size, start=0):
    first = (start + i * size) // LANES
    return jnp.concatenate([counts[pl.ds(first + t, 1), :] for t in range(size // LANES)], axis=1)


def half_rows(x):
    return (0.5 * x).T.astype(BF16)


def half_product(a, b):
    return (0.5 * (a * b).astype(BF16).astype(F32)).astype(BF16)


def negative_weights(rows16, query_rows, number):
    half = 0.5 / number
    return (jnp.tanh(mul(query_rows, rows16, NN)) * half + half).astype(BF16)


def often(weight, times):
    return (weight.astype(F32) * times).astype(BF16)


def negatives(rows16, query, query_rows, times, number):
    weight = negative_weights(rows16, query_rows, number)
    return mul(query, weight, NN) * times, mul(rows16, often(weight, times), NT)


def prepare(step, left, relations, src, dst, rid, nsrc, ndst,
            weight, source, query, query_rows, left16, oh_src, oh_dst, count_l, count_r, kind, weight_rows):
    rows = left.shape[1]
    here = slice(step, step + 1)
    row_onehot(src[here, :], oh_src)
    row_onehot(dst[here, :], oh_dst)
    count_l[...] = row_counts(nsrc[here, :], rows)
    count_r[...] = row_counts(ndst[here, :], rows)
    kinds = lax.broadcasted_iota(jnp.int32, kind.shape, 0)
    kind[...] = jnp.where(rid[here, :] == kinds, 1.0, 0.0).astype(BF16)
    weight[...] = sum(mul(part, kind[...], TN) for part in split(relations[...], 3))
    weight_rows[...] = weight[...].T
    source[...] = jnp.zeros_like(source)

    size = step_of(rows)

    def part(i):
        cut = lanes_at(i, size)
        parts = split(left[:, cut], 3)
        left16[:, cut] = parts[0]
        source[...] += mul_parts(parts, oh_src[:, cut], NT)

    each(rows // size, part)
    product = source[...] * weight[...]
    query[...] = product.astype(BF16)
    query_rows[...] = half_rows(product.astype(BF16).astype(F32))


def take_piece(number, start, piece, query, query_rows, oh_dst, count_r, target, gq, rgrad, fixed=False):
    depth = target.shape[0]
    if start == 0:
        target[...] = jnp.zeros_like(target)
        gq[...] = jnp.zeros_like(gq)

    size = step_of(piece.shape[1], 256 if fixed else 512)

    def part(i):
        cut = lanes_at(i, size)
        parts = split(piece[0:depth, cut], 3)
        hits = oh_dst[:, lanes_at(i, size, start)]
        target[...] += mul_parts(parts, hits, NT)
        times = times_at(count_r, i, size, start)
        rgrad[:, cut], more = negatives(parts[0], query[...], query_rows[...], times, number)
        gq[...] += more

    each(piece.shape[1] // size, part, fixed)


def join(number, weight, source, target, gq, left16, count_l, kind, rel_in,
         probe, probe_rows, gp, lgrad, to_src, to_dst, rel_out, fixed=False):
    rows = left16.shape[1]
    product = weight[...] * target[...]
    probe[...] = product.astype(BF16)
    probe_rows[...] = half_rows(product.astype(BF16).astype(F32))
    gp[...] = jnp.zeros_like(gp)

    size = step_of(rows)

    def part(i):
        cut = lanes_at(i, size)
        lgrad[:, cut], more = negatives(left16[:, cut], probe[...], probe_rows[...], times_at(count_l, i, size), number)
        gp[...] += more

    each(rows // size, part, fixed)
    depth = weight.shape[0]
    w, s, t = weight[...], source[...], target[...]
    coef = -jax.nn.sigmoid(-jnp.sum(s * w * t, axis=0, keepdims=True))
    to_src[0:depth, :], to_src[depth:, :] = split(coef * w * t + gq[...] * w, 2)
    to_dst[0:depth, :], to_dst[depth:, :] = split(coef * w * s + gp[...] * w, 2)
    g_weight = coef * s * t + gq[...] * s + gp[...] * t
    rel_out[...] = rel_in[...] + sum(mul(kind[...], p, NT) for p in split(g_weight, 2))


def adagrad(slab, state, grad, edges, table, start, out, new_state, send=None, fixed=False, more=None):
    depth = grad.shape[0]
    size = step_of(grad.shape[1])

    def part(i):
        cut = lanes_at(i, size)
        hits = table[:, lanes_at(i, size, start)]
        g = grad[:, cut] + mul_parts([edges[0:depth, :], edges[depth:, :]], hits, NN)
        if more is not None:
            g = g + more(i, size)
        new = state[:, cut] + jnp.sum(g * g, axis=0, keepdims=True) * (1.0 / depth)
        new_state[:, cut] = new
        out[0:depth, cut] = slab[0:depth, cut] - g * (rate * lax.rsqrt(new))
        if send is not None:
            send(i).start()

    each(grad.shape[1] // size, part, fixed)


def sender(result, to, start, sems):
    size = step_of(result.shape[1])

    def copy(i):
        here = lanes_at(i, size)
        there = lanes_at(i, size, start)
        return pltpu.make_async_copy(result.at[:, here], to.at[:, there], sems.at[i + start // 256])

    return copy


def update_and_send(pieces, state, grads, edges, table, new_state, to, sems, fixed=False, start=0, more=None):
    sent = []
    for piece, grad in zip(pieces, grads):
        rows = grad.shape[1]
        copy = sender(grad, to, start, sems)
        cut = slice(start, start + rows)
        adagrad(piece, state.at[:, cut], grad, edges, table, start, grad, new_state.at[:, cut], copy, fixed, more)
        sent.append((copy, rows // step_of(rows)))
        start += rows

    def wait():
        for copy, count in sent:
            each(count, lambda i, copy=copy: copy(i).wait(), fixed)

    return wait


def pack_state(state, piece, depth):
    size = state.shape[1] // 8
    for k in range(8):
        piece[depth + k : depth + k + 1, 0:size] = state[:, k * size : (k + 1) * size]


def unpack_state(piece, depth, state):
    size = state.shape[1] // 8
    for k in range(8):
        state[:, k * size : (k + 1) * size] = piece[depth + k : depth + k + 1, 0:size]


def on_parity(parity):
    return pl.when(lax.axis_index("blk") % 2 == parity)


def pieces_of(rows, eighths):
    sizes = [rows // 8 * n for n in eighths]
    return [(sum(sizes[:i]), size) for i, size in enumerate(sizes)]


def rows_of(pieces, at, size):
    found = []
    start = 0
    for piece in pieces:
        begin, end = max(at, start), min(at + size, start + piece.shape[1])
        if begin < end:
            found.append((piece.at[:, begin - start : end - start], begin, end - begin))
        start += piece.shape[1]
    return found


def train(parity, number, last, fixed, kept, takes, gives, *refs):
    refs = list(refs)
    (left, lstate, rstate_in, rel_in) = refs[:4]
    (weight, source, query, query_rows, left16, oh_src, oh_dst, count_l, count_r, kind, _rows) = refs[4:15]
    right = refs[15 : 15 + takes]
    refs = refs[15 + takes + kept :]
    left_out, lstate_out, rel_out = refs[:3]
    right_out = refs[3 : 3 + len(gives)]
    (target, gq, rgrad, probe, probe_rows, gp, lgrad, to_src, to_dst, rstate, spare, sems) = refs[3 + len(gives) :]
    depth, rows = left.shape
    lstate_out[...] = lstate[...]
    rel_out[...] = rel_in[...]

    @on_parity(parity)
    def _():
        grads = []
        at = 0
        for piece in right:
            grads.append(rgrad.at[:, at : at + piece.shape[1]])
            take_piece(number, at, piece, query, query_rows, oh_dst, count_r, target, gq, grads[-1], fixed)
            at += piece.shape[1]
        join(number, weight, source, target, gq, left16, count_l, kind, rel_in,
             probe, probe_rows, gp, lgrad, to_src, to_dst, rel_out, fixed)
        if last:
            unpack_state(right[STATE], depth, rstate)
            wait_right = update_and_send(right, rstate, grads, to_dst, oh_dst, spare, right_out[0], sems.at[0], fixed)
            wait_left = update_and_send([left], lstate, [lgrad], to_src, oh_src, spare, left_out, sems.at[1], fixed)
            wait_right()
            wait_left()
        else:
            for (at, size), out in zip(pieces_of(rows, gives), right_out):
                for old, begin, length in rows_of(right, at, size):
                    cut = slice(begin, begin + length)
                    here = slice(begin - at, begin - at + length)
                    adagrad(old, rstate_in.at[:, cut], rgrad.at[:, cut], to_dst, oh_dst, begin, out.at[:, here], spare.at[:, cut])
            pack_state(spare, right_out[STATE], depth)
            adagrad(left, lstate, lgrad, to_src, oh_src, 0, left_out, lstate_out)


def shape(*dims, dtype=F32):
    return jax.ShapeDtypeStruct(dims, dtype)


def prepared_shapes(depth, rows, edges, kinds):
    return (
        shape(depth, edges), shape(depth, edges), shape(depth, edges, dtype=BF16), shape(edges, depth, dtype=BF16),
        shape(depth, rows, dtype=BF16), shape(edges, rows, dtype=BF16), shape(edges, rows, dtype=BF16),
        shape(rows // LANES, LANES), shape(rows // LANES, LANES), shape(kinds, edges, dtype=BF16), shape(edges, depth),
    )


def scratch(shapes):
    return [pltpu.VMEM(s.shape, s.dtype) for s in shapes]


def call(kernel, name, operands, shapes, in_large=(), out_large=(), scratch_shapes=(), aliases=None):
    vmem = pl.BlockSpec(memory_space=pltpu.VMEM)
    large = pl.BlockSpec(memory_space=pl.ANY)
    return pl.pallas_call(
        kernel,
        out_shape=tuple(shapes),
        in_specs=[large if i in in_large else vmem for i in range(len(operands))],
        out_specs=tuple(large if i in out_large else vmem for i in range(len(shapes))),
        scratch_shapes=list(scratch_shapes),
        input_output_aliases=aliases or {},
        compiler_params=pltpu.CompilerParams(vmem_limit_bytes=VMEM_LIMIT),
        cost_estimate=pl.CostEstimate(flops=1_000_000, bytes_accessed=100_000, transcendentals=0),
        name=name,
    )(*operands)


def prepared(step, left, relations, index):
    depth, rows = left.shape
    return call(
        functools.partial(prepare, step), "prepare%d" % step, [left, relations, *index],
        prepared_shapes(depth, rows, index[0].shape[1], relations.shape[0]),
    )


def trained(parity, name, number, fixed, gives, left, lstate, right, rstate, rel, ready, keep=()):
    depth, rows = left.shape
    edges = ready[0].shape[1]
    last = not gives
    blocks = [shape(depth, size) for _at, size in pieces_of(rows, gives or (8,))]
    if not last:
        blocks[STATE] = shape(depth + 8, blocks[STATE].shape[1])
    edge = shape(depth, edges)
    edge16 = shape(depth, edges, dtype=BF16)
    pair16 = shape(2 * depth, edges, dtype=BF16)
    slab = shape(depth, rows)
    inner = [edge, edge, slab, edge16, shape(edges, depth, dtype=BF16), edge, slab, pair16, pair16, shape(1, rows), shape(1, rows)]
    left_out, lstate_out, rel_out, *right_out = call(
        functools.partial(train, parity, number, last, fixed, len(keep), len(right), gives or (8,)),
        name,
        [left, lstate, rstate, rel, *ready, *right, *keep],
        [slab, shape(1, rows), shape(*rel.shape), *blocks],
        out_large=(0, 3) if last else (),
        scratch_shapes=[*scratch(inner), pltpu.SemaphoreType.DMA((2, rows // 256))],
        aliases={15 + len(right) + i: 0 for i in range(len(keep))},
    )
    return left_out, lstate_out, right_out, rel_out


def only_on(parity, body):
    def kernel(*refs):
        @on_parity(parity)
        def _():
            body(*refs)

    return kernel


def last_piece(parity, name, number, at, piece, ready, after, held=()):
    (_weight, _source, query, query_rows, _left16, _oh_src, oh_dst, _count_l, count_r, _kind, _rows) = ready
    depth, edges = query.shape

    def body(piece, query, query_rows, oh_dst, count_r, *rest):
        take_piece(number, at, piece, query, query_rows, oh_dst, count_r, *rest[len(held) + 1 :], fixed=True)

    operands = [piece, query, query_rows, oh_dst, count_r, *held, after]
    return call(
        only_on(parity, body), name, operands,
        [shape(depth, edges), shape(depth, edges), shape(depth, piece.shape[1])],
        aliases={5: 0, 6: 1} if held else {},
    )


def source_scores(number, probe_rows, left16, count_l, gp, weights=None):
    rows = left16.shape[1]
    size = step_of(rows, 1024)
    gp[...] = jnp.zeros_like(gp)
    for i in range(rows // size):
        cut = lanes_at(i, size)
        rows16 = left16[:, cut]
        part = negative_weights(rows16, probe_rows[...], number)
        if weights is not None:
            weights[:, cut] = part
        gp[...] += mul(rows16, often(part, times_at(count_l, i, size)), NT)


def early_edges(parity, name, number, step, low, high, target, ready, dst):
    (weight, source, _query, _query_rows, left16, _oh_src, _oh_dst, count_l, _count_r, _kind, weight_rows) = ready
    depth = left16.shape[0]
    edges = weight.shape[1]

    def body(weight, source, target, left16, count_l, dst, weight_rows, to_dst, target_rows, gp, probe_rows):
        w, s, t = weight[...], source[...], target[...]
        target_rows[...] = t.T
        probe_rows[...] = half_product(weight_rows[...], target_rows[...])
        source_scores(number, probe_rows, left16, count_l, gp)
        at = dst[step : step + 1, :]
        here = jnp.logical_and(at >= low, at < high)
        coef = -jax.nn.sigmoid(-jnp.sum(s * w * t, axis=0, keepdims=True))
        to_dst[0:depth, :], to_dst[depth:, :] = split(jnp.where(here, coef * w * s + gp[...] * w, 0.0), 2)

    return call(
        only_on(parity, body), name, [weight, source, target, left16, count_l, dst, weight_rows],
        [shape(2 * depth, edges, dtype=BF16), shape(edges, depth)],
        scratch_shapes=scratch([shape(depth, edges), shape(edges, depth, dtype=BF16)]),
    )


def early_right(parity, name, at, piece, state, rgrad, to_dst, oh_dst, keep):
    depth, rows = keep.shape

    def body(piece, rgrad, to_dst, oh_dst, *rest):
        out, new_state, spare, sems = rest[-4:]
        if state is None:
            unpack_state(piece, depth, new_state)
        else:
            new_state[...] = rest[0][...]
        update_and_send([piece], new_state, [rgrad], to_dst, oh_dst, spare, out, sems, fixed=True, start=at)()

    operands = [piece, rgrad, to_dst, oh_dst, *([] if state is None else [state]), keep]
    place = len(operands) - 1
    return call(
        only_on(parity, body), name, operands, [shape(depth, rows), shape(1, rows)],
        in_large=(place,), out_large=(0,),
        scratch_shapes=[*scratch([shape(1, rows)]), pltpu.SemaphoreType.DMA((rows // 256,))],
        aliases={place: 0},
    )


def late_edges(parity, number, step, at, piece, ready, dst, target, target_rows, gq, rel, after):
    (weight, source, query, query_rows, left16, _oh_src, oh_dst, count_l, count_r, kind, weight_rows) = ready
    depth, rows = left16.shape
    edges = weight.shape[1]
    pair16 = shape(2 * depth, edges, dtype=BF16)

    def body(piece, weight, source, query, query_rows, left16, oh_dst, count_l, count_r, kind, dst, weight_rows,
             held_t, held_rows, held_q, rel_in, _after,
             rgrad, to_src, to_dst, rel_out, probe, weights, gp, probe_rows):
        size = piece.shape[1]
        parts = split(piece[...], 3)
        hits = oh_dst[:, at : at + size]
        slab = jnp.concatenate(parts, axis=1)
        table = jnp.concatenate([hits] * 3, axis=1)
        probe_rows[...] = half_product(weight_rows[...], held_rows[...] + mul(table, slab, NT))
        source_scores(number, probe_rows, left16, count_l, gp, weights)
        w, s = weight[...], source[...]
        t = held_t[...] + mul(slab, table, NT)
        probe[...] = (w * t).astype(BF16)
        rgrad[...], more = negatives(parts[0], query[...], query_rows[...], times_at(count_r, 0, size, at), number)
        q = held_q[...] + more
        p = gp[...]
        coef = -jax.nn.sigmoid(-jnp.sum(s * w * t, axis=0, keepdims=True))
        g_weight = coef * s * t + q * s + p * t
        rel_out[...] = rel_in[...] + sum(mul(kind[...], part, NT) for part in split(g_weight, 2))
        to_src[0:depth, :], to_src[depth:, :] = split(coef * w * t + q * w, 2)
        here = dst[step : step + 1, :] >= at
        to_dst[0:depth, :], to_dst[depth:, :] = split(jnp.where(here, coef * w * s + p * w, 0.0), 2)

    return call(
        only_on(parity, body), "late_edges",
        [piece, weight, source, query, query_rows, left16, oh_dst, count_l, count_r, kind, dst, weight_rows,
         target, target_rows, gq, rel, after],
        [shape(depth, piece.shape[1]), pair16, pair16, shape(*rel.shape), shape(depth, edges, dtype=BF16), shape(edges, rows, dtype=BF16)],
        scratch_shapes=scratch([shape(depth, edges), shape(edges, depth, dtype=BF16)]),
        aliases={15: 3},
    )


def left_rows(cut, left, lstate, to_src, oh_src, probe, weights, count_l):
    depth = left.shape[0]
    size = cut.stop - cut.start
    g = mul(probe[...], weights[:, cut], NN) * times_at(count_l, 0, size, cut.start)
    g = g + mul_parts([to_src[0:depth, :], to_src[depth:, :]], oh_src[:, cut], NN)
    new = lstate[:, cut] + jnp.sum(g * g, axis=0, keepdims=True) * (1.0 / depth)
    return left[:, cut] - g * (rate * lax.rsqrt(new))


def ahead_rows(rows):
    return rows // 4


def first_along_rel():
    return lax.axis_index("rel") < lax.axis_size("rel") // 2


def ahead_left(parity, left, lstate, to_src, oh_src, probe, weights, count_l, rel):
    depth, rows = left.shape

    def body(left, lstate, to_src, oh_src, probe, weights, count_l, _rel, result, _rel_out):
        @pl.when(first_along_rel())
        def _():
            for i in range(ahead_rows(rows) // 256):
                cut = slice(i * 256, (i + 1) * 256)
                result[:, cut] = left_rows(cut, left, lstate, to_src, oh_src, probe, weights, count_l)

    return call(
        only_on(parity, body), "ahead_left", [left, lstate, to_src, oh_src, probe, weights, count_l, rel],
        [shape(depth, ahead_rows(rows)), shape(*rel.shape)], aliases={7: 1},
    )


def late_slabs(parity, at, left, lstate, to_src, oh_src, probe, weights, count_l, ahead,
               piece, state, rgrad, to_dst, oh_dst, keep_left, keep_right):
    depth, rows = left.shape

    def body(left, lstate, to_src, oh_src, probe, weights, count_l, ahead, piece, state, rgrad, to_dst, oh_dst,
             _keep_left, _keep_right, left_out, right_out, result, spare, sems):
        def made_ahead():
            return pltpu.make_async_copy(ahead, left_out.at[:, 0 : ahead_rows(rows)], sems.at[0, 0])

        def copy(i):
            cut = slice(i * 256, (i + 1) * 256)
            return pltpu.make_async_copy(result.at[:, cut], left_out.at[:, cut], sems.at[0, i])

        def make(i):
            cut = slice(i * 256, (i + 1) * 256)
            result[:, cut] = left_rows(cut, left, lstate, to_src, oh_src, probe, weights, count_l)

        count = rows // 256
        first = ahead_rows(rows) // 256

        @pl.when(jnp.logical_not(first_along_rel()))
        def _():
            for i in range(first):
                make(i)

        half = (count + first) // 2
        for i in range(first, half):
            make(i)
        wait = update_and_send([piece], state, [rgrad], to_dst, oh_dst, spare, right_out, sems.at[1], fixed=True, start=at)

        @pl.when(first_along_rel())
        def _():
            made_ahead().start()

        @pl.when(jnp.logical_not(first_along_rel()))
        def _():
            for i in range(first):
                copy(i).start()

        for i in range(first, half):
            copy(i).start()
        for i in range(half, count):
            make(i)
            copy(i).start()
        wait()

        @pl.when(first_along_rel())
        def _():
            made_ahead().wait()

        @pl.when(jnp.logical_not(first_along_rel()))
        def _():
            for i in range(first):
                copy(i).wait()

        for i in range(first, count):
            copy(i).wait()

    operands = [left, lstate, to_src, oh_src, probe, weights, count_l, ahead, piece, state, rgrad, to_dst, oh_dst, keep_left, keep_right]
    return call(
        only_on(parity, body), "late_slabs", operands, [shape(depth, rows), shape(depth, rows)], in_large=(13, 14), out_large=(0, 1),
        scratch_shapes=[*scratch([shape(depth, rows), shape(1, rows)]), pltpu.SemaphoreType.DMA((2, rows // 256))],
        aliases={13: 0, 14: 1},
    )


def relation_update(relations, relation_state, rels):
    kinds, depth = relations.shape

    def body(relations, relation_state, *rest):
        grad = sum(ref[...] for ref in rest[:-1])
        first = lax.broadcasted_iota(jnp.int32, (kinds, kinds), 0)
        second = lax.broadcasted_iota(jnp.int32, (kinds, kinds), 1)
        old = jnp.sum(jnp.where(first == second, relation_state[...], 0.0), axis=1, keepdims=True)
        new = old + jnp.sum(grad * grad, axis=1, keepdims=True) * (1.0 / depth)
        rest[-1][...] = relations[...] - grad * (rate * lax.rsqrt(new))

    return call(body, "relation_update", [relations, relation_state, *rels], [shape(kinds, depth)])[0]


def local(
    left_slab, left_state, right_slab, right_state, relations, relation_state,
    src_index, dst_index, relation_id, neg_source, neg_target,
):
    peers = lax.axis_size("blk")
    inside = [(i, i + 1) for i in range(0, peers, 2)]
    swap = inside + [(i + 1, i) for i in range(0, peers, 2)]
    across = [(i, (i + 1) % peers) for i in range(1, peers, 2)]
    skip = [(i, (i + 2) % peers) for i in range(0, peers, 2)]
    index = (src_index, dst_index, relation_id, neg_source, neg_target)
    left = left_slab.T
    right = right_slab.T
    rows = left.shape[1]
    lstate = left_state.reshape(1, rows)
    number = float(neg_source.shape[1])
    right_far = lax.ppermute(right, "blk", across)
    right_near = [lax.ppermute(right[:, at : at + size], "blk", inside) for at, size in pieces_of(rows, NEAR_FIRST)]
    state_near = lax.ppermute(right_state, "blk", swap)
    state_far = lax.ppermute(state_near, "blk", skip).reshape(1, rows)
    state_near = state_near.reshape(1, rows)
    rel = jnp.zeros(relations.shape, F32)
    ready = prepared(0, left, relations, index)
    left_a, lstate, far, rel = trained(1, "first_near", number, False, FAR, left, lstate, right_near, state_near, rel, ready)
    far = [lax.ppermute(piece, "blk", across) for piece in far]
    left_a, lstate, near, rel = trained(
        0, "first_far", number, True, NEAR, left, lstate, [right_far], state_far, rel, ready, (left_a,)
    )
    near = [lax.ppermute(piece, "blk", inside) for piece in near]
    ready = prepared(1, left_a, relations, index)
    first_lstate = lstate
    left_b, lstate, right_b, rel = trained(1, "last_near", number, False, (), left_a, lstate, near, state_near, rel, ready)
    cuts = pieces_of(rows, FAR)
    right_b, = right_b
    held = ()
    state = None
    for i, (at, size) in enumerate(cuts[:-1]):
        after = lstate if state is None else state
        target, gq, rgrad = last_piece(0, "last_piece%d" % i, number, at, far[i], ready, after, held)
        held = (target, gq)
        to_dst, target_rows = early_edges(0, "early_edges%d" % i, number, 1, at, at + size, target, ready, dst_index)
        right_b, state = early_right(0, "early_right%d" % i, at, far[i], state, rgrad, to_dst, ready[6], right_b)
    at = cuts[-1][0]
    rgrad, to_src, to_dst, rel, probe, weights = late_edges(0, number, 1, at, far[-1], ready, dst_index, target, target_rows, gq, rel, state)
    ahead, rel = ahead_left(0, left_a, first_lstate, to_src, ready[5], probe, weights, ready[7], rel)
    if lax.axis_size("rel") == 2:
        rels = [rel, lax.ppermute(rel, "rel", [(0, 1), (1, 0)])]
    else:
        rels = [lax.psum(rel, "rel")]
    left_b, right_b = late_slabs(
        0, at, left_a, first_lstate, to_src, ready[5], probe, weights, ready[7], ahead,
        far[-1], state, rgrad, to_dst, ready[6], left_b, right_b,
    )
    relations_out = relation_update(relations, relation_state.reshape(1, -1), rels)
    return (left_b.T, right_b.T, relations_out[None])


def solution(mesh):
    in_specs = (
        P(("blk", "rel"), None),
        P(("blk", "rel")),
        P(("blk", "rel"), None),
        P(("blk", "rel")),
        P(),
        P(),
        P(None, ("blk", "rel")),
        P(None, ("blk", "rel")),
        P(None, ("blk", "rel")),
        P(None, ("blk", "rel")),
        P(None, ("blk", "rel")),
    )
    out_specs = (P(("blk", "rel"), None), P(("blk", "rel"), None), P("blk", None, None))
    return jax.shard_map(local, mesh=mesh, in_specs=in_specs, out_specs=out_specs, check_vma=False)
```

```python
import functools

import jax
import jax.numpy as jnp
from jax import lax
from jax.experimental import pallas as pl
from jax.experimental.pallas import tpu as pltpu
from jax.sharding import PartitionSpec as P

rate = 0.1
F32 = jnp.float32
BF16 = jnp.bfloat16
LANES = 128
NEAR = (4, 4)
STATE = 0
NEAR_FIRST = (4, 4)
FAR = (5, 2, 1)
VMEM_LIMIT = 30 * 2**20

NN = (((1,), (0,)), ((), ()))
NT = (((1,), (1,)), ((), ()))
TN = (((0,), (0,)), ((), ()))


def mul(a, b, dims):
    return lax.dot_general(a, b, dims, preferred_element_type=F32)


def split(x, parts):
    out = []
    for _ in range(parts):
        part = x.astype(BF16)
        out.append(part)
        x = x - part.astype(F32)
    return out


def mul_parts(parts, table, dims):
    along = dims[0][1][0]
    return mul(jnp.concatenate(parts, axis=1), jnp.concatenate([table] * len(parts), axis=along), dims)


def lanes_at(i, size, start=0):
    if isinstance(i, int):
        return slice(start + i * size, start + (i + 1) * size)
    return pl.ds(pl.multiple_of(start + i * size, LANES), size)


def step_of(rows, most=512):
    return next(size for size in (1024, 512, 256) if size <= most and rows % size == 0)


def each(count, body, fixed=False):
    if fixed:
        for i in range(count):
            body(i)
        return

    def one(i, carry):
        body(i)
        return carry

    lax.fori_loop(0, count, one, 0)


def row_onehot(idx, table):
    count, rows = table.shape
    col = jnp.broadcast_to(idx, (LANES, count)).T
    lane = lax.broadcasted_iota(jnp.int32, (count, LANES), 1)

    def tile(t):
        hit = col == lane + t * LANES
        table[:, lanes_at(t, LANES)] = jnp.where(hit, 1.0, 0.0).astype(BF16)

    each(rows // LANES, tile)


def row_counts(idx, rows):
    count = idx.shape[1]
    high = lax.broadcasted_iota(jnp.int32, (rows // LANES, count), 0)
    low = lax.broadcasted_iota(jnp.int32, (LANES, count), 0)
    high_hit = jnp.where(idx // LANES == high, 1.0, 0.0).astype(BF16)
    low_hit = jnp.where(idx % LANES == low, 1.0, 0.0).astype(BF16)
    return mul(high_hit, low_hit, NT)


def times_at(counts, i, size, start=0):
    first = (start + i * size) // LANES
    return jnp.concatenate([counts[pl.ds(first + t, 1), :] for t in range(size // LANES)], axis=1)


def half_rows(x):
    return (0.5 * x).T.astype(BF16)


def half_product(a, b):
    return (0.5 * (a * b).astype(BF16).astype(F32)).astype(BF16)


def negative_weights(rows16, query_rows, number):
    half = 0.5 / number
    return (jnp.tanh(mul(query_rows, rows16, NN)) * half + half).astype(BF16)


def often(weight, times):
    return (weight.astype(F32) * times).astype(BF16)


def negatives(rows16, query, query_rows, times, number):
    weight = negative_weights(rows16, query_rows, number)
    return mul(query, weight, NN) * times, mul(rows16, often(weight, times), NT)


def prepare(step, left, relations, src, dst, rid, nsrc, ndst,
            weight, source, query, query_rows, left16, oh_src, oh_dst, count_l, count_r, kind, weight_rows):
    rows = left.shape[1]
    here = slice(step, step + 1)
    row_onehot(src[here, :], oh_src)
    row_onehot(dst[here, :], oh_dst)
    count_l[...] = row_counts(nsrc[here, :], rows)
    count_r[...] = row_counts(ndst[here, :], rows)
    kinds = lax.broadcasted_iota(jnp.int32, kind.shape, 0)
    kind[...] = jnp.where(rid[here, :] == kinds, 1.0, 0.0).astype(BF16)
    weight[...] = sum(mul(part, kind[...], TN) for part in split(relations[...], 3))
    weight_rows[...] = weight[...].T
    source[...] = jnp.zeros_like(source)

    size = step_of(rows)

    def part(i):
        cut = lanes_at(i, size)
        parts = split(left[:, cut], 3)
        left16[:, cut] = parts[0]
        source[...] += mul_parts(parts, oh_src[:, cut], NT)

    each(rows // size, part)
    product = source[...] * weight[...]
    query[...] = product.astype(BF16)
    query_rows[...] = half_rows(product.astype(BF16).astype(F32))


def take_piece(number, start, piece, query, query_rows, oh_dst, count_r, target, gq, rgrad, fixed=False):
    depth = target.shape[0]
    if start == 0:
        target[...] = jnp.zeros_like(target)
        gq[...] = jnp.zeros_like(gq)

    size = step_of(piece.shape[1], 256 if fixed else 512)

    def part(i):
        cut = lanes_at(i, size)
        parts = split(piece[0:depth, cut], 3)
        hits = oh_dst[:, lanes_at(i, size, start)]
        target[...] += mul_parts(parts, hits, NT)
        times = times_at(count_r, i, size, start)
        rgrad[:, cut], more = negatives(parts[0], query[...], query_rows[...], times, number)
        gq[...] += more

    each(piece.shape[1] // size, part, fixed)


def join(number, weight, source, target, gq, left16, count_l, kind, rel_in,
         probe, probe_rows, gp, lgrad, to_src, to_dst, rel_out, fixed=False):
    rows = left16.shape[1]
    product = weight[...] * target[...]
    probe[...] = product.astype(BF16)
    probe_rows[...] = half_rows(product.astype(BF16).astype(F32))
    gp[...] = jnp.zeros_like(gp)

    size = step_of(rows)

    def part(i):
        cut = lanes_at(i, size)
        lgrad[:, cut], more = negatives(left16[:, cut], probe[...], probe_rows[...], times_at(count_l, i, size), number)
        gp[...] += more

    each(rows // size, part, fixed)
    depth = weight.shape[0]
    w, s, t = weight[...], source[...], target[...]
    coef = -jax.nn.sigmoid(-jnp.sum(s * w * t, axis=0, keepdims=True))
    to_src[0:depth, :], to_src[depth:, :] = split(coef * w * t + gq[...] * w, 2)
    to_dst[0:depth, :], to_dst[depth:, :] = split(coef * w * s + gp[...] * w, 2)
    g_weight = coef * s * t + gq[...] * s + gp[...] * t
    rel_out[...] = rel_in[...] + sum(mul(kind[...], p, NT) for p in split(g_weight, 2))


def adagrad(slab, state, grad, edges, table, start, out, new_state, send=None, fixed=False, more=None):
    depth = grad.shape[0]
    size = step_of(grad.shape[1])

    def part(i):
        cut = lanes_at(i, size)
        hits = table[:, lanes_at(i, size, start)]
        g = grad[:, cut] + mul_parts([edges[0:depth, :], edges[depth:, :]], hits, NN)
        if more is not None:
            g = g + more(i, size)
        new = state[:, cut] + jnp.sum(g * g, axis=0, keepdims=True) * (1.0 / depth)
        new_state[:, cut] = new
        out[0:depth, cut] = slab[0:depth, cut] - g * (rate * lax.rsqrt(new))
        if send is not None:
            send(i).start()

    each(grad.shape[1] // size, part, fixed)


def sender(result, to, start, sems):
    size = step_of(result.shape[1])

    def copy(i):
        here = lanes_at(i, size)
        there = lanes_at(i, size, start)
        return pltpu.make_async_copy(result.at[:, here], to.at[:, there], sems.at[i + start // 256])

    return copy


def update_and_send(pieces, state, grads, edges, table, new_state, to, sems, fixed=False, start=0, more=None):
    sent = []
    for piece, grad in zip(pieces, grads):
        rows = grad.shape[1]
        copy = sender(grad, to, start, sems)
        cut = slice(start, start + rows)
        adagrad(piece, state.at[:, cut], grad, edges, table, start, grad, new_state.at[:, cut], copy, fixed, more)
        sent.append((copy, rows // step_of(rows)))
        start += rows

    def wait():
        for copy, count in sent:
            each(count, lambda i, copy=copy: copy(i).wait(), fixed)

    return wait


def pack_state(state, piece, depth):
    size = state.shape[1] // 8
    for k in range(8):
        piece[depth + k : depth + k + 1, 0:size] = state[:, k * size : (k + 1) * size]


def unpack_state(piece, depth, state):
    size = state.shape[1] // 8
    for k in range(8):
        state[:, k * size : (k + 1) * size] = piece[depth + k : depth + k + 1, 0:size]


def on_parity(parity):
    return pl.when(lax.axis_index("blk") % 2 == parity)


def pieces_of(rows, eighths):
    sizes = [rows // 8 * n for n in eighths]
    return [(sum(sizes[:i]), size) for i, size in enumerate(sizes)]


def rows_of(pieces, at, size):
    found = []
    start = 0
    for piece in pieces:
        begin, end = max(at, start), min(at + size, start + piece.shape[1])
        if begin < end:
            found.append((piece.at[:, begin - start : end - start], begin, end - begin))
        start += piece.shape[1]
    return found


def train(parity, number, last, fixed, kept, takes, gives, packs, *refs):
    refs = list(refs)
    (left, lstate, rstate_in, rel_in) = refs[:4]
    (weight, source, query, query_rows, left16, oh_src, oh_dst, count_l, count_r, kind, _rows) = refs[4:15]
    right = refs[15 : 15 + takes]
    refs = refs[15 + takes + kept :]
    left_out, lstate_out, rel_out = refs[:3]
    right_out = refs[3 : 3 + len(gives)]
    state_out = refs[3 + len(gives)]
    (target, gq, rgrad, probe, probe_rows, gp, lgrad, to_src, to_dst, rstate, spare, sems) = refs[4 + len(gives) :]
    depth, rows = left.shape
    lstate_out[...] = lstate[...]
    rel_out[...] = rel_in[...]

    @on_parity(parity)
    def _():
        grads = []
        at = 0
        for piece in right:
            grads.append(rgrad.at[:, at : at + piece.shape[1]])
            take_piece(number, at, piece, query, query_rows, oh_dst, count_r, target, gq, grads[-1], fixed)
            at += piece.shape[1]
        join(number, weight, source, target, gq, left16, count_l, kind, rel_in,
             probe, probe_rows, gp, lgrad, to_src, to_dst, rel_out, fixed)
        if last:
            unpack_state(right[STATE], depth, rstate)
            wait_right = update_and_send(right, rstate, grads, to_dst, oh_dst, spare, right_out[0], sems.at[0], fixed)
            wait_left = update_and_send([left], lstate, [lgrad], to_src, oh_src, spare, left_out, sems.at[1], fixed)
            wait_right()
            wait_left()
        else:
            for (at, size), out in zip(pieces_of(rows, gives), right_out):
                for old, begin, length in rows_of(right, at, size):
                    cut = slice(begin, begin + length)
                    here = slice(begin - at, begin - at + length)
                    adagrad(old, rstate_in.at[:, cut], rgrad.at[:, cut], to_dst, oh_dst, begin, out.at[:, here], spare.at[:, cut])
            if packs:
                pack_state(spare, right_out[STATE], depth)
            else:
                state_out[...] = spare[...]
            adagrad(left, lstate, lgrad, to_src, oh_src, 0, left_out, lstate_out)


def shape(*dims, dtype=F32):
    return jax.ShapeDtypeStruct(dims, dtype)


def prepared_shapes(depth, rows, edges, kinds):
    return (
        shape(depth, edges), shape(depth, edges), shape(depth, edges, dtype=BF16), shape(edges, depth, dtype=BF16),
        shape(depth, rows, dtype=BF16), shape(edges, rows, dtype=BF16), shape(edges, rows, dtype=BF16),
        shape(rows // LANES, LANES), shape(rows // LANES, LANES), shape(kinds, edges, dtype=BF16), shape(edges, depth),
    )


def scratch(shapes):
    return [pltpu.VMEM(s.shape, s.dtype) for s in shapes]


def call(kernel, name, operands, shapes, in_large=(), out_large=(), scratch_shapes=(), aliases=None):
    vmem = pl.BlockSpec(memory_space=pltpu.VMEM)
    large = pl.BlockSpec(memory_space=pl.ANY)
    return pl.pallas_call(
        kernel,
        out_shape=tuple(shapes),
        in_specs=[large if i in in_large else vmem for i in range(len(operands))],
        out_specs=tuple(large if i in out_large else vmem for i in range(len(shapes))),
        scratch_shapes=list(scratch_shapes),
        input_output_aliases=aliases or {},
        compiler_params=pltpu.CompilerParams(vmem_limit_bytes=VMEM_LIMIT),
        cost_estimate=pl.CostEstimate(flops=1_000_000, bytes_accessed=100_000, transcendentals=0),
        name=name,
    )(*operands)


def prepared(step, left, relations, index):
    depth, rows = left.shape
    return call(
        functools.partial(prepare, step), "prepare%d" % step, [left, relations, *index],
        prepared_shapes(depth, rows, index[0].shape[1], relations.shape[0]),
    )


def trained(parity, name, number, fixed, gives, left, lstate, right, rstate, rel, ready, keep=(), packs=False, after=()):
    depth, rows = left.shape
    edges = ready[0].shape[1]
    last = not gives
    blocks = [shape(depth, size) for _at, size in pieces_of(rows, gives or (8,))]
    if packs:
        blocks[STATE] = shape(depth + 8, blocks[STATE].shape[1])
    edge = shape(depth, edges)
    edge16 = shape(depth, edges, dtype=BF16)
    pair16 = shape(2 * depth, edges, dtype=BF16)
    slab = shape(depth, rows)
    inner = [edge, edge, slab, edge16, shape(edges, depth, dtype=BF16), edge, slab, pair16, pair16, shape(1, rows), shape(1, rows)]
    left_out, lstate_out, rel_out, *right_out, state_out = call(
        functools.partial(train, parity, number, last, fixed, len(keep) + len(after), len(right), gives or (8,), packs),
        name,
        [left, lstate, rstate, rel, *ready, *right, *keep, *after],
        [slab, shape(1, rows), shape(*rel.shape), *blocks, shape(1, rows)],
        out_large=(0, 3) if last else (),
        scratch_shapes=[*scratch(inner), pltpu.SemaphoreType.DMA((2, rows // 256))],
        aliases={15 + len(right) + i: 0 for i in range(len(keep))},
    )
    return left_out, lstate_out, right_out, rel_out, state_out


def only_on(parity, body):
    def kernel(*refs):
        @on_parity(parity)
        def _():
            body(*refs)

    return kernel


def last_piece(parity, name, number, at, piece, ready, after, held=()):
    (_weight, _source, query, query_rows, _left16, _oh_src, oh_dst, _count_l, count_r, _kind, _rows) = ready
    depth, edges = query.shape

    def body(piece, query, query_rows, oh_dst, count_r, *rest):
        take_piece(number, at, piece, query, query_rows, oh_dst, count_r, *rest[len(held) + 1 :], fixed=True)

    operands = [piece, query, query_rows, oh_dst, count_r, *held, after]
    return call(
        only_on(parity, body), name, operands,
        [shape(depth, edges), shape(depth, edges), shape(depth, piece.shape[1])],
        aliases={5: 0, 6: 1} if held else {},
    )


def source_scores(number, probe_rows, left16, count_l, gp, weights=None):
    rows = left16.shape[1]
    size = step_of(rows, 1024)
    gp[...] = jnp.zeros_like(gp)
    for i in range(rows // size):
        cut = lanes_at(i, size)
        rows16 = left16[:, cut]
        part = negative_weights(rows16, probe_rows[...], number)
        if weights is not None:
            weights[:, cut] = part
        gp[...] += mul(rows16, often(part, times_at(count_l, i, size)), NT)


def early_edges(parity, name, number, step, low, high, target, ready, dst):
    (weight, source, _query, _query_rows, left16, _oh_src, _oh_dst, count_l, _count_r, _kind, weight_rows) = ready
    depth = left16.shape[0]
    edges = weight.shape[1]

    def body(weight, source, target, left16, count_l, dst, weight_rows, to_dst, target_rows, gp, probe_rows):
        w, s, t = weight[...], source[...], target[...]
        target_rows[...] = t.T
        probe_rows[...] = half_product(weight_rows[...], target_rows[...])
        source_scores(number, probe_rows, left16, count_l, gp)
        at = dst[step : step + 1, :]
        here = jnp.logical_and(at >= low, at < high)
        coef = -jax.nn.sigmoid(-jnp.sum(s * w * t, axis=0, keepdims=True))
        to_dst[0:depth, :], to_dst[depth:, :] = split(jnp.where(here, coef * w * s + gp[...] * w, 0.0), 2)

    return call(
        only_on(parity, body), name, [weight, source, target, left16, count_l, dst, weight_rows],
        [shape(2 * depth, edges, dtype=BF16), shape(edges, depth)],
        scratch_shapes=scratch([shape(depth, edges), shape(edges, depth, dtype=BF16)]),
    )


def early_right(parity, name, at, piece, state, rgrad, to_dst, oh_dst, keep, order):
    depth, rows = keep.shape

    def body(piece, state, rgrad, to_dst, oh_dst, _order, _keep, out, _order_out, spare, sems):
        update_and_send([piece], state, [rgrad], to_dst, oh_dst, spare, out, sems, fixed=True, start=at)()

    return call(
        only_on(parity, body), name, [piece, state, rgrad, to_dst, oh_dst, order, keep], [shape(depth, rows), shape(*order.shape)],
        in_large=(6,), out_large=(0,),
        scratch_shapes=[*scratch([shape(1, rows)]), pltpu.SemaphoreType.DMA((rows // 256,))],
        aliases={5: 1, 6: 0},
    )


def late_edges(parity, number, step, at, piece, ready, dst, target, target_rows, gq, rel, after):
    (weight, source, query, query_rows, left16, _oh_src, oh_dst, count_l, count_r, kind, weight_rows) = ready
    depth, rows = left16.shape
    edges = weight.shape[1]
    pair16 = shape(2 * depth, edges, dtype=BF16)

    def body(piece, weight, source, query, query_rows, left16, oh_dst, count_l, count_r, kind, dst, weight_rows,
             held_t, held_rows, held_q, rel_in, _after,
             rgrad, to_src, to_dst, rel_out, probe, weights, gp, probe_rows):
        size = piece.shape[1]
        parts = split(piece[...], 3)
        hits = oh_dst[:, at : at + size]
        slab = jnp.concatenate(parts, axis=1)
        table = jnp.concatenate([hits] * 3, axis=1)
        probe_rows[...] = half_product(weight_rows[...], held_rows[...] + mul(table, slab, NT))
        source_scores(number, probe_rows, left16, count_l, gp, weights)
        w, s = weight[...], source[...]
        t = held_t[...] + mul(slab, table, NT)
        probe[...] = (w * t).astype(BF16)
        rgrad[...], more = negatives(parts[0], query[...], query_rows[...], times_at(count_r, 0, size, at), number)
        q = held_q[...] + more
        p = gp[...]
        coef = -jax.nn.sigmoid(-jnp.sum(s * w * t, axis=0, keepdims=True))
        g_weight = coef * s * t + q * s + p * t
        rel_out[...] = rel_in[...] + sum(mul(kind[...], part, NT) for part in split(g_weight, 2))
        to_src[0:depth, :], to_src[depth:, :] = split(coef * w * t + q * w, 2)
        here = dst[step : step + 1, :] >= at
        to_dst[0:depth, :], to_dst[depth:, :] = split(jnp.where(here, coef * w * s + p * w, 0.0), 2)

    return call(
        only_on(parity, body), "late_edges",
        [piece, weight, source, query, query_rows, left16, oh_dst, count_l, count_r, kind, dst, weight_rows,
         target, target_rows, gq, rel, after],
        [shape(depth, piece.shape[1]), pair16, pair16, shape(*rel.shape), shape(depth, edges, dtype=BF16), shape(edges, rows, dtype=BF16)],
        scratch_shapes=scratch([shape(depth, edges), shape(edges, depth, dtype=BF16)]),
        aliases={15: 3},
    )


def left_rows(cut, left, lstate, to_src, oh_src, probe, weights, count_l):
    depth = left.shape[0]
    size = cut.stop - cut.start
    g = mul(probe[...], weights[:, cut], NN) * times_at(count_l, 0, size, cut.start)
    g = g + mul_parts([to_src[0:depth, :], to_src[depth:, :]], oh_src[:, cut], NN)
    new = lstate[:, cut] + jnp.sum(g * g, axis=0, keepdims=True) * (1.0 / depth)
    return left[:, cut] - g * (rate * lax.rsqrt(new))


def ahead_rows(rows):
    return rows // 8 * 3


def first_along_rel():
    return lax.axis_index("rel") < lax.axis_size("rel") // 2


def ahead_left(parity, left, lstate, to_src, oh_src, probe, weights, count_l, rel):
    depth, rows = left.shape

    def body(left, lstate, to_src, oh_src, probe, weights, count_l, _rel, result, _rel_out):
        @pl.when(first_along_rel())
        def _():
            for i in range(ahead_rows(rows) // 256):
                cut = slice(i * 256, (i + 1) * 256)
                result[:, cut] = left_rows(cut, left, lstate, to_src, oh_src, probe, weights, count_l)

    return call(
        only_on(parity, body), "ahead_left", [left, lstate, to_src, oh_src, probe, weights, count_l, rel],
        [shape(depth, ahead_rows(rows)), shape(*rel.shape)], aliases={7: 1},
    )


def late_slabs(parity, at, left, lstate, to_src, oh_src, probe, weights, count_l, ahead,
               piece, state, rgrad, to_dst, oh_dst, keep_left, keep_right):
    depth, rows = left.shape

    def body(left, lstate, to_src, oh_src, probe, weights, count_l, ahead, piece, state, rgrad, to_dst, oh_dst,
             _keep_left, _keep_right, left_out, right_out, result, spare, sems):
        def made_ahead():
            return pltpu.make_async_copy(ahead, left_out.at[:, 0 : ahead_rows(rows)], sems.at[0, 0])

        def runs(start, stop):
            out = []
            while start < stop:
                size = 512 if start % 512 == 0 and start + 512 <= stop else 256
                out.append(slice(start, start + size))
                start += size
            return out

        def copy(cut):
            return pltpu.make_async_copy(result.at[:, cut], left_out.at[:, cut], sems.at[0, cut.start // 256])

        def make(cut):
            result[:, cut] = left_rows(cut, left, lstate, to_src, oh_src, probe, weights, count_l)
            copy(cut).start()

        first, others = runs(0, ahead_rows(rows)), runs(ahead_rows(rows), rows)

        @pl.when(first_along_rel())
        def _():
            made_ahead().start()

        @pl.when(jnp.logical_not(first_along_rel()))
        def _():
            for cut in first:
                make(cut)

        wait = update_and_send([piece], state, [rgrad], to_dst, oh_dst, spare, right_out, sems.at[1], fixed=True, start=at)
        for cut in others:
            make(cut)
        wait()

        @pl.when(first_along_rel())
        def _():
            made_ahead().wait()

        @pl.when(jnp.logical_not(first_along_rel()))
        def _():
            for cut in first:
                copy(cut).wait()

        for cut in others:
            copy(cut).wait()

    operands = [left, lstate, to_src, oh_src, probe, weights, count_l, ahead, piece, state, rgrad, to_dst, oh_dst, keep_left, keep_right]
    return call(
        only_on(parity, body), "late_slabs", operands, [shape(depth, rows), shape(depth, rows)], in_large=(13, 14), out_large=(0, 1),
        scratch_shapes=[*scratch([shape(depth, rows), shape(1, rows)]), pltpu.SemaphoreType.DMA((2, rows // 256))],
        aliases={13: 0, 14: 1},
    )


def relation_update(relations, relation_state, rels):
    kinds, depth = relations.shape

    def body(relations, relation_state, *rest):
        grad = sum(ref[...] for ref in rest[:-1])
        first = lax.broadcasted_iota(jnp.int32, (kinds, kinds), 0)
        second = lax.broadcasted_iota(jnp.int32, (kinds, kinds), 1)
        old = jnp.sum(jnp.where(first == second, relation_state[...], 0.0), axis=1, keepdims=True)
        new = old + jnp.sum(grad * grad, axis=1, keepdims=True) * (1.0 / depth)
        rest[-1][...] = relations[...] - grad * (rate * lax.rsqrt(new))

    return call(body, "relation_update", [relations, relation_state, *rels], [shape(kinds, depth)])[0]


def local(
    left_slab, left_state, right_slab, right_state, relations, relation_state,
    src_index, dst_index, relation_id, neg_source, neg_target,
):
    peers = lax.axis_size("blk")
    inside = [(i, i + 1) for i in range(0, peers, 2)]
    across = [(i, (i + 1) % peers) for i in range(1, peers, 2)]
    back = [(i + 1, i) for i in range(0, peers, 2)]
    swap = inside + back
    skip = [(i, (i + 2) % peers) for i in range(0, peers, 2)]
    index = (src_index, dst_index, relation_id, neg_source, neg_target)
    left = left_slab.T
    right = right_slab.T
    rows = left.shape[1]
    lstate = left_state.reshape(1, rows)
    number = float(neg_source.shape[1])
    right_far = lax.ppermute(right, "blk", across)
    right_near = [lax.ppermute(right[:, at : at + size], "blk", inside) for at, size in pieces_of(rows, NEAR_FIRST)]
    state_near = lax.ppermute(right_state, "blk", swap)
    state_far = lax.ppermute(state_near, "blk", skip).reshape(1, rows)
    state_near = state_near.reshape(1, rows)
    rel = jnp.zeros(relations.shape, F32)
    ready = prepared(0, left, relations, index)
    left_a, lstate, far, rel, state = trained(1, "first_near", number, False, FAR, left, lstate, right_near, state_near, rel, ready)
    far = [lax.ppermute(piece, "blk", across) for piece in far]
    state = lax.ppermute(lax.ppermute(state, "blk", back), "blk", skip)
    left_a, lstate, near, rel, _ = trained(
        0, "first_far", number, True, NEAR, left, lstate, [right_far], state_far, rel, ready, (left_a,), True, (state,)
    )
    near = [lax.ppermute(piece, "blk", inside) for piece in near]
    ready = prepared(1, left_a, relations, index)
    first_lstate = lstate
    left_b, lstate, right_b, rel, _ = trained(1, "last_near", number, False, (), left_a, lstate, near, state_near, rel, ready)
    cuts = pieces_of(rows, FAR)
    right_b, = right_b
    held = ()
    order = lstate
    for i, (at, size) in enumerate(cuts[:-1]):
        target, gq, rgrad = last_piece(0, "last_piece%d" % i, number, at, far[i], ready, order, held)
        held = (target, gq)
        to_dst, target_rows = early_edges(0, "early_edges%d" % i, number, 1, at, at + size, target, ready, dst_index)
        right_b, order = early_right(0, "early_right%d" % i, at, far[i], state, rgrad, to_dst, ready[6], right_b, order)
    at = cuts[-1][0]
    rgrad, to_src, to_dst, rel, probe, weights = late_edges(0, number, 1, at, far[-1], ready, dst_index, target, target_rows, gq, rel, order)
    ahead, rel = ahead_left(0, left_a, first_lstate, to_src, ready[5], probe, weights, ready[7], rel)
    if lax.axis_size("rel") == 2:
        rels = [rel, lax.ppermute(rel, "rel", [(0, 1), (1, 0)])]
    else:
        rels = [lax.psum(rel, "rel")]
    left_b, right_b = late_slabs(
        0, at, left_a, first_lstate, to_src, ready[5], probe, weights, ready[7], ahead,
        far[-1], state, rgrad, to_dst, ready[6], left_b, right_b,
    )
    relations_out = relation_update(relations, relation_state.reshape(1, -1), rels)
    return (left_b.T, right_b.T, relations_out[None])


def solution(mesh):
    in_specs = (
        P(("blk", "rel"), None),
        P(("blk", "rel")),
        P(("blk", "rel"), None),
        P(("blk", "rel")),
        P(),
        P(),
        P(None, ("blk", "rel")),
        P(None, ("blk", "rel")),
        P(None, ("blk", "rel")),
        P(None, ("blk", "rel")),
        P(None, ("blk", "rel")),
    )
    out_specs = (P(("blk", "rel"), None), P(("blk", "rel"), None), P("blk", None, None))
    return jax.shard_map(local, mesh=mesh, in_specs=in_specs, out_specs=out_specs, check_vma=False)
```

```python
import functools

import jax
import jax.numpy as jnp
from jax import lax
from jax.experimental import pallas as pl
from jax.experimental.pallas import tpu as pltpu
from jax.sharding import PartitionSpec as P

rate = 0.1
F32 = jnp.float32
BF16 = jnp.bfloat16
LANES = 128
NEAR = (4, 4)
STATE = 0
NEAR_FIRST = (4, 4)
FAR = (5, 2, 1)
VMEM_LIMIT = 30 * 2**20

NN = (((1,), (0,)), ((), ()))
NT = (((1,), (1,)), ((), ()))
TN = (((0,), (0,)), ((), ()))


def mul(a, b, dims):
    return lax.dot_general(a, b, dims, preferred_element_type=F32)


def split(x, parts):
    out = []
    for _ in range(parts):
        part = x.astype(BF16)
        out.append(part)
        x = x - part.astype(F32)
    return out


def mul_parts(parts, table, dims):
    along = dims[0][1][0]
    return mul(jnp.concatenate(parts, axis=1), jnp.concatenate([table] * len(parts), axis=along), dims)


def lanes_at(i, size, start=0):
    if isinstance(i, int):
        return slice(start + i * size, start + (i + 1) * size)
    return pl.ds(pl.multiple_of(start + i * size, LANES), size)


def step_of(rows, most=512):
    return next(size for size in (2048, 1024, 512, 256) if size <= most and rows % size == 0)


def each(count, body, fixed=False):
    if fixed:
        for i in range(count):
            body(i)
        return

    def one(i, carry):
        body(i)
        return carry

    lax.fori_loop(0, count, one, 0)


def row_onehot(idx, table):
    count, rows = table.shape
    col = jnp.broadcast_to(idx, (LANES, count)).T
    lane = lax.broadcasted_iota(jnp.int32, (count, LANES), 1)

    def tile(t):
        hit = col == lane + t * LANES
        table[:, lanes_at(t, LANES)] = jnp.where(hit, 1.0, 0.0).astype(BF16)

    each(rows // LANES, tile)


def row_counts(idx, rows):
    count = idx.shape[1]
    high = lax.broadcasted_iota(jnp.int32, (rows // LANES, count), 0)
    low = lax.broadcasted_iota(jnp.int32, (LANES, count), 0)
    high_hit = jnp.where(idx // LANES == high, 1.0, 0.0).astype(BF16)
    low_hit = jnp.where(idx % LANES == low, 1.0, 0.0).astype(BF16)
    return mul(high_hit, low_hit, NT)


def times_at(counts, i, size, start=0):
    first = (start + i * size) // LANES
    return jnp.concatenate([counts[pl.ds(first + t, 1), :] for t in range(size // LANES)], axis=1)


def half_rows(x):
    return (0.5 * x).T.astype(BF16)


def half_product(a, b):
    return (0.5 * (a * b).astype(BF16).astype(F32)).astype(BF16)


def negative_weights(rows16, query_rows, number):
    half = 0.5 / number
    return (jnp.tanh(mul(query_rows, rows16, NN)) * half + half).astype(BF16)


def often(weight, times):
    return (weight.astype(F32) * times).astype(BF16)


def negatives(rows16, query, query_rows, times, number):
    weight = negative_weights(rows16, query_rows, number)
    return mul(query, weight, NN) * times, mul(rows16, often(weight, times), NT)


def prepare(step, left, relations, src, dst, rid, nsrc, ndst,
            weight, source, query, query_rows, left16, oh_src, oh_dst, count_l, count_r, kind, weight_rows):
    rows = left.shape[1]
    here = slice(step, step + 1)
    row_onehot(src[here, :], oh_src)
    row_onehot(dst[here, :], oh_dst)
    count_l[...] = row_counts(nsrc[here, :], rows)
    count_r[...] = row_counts(ndst[here, :], rows)
    kinds = lax.broadcasted_iota(jnp.int32, kind.shape, 0)
    kind[...] = jnp.where(rid[here, :] == kinds, 1.0, 0.0).astype(BF16)
    weight[...] = sum(mul(part, kind[...], TN) for part in split(relations[...], 3))
    weight_rows[...] = weight[...].T
    source[...] = jnp.zeros_like(source)

    size = step_of(rows)

    def part(i):
        cut = lanes_at(i, size)
        parts = split(left[:, cut], 3)
        left16[:, cut] = parts[0]
        source[...] += mul_parts(parts, oh_src[:, cut], NT)

    each(rows // size, part)
    product = source[...] * weight[...]
    query[...] = product.astype(BF16)
    query_rows[...] = half_rows(product.astype(BF16).astype(F32))


def take_piece(number, start, piece, query, query_rows, oh_dst, count_r, target, gq, rgrad, fixed=False):
    depth = target.shape[0]
    if start == 0:
        target[...] = jnp.zeros_like(target)
        gq[...] = jnp.zeros_like(gq)

    size = step_of(piece.shape[1], 256 if fixed else 512)

    def part(i):
        cut = lanes_at(i, size)
        parts = split(piece[0:depth, cut], 3)
        hits = oh_dst[:, lanes_at(i, size, start)]
        target[...] += mul_parts(parts, hits, NT)
        times = times_at(count_r, i, size, start)
        rgrad[:, cut], more = negatives(parts[0], query[...], query_rows[...], times, number)
        gq[...] += more

    each(piece.shape[1] // size, part, fixed)


def join(number, weight, source, target, gq, left16, count_l, kind, rel_in,
         probe, probe_rows, gp, lgrad, to_src, to_dst, rel_out, fixed=False):
    rows = left16.shape[1]
    product = weight[...] * target[...]
    probe[...] = product.astype(BF16)
    probe_rows[...] = half_rows(product.astype(BF16).astype(F32))
    gp[...] = jnp.zeros_like(gp)

    size = step_of(rows)

    def part(i):
        cut = lanes_at(i, size)
        lgrad[:, cut], more = negatives(left16[:, cut], probe[...], probe_rows[...], times_at(count_l, i, size), number)
        gp[...] += more

    each(rows // size, part, fixed)
    depth = weight.shape[0]
    w, s, t = weight[...], source[...], target[...]
    coef = -jax.nn.sigmoid(-jnp.sum(s * w * t, axis=0, keepdims=True))
    to_src[0:depth, :], to_src[depth:, :] = split(coef * w * t + gq[...] * w, 2)
    to_dst[0:depth, :], to_dst[depth:, :] = split(coef * w * s + gp[...] * w, 2)
    g_weight = coef * s * t + gq[...] * s + gp[...] * t
    rel_out[...] = rel_in[...] + sum(mul(kind[...], p, NT) for p in split(g_weight, 2))


def adagrad(slab, state, grad, edges, table, start, out, new_state, send=None, fixed=False, more=None):
    depth = grad.shape[0]
    size = step_of(grad.shape[1])

    def part(i):
        cut = lanes_at(i, size)
        hits = table[:, lanes_at(i, size, start)]
        g = grad[:, cut] + mul_parts([edges[0:depth, :], edges[depth:, :]], hits, NN)
        if more is not None:
            g = g + more(i, size)
        new = state[:, cut] + jnp.sum(g * g, axis=0, keepdims=True) * (1.0 / depth)
        new_state[:, cut] = new
        out[0:depth, cut] = slab[0:depth, cut] - g * (rate * lax.rsqrt(new))
        if send is not None:
            send(i).start()

    each(grad.shape[1] // size, part, fixed)


def sender(result, to, start, sems):
    size = step_of(result.shape[1])

    def copy(i):
        here = lanes_at(i, size)
        there = lanes_at(i, size, start)
        return pltpu.make_async_copy(result.at[:, here], to.at[:, there], sems.at[i + start // 256])

    return copy


def update_and_send(pieces, state, grads, edges, table, new_state, to, sems, fixed=False, start=0, more=None):
    sent = []
    for piece, grad in zip(pieces, grads):
        rows = grad.shape[1]
        copy = sender(grad, to, start, sems)
        cut = slice(start, start + rows)
        adagrad(piece, state.at[:, cut], grad, edges, table, start, grad, new_state.at[:, cut], copy, fixed, more)
        sent.append((copy, rows // step_of(rows)))
        start += rows

    def wait():
        for copy, count in sent:
            each(count, lambda i, copy=copy: copy(i).wait(), fixed)

    return wait


def pack_state(state, piece, depth):
    size = state.shape[1] // 8
    for k in range(8):
        piece[depth + k : depth + k + 1, 0:size] = state[:, k * size : (k + 1) * size]


def unpack_state(piece, depth, state):
    size = state.shape[1] // 8
    for k in range(8):
        state[:, k * size : (k + 1) * size] = piece[depth + k : depth + k + 1, 0:size]


def on_parity(parity):
    return pl.when(lax.axis_index("blk") % 2 == parity)


def pieces_of(rows, eighths):
    sizes = [rows // 8 * n for n in eighths]
    return [(sum(sizes[:i]), size) for i, size in enumerate(sizes)]


def rows_of(pieces, at, size):
    found = []
    start = 0
    for piece in pieces:
        begin, end = max(at, start), min(at + size, start + piece.shape[1])
        if begin < end:
            found.append((piece.at[:, begin - start : end - start], begin, end - begin))
        start += piece.shape[1]
    return found


def train(parity, number, last, fixed, kept, takes, gives, packs, *refs):
    refs = list(refs)
    (left, lstate, rstate_in, rel_in) = refs[:4]
    (weight, source, query, query_rows, left16, oh_src, oh_dst, count_l, count_r, kind, _rows) = refs[4:15]
    right = refs[15 : 15 + takes]
    refs = refs[15 + takes + kept :]
    left_out, lstate_out, rel_out = refs[:3]
    right_out = refs[3 : 3 + len(gives)]
    state_out = refs[3 + len(gives)]
    (target, gq, rgrad, probe, probe_rows, gp, lgrad, to_src, to_dst, rstate, spare, sems) = refs[4 + len(gives) :]
    depth, rows = left.shape
    lstate_out[...] = lstate[...]
    rel_out[...] = rel_in[...]

    @on_parity(parity)
    def _():
        grads = []
        at = 0
        for piece in right:
            grads.append(rgrad.at[:, at : at + piece.shape[1]])
            take_piece(number, at, piece, query, query_rows, oh_dst, count_r, target, gq, grads[-1], fixed)
            at += piece.shape[1]
        join(number, weight, source, target, gq, left16, count_l, kind, rel_in,
             probe, probe_rows, gp, lgrad, to_src, to_dst, rel_out, fixed)
        if last:
            unpack_state(right[STATE], depth, rstate)
            wait_right = update_and_send(right, rstate, grads, to_dst, oh_dst, spare, right_out[0], sems.at[0], fixed)
            wait_left = update_and_send([left], lstate, [lgrad], to_src, oh_src, spare, left_out, sems.at[1], fixed)
            wait_right()
            wait_left()
        else:
            for (at, size), out in zip(pieces_of(rows, gives), right_out):
                for old, begin, length in rows_of(right, at, size):
                    cut = slice(begin, begin + length)
                    here = slice(begin - at, begin - at + length)
                    adagrad(old, rstate_in.at[:, cut], rgrad.at[:, cut], to_dst, oh_dst, begin, out.at[:, here], spare.at[:, cut])
            if packs:
                pack_state(spare, right_out[STATE], depth)
            else:
                state_out[...] = spare[...]
            adagrad(left, lstate, lgrad, to_src, oh_src, 0, left_out, lstate_out)


def shape(*dims, dtype=F32):
    return jax.ShapeDtypeStruct(dims, dtype)


def prepared_shapes(depth, rows, edges, kinds):
    return (
        shape(depth, edges), shape(depth, edges), shape(depth, edges, dtype=BF16), shape(edges, depth, dtype=BF16),
        shape(depth, rows, dtype=BF16), shape(edges, rows, dtype=BF16), shape(edges, rows, dtype=BF16),
        shape(rows // LANES, LANES), shape(rows // LANES, LANES), shape(kinds, edges, dtype=BF16), shape(edges, depth),
    )


def scratch(shapes):
    return [pltpu.VMEM(s.shape, s.dtype) for s in shapes]


def call(kernel, name, operands, shapes, in_large=(), out_large=(), scratch_shapes=(), aliases=None):
    vmem = pl.BlockSpec(memory_space=pltpu.VMEM)
    large = pl.BlockSpec(memory_space=pl.ANY)
    return pl.pallas_call(
        kernel,
        out_shape=tuple(shapes),
        in_specs=[large if i in in_large else vmem for i in range(len(operands))],
        out_specs=tuple(large if i in out_large else vmem for i in range(len(shapes))),
        scratch_shapes=list(scratch_shapes),
        input_output_aliases=aliases or {},
        compiler_params=pltpu.CompilerParams(vmem_limit_bytes=VMEM_LIMIT),
        cost_estimate=pl.CostEstimate(flops=1_000_000, bytes_accessed=100_000, transcendentals=0),
        name=name,
    )(*operands)


def prepared(step, left, relations, index):
    depth, rows = left.shape
    return call(
        functools.partial(prepare, step), "prepare%d" % step, [left, relations, *index],
        prepared_shapes(depth, rows, index[0].shape[1], relations.shape[0]),
    )


def trained(parity, name, number, fixed, gives, left, lstate, right, rstate, rel, ready, keep=(), packs=False, after=()):
    depth, rows = left.shape
    edges = ready[0].shape[1]
    last = not gives
    blocks = [shape(depth, size) for _at, size in pieces_of(rows, gives or (8,))]
    if packs:
        blocks[STATE] = shape(depth + 8, blocks[STATE].shape[1])
    edge = shape(depth, edges)
    edge16 = shape(depth, edges, dtype=BF16)
    pair16 = shape(2 * depth, edges, dtype=BF16)
    slab = shape(depth, rows)
    inner = [edge, edge, slab, edge16, shape(edges, depth, dtype=BF16), edge, slab, pair16, pair16, shape(1, rows), shape(1, rows)]
    left_out, lstate_out, rel_out, *right_out, state_out = call(
        functools.partial(train, parity, number, last, fixed, len(keep) + len(after), len(right), gives or (8,), packs),
        name,
        [left, lstate, rstate, rel, *ready, *right, *keep, *after],
        [slab, shape(1, rows), shape(*rel.shape), *blocks, shape(1, rows)],
        out_large=(0, 3) if last else (),
        scratch_shapes=[*scratch(inner), pltpu.SemaphoreType.DMA((2, rows // 256))],
        aliases={15 + len(right) + i: 0 for i in range(len(keep))},
    )
    return left_out, lstate_out, right_out, rel_out, state_out


def only_on(parity, body):
    def kernel(*refs):
        @on_parity(parity)
        def _():
            body(*refs)

    return kernel


def last_piece(parity, name, number, at, piece, ready, after, held=()):
    (_weight, _source, query, query_rows, _left16, _oh_src, oh_dst, _count_l, count_r, _kind, _rows) = ready
    depth, edges = query.shape

    def body(piece, query, query_rows, oh_dst, count_r, *rest):
        take_piece(number, at, piece, query, query_rows, oh_dst, count_r, *rest[len(held) + 1 :], fixed=True)

    operands = [piece, query, query_rows, oh_dst, count_r, *held, after]
    return call(
        only_on(parity, body), name, operands,
        [shape(depth, edges), shape(depth, edges), shape(depth, piece.shape[1])],
        aliases={5: 0, 6: 1} if held else {},
    )


def source_scores(number, probe_rows, left16, count_l, gp, weights=None):
    rows = left16.shape[1]
    size = step_of(rows, 2048)
    total = None
    for i in range(rows // size):
        cut = lanes_at(i, size)
        rows16 = left16[:, cut]
        part = negative_weights(rows16, probe_rows[...], number)
        if weights is not None:
            weights[:, cut] = part
        more = mul(rows16, often(part, times_at(count_l, i, size)), NT)
        total = more if total is None else total + more
    gp[...] = total


def early_edges(parity, name, number, step, low, high, target, ready, dst):
    (weight, source, _query, _query_rows, left16, _oh_src, _oh_dst, count_l, _count_r, _kind, weight_rows) = ready
    depth = left16.shape[0]
    edges = weight.shape[1]

    def body(weight, source, target, left16, count_l, dst, weight_rows, to_dst, target_rows, gp, probe_rows):
        w, s, t = weight[...], source[...], target[...]
        target_rows[...] = t.T
        probe_rows[...] = half_product(weight_rows[...], target_rows[...])
        source_scores(number, probe_rows, left16, count_l, gp)
        at = dst[step : step + 1, :]
        here = jnp.logical_and(at >= low, at < high)
        coef = -jax.nn.sigmoid(-jnp.sum(s * w * t, axis=0, keepdims=True))
        to_dst[0:depth, :], to_dst[depth:, :] = split(jnp.where(here, coef * w * s + gp[...] * w, 0.0), 2)

    return call(
        only_on(parity, body), name, [weight, source, target, left16, count_l, dst, weight_rows],
        [shape(2 * depth, edges, dtype=BF16), shape(edges, depth)],
        scratch_shapes=scratch([shape(depth, edges), shape(edges, depth, dtype=BF16)]),
    )


def early_right(parity, name, at, piece, state, rgrad, to_dst, oh_dst, keep, order):
    depth, rows = keep.shape

    def body(piece, state, rgrad, to_dst, oh_dst, _order, _keep, out, _order_out, spare, sems):
        update_and_send([piece], state, [rgrad], to_dst, oh_dst, spare, out, sems, fixed=True, start=at)()

    return call(
        only_on(parity, body), name, [piece, state, rgrad, to_dst, oh_dst, order, keep], [shape(depth, rows), shape(*order.shape)],
        in_large=(6,), out_large=(0,),
        scratch_shapes=[*scratch([shape(1, rows)]), pltpu.SemaphoreType.DMA((rows // 256,))],
        aliases={5: 1, 6: 0},
    )


def late_edges(parity, number, step, at, piece, ready, dst, target_rows, gq, rel, after):
    (weight, source, query, query_rows, left16, _oh_src, oh_dst, count_l, count_r, kind, weight_rows) = ready
    depth, rows = left16.shape
    edges = weight.shape[1]
    pair16 = shape(2 * depth, edges, dtype=BF16)

    def body(piece, weight, source, query, query_rows, left16, oh_dst, count_l, count_r, kind, dst, weight_rows,
             held_rows, held_q, rel_in, _after,
             rgrad, to_src, to_dst, rel_out, probe, weights, gp, probe_rows):
        size = piece.shape[1]
        parts = split(piece[...], 3)
        hits = oh_dst[:, at : at + size]
        slab = jnp.concatenate(parts, axis=1)
        table = jnp.concatenate([hits] * 3, axis=1)
        t_rows = held_rows[...] + mul(table, slab, NT)
        probe_rows[...] = half_product(weight_rows[...], t_rows)
        source_scores(number, probe_rows, left16, count_l, gp, weights)
        w, s = weight[...], source[...]
        t = t_rows.T
        probe[...] = (w * t).astype(BF16)
        rgrad[...], more = negatives(parts[0], query[...], query_rows[...], times_at(count_r, 0, size, at), number)
        q = held_q[...] + more
        p = gp[...]
        coef = -jax.nn.sigmoid(-jnp.sum(s * w * t, axis=0, keepdims=True))
        g_weight = coef * s * t + q * s + p * t
        rel_out[...] = rel_in[...] + sum(mul(kind[...], part, NT) for part in split(g_weight, 2))
        to_src[0:depth, :], to_src[depth:, :] = split(coef * w * t + q * w, 2)
        here = dst[step : step + 1, :] >= at
        to_dst[0:depth, :], to_dst[depth:, :] = split(jnp.where(here, coef * w * s + p * w, 0.0), 2)

    return call(
        only_on(parity, body), "late_edges",
        [piece, weight, source, query, query_rows, left16, oh_dst, count_l, count_r, kind, dst, weight_rows,
         target_rows, gq, rel, after],
        [shape(depth, piece.shape[1]), pair16, pair16, shape(*rel.shape), shape(depth, edges, dtype=BF16), shape(edges, rows, dtype=BF16)],
        scratch_shapes=scratch([shape(depth, edges), shape(edges, depth, dtype=BF16)]),
        aliases={14: 3},
    )


def left_rows(cut, left, lstate, to_src, oh_src, probe, weights, count_l):
    depth = left.shape[0]
    size = cut.stop - cut.start
    g = mul(probe[...], weights[:, cut], NN) * times_at(count_l, 0, size, cut.start)
    g = g + mul_parts([to_src[0:depth, :], to_src[depth:, :]], oh_src[:, cut], NN)
    new = lstate[:, cut] + jnp.sum(g * g, axis=0, keepdims=True) * (1.0 / depth)
    return left[:, cut] - g * (rate * lax.rsqrt(new))


def ahead_rows(rows):
    return rows // 8 * 3


def first_along_rel():
    return lax.axis_index("rel") < lax.axis_size("rel") // 2


def ahead_left(parity, left, lstate, to_src, oh_src, probe, weights, count_l, rel):
    depth, rows = left.shape

    def body(left, lstate, to_src, oh_src, probe, weights, count_l, _rel, result, _rel_out):
        @pl.when(first_along_rel())
        def _():
            for i in range(ahead_rows(rows) // 256):
                cut = slice(i * 256, (i + 1) * 256)
                result[:, cut] = left_rows(cut, left, lstate, to_src, oh_src, probe, weights, count_l)

    return call(
        only_on(parity, body), "ahead_left", [left, lstate, to_src, oh_src, probe, weights, count_l, rel],
        [shape(depth, ahead_rows(rows)), shape(*rel.shape)], aliases={7: 1},
    )


def late_slabs(parity, at, left, lstate, to_src, oh_src, probe, weights, count_l, ahead,
               piece, state, rgrad, to_dst, oh_dst, keep_left, keep_right):
    depth, rows = left.shape

    def body(left, lstate, to_src, oh_src, probe, weights, count_l, ahead, piece, state, rgrad, to_dst, oh_dst,
             _keep_left, _keep_right, left_out, right_out, result, spare, sems):
        def made_ahead():
            return pltpu.make_async_copy(ahead, left_out.at[:, 0 : ahead_rows(rows)], sems.at[0, 0])

        def runs(start, stop):
            out = []
            while start < stop:
                size = 512 if start % 512 == 0 and start + 512 < rows and start + 512 <= stop else 256
                out.append(slice(start, start + size))
                start += size
            return out

        def copy(cut):
            return pltpu.make_async_copy(result.at[:, cut], left_out.at[:, cut], sems.at[0, cut.start // 256])

        def make(cut):
            result[:, cut] = left_rows(cut, left, lstate, to_src, oh_src, probe, weights, count_l)
            copy(cut).start()

        first, others = runs(0, ahead_rows(rows)), runs(ahead_rows(rows), rows)

        @pl.when(first_along_rel())
        def _():
            made_ahead().start()

        @pl.when(jnp.logical_not(first_along_rel()))
        def _():
            for cut in first:
                make(cut)

        wait = update_and_send([piece], state, [rgrad], to_dst, oh_dst, spare, right_out, sems.at[1], fixed=True, start=at)
        for cut in others:
            make(cut)
        wait()

        @pl.when(first_along_rel())
        def _():
            made_ahead().wait()

        @pl.when(jnp.logical_not(first_along_rel()))
        def _():
            for cut in first:
                copy(cut).wait()

        for cut in others:
            copy(cut).wait()

    operands = [left, lstate, to_src, oh_src, probe, weights, count_l, ahead, piece, state, rgrad, to_dst, oh_dst, keep_left, keep_right]
    return call(
        only_on(parity, body), "late_slabs", operands, [shape(depth, rows), shape(depth, rows)], in_large=(13, 14), out_large=(0, 1),
        scratch_shapes=[*scratch([shape(depth, rows), shape(1, rows)]), pltpu.SemaphoreType.DMA((2, rows // 256))],
        aliases={13: 0, 14: 1},
    )


def relation_update(relations, relation_state, rels):
    kinds, depth = relations.shape

    def body(relations, relation_state, *rest):
        grad = sum(ref[...] for ref in rest[:-1])
        first = lax.broadcasted_iota(jnp.int32, (kinds, kinds), 0)
        second = lax.broadcasted_iota(jnp.int32, (kinds, kinds), 1)
        old = jnp.sum(jnp.where(first == second, relation_state[...], 0.0), axis=1, keepdims=True)
        new = old + jnp.sum(grad * grad, axis=1, keepdims=True) * (1.0 / depth)
        rest[-1][...] = relations[...] - grad * (rate * lax.rsqrt(new))

    return call(body, "relation_update", [relations, relation_state, *rels], [shape(kinds, depth)])[0]


def local(
    left_slab, left_state, right_slab, right_state, relations, relation_state,
    src_index, dst_index, relation_id, neg_source, neg_target,
):
    peers = lax.axis_size("blk")
    inside = [(i, i + 1) for i in range(0, peers, 2)]
    across = [(i, (i + 1) % peers) for i in range(1, peers, 2)]
    back = [(i + 1, i) for i in range(0, peers, 2)]
    swap = inside + back
    skip = [(i, (i + 2) % peers) for i in range(0, peers, 2)]
    index = (src_index, dst_index, relation_id, neg_source, neg_target)
    left = left_slab.T
    right = right_slab.T
    rows = left.shape[1]
    lstate = left_state.reshape(1, rows)
    number = float(neg_source.shape[1])
    right_far = lax.ppermute(right, "blk", across)
    right_near = [lax.ppermute(right[:, at : at + size], "blk", inside) for at, size in pieces_of(rows, NEAR_FIRST)]
    state_near = lax.ppermute(right_state, "blk", swap)
    state_far = lax.ppermute(state_near, "blk", skip).reshape(1, rows)
    state_near = state_near.reshape(1, rows)
    rel = jnp.zeros(relations.shape, F32)
    ready = prepared(0, left, relations, index)
    left_a, lstate, far, rel, state = trained(1, "first_near", number, False, FAR, left, lstate, right_near, state_near, rel, ready)
    far = [lax.ppermute(piece, "blk", across) for piece in far]
    state = lax.ppermute(lax.ppermute(state, "blk", back), "blk", skip)
    left_a, lstate, near, rel, _ = trained(
        0, "first_far", number, True, NEAR, left, lstate, [right_far], state_far, rel, ready, (left_a,), True, (state,)
    )
    near = [lax.ppermute(piece, "blk", inside) for piece in near]
    ready = prepared(1, left_a, relations, index)
    first_lstate = lstate
    left_b, lstate, right_b, rel, _ = trained(1, "last_near", number, False, (), left_a, lstate, near, state_near, rel, ready)
    cuts = pieces_of(rows, FAR)
    right_b, = right_b
    held = ()
    order = lstate
    for i, (at, size) in enumerate(cuts[:-1]):
        target, gq, rgrad = last_piece(0, "last_piece%d" % i, number, at, far[i], ready, order, held)
        held = (target, gq)
        to_dst, target_rows = early_edges(0, "early_edges%d" % i, number, 1, at, at + size, target, ready, dst_index)
        right_b, order = early_right(0, "early_right%d" % i, at, far[i], state, rgrad, to_dst, ready[6], right_b, order)
    at = cuts[-1][0]
    rgrad, to_src, to_dst, rel, probe, weights = late_edges(0, number, 1, at, far[-1], ready, dst_index, target_rows, gq, rel, order)
    ahead, rel = ahead_left(0, left_a, first_lstate, to_src, ready[5], probe, weights, ready[7], rel)
    if lax.axis_size("rel") == 2:
        rels = [rel, lax.ppermute(rel, "rel", [(0, 1), (1, 0)])]
    else:
        rels = [lax.psum(rel, "rel")]
    left_b, right_b = late_slabs(
        0, at, left_a, first_lstate, to_src, ready[5], probe, weights, ready[7], ahead,
        far[-1], state, rgrad, to_dst, ready[6], left_b, right_b,
    )
    relations_out = relation_update(relations, relation_state.reshape(1, -1), rels)
    return (left_b.T, right_b.T, relations_out[None])


def solution(mesh):
    in_specs = (
        P(("blk", "rel"), None),
        P(("blk", "rel")),
        P(("blk", "rel"), None),
        P(("blk", "rel")),
        P(),
        P(),
        P(None, ("blk", "rel")),
        P(None, ("blk", "rel")),
        P(None, ("blk", "rel")),
        P(None, ("blk", "rel")),
        P(None, ("blk", "rel")),
    )
    out_specs = (P(("blk", "rel"), None), P(("blk", "rel"), None), P("blk", None, None))
    return jax.shard_map(local, mesh=mesh, in_specs=in_specs, out_specs=out_specs, check_vma=False)
```

```python
import functools

import jax
import jax.numpy as jnp
from jax import lax
from jax.experimental import pallas as pl
from jax.experimental.pallas import tpu as pltpu
from jax.sharding import PartitionSpec as P

rate = 0.1
F32 = jnp.float32
BF16 = jnp.bfloat16
LANES = 128
NEAR = (4, 4)
STATE = 0
NEAR_FIRST = (4, 4)
FAR = (5, 2, 1)
VMEM_LIMIT = 30 * 2**20

NN = (((1,), (0,)), ((), ()))
NT = (((1,), (1,)), ((), ()))
TN = (((0,), (0,)), ((), ()))


def mul(a, b, dims):
    return lax.dot_general(a, b, dims, preferred_element_type=F32)


def split(x, parts):
    out = []
    for _ in range(parts):
        part = x.astype(BF16)
        out.append(part)
        x = x - part.astype(F32)
    return out


def mul_parts(parts, table, dims):
    along = dims[0][1][0]
    return mul(jnp.concatenate(parts, axis=1), jnp.concatenate([table] * len(parts), axis=along), dims)


def lanes_at(i, size, start=0):
    if isinstance(i, int):
        return slice(start + i * size, start + (i + 1) * size)
    return pl.ds(pl.multiple_of(start + i * size, LANES), size)


def step_of(rows, most=512):
    return next(size for size in (2048, 1024, 512, 256) if size <= most and rows % size == 0)


def each(count, body, fixed=False):
    if fixed:
        for i in range(count):
            body(i)
        return

    def one(i, carry):
        body(i)
        return carry

    lax.fori_loop(0, count, one, 0)


def row_onehot(idx, table):
    count, rows = table.shape
    col = jnp.broadcast_to(idx, (LANES, count)).T
    lane = lax.broadcasted_iota(jnp.int32, (count, LANES), 1)

    def tile(t):
        hit = col == lane + t * LANES
        table[:, lanes_at(t, LANES)] = jnp.where(hit, 1.0, 0.0).astype(BF16)

    each(rows // LANES, tile)


def row_counts(idx, rows):
    count = idx.shape[1]
    high = lax.broadcasted_iota(jnp.int32, (rows // LANES, count), 0)
    low = lax.broadcasted_iota(jnp.int32, (LANES, count), 0)
    high_hit = jnp.where(idx // LANES == high, 1.0, 0.0).astype(BF16)
    low_hit = jnp.where(idx % LANES == low, 1.0, 0.0).astype(BF16)
    return mul(high_hit, low_hit, NT)


def times_at(counts, i, size, start=0):
    first = (start + i * size) // LANES
    return jnp.concatenate([counts[pl.ds(first + t, 1), :] for t in range(size // LANES)], axis=1)


def half_rows(x):
    return (0.5 * x).T.astype(BF16)


def half_product(a, b):
    return (0.5 * (a * b).astype(BF16).astype(F32)).astype(BF16)


def negative_weights(rows16, query_rows, number):
    half = 0.5 / number
    return (jnp.tanh(mul(query_rows, rows16, NN)) * half + half).astype(BF16)


def often(weight, times):
    return (weight.astype(F32) * times).astype(BF16)


def negatives(rows16, query, query_rows, times, number):
    weight = negative_weights(rows16, query_rows, number)
    return mul(query, weight, NN) * times, mul(rows16, often(weight, times), NT)


def late_last(bound, src, dst, rid):
    edges = dst.shape[1]
    first = lax.broadcasted_iota(jnp.int32, (edges, edges), 0)
    second = lax.broadcasted_iota(jnp.int32, (edges, edges), 1)
    late = jnp.where(dst >= bound, 1.0, 0.0)
    ahead = jnp.where(first < second, 1.0, 0.0).astype(BF16)
    before = mul(jnp.broadcast_to(late, (8, edges)).astype(BF16), ahead, NN)[0:1, :]
    total = jnp.sum(late, axis=1, keepdims=True)
    lane = lax.broadcasted_iota(jnp.int32, (1, edges), 1).astype(F32)
    place = jnp.where(dst >= bound, edges - total + before, lane - before)
    order = jnp.where(place == first.astype(F32), 1.0, 0.0).astype(BF16)
    row = lax.broadcasted_iota(jnp.int32, (8, edges), 0)
    packed = jnp.zeros((8, edges), jnp.int32)
    for k, part in enumerate((src // 64, src % 64, dst // 64, dst % 64, rid)):
        packed = jnp.where(row == k, part, packed)
    moved = (mul(packed.astype(F32).astype(BF16), order, NT) + 0.5).astype(jnp.int32)
    return moved[0:1] * 64 + moved[1:2], moved[2:3] * 64 + moved[3:4], moved[4:5]


def prepare(step, bound, left, relations, src, dst, rid, nsrc, ndst,
            weight, source, query, query_rows, left16, oh_src, oh_dst, count_l, count_r, kind, weight_rows, targets):
    rows = left.shape[1]
    here = slice(step, step + 1)
    sources, aims, relation = src[here, :], dst[here, :], rid[here, :]
    if bound is not None:
        sources, aims, relation = late_last(bound, sources, aims, relation)
    targets[...] = aims
    row_onehot(sources, oh_src)
    row_onehot(aims, oh_dst)
    count_l[...] = row_counts(nsrc[here, :], rows)
    count_r[...] = row_counts(ndst[here, :], rows)
    kinds = lax.broadcasted_iota(jnp.int32, kind.shape, 0)
    kind[...] = jnp.where(relation == kinds, 1.0, 0.0).astype(BF16)
    weight[...] = sum(mul(part, kind[...], TN) for part in split(relations[...], 3))
    weight_rows[...] = weight[...].T
    source[...] = jnp.zeros_like(source)

    size = step_of(rows)

    def part(i):
        cut = lanes_at(i, size)
        parts = split(left[:, cut], 3)
        left16[:, cut] = parts[0]
        source[...] += mul_parts(parts, oh_src[:, cut], NT)

    each(rows // size, part)
    product = source[...] * weight[...]
    query[...] = product.astype(BF16)
    query_rows[...] = half_rows(product.astype(BF16).astype(F32))


def take_piece(number, start, piece, query, query_rows, oh_dst, count_r, target, gq, rgrad, fixed=False):
    depth = target.shape[0]
    if start == 0:
        target[...] = jnp.zeros_like(target)
        gq[...] = jnp.zeros_like(gq)

    size = step_of(piece.shape[1], 256)

    def part(i):
        cut = lanes_at(i, size)
        parts = split(piece[0:depth, cut], 3)
        hits = oh_dst[:, lanes_at(i, size, start)]
        target[...] += mul_parts(parts, hits, NT)
        times = times_at(count_r, i, size, start)
        rgrad[:, cut], more = negatives(parts[0], query[...], query_rows[...], times, number)
        gq[...] += more

    each(piece.shape[1] // size, part, fixed)


def join(number, weight, source, target, gq, left16, count_l, kind, rel_in,
         probe, probe_rows, gp, lgrad, to_src, to_dst, rel_out, fixed=False, most=512):
    rows = left16.shape[1]
    product = weight[...] * target[...]
    probe[...] = product.astype(BF16)
    probe_rows[...] = half_rows(product.astype(BF16).astype(F32))
    gp[...] = jnp.zeros_like(gp)

    size = step_of(rows, most)

    def part(i):
        cut = lanes_at(i, size)
        lgrad[:, cut], more = negatives(left16[:, cut], probe[...], probe_rows[...], times_at(count_l, i, size), number)
        gp[...] += more

    each(rows // size, part, fixed)
    depth = weight.shape[0]
    w, s, t = weight[...], source[...], target[...]
    coef = -jax.nn.sigmoid(-jnp.sum(s * w * t, axis=0, keepdims=True))
    to_src[0:depth, :], to_src[depth:, :] = split(coef * w * t + gq[...] * w, 2)
    to_dst[0:depth, :], to_dst[depth:, :] = split(coef * w * s + gp[...] * w, 2)
    g_weight = coef * s * t + gq[...] * s + gp[...] * t
    rel_out[...] = rel_in[...] + sum(mul(kind[...], p, NT) for p in split(g_weight, 2))


def adagrad(slab, state, grad, edges, table, start, out, new_state, send=None, fixed=False, more=None):
    depth = grad.shape[0]
    size = step_of(grad.shape[1])

    def part(i):
        cut = lanes_at(i, size)
        hits = table[:, lanes_at(i, size, start)]
        g = grad[:, cut] + mul_parts([edges[0:depth, :], edges[depth:, :]], hits, NN)
        if more is not None:
            g = g + more(i, size)
        new = state[:, cut] + jnp.sum(g * g, axis=0, keepdims=True) * (1.0 / depth)
        new_state[:, cut] = new
        out[0:depth, cut] = slab[0:depth, cut] - g * (rate * lax.rsqrt(new))
        if send is not None:
            send(i).start()

    each(grad.shape[1] // size, part, fixed)


def sender(result, to, start, sems):
    size = step_of(result.shape[1])

    def copy(i):
        here = lanes_at(i, size)
        there = lanes_at(i, size, start)
        return pltpu.make_async_copy(result.at[:, here], to.at[:, there], sems.at[i + start // 256])

    return copy


def update_and_send(pieces, state, grads, edges, table, new_state, to, sems, fixed=False, start=0, more=None):
    sent = []
    for piece, grad in zip(pieces, grads):
        rows = grad.shape[1]
        copy = sender(grad, to, start, sems)
        cut = slice(start, start + rows)
        adagrad(piece, state.at[:, cut], grad, edges, table, start, grad, new_state.at[:, cut], copy, fixed, more)
        sent.append((copy, rows // step_of(rows)))
        start += rows

    def wait():
        for copy, count in sent:
            each(count, lambda i, copy=copy: copy(i).wait(), fixed)

    return wait


def pack_state(state, piece, depth):
    size = state.shape[1] // 8
    for k in range(8):
        piece[depth + k : depth + k + 1, 0:size] = state[:, k * size : (k + 1) * size]


def unpack_state(piece, depth, state):
    size = state.shape[1] // 8
    for k in range(8):
        state[:, k * size : (k + 1) * size] = piece[depth + k : depth + k + 1, 0:size]


def on_parity(parity):
    return pl.when(lax.axis_index("blk") % 2 == parity)


def pieces_of(rows, eighths):
    sizes = [rows // 8 * n for n in eighths]
    return [(sum(sizes[:i]), size) for i, size in enumerate(sizes)]


def rows_of(pieces, at, size):
    found = []
    start = 0
    for piece in pieces:
        begin, end = max(at, start), min(at + size, start + piece.shape[1])
        if begin < end:
            found.append((piece.at[:, begin - start : end - start], begin, end - begin))
        start += piece.shape[1]
    return found


def train(parity, number, last, fixed, kept, takes, gives, packs, *refs):
    refs = list(refs)
    (left, lstate, rstate_in, rel_in) = refs[:4]
    (weight, source, query, query_rows, left16, oh_src, oh_dst, count_l, count_r, kind, _rows, _targets) = refs[4:16]
    right = refs[16 : 16 + takes]
    refs = refs[16 + takes + kept :]
    left_out, lstate_out, rel_out = refs[:3]
    right_out = refs[3 : 3 + len(gives)]
    state_out = refs[3 + len(gives)]
    (target, gq, rgrad, probe, probe_rows, gp, lgrad, to_src, to_dst, rstate, spare, sems) = refs[4 + len(gives) :]
    depth, rows = left.shape
    lstate_out[...] = lstate[...]
    rel_out[...] = rel_in[...]

    @on_parity(parity)
    def _():
        grads = []
        at = 0
        for piece in right:
            grads.append(rgrad.at[:, at : at + piece.shape[1]])
            take_piece(number, at, piece, query, query_rows, oh_dst, count_r, target, gq, grads[-1], fixed)
            at += piece.shape[1]
        join(number, weight, source, target, gq, left16, count_l, kind, rel_in,
             probe, probe_rows, gp, lgrad, to_src, to_dst, rel_out, fixed, 2048 if fixed else 1024 if last else 512)
        if last:
            unpack_state(right[STATE], depth, rstate)
            wait_right = update_and_send(right, rstate, grads, to_dst, oh_dst, spare, right_out[0], sems.at[0], fixed)
            wait_left = update_and_send([left], lstate, [lgrad], to_src, oh_src, spare, left_out, sems.at[1], fixed)
            wait_right()
            wait_left()
        else:
            for (at, size), out in zip(pieces_of(rows, gives), right_out):
                for old, begin, length in rows_of(right, at, size):
                    cut = slice(begin, begin + length)
                    here = slice(begin - at, begin - at + length)
                    adagrad(old, rstate_in.at[:, cut], rgrad.at[:, cut], to_dst, oh_dst, begin, out.at[:, here], spare.at[:, cut])
            if packs:
                pack_state(spare, right_out[STATE], depth)
            else:
                state_out[...] = spare[...]
            adagrad(left, lstate, lgrad, to_src, oh_src, 0, left_out, lstate_out)


def shape(*dims, dtype=F32):
    return jax.ShapeDtypeStruct(dims, dtype)


def prepared_shapes(depth, rows, edges, kinds):
    return (
        shape(depth, edges), shape(depth, edges), shape(depth, edges, dtype=BF16), shape(edges, depth, dtype=BF16),
        shape(depth, rows, dtype=BF16), shape(edges, rows, dtype=BF16), shape(edges, rows, dtype=BF16),
        shape(rows // LANES, LANES), shape(rows // LANES, LANES), shape(kinds, edges, dtype=BF16), shape(edges, depth),
        shape(1, edges, dtype=jnp.int32),
    )


def scratch(shapes):
    return [pltpu.VMEM(s.shape, s.dtype) for s in shapes]


def call(kernel, name, operands, shapes, in_large=(), out_large=(), scratch_shapes=(), aliases=None):
    vmem = pl.BlockSpec(memory_space=pltpu.VMEM)
    large = pl.BlockSpec(memory_space=pl.ANY)
    return pl.pallas_call(
        kernel,
        out_shape=tuple(shapes),
        in_specs=[large if i in in_large else vmem for i in range(len(operands))],
        out_specs=tuple(large if i in out_large else vmem for i in range(len(shapes))),
        scratch_shapes=list(scratch_shapes),
        input_output_aliases=aliases or {},
        compiler_params=pltpu.CompilerParams(vmem_limit_bytes=VMEM_LIMIT),
        cost_estimate=pl.CostEstimate(flops=1_000_000, bytes_accessed=100_000, transcendentals=0),
        name=name,
    )(*operands)


def prepared(step, bound, left, relations, index):
    depth, rows = left.shape
    return call(
        functools.partial(prepare, step, bound), "prepare%d" % step, [left, relations, *index],
        prepared_shapes(depth, rows, index[0].shape[1], relations.shape[0]),
    )


def trained(parity, name, number, fixed, gives, left, lstate, right, rstate, rel, ready, keep=(), packs=False, after=()):
    depth, rows = left.shape
    edges = ready[0].shape[1]
    last = not gives
    blocks = [shape(depth, size) for _at, size in pieces_of(rows, gives or (8,))]
    if packs:
        blocks[STATE] = shape(depth + 8, blocks[STATE].shape[1])
    edge = shape(depth, edges)
    edge16 = shape(depth, edges, dtype=BF16)
    pair16 = shape(2 * depth, edges, dtype=BF16)
    slab = shape(depth, rows)
    inner = [edge, edge, slab, edge16, shape(edges, depth, dtype=BF16), edge, slab, pair16, pair16, shape(1, rows), shape(1, rows)]
    left_out, lstate_out, rel_out, *right_out, state_out = call(
        functools.partial(train, parity, number, last, fixed, len(keep) + len(after), len(right), gives or (8,), packs),
        name,
        [left, lstate, rstate, rel, *ready, *right, *keep, *after],
        [slab, shape(1, rows), shape(*rel.shape), *blocks, shape(1, rows)],
        out_large=(0, 3) if last else (),
        scratch_shapes=[*scratch(inner), pltpu.SemaphoreType.DMA((2, rows // 256))],
        aliases={16 + len(right) + i: 0 for i in range(len(keep))},
    )
    return left_out, lstate_out, right_out, rel_out, state_out


def only_on(parity, body):
    def kernel(*refs):
        @on_parity(parity)
        def _():
            body(*refs)

    return kernel


def last_piece(parity, name, number, at, piece, ready, after, held=()):
    (_weight, _source, query, query_rows, _left16, _oh_src, oh_dst, _count_l, count_r, _kind, _rows, _targets) = ready
    depth, edges = query.shape

    def body(piece, query, query_rows, oh_dst, count_r, *rest):
        take_piece(number, at, piece, query, query_rows, oh_dst, count_r, *rest[len(held) + 1 :], fixed=True)

    operands = [piece, query, query_rows, oh_dst, count_r, *held, after]
    return call(
        only_on(parity, body), name, operands,
        [shape(depth, edges), shape(depth, edges), shape(depth, piece.shape[1])],
        aliases={5: 0, 6: 1} if held else {},
    )


def source_scores(number, edges, probe_rows, left16, count_l, gp, weights):
    rows16 = left16[...]
    part = negative_weights(rows16, probe_rows[edges, :], number)
    weights[edges, :] = part
    gp[:, edges] = mul(rows16, often(part, times_at(count_l, 0, rows16.shape[1])), NT)


def early_edges(parity, name, number, low, high, target, ready):
    (weight, source, _query, _query_rows, left16, _oh_src, _oh_dst, count_l, _count_r, _kind, weight_rows, targets) = ready
    depth, rows = left16.shape
    edges = weight.shape[1]

    def body(weight, source, target, left16, count_l, weight_rows, targets, to_dst, target_rows, weights, gp, probe_rows):
        w, s, t = weight[...], source[...], target[...]
        target_rows[...] = t.T
        probe_rows[...] = half_product(weight_rows[...], target_rows[...])
        source_scores(number, slice(0, edges), probe_rows, left16, count_l, gp, weights)
        at = targets[...]
        here = jnp.logical_and(at >= low, at < high)
        coef = -jax.nn.sigmoid(-jnp.sum(s * w * t, axis=0, keepdims=True))
        to_dst[0:depth, :], to_dst[depth:, :] = split(jnp.where(here, coef * w * s + gp[...] * w, 0.0), 2)

    return call(
        only_on(parity, body), name, [weight, source, target, left16, count_l, weight_rows, targets],
        [shape(2 * depth, edges, dtype=BF16), shape(edges, depth), shape(edges, rows, dtype=BF16), shape(depth, edges)],
        scratch_shapes=scratch([shape(edges, depth, dtype=BF16)]),
    )


def early_right(parity, name, at, piece, state, rgrad, to_dst, oh_dst, keep, order):
    depth, rows = keep.shape

    def body(piece, state, rgrad, to_dst, oh_dst, _order, _keep, out, _order_out, spare, sems):
        update_and_send([piece], state, [rgrad], to_dst, oh_dst, spare, out, sems, fixed=True, start=at)()

    return call(
        only_on(parity, body), name, [piece, state, rgrad, to_dst, oh_dst, order, keep], [shape(depth, rows), shape(*order.shape)],
        in_large=(6,), out_large=(0,),
        scratch_shapes=[*scratch([shape(1, rows)]), pltpu.SemaphoreType.DMA((rows // 256,))],
        aliases={5: 1, 6: 0},
    )


def late_edges(parity, number, at, piece, ready, target_rows, weights, gp, gq, rel, after):
    (weight, source, query, query_rows, left16, _oh_src, oh_dst, count_l, count_r, kind, weight_rows, targets) = ready
    depth, rows = left16.shape
    edges = weight.shape[1]
    half = edges // 2
    pair16 = shape(2 * depth, edges, dtype=BF16)

    def body(piece, weight, source, query, query_rows, left16, oh_dst, count_l, count_r, kind, weight_rows, targets,
             held_rows, _weights, _gp, held_q, rel_in, _after,
             weights, gp, rel_out, rgrad, to_src, to_dst, probe, t_rows, probe_rows):
        size = piece.shape[1]
        parts = split(piece[...], 3)
        hits = oh_dst[:, at : at + size]
        t_rows[...] = held_rows[...] + mul(
            jnp.concatenate([hits] * 3, axis=1), jnp.concatenate(parts, axis=1), NT
        )

        def scores(some):
            probe_rows[some, :] = half_product(weight_rows[some, :], t_rows[some, :])
            source_scores(number, some, probe_rows, left16, count_l, gp, weights)

        scores(slice(half, edges))

        @pl.when(jnp.max(targets[:, 0:half]) >= at)
        def _():
            scores(slice(0, half))

        w, s = weight[...], source[...]
        t = t_rows[...].T
        probe[...] = (w * t).astype(BF16)
        rgrad[...], more = negatives(parts[0], query[...], query_rows[...], times_at(count_r, 0, size, at), number)
        q = held_q[...] + more
        p = gp[...]
        coef = -jax.nn.sigmoid(-jnp.sum(s * w * t, axis=0, keepdims=True))
        g_weight = coef * s * t + q * s + p * t
        rel_out[...] = rel_in[...] + sum(mul(kind[...], part, NT) for part in split(g_weight, 2))
        to_src[0:depth, :], to_src[depth:, :] = split(coef * w * t + q * w, 2)
        here = targets[...] >= at
        to_dst[0:depth, :], to_dst[depth:, :] = split(jnp.where(here, coef * w * s + p * w, 0.0), 2)

    return call(
        only_on(parity, body), "late_edges",
        [piece, weight, source, query, query_rows, left16, oh_dst, count_l, count_r, kind, weight_rows, targets,
         target_rows, weights, gp, gq, rel, after],
        [shape(edges, rows, dtype=BF16), shape(depth, edges), shape(*rel.shape),
         shape(depth, piece.shape[1]), pair16, pair16, shape(depth, edges, dtype=BF16)],
        scratch_shapes=scratch([shape(edges, depth), shape(edges, depth, dtype=BF16)]),
        aliases={13: 0, 14: 1, 16: 2},
    )


def left_rows(cut, left, lstate, to_src, oh_src, probe, weights, count_l):
    depth = left.shape[0]
    size = cut.stop - cut.start
    g = mul(probe[...], weights[:, cut], NN) * times_at(count_l, 0, size, cut.start)
    g = g + mul_parts([to_src[0:depth, :], to_src[depth:, :]], oh_src[:, cut], NN)
    new = lstate[:, cut] + jnp.sum(g * g, axis=0, keepdims=True) * (1.0 / depth)
    return left[:, cut] - g * (rate * lax.rsqrt(new))


def ahead_rows(rows):
    return rows // 8 * 3


def first_along_rel():
    return lax.axis_index("rel") < lax.axis_size("rel") // 2


def ahead_left(parity, left, lstate, to_src, oh_src, probe, weights, count_l, rel):
    depth, rows = left.shape

    def body(left, lstate, to_src, oh_src, probe, weights, count_l, _rel, result, _rel_out):
        @pl.when(first_along_rel())
        def _():
            for i in range(ahead_rows(rows) // 256):
                cut = slice(i * 256, (i + 1) * 256)
                result[:, cut] = left_rows(cut, left, lstate, to_src, oh_src, probe, weights, count_l)

    return call(
        only_on(parity, body), "ahead_left", [left, lstate, to_src, oh_src, probe, weights, count_l, rel],
        [shape(depth, ahead_rows(rows)), shape(*rel.shape)], aliases={7: 1},
    )


def late_slabs(parity, at, left, lstate, to_src, oh_src, probe, weights, count_l, ahead,
               piece, state, rgrad, to_dst, oh_dst, keep_left, keep_right):
    depth, rows = left.shape

    def body(left, lstate, to_src, oh_src, probe, weights, count_l, ahead, piece, state, rgrad, to_dst, oh_dst,
             _keep_left, _keep_right, left_out, right_out, result, spare, sems):
        def made_ahead():
            return pltpu.make_async_copy(ahead, left_out.at[:, 0 : ahead_rows(rows)], sems.at[0, 0])

        def runs(start, stop):
            out = []
            while start < stop:
                size = 512 if start % 512 == 0 and start + 512 < rows and start + 512 <= stop else 256
                out.append(slice(start, start + size))
                start += size
            return out

        def copy(cut):
            return pltpu.make_async_copy(result.at[:, cut], left_out.at[:, cut], sems.at[0, cut.start // 256])

        def make(cut):
            result[:, cut] = left_rows(cut, left, lstate, to_src, oh_src, probe, weights, count_l)
            copy(cut).start()

        first, others = runs(0, ahead_rows(rows)), runs(ahead_rows(rows), rows)

        @pl.when(first_along_rel())
        def _():
            made_ahead().start()

        @pl.when(jnp.logical_not(first_along_rel()))
        def _():
            for cut in first:
                make(cut)

        wait = update_and_send([piece], state, [rgrad], to_dst, oh_dst, spare, right_out, sems.at[1], fixed=True, start=at)
        for cut in others:
            make(cut)
        wait()

        @pl.when(first_along_rel())
        def _():
            made_ahead().wait()

        @pl.when(jnp.logical_not(first_along_rel()))
        def _():
            for cut in first:
                copy(cut).wait()

        for cut in others:
            copy(cut).wait()

    operands = [left, lstate, to_src, oh_src, probe, weights, count_l, ahead, piece, state, rgrad, to_dst, oh_dst, keep_left, keep_right]
    return call(
        only_on(parity, body), "late_slabs", operands, [shape(depth, rows), shape(depth, rows)], in_large=(13, 14), out_large=(0, 1),
        scratch_shapes=[*scratch([shape(depth, rows), shape(1, rows)]), pltpu.SemaphoreType.DMA((2, rows // 256))],
        aliases={13: 0, 14: 1},
    )


def relation_update(relations, relation_state, rels):
    kinds, depth = relations.shape

    def body(relations, relation_state, *rest):
        grad = sum(ref[...] for ref in rest[:-1])
        first = lax.broadcasted_iota(jnp.int32, (kinds, kinds), 0)
        second = lax.broadcasted_iota(jnp.int32, (kinds, kinds), 1)
        old = jnp.sum(jnp.where(first == second, relation_state[...], 0.0), axis=1, keepdims=True)
        new = old + jnp.sum(grad * grad, axis=1, keepdims=True) * (1.0 / depth)
        rest[-1][...] = relations[...] - grad * (rate * lax.rsqrt(new))

    return call(body, "relation_update", [relations, relation_state, *rels], [shape(kinds, depth)])[0]


def local(
    left_slab, left_state, right_slab, right_state, relations, relation_state,
    src_index, dst_index, relation_id, neg_source, neg_target,
):
    peers = lax.axis_size("blk")
    inside = [(i, i + 1) for i in range(0, peers, 2)]
    across = [(i, (i + 1) % peers) for i in range(1, peers, 2)]
    back = [(i + 1, i) for i in range(0, peers, 2)]
    swap = inside + back
    skip = [(i, (i + 2) % peers) for i in range(0, peers, 2)]
    index = (src_index, dst_index, relation_id, neg_source, neg_target)
    left = left_slab.T
    right = right_slab.T
    rows = left.shape[1]
    lstate = left_state.reshape(1, rows)
    number = float(neg_source.shape[1])
    right_far = lax.ppermute(right, "blk", across)
    right_near = [lax.ppermute(right[:, at : at + size], "blk", inside) for at, size in pieces_of(rows, NEAR_FIRST)]
    state_near = lax.ppermute(right_state, "blk", swap)
    state_far = lax.ppermute(state_near, "blk", skip).reshape(1, rows)
    state_near = state_near.reshape(1, rows)
    rel = jnp.zeros(relations.shape, F32)
    ready = prepared(0, None, left, relations, index)
    left_a, lstate, far, rel, state = trained(1, "first_near", number, False, FAR, left, lstate, right_near, state_near, rel, ready)
    far = [lax.ppermute(piece, "blk", across) for piece in far]
    state = lax.ppermute(lax.ppermute(state, "blk", back), "blk", skip)
    left_a, lstate, near, rel, _ = trained(
        0, "first_far", number, True, NEAR, left, lstate, [right_far], state_far, rel, ready, (left_a,), True, (state,)
    )
    near = [lax.ppermute(piece, "blk", inside) for piece in near]
    cuts = pieces_of(rows, FAR)
    ready = prepared(1, cuts[-1][0], left_a, relations, index)
    first_lstate = lstate
    left_b, lstate, right_b, rel, _ = trained(1, "last_near", number, False, (), left_a, lstate, near, state_near, rel, ready)
    right_b, = right_b
    held = ()
    order = lstate
    for i, (at, size) in enumerate(cuts[:-1]):
        target, gq, rgrad = last_piece(0, "last_piece%d" % i, number, at, far[i], ready, order, held)
        held = (target, gq)
        to_dst, target_rows, weights, gp = early_edges(0, "early_edges%d" % i, number, at, at + size, target, ready)
        right_b, order = early_right(0, "early_right%d" % i, at, far[i], state, rgrad, to_dst, ready[6], right_b, order)
    at = cuts[-1][0]
    weights, gp, rel, rgrad, to_src, to_dst, probe = late_edges(
        0, number, at, far[-1], ready, target_rows, weights, gp, gq, rel, order
    )
    ahead, rel = ahead_left(0, left_a, first_lstate, to_src, ready[5], probe, weights, ready[7], rel)
    if lax.axis_size("rel") == 2:
        rels = [rel, lax.ppermute(rel, "rel", [(0, 1), (1, 0)])]
    else:
        rels = [lax.psum(rel, "rel")]
    left_b, right_b = late_slabs(
        0, at, left_a, first_lstate, to_src, ready[5], probe, weights, ready[7], ahead,
        far[-1], state, rgrad, to_dst, ready[6], left_b, right_b,
    )
    relations_out = relation_update(relations, relation_state.reshape(1, -1), rels)
    return (left_b.T, right_b.T, relations_out[None])


def solution(mesh):
    in_specs = (
        P(("blk", "rel"), None),
        P(("blk", "rel")),
        P(("blk", "rel"), None),
        P(("blk", "rel")),
        P(),
        P(),
        P(None, ("blk", "rel")),
        P(None, ("blk", "rel")),
        P(None, ("blk", "rel")),
        P(None, ("blk", "rel")),
        P(None, ("blk", "rel")),
    )
    out_specs = (P(("blk", "rel"), None), P(("blk", "rel"), None), P("blk", None, None))
    return jax.shard_map(local, mesh=mesh, in_specs=in_specs, out_specs=out_specs, check_vma=False)
```

```python
import functools

import jax
import jax.numpy as jnp
from jax import lax
from jax.experimental import pallas as pl
from jax.experimental.pallas import tpu as pltpu
from jax.sharding import PartitionSpec as P

rate = 0.1
F32 = jnp.float32
BF16 = jnp.bfloat16
LANES = 128
NEAR = (4, 4)
STATE = 0
NEAR_FIRST = (4, 4)
FAR = (5, 2, 1)
VMEM_LIMIT = 30 * 2**20

NN = (((1,), (0,)), ((), ()))
NT = (((1,), (1,)), ((), ()))
TN = (((0,), (0,)), ((), ()))


def mul(a, b, dims):
    return lax.dot_general(a, b, dims, preferred_element_type=F32)


def split(x, parts):
    out = []
    for _ in range(parts):
        part = x.astype(BF16)
        out.append(part)
        x = x - part.astype(F32)
    return out


def mul_parts(parts, table, dims):
    along = dims[0][1][0]
    return mul(jnp.concatenate(parts, axis=1), jnp.concatenate([table] * len(parts), axis=along), dims)


def lanes_at(i, size, start=0):
    if isinstance(i, int):
        return slice(start + i * size, start + (i + 1) * size)
    return pl.ds(pl.multiple_of(start + i * size, LANES), size)


def step_of(rows, most=512):
    return next(size for size in (2048, 1024, 512, 256) if size <= most and rows % size == 0)


def each(count, body, fixed=False):
    if fixed:
        for i in range(count):
            body(i)
        return

    def one(i, carry):
        body(i)
        return carry

    lax.fori_loop(0, count, one, 0)


def row_onehot(idx, table):
    count, rows = table.shape
    col = jnp.broadcast_to(idx, (LANES, count)).T
    lane = lax.broadcasted_iota(jnp.int32, (count, LANES), 1)

    def tile(t):
        hit = col == lane + t * LANES
        table[:, lanes_at(t, LANES)] = jnp.where(hit, 1.0, 0.0).astype(BF16)

    each(rows // LANES, tile)


def row_counts(idx, rows):
    count = idx.shape[1]
    high = lax.broadcasted_iota(jnp.int32, (rows // LANES, count), 0)
    low = lax.broadcasted_iota(jnp.int32, (LANES, count), 0)
    high_hit = jnp.where(idx // LANES == high, 1.0, 0.0).astype(BF16)
    low_hit = jnp.where(idx % LANES == low, 1.0, 0.0).astype(BF16)
    return mul(high_hit, low_hit, NT)


def times_at(counts, i, size, start=0):
    first = (start + i * size) // LANES
    return jnp.concatenate([counts[pl.ds(first + t, 1), :] for t in range(size // LANES)], axis=1)


def half_rows(x):
    return (0.5 * x).T.astype(BF16)


def half_product(a, b):
    return (0.5 * (a * b).astype(BF16).astype(F32)).astype(BF16)


def negative_weights(rows16, query_rows, number):
    half = 0.5 / number
    return (jnp.tanh(mul(query_rows, rows16, NN)) * half + half).astype(BF16)


def often(weight, times):
    return (weight.astype(F32) * times).astype(BF16)


def negatives(rows16, query, query_rows, times, number):
    weight = negative_weights(rows16, query_rows, number)
    return mul(query, weight, NN) * times, mul(rows16, often(weight, times), NT)


def prepare(step, left, relations, src, dst, rid, nsrc, ndst,
            weight, source, query, query_rows, left16, oh_src, oh_dst, count_l, count_r, kind, weight_rows):
    rows = left.shape[1]
    here = slice(step, step + 1)
    row_onehot(src[here, :], oh_src)
    row_onehot(dst[here, :], oh_dst)
    count_l[...] = row_counts(nsrc[here, :], rows)
    count_r[...] = row_counts(ndst[here, :], rows)
    kinds = lax.broadcasted_iota(jnp.int32, kind.shape, 0)
    kind[...] = jnp.where(rid[here, :] == kinds, 1.0, 0.0).astype(BF16)
    weight[...] = sum(mul(part, kind[...], TN) for part in split(relations[...], 3))
    weight_rows[...] = weight[...].T
    source[...] = jnp.zeros_like(source)

    size = step_of(rows)

    def part(i):
        cut = lanes_at(i, size)
        parts = split(left[:, cut], 3)
        left16[:, cut] = parts[0]
        source[...] += mul_parts(parts, oh_src[:, cut], NT)

    each(rows // size, part)
    product = source[...] * weight[...]
    query[...] = product.astype(BF16)
    query_rows[...] = half_rows(product.astype(BF16).astype(F32))


def take_piece(number, start, piece, query, query_rows, oh_dst, count_r, target, gq, rgrad, fixed=False):
    depth = target.shape[0]
    if start == 0:
        target[...] = jnp.zeros_like(target)
        gq[...] = jnp.zeros_like(gq)

    size = step_of(piece.shape[1], 256 if fixed else 512)

    def part(i):
        cut = lanes_at(i, size)
        parts = split(piece[0:depth, cut], 3)
        hits = oh_dst[:, lanes_at(i, size, start)]
        target[...] += mul_parts(parts, hits, NT)
        times = times_at(count_r, i, size, start)
        rgrad[:, cut], more = negatives(parts[0], query[...], query_rows[...], times, number)
        gq[...] += more

    each(piece.shape[1] // size, part, fixed)


def join(number, weight, source, target, gq, left16, count_l, kind, rel_in,
         probe, probe_rows, gp, lgrad, to_src, to_dst, rel_out, fixed=False):
    rows = left16.shape[1]
    product = weight[...] * target[...]
    probe[...] = product.astype(BF16)
    probe_rows[...] = half_rows(product.astype(BF16).astype(F32))
    gp[...] = jnp.zeros_like(gp)

    size = step_of(rows)

    def part(i):
        cut = lanes_at(i, size)
        lgrad[:, cut], more = negatives(left16[:, cut], probe[...], probe_rows[...], times_at(count_l, i, size), number)
        gp[...] += more

    each(rows // size, part, fixed)
    depth = weight.shape[0]
    w, s, t = weight[...], source[...], target[...]
    coef = -jax.nn.sigmoid(-jnp.sum(s * w * t, axis=0, keepdims=True))
    to_src[0:depth, :], to_src[depth:, :] = split(coef * w * t + gq[...] * w, 2)
    to_dst[0:depth, :], to_dst[depth:, :] = split(coef * w * s + gp[...] * w, 2)
    g_weight = coef * s * t + gq[...] * s + gp[...] * t
    rel_out[...] = rel_in[...] + sum(mul(kind[...], p, NT) for p in split(g_weight, 2))


def adagrad(slab, state, grad, edges, table, start, out, new_state, send=None, fixed=False, more=None):
    depth = grad.shape[0]
    size = step_of(grad.shape[1])

    def part(i):
        cut = lanes_at(i, size)
        hits = table[:, lanes_at(i, size, start)]
        g = grad[:, cut] + mul_parts([edges[0:depth, :], edges[depth:, :]], hits, NN)
        if more is not None:
            g = g + more(i, size)
        new = state[:, cut] + jnp.sum(g * g, axis=0, keepdims=True) * (1.0 / depth)
        new_state[:, cut] = new
        out[0:depth, cut] = slab[0:depth, cut] - g * (rate * lax.rsqrt(new))
        if send is not None:
            send(i).start()

    each(grad.shape[1] // size, part, fixed)


def sender(result, to, start, sems):
    size = step_of(result.shape[1])

    def copy(i):
        here = lanes_at(i, size)
        there = lanes_at(i, size, start)
        return pltpu.make_async_copy(result.at[:, here], to.at[:, there], sems.at[i + start // 256])

    return copy


def update_and_send(pieces, state, grads, edges, table, new_state, to, sems, fixed=False, start=0, more=None):
    sent = []
    for piece, grad in zip(pieces, grads):
        rows = grad.shape[1]
        copy = sender(grad, to, start, sems)
        cut = slice(start, start + rows)
        adagrad(piece, state.at[:, cut], grad, edges, table, start, grad, new_state.at[:, cut], copy, fixed, more)
        sent.append((copy, rows // step_of(rows)))
        start += rows

    def wait():
        for copy, count in sent:
            each(count, lambda i, copy=copy: copy(i).wait(), fixed)

    return wait


def pack_state(state, piece, depth):
    size = state.shape[1] // 8
    for k in range(8):
        piece[depth + k : depth + k + 1, 0:size] = state[:, k * size : (k + 1) * size]


def unpack_state(piece, depth, state):
    size = state.shape[1] // 8
    for k in range(8):
        state[:, k * size : (k + 1) * size] = piece[depth + k : depth + k + 1, 0:size]


def on_parity(parity):
    return pl.when(lax.axis_index("blk") % 2 == parity)


def pieces_of(rows, eighths):
    sizes = [rows // 8 * n for n in eighths]
    return [(sum(sizes[:i]), size) for i, size in enumerate(sizes)]


def rows_of(pieces, at, size):
    found = []
    start = 0
    for piece in pieces:
        begin, end = max(at, start), min(at + size, start + piece.shape[1])
        if begin < end:
            found.append((piece.at[:, begin - start : end - start], begin, end - begin))
        start += piece.shape[1]
    return found


def train(parity, number, last, fixed, kept, takes, gives, packs, *refs):
    refs = list(refs)
    (left, lstate, rstate_in, rel_in) = refs[:4]
    (weight, source, query, query_rows, left16, oh_src, oh_dst, count_l, count_r, kind, _rows) = refs[4:15]
    right = refs[15 : 15 + takes]
    refs = refs[15 + takes + kept :]
    left_out, lstate_out, rel_out = refs[:3]
    right_out = refs[3 : 3 + len(gives)]
    state_out = refs[3 + len(gives)]
    (target, gq, rgrad, probe, probe_rows, gp, lgrad, to_src, to_dst, rstate, spare, sems) = refs[4 + len(gives) :]
    depth, rows = left.shape
    lstate_out[...] = lstate[...]
    rel_out[...] = rel_in[...]

    @on_parity(parity)
    def _():
        grads = []
        at = 0
        for piece in right:
            grads.append(rgrad.at[:, at : at + piece.shape[1]])
            take_piece(number, at, piece, query, query_rows, oh_dst, count_r, target, gq, grads[-1], fixed)
            at += piece.shape[1]
        join(number, weight, source, target, gq, left16, count_l, kind, rel_in,
             probe, probe_rows, gp, lgrad, to_src, to_dst, rel_out, fixed)
        if last:
            unpack_state(right[STATE], depth, rstate)
            wait_right = update_and_send(right, rstate, grads, to_dst, oh_dst, spare, right_out[0], sems.at[0], fixed)
            wait_left = update_and_send([left], lstate, [lgrad], to_src, oh_src, spare, left_out, sems.at[1], fixed)
            wait_right()
            wait_left()
        else:
            for (at, size), out in zip(pieces_of(rows, gives), right_out):
                for old, begin, length in rows_of(right, at, size):
                    cut = slice(begin, begin + length)
                    here = slice(begin - at, begin - at + length)
                    adagrad(old, rstate_in.at[:, cut], rgrad.at[:, cut], to_dst, oh_dst, begin, out.at[:, here], spare.at[:, cut])
            if packs:
                pack_state(spare, right_out[STATE], depth)
            else:
                state_out[...] = spare[...]
            adagrad(left, lstate, lgrad, to_src, oh_src, 0, left_out, lstate_out)


def shape(*dims, dtype=F32):
    return jax.ShapeDtypeStruct(dims, dtype)


def prepared_shapes(depth, rows, edges, kinds):
    return (
        shape(depth, edges), shape(depth, edges), shape(depth, edges, dtype=BF16), shape(edges, depth, dtype=BF16),
        shape(depth, rows, dtype=BF16), shape(edges, rows, dtype=BF16), shape(edges, rows, dtype=BF16),
        shape(rows // LANES, LANES), shape(rows // LANES, LANES), shape(kinds, edges, dtype=BF16), shape(edges, depth),
    )


def scratch(shapes):
    return [pltpu.VMEM(s.shape, s.dtype) for s in shapes]


def call(kernel, name, operands, shapes, in_large=(), out_large=(), scratch_shapes=(), aliases=None):
    vmem = pl.BlockSpec(memory_space=pltpu.VMEM)
    large = pl.BlockSpec(memory_space=pl.ANY)
    return pl.pallas_call(
        kernel,
        out_shape=tuple(shapes),
        in_specs=[large if i in in_large else vmem for i in range(len(operands))],
        out_specs=tuple(large if i in out_large else vmem for i in range(len(shapes))),
        scratch_shapes=list(scratch_shapes),
        input_output_aliases=aliases or {},
        compiler_params=pltpu.CompilerParams(vmem_limit_bytes=VMEM_LIMIT),
        cost_estimate=pl.CostEstimate(flops=1_000_000, bytes_accessed=100_000, transcendentals=0),
        name=name,
    )(*operands)


def prepared(step, left, relations, index):
    depth, rows = left.shape
    return call(
        functools.partial(prepare, step), "prepare%d" % step, [left, relations, *index],
        prepared_shapes(depth, rows, index[0].shape[1], relations.shape[0]),
    )


def trained(parity, name, number, fixed, gives, left, lstate, right, rstate, rel, ready, keep=(), packs=False, after=()):
    depth, rows = left.shape
    edges = ready[0].shape[1]
    last = not gives
    blocks = [shape(depth, size) for _at, size in pieces_of(rows, gives or (8,))]
    if packs:
        blocks[STATE] = shape(depth + 8, blocks[STATE].shape[1])
    edge = shape(depth, edges)
    edge16 = shape(depth, edges, dtype=BF16)
    pair16 = shape(2 * depth, edges, dtype=BF16)
    slab = shape(depth, rows)
    inner = [edge, edge, slab, edge16, shape(edges, depth, dtype=BF16), edge, slab, pair16, pair16, shape(1, rows), shape(1, rows)]
    left_out, lstate_out, rel_out, *right_out, state_out = call(
        functools.partial(train, parity, number, last, fixed, len(keep) + len(after), len(right), gives or (8,), packs),
        name,
        [left, lstate, rstate, rel, *ready, *right, *keep, *after],
        [slab, shape(1, rows), shape(*rel.shape), *blocks, shape(1, rows)],
        out_large=(0, 3) if last else (),
        scratch_shapes=[*scratch(inner), pltpu.SemaphoreType.DMA((2, rows // 256))],
        aliases={15 + len(right) + i: 0 for i in range(len(keep))},
    )
    return left_out, lstate_out, right_out, rel_out, state_out


def only_on(parity, body):
    def kernel(*refs):
        @on_parity(parity)
        def _():
            body(*refs)

    return kernel


def last_piece(parity, name, number, at, piece, ready, after, held=()):
    (_weight, _source, query, query_rows, _left16, _oh_src, oh_dst, _count_l, count_r, _kind, _rows) = ready
    depth, edges = query.shape

    def body(piece, query, query_rows, oh_dst, count_r, *rest):
        take_piece(number, at, piece, query, query_rows, oh_dst, count_r, *rest[len(held) + 1 :], fixed=True)

    operands = [piece, query, query_rows, oh_dst, count_r, *held, after]
    return call(
        only_on(parity, body), name, operands,
        [shape(depth, edges), shape(depth, edges), shape(depth, piece.shape[1])],
        aliases={5: 0, 6: 1} if held else {},
    )


def source_scores(number, probe_rows, left16, count_l, gp, weights=None):
    rows = left16.shape[1]
    size = step_of(rows, 2048)
    total = None
    for i in range(rows // size):
        cut = lanes_at(i, size)
        rows16 = left16[:, cut]
        part = negative_weights(rows16, probe_rows[...], number)
        if weights is not None:
            weights[:, cut] = part
        more = mul(rows16, often(part, times_at(count_l, i, size)), NT)
        total = more if total is None else total + more
    gp[...] = total


def early_edges(parity, name, number, step, low, high, target, ready, dst):
    (weight, source, _query, _query_rows, left16, _oh_src, _oh_dst, count_l, _count_r, _kind, weight_rows) = ready
    depth = left16.shape[0]
    edges = weight.shape[1]

    def body(weight, source, target, left16, count_l, dst, weight_rows, to_dst, target_rows, gp, probe_rows):
        w, s, t = weight[...], source[...], target[...]
        target_rows[...] = t.T
        probe_rows[...] = half_product(weight_rows[...], target_rows[...])
        source_scores(number, probe_rows, left16, count_l, gp)
        at = dst[step : step + 1, :]
        here = jnp.logical_and(at >= low, at < high)
        coef = -jax.nn.sigmoid(-jnp.sum(s * w * t, axis=0, keepdims=True))
        to_dst[0:depth, :], to_dst[depth:, :] = split(jnp.where(here, coef * w * s + gp[...] * w, 0.0), 2)

    return call(
        only_on(parity, body), name, [weight, source, target, left16, count_l, dst, weight_rows],
        [shape(2 * depth, edges, dtype=BF16), shape(edges, depth)],
        scratch_shapes=scratch([shape(depth, edges), shape(edges, depth, dtype=BF16)]),
    )


def early_right(parity, name, at, piece, state, rgrad, to_dst, oh_dst, keep, order):
    depth, rows = keep.shape

    def body(piece, state, rgrad, to_dst, oh_dst, _order, _keep, out, _order_out, spare, sems):
        update_and_send([piece], state, [rgrad], to_dst, oh_dst, spare, out, sems, fixed=True, start=at)()

    return call(
        only_on(parity, body), name, [piece, state, rgrad, to_dst, oh_dst, order, keep], [shape(depth, rows), shape(*order.shape)],
        in_large=(6,), out_large=(0,),
        scratch_shapes=[*scratch([shape(1, rows)]), pltpu.SemaphoreType.DMA((rows // 256,))],
        aliases={5: 1, 6: 0},
    )


def late_edges(parity, number, step, at, piece, ready, dst, target_rows, gq, rel, after):
    (weight, source, query, query_rows, left16, _oh_src, oh_dst, count_l, count_r, kind, weight_rows) = ready
    depth, rows = left16.shape
    edges = weight.shape[1]
    pair16 = shape(2 * depth, edges, dtype=BF16)

    def body(piece, weight, source, query, query_rows, left16, oh_dst, count_l, count_r, kind, dst, weight_rows,
             held_rows, held_q, rel_in, _after,
             rgrad, to_src, to_dst, rel_out, probe, weights, gp, probe_rows):
        size = piece.shape[1]
        parts = split(piece[...], 3)
        hits = oh_dst[:, at : at + size]
        slab = jnp.concatenate(parts, axis=1)
        table = jnp.concatenate([hits] * 3, axis=1)
        t_rows = held_rows[...] + mul(table, slab, NT)
        probe_rows[...] = half_product(weight_rows[...], t_rows)
        source_scores(number, probe_rows, left16, count_l, gp, weights)
        w, s = weight[...], source[...]
        t = t_rows.T
        probe[...] = (w * t).astype(BF16)
        rgrad[...], more = negatives(parts[0], query[...], query_rows[...], times_at(count_r, 0, size, at), number)
        q = held_q[...] + more
        p = gp[...]
        coef = -jax.nn.sigmoid(-jnp.sum(s * w * t, axis=0, keepdims=True))
        g_weight = coef * s * t + q * s + p * t
        rel_out[...] = rel_in[...] + sum(mul(kind[...], part, NT) for part in split(g_weight, 2))
        to_src[0:depth, :], to_src[depth:, :] = split(coef * w * t + q * w, 2)
        here = dst[step : step + 1, :] >= at
        to_dst[0:depth, :], to_dst[depth:, :] = split(jnp.where(here, coef * w * s + p * w, 0.0), 2)

    return call(
        only_on(parity, body), "late_edges",
        [piece, weight, source, query, query_rows, left16, oh_dst, count_l, count_r, kind, dst, weight_rows,
         target_rows, gq, rel, after],
        [shape(depth, piece.shape[1]), pair16, pair16, shape(*rel.shape), shape(depth, edges, dtype=BF16), shape(edges, rows, dtype=BF16)],
        scratch_shapes=scratch([shape(depth, edges), shape(edges, depth, dtype=BF16)]),
        aliases={14: 3},
    )


def left_rows(cut, left, lstate, to_src, oh_src, probe, weights, count_l):
    depth = left.shape[0]
    size = cut.stop - cut.start
    g = mul(probe[...], weights[:, cut], NN) * times_at(count_l, 0, size, cut.start)
    g = g + mul_parts([to_src[0:depth, :], to_src[depth:, :]], oh_src[:, cut], NN)
    new = lstate[:, cut] + jnp.sum(g * g, axis=0, keepdims=True) * (1.0 / depth)
    return left[:, cut] - g * (rate * lax.rsqrt(new))


def ahead_rows(rows):
    return rows // 8 * 3


def first_along_rel():
    return lax.axis_index("rel") < lax.axis_size("rel") // 2


def ahead_left(parity, left, lstate, to_src, oh_src, probe, weights, count_l, rel):
    depth, rows = left.shape

    def body(left, lstate, to_src, oh_src, probe, weights, count_l, _rel, result, _rel_out):
        @pl.when(first_along_rel())
        def _():
            result[...] = left_rows(slice(0, ahead_rows(rows)), left, lstate, to_src, oh_src, probe, weights, count_l)

    return call(
        only_on(parity, body), "ahead_left", [left, lstate, to_src, oh_src, probe, weights, count_l, rel],
        [shape(depth, ahead_rows(rows)), shape(*rel.shape)], aliases={7: 1},
    )


def late_slabs(parity, at, left, lstate, to_src, oh_src, probe, weights, count_l, ahead,
               piece, state, rgrad, to_dst, oh_dst, keep_left, keep_right):
    depth, rows = left.shape

    def body(left, lstate, to_src, oh_src, probe, weights, count_l, ahead, piece, state, rgrad, to_dst, oh_dst,
             _keep_left, _keep_right, left_out, right_out, result, spare, sems):
        def made_ahead():
            return pltpu.make_async_copy(ahead, left_out.at[:, 0 : ahead_rows(rows)], sems.at[0, 0])

        def copy(cut):
            return pltpu.make_async_copy(result.at[:, cut], left_out.at[:, cut], sems.at[0, cut.start // 256])

        def make(cut):
            result[:, cut] = left_rows(cut, left, lstate, to_src, oh_src, probe, weights, count_l)
            copy(cut).start()

        first = [slice(0, ahead_rows(rows))]
        others = [slice(ahead_rows(rows), rows - 256), slice(rows - 256, rows)]

        @pl.when(first_along_rel())
        def _():
            made_ahead().start()

        @pl.when(jnp.logical_not(first_along_rel()))
        def _():
            for cut in first:
                make(cut)

        wait = update_and_send([piece], state, [rgrad], to_dst, oh_dst, spare, right_out, sems.at[1], fixed=True, start=at)
        for cut in others:
            make(cut)
        wait()

        @pl.when(first_along_rel())
        def _():
            made_ahead().wait()

        @pl.when(jnp.logical_not(first_along_rel()))
        def _():
            for cut in first:
                copy(cut).wait()

        for cut in others:
            copy(cut).wait()

    operands = [left, lstate, to_src, oh_src, probe, weights, count_l, ahead, piece, state, rgrad, to_dst, oh_dst, keep_left, keep_right]
    return call(
        only_on(parity, body), "late_slabs", operands, [shape(depth, rows), shape(depth, rows)], in_large=(13, 14), out_large=(0, 1),
        scratch_shapes=[*scratch([shape(depth, rows), shape(1, rows)]), pltpu.SemaphoreType.DMA((2, rows // 256))],
        aliases={13: 0, 14: 1},
    )


def relation_update(relations, relation_state, rels):
    kinds, depth = relations.shape

    def body(relations, relation_state, *rest):
        grad = sum(ref[...] for ref in rest[:-1])
        first = lax.broadcasted_iota(jnp.int32, (kinds, kinds), 0)
        second = lax.broadcasted_iota(jnp.int32, (kinds, kinds), 1)
        old = jnp.sum(jnp.where(first == second, relation_state[...], 0.0), axis=1, keepdims=True)
        new = old + jnp.sum(grad * grad, axis=1, keepdims=True) * (1.0 / depth)
        rest[-1][...] = relations[...] - grad * (rate * lax.rsqrt(new))

    return call(body, "relation_update", [relations, relation_state, *rels], [shape(kinds, depth)])[0]


def local(
    left_slab, left_state, right_slab, right_state, relations, relation_state,
    src_index, dst_index, relation_id, neg_source, neg_target,
):
    peers = lax.axis_size("blk")
    inside = [(i, i + 1) for i in range(0, peers, 2)]
    across = [(i, (i + 1) % peers) for i in range(1, peers, 2)]
    back = [(i + 1, i) for i in range(0, peers, 2)]
    swap = inside + back
    skip = [(i, (i + 2) % peers) for i in range(0, peers, 2)]
    index = (src_index, dst_index, relation_id, neg_source, neg_target)
    left = left_slab.T
    right = right_slab.T
    rows = left.shape[1]
    lstate = left_state.reshape(1, rows)
    number = float(neg_source.shape[1])
    right_far = lax.ppermute(right, "blk", across)
    right_near = [lax.ppermute(right[:, at : at + size], "blk", inside) for at, size in pieces_of(rows, NEAR_FIRST)]
    state_near = lax.ppermute(right_state, "blk", swap)
    state_far = lax.ppermute(state_near, "blk", skip).reshape(1, rows)
    state_near = state_near.reshape(1, rows)
    rel = jnp.zeros(relations.shape, F32)
    ready = prepared(0, left, relations, index)
    left_a, lstate, far, rel, state = trained(1, "first_near", number, False, FAR, left, lstate, right_near, state_near, rel, ready)
    far = [lax.ppermute(piece, "blk", across) for piece in far]
    state = lax.ppermute(lax.ppermute(state, "blk", back), "blk", skip)
    left_a, lstate, near, rel, _ = trained(
        0, "first_far", number, True, NEAR, left, lstate, [right_far], state_far, rel, ready, (left_a,), True, (state,)
    )
    near = [lax.ppermute(piece, "blk", inside) for piece in near]
    ready = prepared(1, left_a, relations, index)
    first_lstate = lstate
    left_b, lstate, right_b, rel, _ = trained(1, "last_near", number, False, (), left_a, lstate, near, state_near, rel, ready)
    cuts = pieces_of(rows, FAR)
    right_b, = right_b
    held = ()
    order = lstate
    for i, (at, size) in enumerate(cuts[:-1]):
        target, gq, rgrad = last_piece(0, "last_piece%d" % i, number, at, far[i], ready, order, held)
        held = (target, gq)
        to_dst, target_rows = early_edges(0, "early_edges%d" % i, number, 1, at, at + size, target, ready, dst_index)
        right_b, order = early_right(0, "early_right%d" % i, at, far[i], state, rgrad, to_dst, ready[6], right_b, order)
    at = cuts[-1][0]
    rgrad, to_src, to_dst, rel, probe, weights = late_edges(0, number, 1, at, far[-1], ready, dst_index, target_rows, gq, rel, order)
    ahead, rel = ahead_left(0, left_a, first_lstate, to_src, ready[5], probe, weights, ready[7], rel)
    if lax.axis_size("rel") == 2:
        rels = [rel, lax.ppermute(rel, "rel", [(0, 1), (1, 0)])]
    else:
        rels = [lax.psum(rel, "rel")]
    left_b, right_b = late_slabs(
        0, at, left_a, first_lstate, to_src, ready[5], probe, weights, ready[7], ahead,
        far[-1], state, rgrad, to_dst, ready[6], left_b, right_b,
    )
    relations_out = relation_update(relations, relation_state.reshape(1, -1), rels)
    return (left_b.T, right_b.T, relations_out[None])


def solution(mesh):
    in_specs = (
        P(("blk", "rel"), None),
        P(("blk", "rel")),
        P(("blk", "rel"), None),
        P(("blk", "rel")),
        P(),
        P(),
        P(None, ("blk", "rel")),
        P(None, ("blk", "rel")),
        P(None, ("blk", "rel")),
        P(None, ("blk", "rel")),
        P(None, ("blk", "rel")),
    )
    out_specs = (P(("blk", "rel"), None), P(("blk", "rel"), None), P("blk", None, None))
    return jax.shard_map(local, mesh=mesh, in_specs=in_specs, out_specs=out_specs, check_vma=False)
```

```python
import functools

import jax
import jax.numpy as jnp
from jax import lax
from jax.experimental import pallas as pl
from jax.experimental.pallas import tpu as pltpu
from jax.sharding import PartitionSpec as P

rate = 0.1
F32 = jnp.float32
BF16 = jnp.bfloat16
LANES = 128
NEAR = (4, 4)
STATE = 0
NEAR_FIRST = (4, 4)
FAR = (5, 2, 1)
VMEM_LIMIT = 30 * 2**20

NN = (((1,), (0,)), ((), ()))
NT = (((1,), (1,)), ((), ()))
TN = (((0,), (0,)), ((), ()))


def mul(a, b, dims):
    return lax.dot_general(a, b, dims, preferred_element_type=F32)


def split(x, parts):
    out = []
    for _ in range(parts):
        part = x.astype(BF16)
        out.append(part)
        x = x - part.astype(F32)
    return out


def mul_parts(parts, table, dims):
    along = dims[0][1][0]
    return mul(jnp.concatenate(parts, axis=1), jnp.concatenate([table] * len(parts), axis=along), dims)


def lanes_at(i, size, start=0):
    if isinstance(i, int):
        return slice(start + i * size, start + (i + 1) * size)
    return pl.ds(pl.multiple_of(start + i * size, LANES), size)


def step_of(rows, most=512):
    return next(size for size in (2048, 1024, 512, 256) if size <= most and rows % size == 0)


def each(count, body, fixed=False):
    if fixed:
        for i in range(count):
            body(i)
        return

    def one(i, carry):
        body(i)
        return carry

    lax.fori_loop(0, count, one, 0)


def row_onehot(idx, table):
    count, rows = table.shape
    col = jnp.broadcast_to(idx, (LANES, count)).T
    lane = lax.broadcasted_iota(jnp.int32, (count, LANES), 1)

    def tile(t):
        hit = col == lane + t * LANES
        table[:, lanes_at(t, LANES)] = jnp.where(hit, 1.0, 0.0).astype(BF16)

    each(rows // LANES, tile)


def row_counts(idx, rows):
    count = idx.shape[1]
    high = lax.broadcasted_iota(jnp.int32, (rows // LANES, count), 0)
    low = lax.broadcasted_iota(jnp.int32, (LANES, count), 0)
    high_hit = jnp.where(idx // LANES == high, 1.0, 0.0).astype(BF16)
    low_hit = jnp.where(idx % LANES == low, 1.0, 0.0).astype(BF16)
    return mul(high_hit, low_hit, NT)


def times_at(counts, i, size, start=0):
    first = (start + i * size) // LANES
    return jnp.concatenate([counts[pl.ds(first + t, 1), :] for t in range(size // LANES)], axis=1)


def half_rows(x):
    return (0.5 * x).T.astype(BF16)


def half_product(a, b):
    return (0.5 * (a * b).astype(BF16).astype(F32)).astype(BF16)


def negative_weights(rows16, query_rows, number):
    half = 0.5 / number
    return (jnp.tanh(mul(query_rows, rows16, NN)) * half + half).astype(BF16)


def often(weight, times):
    return (weight.astype(F32) * times).astype(BF16)


def negatives(rows16, query, query_rows, times, number):
    weight = negative_weights(rows16, query_rows, number)
    return mul(query, weight, NN) * times, mul(rows16, often(weight, times), NT)


def prepare(step, left, relations, src, dst, rid, nsrc, ndst,
            weight, source, query, query_rows, left16, oh_src, oh_dst, count_l, count_r, kind, weight_rows):
    rows = left.shape[1]
    here = slice(step, step + 1)
    row_onehot(src[here, :], oh_src)
    row_onehot(dst[here, :], oh_dst)
    count_l[...] = row_counts(nsrc[here, :], rows)
    count_r[...] = row_counts(ndst[here, :], rows)
    kinds = lax.broadcasted_iota(jnp.int32, kind.shape, 0)
    kind[...] = jnp.where(rid[here, :] == kinds, 1.0, 0.0).astype(BF16)
    weight[...] = sum(mul(part, kind[...], TN) for part in split(relations[...], 3))
    weight_rows[...] = weight[...].T
    source[...] = jnp.zeros_like(source)

    size = step_of(rows)

    def part(i):
        cut = lanes_at(i, size)
        parts = split(left[:, cut], 3)
        left16[:, cut] = parts[0]
        source[...] += mul_parts(parts, oh_src[:, cut], NT)

    each(rows // size, part)
    product = source[...] * weight[...]
    query[...] = product.astype(BF16)
    query_rows[...] = half_rows(product.astype(BF16).astype(F32))


def take_piece(number, start, piece, query, query_rows, oh_dst, count_r, target, gq, rgrad, fixed=False):
    depth = target.shape[0]
    if start == 0:
        target[...] = jnp.zeros_like(target)
        gq[...] = jnp.zeros_like(gq)

    size = step_of(piece.shape[1], 256)

    def part(i):
        cut = lanes_at(i, size)
        parts = split(piece[0:depth, cut], 3)
        hits = oh_dst[:, lanes_at(i, size, start)]
        target[...] += mul_parts(parts, hits, NT)
        times = times_at(count_r, i, size, start)
        rgrad[:, cut], more = negatives(parts[0], query[...], query_rows[...], times, number)
        gq[...] += more

    each(piece.shape[1] // size, part, fixed)


def join(number, weight, source, target, gq, left16, count_l, kind, rel_in,
         probe, probe_rows, gp, lgrad, to_src, to_dst, rel_out, fixed=False, most=512):
    rows = left16.shape[1]
    product = weight[...] * target[...]
    probe[...] = product.astype(BF16)
    probe_rows[...] = half_rows(product.astype(BF16).astype(F32))
    gp[...] = jnp.zeros_like(gp)

    size = step_of(rows, most)

    def part(i):
        cut = lanes_at(i, size)
        lgrad[:, cut], more = negatives(left16[:, cut], probe[...], probe_rows[...], times_at(count_l, i, size), number)
        gp[...] += more

    each(rows // size, part, fixed)
    depth = weight.shape[0]
    w, s, t = weight[...], source[...], target[...]
    coef = -jax.nn.sigmoid(-jnp.sum(s * w * t, axis=0, keepdims=True))
    to_src[0:depth, :], to_src[depth:, :] = split(coef * w * t + gq[...] * w, 2)
    to_dst[0:depth, :], to_dst[depth:, :] = split(coef * w * s + gp[...] * w, 2)
    g_weight = coef * s * t + gq[...] * s + gp[...] * t
    rel_out[...] = rel_in[...] + sum(mul(kind[...], p, NT) for p in split(g_weight, 2))


def adagrad(slab, state, grad, edges, table, start, out, new_state, send=None, fixed=False, more=None):
    depth = grad.shape[0]
    size = step_of(grad.shape[1])

    def part(i):
        cut = lanes_at(i, size)
        hits = table[:, lanes_at(i, size, start)]
        g = grad[:, cut] + mul_parts([edges[0:depth, :], edges[depth:, :]], hits, NN)
        if more is not None:
            g = g + more(i, size)
        new = state[:, cut] + jnp.sum(g * g, axis=0, keepdims=True) * (1.0 / depth)
        new_state[:, cut] = new
        out[0:depth, cut] = slab[0:depth, cut] - g * (rate * lax.rsqrt(new))
        if send is not None:
            send(i).start()

    each(grad.shape[1] // size, part, fixed)


def sender(result, to, start, sems):
    size = step_of(result.shape[1])

    def copy(i):
        here = lanes_at(i, size)
        there = lanes_at(i, size, start)
        return pltpu.make_async_copy(result.at[:, here], to.at[:, there], sems.at[i + start // 256])

    return copy


def update_and_send(pieces, state, grads, edges, table, new_state, to, sems, fixed=False, start=0, more=None):
    sent = []
    for piece, grad in zip(pieces, grads):
        rows = grad.shape[1]
        copy = sender(grad, to, start, sems)
        cut = slice(start, start + rows)
        adagrad(piece, state.at[:, cut], grad, edges, table, start, grad, new_state.at[:, cut], copy, fixed, more)
        sent.append((copy, rows // step_of(rows)))
        start += rows

    def wait():
        for copy, count in sent:
            each(count, lambda i, copy=copy: copy(i).wait(), fixed)

    return wait


def pack_state(state, piece, depth):
    size = state.shape[1] // 8
    for k in range(8):
        piece[depth + k : depth + k + 1, 0:size] = state[:, k * size : (k + 1) * size]


def unpack_state(piece, depth, state):
    size = state.shape[1] // 8
    for k in range(8):
        state[:, k * size : (k + 1) * size] = piece[depth + k : depth + k + 1, 0:size]


def on_parity(parity):
    return pl.when(lax.axis_index("blk") % 2 == parity)


def pieces_of(rows, eighths):
    sizes = [rows // 8 * n for n in eighths]
    return [(sum(sizes[:i]), size) for i, size in enumerate(sizes)]


def rows_of(pieces, at, size):
    found = []
    start = 0
    for piece in pieces:
        begin, end = max(at, start), min(at + size, start + piece.shape[1])
        if begin < end:
            found.append((piece.at[:, begin - start : end - start], begin, end - begin))
        start += piece.shape[1]
    return found


def train(parity, number, last, fixed, kept, takes, gives, packs, *refs):
    refs = list(refs)
    (left, lstate, rstate_in, rel_in) = refs[:4]
    (weight, source, query, query_rows, left16, oh_src, oh_dst, count_l, count_r, kind, _rows) = refs[4:15]
    right = refs[15 : 15 + takes]
    refs = refs[15 + takes + kept :]
    left_out, lstate_out, rel_out = refs[:3]
    right_out = refs[3 : 3 + len(gives)]
    state_out = refs[3 + len(gives)]
    (target, gq, rgrad, probe, probe_rows, gp, lgrad, to_src, to_dst, rstate, spare, sems) = refs[4 + len(gives) :]
    depth, rows = left.shape
    lstate_out[...] = lstate[...]
    rel_out[...] = rel_in[...]

    @on_parity(parity)
    def _():
        grads = []
        at = 0
        for piece in right:
            grads.append(rgrad.at[:, at : at + piece.shape[1]])
            take_piece(number, at, piece, query, query_rows, oh_dst, count_r, target, gq, grads[-1], fixed)
            at += piece.shape[1]
        join(number, weight, source, target, gq, left16, count_l, kind, rel_in,
             probe, probe_rows, gp, lgrad, to_src, to_dst, rel_out, fixed, 1024 if last else 512)
        if last:
            unpack_state(right[STATE], depth, rstate)
            wait_right = update_and_send(right, rstate, grads, to_dst, oh_dst, spare, right_out[0], sems.at[0], fixed)
            wait_left = update_and_send([left], lstate, [lgrad], to_src, oh_src, spare, left_out, sems.at[1], fixed)
            wait_right()
            wait_left()
        else:
            for (at, size), out in zip(pieces_of(rows, gives), right_out):
                for old, begin, length in rows_of(right, at, size):
                    cut = slice(begin, begin + length)
                    here = slice(begin - at, begin - at + length)
                    adagrad(old, rstate_in.at[:, cut], rgrad.at[:, cut], to_dst, oh_dst, begin, out.at[:, here], spare.at[:, cut], None, fixed)
            if packs:
                pack_state(spare, right_out[STATE], depth)
            else:
                state_out[...] = spare[...]
            adagrad(left, lstate, lgrad, to_src, oh_src, 0, left_out, lstate_out, None, fixed)


def shape(*dims, dtype=F32):
    return jax.ShapeDtypeStruct(dims, dtype)


def prepared_shapes(depth, rows, edges, kinds):
    return (
        shape(depth, edges), shape(depth, edges), shape(depth, edges, dtype=BF16), shape(edges, depth, dtype=BF16),
        shape(depth, rows, dtype=BF16), shape(edges, rows, dtype=BF16), shape(edges, rows, dtype=BF16),
        shape(rows // LANES, LANES), shape(rows // LANES, LANES), shape(kinds, edges, dtype=BF16), shape(edges, depth),
    )


def scratch(shapes):
    return [pltpu.VMEM(s.shape, s.dtype) for s in shapes]


def call(kernel, name, operands, shapes, in_large=(), out_large=(), scratch_shapes=(), aliases=None):
    vmem = pl.BlockSpec(memory_space=pltpu.VMEM)
    large = pl.BlockSpec(memory_space=pl.ANY)
    return pl.pallas_call(
        kernel,
        out_shape=tuple(shapes),
        in_specs=[large if i in in_large else vmem for i in range(len(operands))],
        out_specs=tuple(large if i in out_large else vmem for i in range(len(shapes))),
        scratch_shapes=list(scratch_shapes),
        input_output_aliases=aliases or {},
        compiler_params=pltpu.CompilerParams(vmem_limit_bytes=VMEM_LIMIT),
        cost_estimate=pl.CostEstimate(flops=1_000_000, bytes_accessed=100_000, transcendentals=0),
        name=name,
    )(*operands)


def prepared(step, left, relations, index):
    depth, rows = left.shape
    return call(
        functools.partial(prepare, step), "prepare%d" % step, [left, relations, *index],
        prepared_shapes(depth, rows, index[0].shape[1], relations.shape[0]),
    )


def trained(parity, name, number, fixed, gives, left, lstate, right, rstate, rel, ready, keep=(), packs=False, after=()):
    depth, rows = left.shape
    edges = ready[0].shape[1]
    last = not gives
    blocks = [shape(depth, size) for _at, size in pieces_of(rows, gives or (8,))]
    if packs:
        blocks[STATE] = shape(depth + 8, blocks[STATE].shape[1])
    edge = shape(depth, edges)
    edge16 = shape(depth, edges, dtype=BF16)
    pair16 = shape(2 * depth, edges, dtype=BF16)
    slab = shape(depth, rows)
    inner = [edge, edge, slab, edge16, shape(edges, depth, dtype=BF16), edge, slab, pair16, pair16, shape(1, rows), shape(1, rows)]
    left_out, lstate_out, rel_out, *right_out, state_out = call(
        functools.partial(train, parity, number, last, fixed, len(keep) + len(after), len(right), gives or (8,), packs),
        name,
        [left, lstate, rstate, rel, *ready, *right, *keep, *after],
        [slab, shape(1, rows), shape(*rel.shape), *blocks, shape(1, rows)],
        out_large=(0, 3) if last else (),
        scratch_shapes=[*scratch(inner), pltpu.SemaphoreType.DMA((2, rows // 256))],
        aliases={15 + len(right) + i: 0 for i in range(len(keep))},
    )
    return left_out, lstate_out, right_out, rel_out, state_out


def only_on(parity, body):
    def kernel(*refs):
        @on_parity(parity)
        def _():
            body(*refs)

    return kernel


def last_piece(parity, name, number, at, piece, ready, after, held=()):
    (_weight, _source, query, query_rows, _left16, _oh_src, oh_dst, _count_l, count_r, _kind, _rows) = ready
    depth, edges = query.shape

    def body(piece, query, query_rows, oh_dst, count_r, *rest):
        take_piece(number, at, piece, query, query_rows, oh_dst, count_r, *rest[len(held) + 1 :], fixed=True)

    operands = [piece, query, query_rows, oh_dst, count_r, *held, after]
    return call(
        only_on(parity, body), name, operands,
        [shape(depth, edges), shape(depth, edges), shape(depth, piece.shape[1])],
        aliases={5: 0, 6: 1} if held else {},
    )


def source_scores(number, probe_rows, left16, count_l, gp, weights=None):
    rows = left16.shape[1]
    size = step_of(rows, 2048)
    total = None
    for i in range(rows // size):
        cut = lanes_at(i, size)
        rows16 = left16[:, cut]
        part = negative_weights(rows16, probe_rows[...], number)
        if weights is not None:
            weights[:, cut] = part
        more = mul(rows16, often(part, times_at(count_l, i, size)), NT)
        total = more if total is None else total + more
    gp[...] = total


def early_edges(parity, name, number, step, low, high, target, ready, dst):
    (weight, source, _query, _query_rows, left16, _oh_src, _oh_dst, count_l, _count_r, _kind, weight_rows) = ready
    depth = left16.shape[0]
    edges = weight.shape[1]

    def body(weight, source, target, left16, count_l, dst, weight_rows, to_dst, target_rows, gp, probe_rows):
        w, s, t = weight[...], source[...], target[...]
        target_rows[...] = t.T
        probe_rows[...] = half_product(weight_rows[...], target_rows[...])
        source_scores(number, probe_rows, left16, count_l, gp)
        at = dst[step : step + 1, :]
        here = jnp.logical_and(at >= low, at < high)
        coef = -jax.nn.sigmoid(-jnp.sum(s * w * t, axis=0, keepdims=True))
        to_dst[0:depth, :], to_dst[depth:, :] = split(jnp.where(here, coef * w * s + gp[...] * w, 0.0), 2)

    return call(
        only_on(parity, body), name, [weight, source, target, left16, count_l, dst, weight_rows],
        [shape(2 * depth, edges, dtype=BF16), shape(edges, depth)],
        scratch_shapes=scratch([shape(depth, edges), shape(edges, depth, dtype=BF16)]),
    )


def early_right(parity, name, at, piece, state, rgrad, to_dst, oh_dst, keep, order):
    depth, rows = keep.shape

    def body(piece, state, rgrad, to_dst, oh_dst, _order, _keep, out, _order_out, spare, sems):
        update_and_send([piece], state, [rgrad], to_dst, oh_dst, spare, out, sems, fixed=True, start=at)()

    return call(
        only_on(parity, body), name, [piece, state, rgrad, to_dst, oh_dst, order, keep], [shape(depth, rows), shape(*order.shape)],
        in_large=(6,), out_large=(0,),
        scratch_shapes=[*scratch([shape(1, rows)]), pltpu.SemaphoreType.DMA((rows // 256,))],
        aliases={5: 1, 6: 0},
    )


def late_edges(parity, number, step, at, piece, ready, dst, target_rows, gq, rel, after):
    (weight, source, query, query_rows, left16, _oh_src, oh_dst, count_l, count_r, kind, weight_rows) = ready
    depth, rows = left16.shape
    edges = weight.shape[1]
    pair16 = shape(2 * depth, edges, dtype=BF16)

    def body(piece, weight, source, query, query_rows, left16, oh_dst, count_l, count_r, kind, dst, weight_rows,
             held_rows, held_q, rel_in, _after,
             rgrad, to_src, to_dst, rel_out, probe, weights, gp, probe_rows):
        size = piece.shape[1]
        parts = split(piece[...], 3)
        hits = oh_dst[:, at : at + size]
        slab = jnp.concatenate(parts, axis=1)
        table = jnp.concatenate([hits] * 3, axis=1)
        t_rows = held_rows[...] + mul(table, slab, NT)
        probe_rows[...] = half_product(weight_rows[...], t_rows)
        source_scores(number, probe_rows, left16, count_l, gp, weights)
        w, s = weight[...], source[...]
        t = t_rows.T
        probe[...] = (w * t).astype(BF16)
        rgrad[...], more = negatives(parts[0], query[...], query_rows[...], times_at(count_r, 0, size, at), number)
        q = held_q[...] + more
        p = gp[...]
        coef = -jax.nn.sigmoid(-jnp.sum(s * w * t, axis=0, keepdims=True))
        g_weight = coef * s * t + q * s + p * t
        rel_out[...] = rel_in[...] + mul(
            jnp.concatenate([kind[...]] * 2, axis=1), jnp.concatenate(split(g_weight, 2), axis=1), NT
        )
        to_src[0:depth, :], to_src[depth:, :] = split(coef * w * t + q * w, 2)
        here = dst[step : step + 1, :] >= at
        to_dst[0:depth, :], to_dst[depth:, :] = split(jnp.where(here, coef * w * s + p * w, 0.0), 2)

    return call(
        only_on(parity, body), "late_edges",
        [piece, weight, source, query, query_rows, left16, oh_dst, count_l, count_r, kind, dst, weight_rows,
         target_rows, gq, rel, after],
        [shape(depth, piece.shape[1]), pair16, pair16, shape(*rel.shape), shape(depth, edges, dtype=BF16), shape(edges, rows, dtype=BF16)],
        scratch_shapes=scratch([shape(depth, edges), shape(edges, depth, dtype=BF16)]),
        aliases={14: 3},
    )


def left_rows(cut, left, lstate, to_src, oh_src, probe, weights, count_l):
    depth = left.shape[0]
    size = cut.stop - cut.start
    g = mul(probe[...], weights[:, cut], NN) * times_at(count_l, 0, size, cut.start)
    g = g + mul_parts([to_src[0:depth, :], to_src[depth:, :]], oh_src[:, cut], NN)
    new = lstate[:, cut] + jnp.sum(g * g, axis=0, keepdims=True) * (1.0 / depth)
    return left[:, cut] - g * (rate * lax.rsqrt(new))


def ahead_rows(rows):
    return rows // 8 * 3


def first_along_rel():
    return lax.axis_index("rel") < lax.axis_size("rel") // 2


def ahead_left(parity, left, lstate, to_src, oh_src, probe, weights, count_l, rel):
    depth, rows = left.shape

    def body(left, lstate, to_src, oh_src, probe, weights, count_l, _rel, result, _rel_out):
        @pl.when(first_along_rel())
        def _():
            for i in range(ahead_rows(rows) // 256):
                cut = slice(i * 256, (i + 1) * 256)
                result[:, cut] = left_rows(cut, left, lstate, to_src, oh_src, probe, weights, count_l)

    return call(
        only_on(parity, body), "ahead_left", [left, lstate, to_src, oh_src, probe, weights, count_l, rel],
        [shape(depth, ahead_rows(rows)), shape(*rel.shape)], aliases={7: 1},
    )


def late_slabs(parity, at, left, lstate, to_src, oh_src, probe, weights, count_l, ahead,
               piece, state, rgrad, to_dst, oh_dst, keep_left, keep_right):
    depth, rows = left.shape

    def body(left, lstate, to_src, oh_src, probe, weights, count_l, ahead, piece, state, rgrad, to_dst, oh_dst,
             _keep_left, _keep_right, left_out, right_out, result, spare, sems):
        def made_ahead():
            return pltpu.make_async_copy(ahead, left_out.at[:, 0 : ahead_rows(rows)], sems.at[0, 0])

        def runs(start, stop):
            out = []
            while start < stop:
                size = 512 if start % 512 == 0 and start + 512 < rows and start + 512 <= stop else 256
                out.append(slice(start, start + size))
                start += size
            return out

        def copy(cut):
            return pltpu.make_async_copy(result.at[:, cut], left_out.at[:, cut], sems.at[0, cut.start // 256])

        def make(cut):
            result[:, cut] = left_rows(cut, left, lstate, to_src, oh_src, probe, weights, count_l)
            copy(cut).start()

        first, others = runs(0, ahead_rows(rows)), runs(ahead_rows(rows), rows)

        @pl.when(first_along_rel())
        def _():
            made_ahead().start()

        @pl.when(jnp.logical_not(first_along_rel()))
        def _():
            for cut in first:
                make(cut)

        wait = update_and_send([piece], state, [rgrad], to_dst, oh_dst, spare, right_out, sems.at[1], fixed=True, start=at)
        for cut in others:
            make(cut)
        wait()

        @pl.when(first_along_rel())
        def _():
            made_ahead().wait()

        @pl.when(jnp.logical_not(first_along_rel()))
        def _():
            for cut in first:
                copy(cut).wait()

        for cut in others:
            copy(cut).wait()

    operands = [left, lstate, to_src, oh_src, probe, weights, count_l, ahead, piece, state, rgrad, to_dst, oh_dst, keep_left, keep_right]
    return call(
        only_on(parity, body), "late_slabs", operands, [shape(depth, rows), shape(depth, rows)], in_large=(13, 14), out_large=(0, 1),
        scratch_shapes=[*scratch([shape(depth, rows), shape(1, rows)]), pltpu.SemaphoreType.DMA((2, rows // 256))],
        aliases={13: 0, 14: 1},
    )


def relation_update(relations, relation_state, rels):
    kinds, depth = relations.shape

    def body(relations, relation_state, *rest):
        grad = sum(ref[...] for ref in rest[:-1])
        first = lax.broadcasted_iota(jnp.int32, (kinds, kinds), 0)
        second = lax.broadcasted_iota(jnp.int32, (kinds, kinds), 1)
        old = jnp.sum(jnp.where(first == second, relation_state[...], 0.0), axis=1, keepdims=True)
        new = old + jnp.sum(grad * grad, axis=1, keepdims=True) * (1.0 / depth)
        rest[-1][...] = relations[...] - grad * (rate * lax.rsqrt(new))

    return call(body, "relation_update", [relations, relation_state, *rels], [shape(kinds, depth)])[0]


def local(
    left_slab, left_state, right_slab, right_state, relations, relation_state,
    src_index, dst_index, relation_id, neg_source, neg_target,
):
    peers = lax.axis_size("blk")
    inside = [(i, i + 1) for i in range(0, peers, 2)]
    across = [(i, (i + 1) % peers) for i in range(1, peers, 2)]
    back = [(i + 1, i) for i in range(0, peers, 2)]
    swap = inside + back
    skip = [(i, (i + 2) % peers) for i in range(0, peers, 2)]
    index = (src_index, dst_index, relation_id, neg_source, neg_target)
    left = left_slab.T
    right = right_slab.T
    rows = left.shape[1]
    lstate = left_state.reshape(1, rows)
    number = float(neg_source.shape[1])
    right_far = lax.ppermute(right, "blk", across)
    right_near = [lax.ppermute(right[:, at : at + size], "blk", inside) for at, size in pieces_of(rows, NEAR_FIRST)]
    state_near = lax.ppermute(right_state, "blk", swap)
    state_far = lax.ppermute(state_near, "blk", skip).reshape(1, rows)
    state_near = state_near.reshape(1, rows)
    rel = jnp.zeros(relations.shape, F32)
    ready = prepared(0, left, relations, index)
    left_a, lstate, far, rel, state = trained(1, "first_near", number, False, FAR, left, lstate, right_near, state_near, rel, ready)
    far = [lax.ppermute(piece, "blk", across) for piece in far]
    state = lax.ppermute(lax.ppermute(state, "blk", back), "blk", skip)
    left_a, lstate, near, rel, _ = trained(
        0, "first_far", number, True, NEAR, left, lstate, [right_far], state_far, rel, ready, (left_a,), True, (state,)
    )
    near = [lax.ppermute(piece, "blk", inside) for piece in near]
    ready = prepared(1, left_a, relations, index)
    first_lstate = lstate
    left_b, lstate, right_b, rel, _ = trained(1, "last_near", number, False, (), left_a, lstate, near, state_near, rel, ready)
    cuts = pieces_of(rows, FAR)
    right_b, = right_b
    held = ()
    order = lstate
    for i, (at, size) in enumerate(cuts[:-1]):
        target, gq, rgrad = last_piece(0, "last_piece%d" % i, number, at, far[i], ready, order, held)
        held = (target, gq)
        to_dst, target_rows = early_edges(0, "early_edges%d" % i, number, 1, at, at + size, target, ready, dst_index)
        right_b, order = early_right(0, "early_right%d" % i, at, far[i], state, rgrad, to_dst, ready[6], right_b, order)
    at = cuts[-1][0]
    rgrad, to_src, to_dst, rel, probe, weights = late_edges(0, number, 1, at, far[-1], ready, dst_index, target_rows, gq, rel, order)
    ahead, rel = ahead_left(0, left_a, first_lstate, to_src, ready[5], probe, weights, ready[7], rel)
    if lax.axis_size("rel") == 2:
        rels = [rel, lax.ppermute(rel, "rel", [(0, 1), (1, 0)])]
    else:
        rels = [lax.psum(rel, "rel")]
    left_b, right_b = late_slabs(
        0, at, left_a, first_lstate, to_src, ready[5], probe, weights, ready[7], ahead,
        far[-1], state, rgrad, to_dst, ready[6], left_b, right_b,
    )
    relations_out = relation_update(relations, relation_state.reshape(1, -1), rels)
    return (left_b.T, right_b.T, relations_out[None])


def solution(mesh):
    in_specs = (
        P(("blk", "rel"), None),
        P(("blk", "rel")),
        P(("blk", "rel"), None),
        P(("blk", "rel")),
        P(),
        P(),
        P(None, ("blk", "rel")),
        P(None, ("blk", "rel")),
        P(None, ("blk", "rel")),
        P(None, ("blk", "rel")),
        P(None, ("blk", "rel")),
    )
    out_specs = (P(("blk", "rel"), None), P(("blk", "rel"), None), P("blk", None, None))
    return jax.shard_map(local, mesh=mesh, in_specs=in_specs, out_specs=out_specs, check_vma=False)
```

```python
import functools

import jax
import jax.numpy as jnp
from jax import lax
from jax.experimental import pallas as pl
from jax.experimental.pallas import tpu as pltpu
from jax.sharding import PartitionSpec as P

rate = 0.1
F32 = jnp.float32
BF16 = jnp.bfloat16
LANES = 128
NEAR = (4, 4)
STATE = 0
NEAR_FIRST = (4, 4)
FAR = (5, 2, 1)
VMEM_LIMIT = 30 * 2**20

NN = (((1,), (0,)), ((), ()))
NT = (((1,), (1,)), ((), ()))
TN = (((0,), (0,)), ((), ()))


def mul(a, b, dims):
    return lax.dot_general(a, b, dims, preferred_element_type=F32)


def split(x, parts):
    out = []
    for _ in range(parts):
        part = x.astype(BF16)
        out.append(part)
        x = x - part.astype(F32)
    return out


def mul_parts(parts, table, dims):
    along = dims[0][1][0]
    return mul(jnp.concatenate(parts, axis=1), jnp.concatenate([table] * len(parts), axis=along), dims)


def lanes_at(i, size, start=0):
    if isinstance(i, int):
        return slice(start + i * size, start + (i + 1) * size)
    return pl.ds(pl.multiple_of(start + i * size, LANES), size)


def step_of(rows, most=512):
    return next(size for size in (2048, 1024, 512, 256) if size <= most and rows % size == 0)


def each(count, body, fixed=False):
    if fixed:
        for i in range(count):
            body(i)
        return

    def one(i, carry):
        body(i)
        return carry

    lax.fori_loop(0, count, one, 0)


def row_onehot(idx, table):
    count, rows = table.shape
    col = jnp.broadcast_to(idx, (LANES, count)).T
    lane = lax.broadcasted_iota(jnp.int32, (count, LANES), 1)

    def tile(t):
        hit = col == lane + t * LANES
        table[:, lanes_at(t, LANES)] = jnp.where(hit, 1.0, 0.0).astype(BF16)

    each(rows // LANES, tile)


def row_counts(idx, rows):
    count = idx.shape[1]
    high = lax.broadcasted_iota(jnp.int32, (rows // LANES, count), 0)
    low = lax.broadcasted_iota(jnp.int32, (LANES, count), 0)
    high_hit = jnp.where(idx // LANES == high, 1.0, 0.0).astype(BF16)
    low_hit = jnp.where(idx % LANES == low, 1.0, 0.0).astype(BF16)
    return mul(high_hit, low_hit, NT)


def times_at(counts, i, size, start=0):
    first = (start + i * size) // LANES
    return jnp.concatenate([counts[pl.ds(first + t, 1), :] for t in range(size // LANES)], axis=1)


def half_rows(x):
    return (0.5 * x).T.astype(BF16)


def half_product(a, b):
    return (0.5 * (a * b).astype(BF16).astype(F32)).astype(BF16)


def negative_weights(rows16, query_rows, number):
    half = 0.5 / number
    return (jnp.tanh(mul(query_rows, rows16, NN)) * half + half).astype(BF16)


def often(weight, times):
    return weight * times.astype(BF16)


def negatives(rows16, query, query_rows, times, number):
    weight = negative_weights(rows16, query_rows, number)
    return mul(query, weight, NN) * times, mul(rows16, often(weight, times), NT)


def prepare(step, left, relations, src, dst, rid, nsrc, ndst,
            weight, source, query, query_rows, left16, oh_src, oh_dst, count_l, count_r, kind, weight_rows):
    rows = left.shape[1]
    here = slice(step, step + 1)
    row_onehot(src[here, :], oh_src)
    row_onehot(dst[here, :], oh_dst)
    count_l[...] = row_counts(nsrc[here, :], rows)
    count_r[...] = row_counts(ndst[here, :], rows)
    kinds = lax.broadcasted_iota(jnp.int32, kind.shape, 0)
    kind[...] = jnp.where(rid[here, :] == kinds, 1.0, 0.0).astype(BF16)
    weight[...] = sum(mul(part, kind[...], TN) for part in split(relations[...], 3))
    weight_rows[...] = weight[...].T
    source[...] = jnp.zeros_like(source)

    size = step_of(rows)

    def part(i):
        cut = lanes_at(i, size)
        parts = split(left[:, cut], 3)
        left16[:, cut] = parts[0]
        source[...] += mul_parts(parts, oh_src[:, cut], NT)

    each(rows // size, part)
    product = source[...] * weight[...]
    query[...] = product.astype(BF16)
    query_rows[...] = half_rows(product.astype(BF16).astype(F32))


def take_piece(number, start, piece, query, query_rows, oh_dst, count_r, target, gq, rgrad, fixed=False):
    depth = target.shape[0]
    if start == 0:
        target[...] = jnp.zeros_like(target)
        gq[...] = jnp.zeros_like(gq)

    size = step_of(piece.shape[1], 256 if fixed else 512)

    def part(i):
        cut = lanes_at(i, size)
        parts = split(piece[0:depth, cut], 3)
        hits = oh_dst[:, lanes_at(i, size, start)]
        target[...] += mul_parts(parts, hits, NT)
        times = times_at(count_r, i, size, start)
        rgrad[:, cut], more = negatives(parts[0], query[...], query_rows[...], times, number)
        gq[...] += more

    each(piece.shape[1] // size, part, fixed)


def join(number, weight, source, target, gq, left16, count_l, kind, rel_in,
         probe, probe_rows, gp, lgrad, to_src, to_dst, rel_out, fixed=False):
    rows = left16.shape[1]
    product = weight[...] * target[...]
    probe[...] = product.astype(BF16)
    probe_rows[...] = half_rows(product.astype(BF16).astype(F32))
    gp[...] = jnp.zeros_like(gp)

    size = step_of(rows)

    def part(i):
        cut = lanes_at(i, size)
        lgrad[:, cut], more = negatives(left16[:, cut], probe[...], probe_rows[...], times_at(count_l, i, size), number)
        gp[...] += more

    each(rows // size, part, fixed)
    depth = weight.shape[0]
    w, s, t = weight[...], source[...], target[...]
    coef = -jax.nn.sigmoid(-jnp.sum(s * w * t, axis=0, keepdims=True))
    to_src[0:depth, :], to_src[depth:, :] = split(coef * w * t + gq[...] * w, 2)
    to_dst[0:depth, :], to_dst[depth:, :] = split(coef * w * s + gp[...] * w, 2)
    g_weight = coef * s * t + gq[...] * s + gp[...] * t
    rel_out[...] = rel_in[...] + sum(mul(kind[...], p, NT) for p in split(g_weight, 2))


def adagrad(slab, state, grad, edges, table, start, out, new_state, send=None, fixed=False, more=None):
    depth = grad.shape[0]
    size = step_of(grad.shape[1])

    def part(i):
        cut = lanes_at(i, size)
        hits = table[:, lanes_at(i, size, start)]
        g = grad[:, cut] + mul_parts([edges[0:depth, :], edges[depth:, :]], hits, NN)
        if more is not None:
            g = g + more(i, size)
        new = state[:, cut] + jnp.sum(g * g, axis=0, keepdims=True) * (1.0 / depth)
        new_state[:, cut] = new
        out[0:depth, cut] = slab[0:depth, cut] - g * (rate * lax.rsqrt(new))
        if send is not None:
            send(i).start()

    each(grad.shape[1] // size, part, fixed)


def sender(result, to, start, sems):
    size = step_of(result.shape[1])

    def copy(i):
        here = lanes_at(i, size)
        there = lanes_at(i, size, start)
        return pltpu.make_async_copy(result.at[:, here], to.at[:, there], sems.at[i + start // 256])

    return copy


def update_and_send(pieces, state, grads, edges, table, new_state, to, sems, fixed=False, start=0, more=None):
    sent = []
    for piece, grad in zip(pieces, grads):
        rows = grad.shape[1]
        copy = sender(grad, to, start, sems)
        cut = slice(start, start + rows)
        adagrad(piece, state.at[:, cut], grad, edges, table, start, grad, new_state.at[:, cut], copy, fixed, more)
        sent.append((copy, rows // step_of(rows)))
        start += rows

    def wait():
        for copy, count in sent:
            each(count, lambda i, copy=copy: copy(i).wait(), fixed)

    return wait


def pack_state(state, piece, depth):
    size = state.shape[1] // 8
    for k in range(8):
        piece[depth + k : depth + k + 1, 0:size] = state[:, k * size : (k + 1) * size]


def unpack_state(piece, depth, state):
    size = state.shape[1] // 8
    for k in range(8):
        state[:, k * size : (k + 1) * size] = piece[depth + k : depth + k + 1, 0:size]


def on_parity(parity):
    return pl.when(lax.axis_index("blk") % 2 == parity)


def pieces_of(rows, eighths):
    sizes = [rows // 8 * n for n in eighths]
    return [(sum(sizes[:i]), size) for i, size in enumerate(sizes)]


def rows_of(pieces, at, size):
    found = []
    start = 0
    for piece in pieces:
        begin, end = max(at, start), min(at + size, start + piece.shape[1])
        if begin < end:
            found.append((piece.at[:, begin - start : end - start], begin, end - begin))
        start += piece.shape[1]
    return found


def train(parity, number, last, fixed, kept, takes, gives, packs, *refs):
    refs = list(refs)
    (left, lstate, rstate_in, rel_in) = refs[:4]
    (weight, source, query, query_rows, left16, oh_src, oh_dst, count_l, count_r, kind, _rows) = refs[4:15]
    right = refs[15 : 15 + takes]
    refs = refs[15 + takes + kept :]
    left_out, lstate_out, rel_out = refs[:3]
    right_out = refs[3 : 3 + len(gives)]
    state_out = refs[3 + len(gives)]
    (target, gq, rgrad, probe, probe_rows, gp, lgrad, to_src, to_dst, rstate, spare, sems) = refs[4 + len(gives) :]
    depth, rows = left.shape
    lstate_out[...] = lstate[...]
    rel_out[...] = rel_in[...]

    @on_parity(parity)
    def _():
        grads = []
        at = 0
        for piece in right:
            grads.append(rgrad.at[:, at : at + piece.shape[1]])
            take_piece(number, at, piece, query, query_rows, oh_dst, count_r, target, gq, grads[-1], fixed)
            at += piece.shape[1]
        join(number, weight, source, target, gq, left16, count_l, kind, rel_in,
             probe, probe_rows, gp, lgrad, to_src, to_dst, rel_out, fixed)
        if last:
            unpack_state(right[STATE], depth, rstate)
            wait_right = update_and_send(right, rstate, grads, to_dst, oh_dst, spare, right_out[0], sems.at[0], fixed)
            wait_left = update_and_send([left], lstate, [lgrad], to_src, oh_src, spare, left_out, sems.at[1], fixed)
            wait_right()
            wait_left()
        else:
            for (at, size), out in zip(pieces_of(rows, gives), right_out):
                for old, begin, length in rows_of(right, at, size):
                    cut = slice(begin, begin + length)
                    here = slice(begin - at, begin - at + length)
                    adagrad(old, rstate_in.at[:, cut], rgrad.at[:, cut], to_dst, oh_dst, begin, out.at[:, here], spare.at[:, cut])
            if packs:
                pack_state(spare, right_out[STATE], depth)
            else:
                state_out[...] = spare[...]
            adagrad(left, lstate, lgrad, to_src, oh_src, 0, left_out, lstate_out)


def shape(*dims, dtype=F32):
    return jax.ShapeDtypeStruct(dims, dtype)


def prepared_shapes(depth, rows, edges, kinds):
    return (
        shape(depth, edges), shape(depth, edges), shape(depth, edges, dtype=BF16), shape(edges, depth, dtype=BF16),
        shape(depth, rows, dtype=BF16), shape(edges, rows, dtype=BF16), shape(edges, rows, dtype=BF16),
        shape(rows // LANES, LANES), shape(rows // LANES, LANES), shape(kinds, edges, dtype=BF16), shape(edges, depth),
    )


def scratch(shapes):
    return [pltpu.VMEM(s.shape, s.dtype) for s in shapes]


def call(kernel, name, operands, shapes, in_large=(), out_large=(), scratch_shapes=(), aliases=None):
    vmem = pl.BlockSpec(memory_space=pltpu.VMEM)
    large = pl.BlockSpec(memory_space=pl.ANY)
    return pl.pallas_call(
        kernel,
        out_shape=tuple(shapes),
        in_specs=[large if i in in_large else vmem for i in range(len(operands))],
        out_specs=tuple(large if i in out_large else vmem for i in range(len(shapes))),
        scratch_shapes=list(scratch_shapes),
        input_output_aliases=aliases or {},
        compiler_params=pltpu.CompilerParams(vmem_limit_bytes=VMEM_LIMIT),
        cost_estimate=pl.CostEstimate(flops=1_000_000, bytes_accessed=100_000, transcendentals=0),
        name=name,
    )(*operands)


def prepared(step, left, relations, index):
    depth, rows = left.shape
    return call(
        functools.partial(prepare, step), "prepare%d" % step, [left, relations, *index],
        prepared_shapes(depth, rows, index[0].shape[1], relations.shape[0]),
    )


def trained(parity, name, number, fixed, gives, left, lstate, right, rstate, rel, ready, keep=(), packs=False, after=()):
    depth, rows = left.shape
    edges = ready[0].shape[1]
    last = not gives
    blocks = [shape(depth, size) for _at, size in pieces_of(rows, gives or (8,))]
    if packs:
        blocks[STATE] = shape(depth + 8, blocks[STATE].shape[1])
    edge = shape(depth, edges)
    edge16 = shape(depth, edges, dtype=BF16)
    pair16 = shape(2 * depth, edges, dtype=BF16)
    slab = shape(depth, rows)
    inner = [edge, edge, slab, edge16, shape(edges, depth, dtype=BF16), edge, slab, pair16, pair16, shape(1, rows), shape(1, rows)]
    left_out, lstate_out, rel_out, *right_out, state_out = call(
        functools.partial(train, parity, number, last, fixed, len(keep) + len(after), len(right), gives or (8,), packs),
        name,
        [left, lstate, rstate, rel, *ready, *right, *keep, *after],
        [slab, shape(1, rows), shape(*rel.shape), *blocks, shape(1, rows)],
        out_large=(0, 3) if last else (),
        scratch_shapes=[*scratch(inner), pltpu.SemaphoreType.DMA((2, rows // 256))],
        aliases={15 + len(right) + i: 0 for i in range(len(keep))},
    )
    return left_out, lstate_out, right_out, rel_out, state_out


def only_on(parity, body):
    def kernel(*refs):
        @on_parity(parity)
        def _():
            body(*refs)

    return kernel


def last_piece(parity, name, number, at, piece, ready, after, held=()):
    (_weight, _source, query, query_rows, _left16, _oh_src, oh_dst, _count_l, count_r, _kind, _rows) = ready
    depth, edges = query.shape

    def body(piece, query, query_rows, oh_dst, count_r, *rest):
        take_piece(number, at, piece, query, query_rows, oh_dst, count_r, *rest[len(held) + 1 :], fixed=True)

    operands = [piece, query, query_rows, oh_dst, count_r, *held, after]
    return call(
        only_on(parity, body), name, operands,
        [shape(depth, edges), shape(depth, edges), shape(depth, piece.shape[1])],
        aliases={5: 0, 6: 1} if held else {},
    )


def source_scores(number, probe_rows, left16, count_l, gp, weights=None):
    rows = left16.shape[1]
    size = step_of(rows, 2048)
    total = None
    for i in range(rows // size):
        cut = lanes_at(i, size)
        rows16 = left16[:, cut]
        part = negative_weights(rows16, probe_rows[...], number)
        if weights is not None:
            weights[:, cut] = part
        more = mul(rows16, often(part, times_at(count_l, i, size)), NT)
        total = more if total is None else total + more
    gp[...] = total


def early_edges(parity, name, number, step, low, high, target, ready, dst):
    (weight, source, _query, _query_rows, left16, _oh_src, _oh_dst, count_l, _count_r, _kind, weight_rows) = ready
    depth = left16.shape[0]
    edges = weight.shape[1]

    def body(weight, source, target, left16, count_l, dst, weight_rows, to_dst, target_rows, gp, probe_rows):
        w, s, t = weight[...], source[...], target[...]
        target_rows[...] = t.T
        probe_rows[...] = half_product(weight_rows[...], target_rows[...])
        source_scores(number, probe_rows, left16, count_l, gp)
        at = dst[step : step + 1, :]
        here = jnp.logical_and(at >= low, at < high)
        coef = -jax.nn.sigmoid(-jnp.sum(s * w * t, axis=0, keepdims=True))
        to_dst[0:depth, :], to_dst[depth:, :] = split(jnp.where(here, coef * w * s + gp[...] * w, 0.0), 2)

    return call(
        only_on(parity, body), name, [weight, source, target, left16, count_l, dst, weight_rows],
        [shape(2 * depth, edges, dtype=BF16), shape(edges, depth)],
        scratch_shapes=scratch([shape(depth, edges), shape(edges, depth, dtype=BF16)]),
    )


def early_right(parity, name, at, piece, state, rgrad, to_dst, oh_dst, keep, order):
    depth, rows = keep.shape

    def body(piece, state, rgrad, to_dst, oh_dst, _order, _keep, out, _order_out, spare, sems):
        update_and_send([piece], state, [rgrad], to_dst, oh_dst, spare, out, sems, fixed=True, start=at)()

    return call(
        only_on(parity, body), name, [piece, state, rgrad, to_dst, oh_dst, order, keep], [shape(depth, rows), shape(*order.shape)],
        in_large=(6,), out_large=(0,),
        scratch_shapes=[*scratch([shape(1, rows)]), pltpu.SemaphoreType.DMA((rows // 256,))],
        aliases={5: 1, 6: 0},
    )


def late_edges(parity, number, step, at, piece, ready, dst, target_rows, gq, rel, after):
    (weight, source, query, query_rows, left16, _oh_src, oh_dst, count_l, count_r, kind, weight_rows) = ready
    depth, rows = left16.shape
    edges = weight.shape[1]
    pair16 = shape(2 * depth, edges, dtype=BF16)

    def body(piece, weight, source, query, query_rows, left16, oh_dst, count_l, count_r, kind, dst, weight_rows,
             held_rows, held_q, rel_in, _after,
             rgrad, to_src, to_dst, rel_out, probe, weights, gp, probe_rows):
        size = piece.shape[1]
        parts = split(piece[...], 3)
        hits = oh_dst[:, at : at + size]
        slab = jnp.concatenate(parts, axis=1)
        table = jnp.concatenate([hits] * 3, axis=1)
        t_rows = held_rows[...] + mul(table, slab, NT)
        probe_rows[...] = half_product(weight_rows[...], t_rows)
        source_scores(number, probe_rows, left16, count_l, gp, weights)
        w, s = weight[...], source[...]
        t = t_rows.T
        probe[...] = (w * t).astype(BF16)
        rgrad[...], more = negatives(parts[0], query[...], query_rows[...], times_at(count_r, 0, size, at), number)
        q = held_q[...] + more
        p = gp[...]
        coef = -jax.nn.sigmoid(-jnp.sum(s * w * t, axis=0, keepdims=True))
        g_weight = coef * s * t + q * s + p * t
        rel_out[...] = rel_in[...] + sum(mul(kind[...], part, NT) for part in split(g_weight, 2))
        to_src[0:depth, :], to_src[depth:, :] = split(coef * w * t + q * w, 2)
        here = dst[step : step + 1, :] >= at
        to_dst[0:depth, :], to_dst[depth:, :] = split(jnp.where(here, coef * w * s + p * w, 0.0), 2)

    return call(
        only_on(parity, body), "late_edges",
        [piece, weight, source, query, query_rows, left16, oh_dst, count_l, count_r, kind, dst, weight_rows,
         target_rows, gq, rel, after],
        [shape(depth, piece.shape[1]), pair16, pair16, shape(*rel.shape), shape(depth, edges, dtype=BF16), shape(edges, rows, dtype=BF16)],
        scratch_shapes=scratch([shape(depth, edges), shape(edges, depth, dtype=BF16)]),
        aliases={14: 3},
    )


def left_rows(cut, left, lstate, to_src, oh_src, probe, weights, count_l):
    depth = left.shape[0]
    size = cut.stop - cut.start
    g = mul(probe[...], weights[:, cut], NN) * times_at(count_l, 0, size, cut.start)
    g = g + mul_parts([to_src[0:depth, :], to_src[depth:, :]], oh_src[:, cut], NN)
    new = lstate[:, cut] + jnp.sum(g * g, axis=0, keepdims=True) * (1.0 / depth)
    return left[:, cut] - g * (rate * lax.rsqrt(new))


def ahead_rows(rows):
    return rows // 8 * 3


def first_along_rel():
    return lax.axis_index("rel") < lax.axis_size("rel") // 2


def ahead_left(parity, left, lstate, to_src, oh_src, probe, weights, count_l, rel):
    depth, rows = left.shape

    def body(left, lstate, to_src, oh_src, probe, weights, count_l, _rel, result, _rel_out):
        @pl.when(first_along_rel())
        def _():
            for i in range(ahead_rows(rows) // 256):
                cut = slice(i * 256, (i + 1) * 256)
                result[:, cut] = left_rows(cut, left, lstate, to_src, oh_src, probe, weights, count_l)

    return call(
        only_on(parity, body), "ahead_left", [left, lstate, to_src, oh_src, probe, weights, count_l, rel],
        [shape(depth, ahead_rows(rows)), shape(*rel.shape)], aliases={7: 1},
    )


def late_slabs(parity, at, left, lstate, to_src, oh_src, probe, weights, count_l, ahead,
               piece, state, rgrad, to_dst, oh_dst, keep_left, keep_right):
    depth, rows = left.shape

    def body(left, lstate, to_src, oh_src, probe, weights, count_l, ahead, piece, state, rgrad, to_dst, oh_dst,
             _keep_left, _keep_right, left_out, right_out, result, spare, sems):
        def made_ahead():
            return pltpu.make_async_copy(ahead, left_out.at[:, 0 : ahead_rows(rows)], sems.at[0, 0])

        def runs(start, stop):
            out = []
            while start < stop:
                size = 512 if start % 512 == 0 and start + 512 < rows and start + 512 <= stop else 256
                out.append(slice(start, start + size))
                start += size
            return out

        def copy(cut):
            return pltpu.make_async_copy(result.at[:, cut], left_out.at[:, cut], sems.at[0, cut.start // 256])

        def make(cut):
            result[:, cut] = left_rows(cut, left, lstate, to_src, oh_src, probe, weights, count_l)
            copy(cut).start()

        first, others = runs(0, ahead_rows(rows)), runs(ahead_rows(rows), rows)

        @pl.when(first_along_rel())
        def _():
            made_ahead().start()

        @pl.when(jnp.logical_not(first_along_rel()))
        def _():
            for cut in first:
                make(cut)

        wait = update_and_send([piece], state, [rgrad], to_dst, oh_dst, spare, right_out, sems.at[1], fixed=True, start=at)
        for cut in others:
            make(cut)
        wait()

        @pl.when(first_along_rel())
        def _():
            made_ahead().wait()

        @pl.when(jnp.logical_not(first_along_rel()))
        def _():
            for cut in first:
                copy(cut).wait()

        for cut in others:
            copy(cut).wait()

    operands = [left, lstate, to_src, oh_src, probe, weights, count_l, ahead, piece, state, rgrad, to_dst, oh_dst, keep_left, keep_right]
    return call(
        only_on(parity, body), "late_slabs", operands, [shape(depth, rows), shape(depth, rows)], in_large=(13, 14), out_large=(0, 1),
        scratch_shapes=[*scratch([shape(depth, rows), shape(1, rows)]), pltpu.SemaphoreType.DMA((2, rows // 256))],
        aliases={13: 0, 14: 1},
    )


def relation_update(relations, relation_state, rels):
    kinds, depth = relations.shape

    def body(relations, relation_state, *rest):
        grad = sum(ref[...] for ref in rest[:-1])
        first = lax.broadcasted_iota(jnp.int32, (kinds, kinds), 0)
        second = lax.broadcasted_iota(jnp.int32, (kinds, kinds), 1)
        old = jnp.sum(jnp.where(first == second, relation_state[...], 0.0), axis=1, keepdims=True)
        new = old + jnp.sum(grad * grad, axis=1, keepdims=True) * (1.0 / depth)
        rest[-1][...] = relations[...] - grad * (rate * lax.rsqrt(new))

    return call(body, "relation_update", [relations, relation_state, *rels], [shape(kinds, depth)])[0]


def local(
    left_slab, left_state, right_slab, right_state, relations, relation_state,
    src_index, dst_index, relation_id, neg_source, neg_target,
):
    peers = lax.axis_size("blk")
    inside = [(i, i + 1) for i in range(0, peers, 2)]
    across = [(i, (i + 1) % peers) for i in range(1, peers, 2)]
    back = [(i + 1, i) for i in range(0, peers, 2)]
    swap = inside + back
    skip = [(i, (i + 2) % peers) for i in range(0, peers, 2)]
    index = (src_index, dst_index, relation_id, neg_source, neg_target)
    left = left_slab.T
    right = right_slab.T
    rows = left.shape[1]
    lstate = left_state.reshape(1, rows)
    number = float(neg_source.shape[1])
    right_far = lax.ppermute(right, "blk", across)
    right_near = [lax.ppermute(right[:, at : at + size], "blk", inside) for at, size in pieces_of(rows, NEAR_FIRST)]
    state_near = lax.ppermute(right_state, "blk", swap)
    state_far = lax.ppermute(state_near, "blk", skip).reshape(1, rows)
    state_near = state_near.reshape(1, rows)
    rel = jnp.zeros(relations.shape, F32)
    ready = prepared(0, left, relations, index)
    left_a, lstate, far, rel, state = trained(1, "first_near", number, False, FAR, left, lstate, right_near, state_near, rel, ready)
    far = [lax.ppermute(piece, "blk", across) for piece in far]
    state = lax.ppermute(lax.ppermute(state, "blk", back), "blk", skip)
    left_a, lstate, near, rel, _ = trained(
        0, "first_far", number, True, NEAR, left, lstate, [right_far], state_far, rel, ready, (left_a,), True, (state,)
    )
    near = [lax.ppermute(piece, "blk", inside) for piece in near]
    ready = prepared(1, left_a, relations, index)
    first_lstate = lstate
    left_b, lstate, right_b, rel, _ = trained(1, "last_near", number, False, (), left_a, lstate, near, state_near, rel, ready)
    cuts = pieces_of(rows, FAR)
    right_b, = right_b
    held = ()
    order = lstate
    for i, (at, size) in enumerate(cuts[:-1]):
        target, gq, rgrad = last_piece(0, "last_piece%d" % i, number, at, far[i], ready, order, held)
        held = (target, gq)
        to_dst, target_rows = early_edges(0, "early_edges%d" % i, number, 1, at, at + size, target, ready, dst_index)
        right_b, order = early_right(0, "early_right%d" % i, at, far[i], state, rgrad, to_dst, ready[6], right_b, order)
    at = cuts[-1][0]
    rgrad, to_src, to_dst, rel, probe, weights = late_edges(0, number, 1, at, far[-1], ready, dst_index, target_rows, gq, rel, order)
    ahead, rel = ahead_left(0, left_a, first_lstate, to_src, ready[5], probe, weights, ready[7], rel)
    if lax.axis_size("rel") == 2:
        rels = [rel, lax.ppermute(rel, "rel", [(0, 1), (1, 0)])]
    else:
        rels = [lax.psum(rel, "rel")]
    left_b, right_b = late_slabs(
        0, at, left_a, first_lstate, to_src, ready[5], probe, weights, ready[7], ahead,
        far[-1], state, rgrad, to_dst, ready[6], left_b, right_b,
    )
    relations_out = relation_update(relations, relation_state.reshape(1, -1), rels)
    return (left_b.T, right_b.T, relations_out[None])


def solution(mesh):
    in_specs = (
        P(("blk", "rel"), None),
        P(("blk", "rel")),
        P(("blk", "rel"), None),
        P(("blk", "rel")),
        P(),
        P(),
        P(None, ("blk", "rel")),
        P(None, ("blk", "rel")),
        P(None, ("blk", "rel")),
        P(None, ("blk", "rel")),
        P(None, ("blk", "rel")),
    )
    out_specs = (P(("blk", "rel"), None), P(("blk", "rel"), None), P("blk", None, None))
    return jax.shard_map(local, mesh=mesh, in_specs=in_specs, out_specs=out_specs, check_vma=False)
```

```python
import functools

import jax
import jax.numpy as jnp
from jax import lax
from jax.experimental import pallas as pl
from jax.experimental.pallas import tpu as pltpu
from jax.sharding import PartitionSpec as P

rate = 0.1
F32 = jnp.float32
BF16 = jnp.bfloat16
LANES = 128
NEAR = (4, 4)
STATE = 0
NEAR_FIRST = (4, 4)
FAR = (5, 2, 1)
VMEM_LIMIT = 30 * 2**20

NN = (((1,), (0,)), ((), ()))
NT = (((1,), (1,)), ((), ()))
TN = (((0,), (0,)), ((), ()))


def mul(a, b, dims):
    return lax.dot_general(a, b, dims, preferred_element_type=F32)


def split(x, parts):
    out = []
    for _ in range(parts):
        part = x.astype(BF16)
        out.append(part)
        x = x - part.astype(F32)
    return out


def mul_parts(parts, table, dims):
    along = dims[0][1][0]
    return mul(jnp.concatenate(parts, axis=1), jnp.concatenate([table] * len(parts), axis=along), dims)


def lanes_at(i, size, start=0):
    if isinstance(i, int):
        return slice(start + i * size, start + (i + 1) * size)
    return pl.ds(pl.multiple_of(start + i * size, LANES), size)


def step_of(rows, most=512):
    return next(size for size in (2048, 1024, 512, 256) if size <= most and rows % size == 0)


def each(count, body, fixed=False):
    if fixed:
        for i in range(count):
            body(i)
        return

    def one(i, carry):
        body(i)
        return carry

    lax.fori_loop(0, count, one, 0)


def row_onehot(idx, table):
    count, rows = table.shape
    col = jnp.broadcast_to(idx, (LANES, count)).T
    lane = lax.broadcasted_iota(jnp.int32, (count, LANES), 1)

    def tile(t):
        hit = col == lane + t * LANES
        table[:, lanes_at(t, LANES)] = jnp.where(hit, 1.0, 0.0).astype(BF16)

    each(rows // LANES, tile)


def row_counts(idx, rows):
    count = idx.shape[1]
    high = lax.broadcasted_iota(jnp.int32, (rows // LANES, count), 0)
    low = lax.broadcasted_iota(jnp.int32, (LANES, count), 0)
    high_hit = jnp.where(idx // LANES == high, 1.0, 0.0).astype(BF16)
    low_hit = jnp.where(idx % LANES == low, 1.0, 0.0).astype(BF16)
    return mul(high_hit, low_hit, NT)


def times_at(counts, i, size, start=0):
    first = (start + i * size) // LANES
    return jnp.concatenate([counts[pl.ds(first + t, 1), :] for t in range(size // LANES)], axis=1)


def half_rows(x):
    return (0.5 * x).T.astype(BF16)


def half_product(a, b):
    return (0.5 * (a * b).astype(BF16).astype(F32)).astype(BF16)


def negative_weights(rows16, query_rows, number):
    half = 0.5 / number
    return (jnp.tanh(mul(query_rows, rows16, NN)) * half + half).astype(BF16)


def often(weight, times):
    return (weight.astype(F32) * times).astype(BF16)


def negatives(rows16, query, query_rows, times, number):
    weight = negative_weights(rows16, query_rows, number)
    return mul(query, weight, NN) * times, mul(rows16, often(weight, times), NT)


def prepare(step, left, relations, src, dst, rid, nsrc, ndst,
            weight, source, query, query_rows, left16, oh_src, oh_dst, count_l, count_r, kind, weight_rows):
    rows = left.shape[1]
    here = slice(step, step + 1)
    row_onehot(src[here, :], oh_src)
    row_onehot(dst[here, :], oh_dst)
    count_l[...] = row_counts(nsrc[here, :], rows)
    count_r[...] = row_counts(ndst[here, :], rows)
    kinds = lax.broadcasted_iota(jnp.int32, kind.shape, 0)
    kind[...] = jnp.where(rid[here, :] == kinds, 1.0, 0.0).astype(BF16)
    weight[...] = sum(mul(part, kind[...], TN) for part in split(relations[...], 3))
    weight_rows[...] = weight[...].T
    source[...] = jnp.zeros_like(source)

    size = step_of(rows)

    def part(i):
        cut = lanes_at(i, size)
        parts = split(left[:, cut], 3)
        left16[:, cut] = parts[0]
        source[...] += mul_parts(parts, oh_src[:, cut], NT)

    each(rows // size, part)
    product = source[...] * weight[...]
    query[...] = product.astype(BF16)
    query_rows[...] = half_rows(product.astype(BF16).astype(F32))


def take_piece(number, start, piece, query, query_rows, oh_dst, count_r, target, gq, rgrad, fixed=False):
    depth = target.shape[0]
    if start == 0:
        target[...] = jnp.zeros_like(target)
        gq[...] = jnp.zeros_like(gq)

    size = step_of(piece.shape[1], 256 if fixed else 512)

    def part(i):
        cut = lanes_at(i, size)
        parts = split(piece[0:depth, cut], 3)
        hits = oh_dst[:, lanes_at(i, size, start)]
        target[...] += mul_parts(parts, hits, NT)
        times = times_at(count_r, i, size, start)
        rgrad[:, cut], more = negatives(parts[0], query[...], query_rows[...], times, number)
        gq[...] += more

    each(piece.shape[1] // size, part, fixed)


def join(number, weight, source, target, gq, left16, count_l, kind, rel_in,
         probe, probe_rows, gp, lgrad, to_src, to_dst, rel_out, fixed=False):
    rows = left16.shape[1]
    product = weight[...] * target[...]
    probe[...] = product.astype(BF16)
    probe_rows[...] = half_rows(product.astype(BF16).astype(F32))
    gp[...] = jnp.zeros_like(gp)

    size = step_of(rows)

    def part(i):
        cut = lanes_at(i, size)
        lgrad[:, cut], more = negatives(left16[:, cut], probe[...], probe_rows[...], times_at(count_l, i, size), number)
        gp[...] += more

    each(rows // size, part, fixed)
    depth = weight.shape[0]
    w, s, t = weight[...], source[...], target[...]
    coef = -jax.nn.sigmoid(-jnp.sum(s * w * t, axis=0, keepdims=True))
    to_src[0:depth, :], to_src[depth:, :] = split(coef * w * t + gq[...] * w, 2)
    to_dst[0:depth, :], to_dst[depth:, :] = split(coef * w * s + gp[...] * w, 2)
    g_weight = coef * s * t + gq[...] * s + gp[...] * t
    rel_out[...] = rel_in[...] + sum(mul(kind[...], p, NT) for p in split(g_weight, 2))


def adagrad(slab, state, grad, edges, table, start, out, new_state, send=None, fixed=False, more=None):
    depth = grad.shape[0]
    size = step_of(grad.shape[1])

    def part(i):
        cut = lanes_at(i, size)
        hits = table[:, lanes_at(i, size, start)]
        g = grad[:, cut] + mul_parts([edges[0:depth, :], edges[depth:, :]], hits, NN)
        if more is not None:
            g = g + more(i, size)
        new = state[:, cut] + jnp.sum(g * g, axis=0, keepdims=True) * (1.0 / depth)
        new_state[:, cut] = new
        out[0:depth, cut] = slab[0:depth, cut] - g * (rate * lax.rsqrt(new))
        if send is not None:
            send(i).start()

    each(grad.shape[1] // size, part, fixed)


def sender(result, to, start, sems):
    size = step_of(result.shape[1])

    def copy(i):
        here = lanes_at(i, size)
        there = lanes_at(i, size, start)
        return pltpu.make_async_copy(result.at[:, here], to.at[:, there], sems.at[i + start // 256])

    return copy


def update_and_send(pieces, state, grads, edges, table, new_state, to, sems, fixed=False, start=0, more=None):
    sent = []
    for piece, grad in zip(pieces, grads):
        rows = grad.shape[1]
        copy = sender(grad, to, start, sems)
        cut = slice(start, start + rows)
        adagrad(piece, state.at[:, cut], grad, edges, table, start, grad, new_state.at[:, cut], copy, fixed, more)
        sent.append((copy, rows // step_of(rows)))
        start += rows

    def wait():
        for copy, count in sent:
            each(count, lambda i, copy=copy: copy(i).wait(), fixed)

    return wait


def pack_state(state, piece, depth):
    size = state.shape[1] // 8
    for k in range(8):
        piece[depth + k : depth + k + 1, 0:size] = state[:, k * size : (k + 1) * size]


def unpack_state(piece, depth, state):
    size = state.shape[1] // 8
    for k in range(8):
        state[:, k * size : (k + 1) * size] = piece[depth + k : depth + k + 1, 0:size]


def on_parity(parity):
    return pl.when(lax.axis_index("blk") % 2 == parity)


def pieces_of(rows, eighths):
    sizes = [rows // 8 * n for n in eighths]
    return [(sum(sizes[:i]), size) for i, size in enumerate(sizes)]


def rows_of(pieces, at, size):
    found = []
    start = 0
    for piece in pieces:
        begin, end = max(at, start), min(at + size, start + piece.shape[1])
        if begin < end:
            found.append((piece.at[:, begin - start : end - start], begin, end - begin))
        start += piece.shape[1]
    return found


def train(parity, number, last, fixed, kept, takes, gives, packs, *refs):
    refs = list(refs)
    (left, lstate, rstate_in, rel_in) = refs[:4]
    (weight, source, query, query_rows, left16, oh_src, oh_dst, count_l, count_r, kind, _rows) = refs[4:15]
    right = refs[15 : 15 + takes]
    refs = refs[15 + takes + kept :]
    left_out, lstate_out, rel_out = refs[:3]
    right_out = refs[3 : 3 + len(gives)]
    state_out = refs[3 + len(gives)]
    (target, gq, rgrad, probe, probe_rows, gp, lgrad, to_src, to_dst, rstate, spare, sems) = refs[4 + len(gives) :]
    depth, rows = left.shape
    lstate_out[...] = lstate[...]
    rel_out[...] = rel_in[...]

    @on_parity(parity)
    def _():
        grads = []
        at = 0
        for piece in right:
            grads.append(rgrad.at[:, at : at + piece.shape[1]])
            take_piece(number, at, piece, query, query_rows, oh_dst, count_r, target, gq, grads[-1], fixed)
            at += piece.shape[1]
        join(number, weight, source, target, gq, left16, count_l, kind, rel_in,
             probe, probe_rows, gp, lgrad, to_src, to_dst, rel_out, fixed)
        if last:
            unpack_state(right[STATE], depth, rstate)
            wait_right = update_and_send(right, rstate, grads, to_dst, oh_dst, spare, right_out[0], sems.at[0], fixed)
            wait_left = update_and_send([left], lstate, [lgrad], to_src, oh_src, spare, left_out, sems.at[1], fixed)
            wait_right()
            wait_left()
        else:
            for (at, size), out in zip(pieces_of(rows, gives), right_out):
                for old, begin, length in rows_of(right, at, size):
                    cut = slice(begin, begin + length)
                    here = slice(begin - at, begin - at + length)
                    adagrad(old, rstate_in.at[:, cut], rgrad.at[:, cut], to_dst, oh_dst, begin, out.at[:, here], spare.at[:, cut])
            if packs:
                pack_state(spare, right_out[STATE], depth)
            else:
                state_out[...] = spare[...]
            adagrad(left, lstate, lgrad, to_src, oh_src, 0, left_out, lstate_out)


def shape(*dims, dtype=F32):
    return jax.ShapeDtypeStruct(dims, dtype)


def prepared_shapes(depth, rows, edges, kinds):
    return (
        shape(depth, edges), shape(depth, edges), shape(depth, edges, dtype=BF16), shape(edges, depth, dtype=BF16),
        shape(depth, rows, dtype=BF16), shape(edges, rows, dtype=BF16), shape(edges, rows, dtype=BF16),
        shape(rows // LANES, LANES), shape(rows // LANES, LANES), shape(kinds, edges, dtype=BF16), shape(edges, depth),
    )


def scratch(shapes):
    return [pltpu.VMEM(s.shape, s.dtype) for s in shapes]


def call(kernel, name, operands, shapes, in_large=(), out_large=(), scratch_shapes=(), aliases=None):
    vmem = pl.BlockSpec(memory_space=pltpu.VMEM)
    large = pl.BlockSpec(memory_space=pl.ANY)
    return pl.pallas_call(
        kernel,
        out_shape=tuple(shapes),
        in_specs=[large if i in in_large else vmem for i in range(len(operands))],
        out_specs=tuple(large if i in out_large else vmem for i in range(len(shapes))),
        scratch_shapes=list(scratch_shapes),
        input_output_aliases=aliases or {},
        compiler_params=pltpu.CompilerParams(vmem_limit_bytes=VMEM_LIMIT),
        cost_estimate=pl.CostEstimate(flops=1_000_000, bytes_accessed=100_000, transcendentals=0),
        name=name,
    )(*operands)


def prepared(step, left, relations, index):
    depth, rows = left.shape
    return call(
        functools.partial(prepare, step), "prepare%d" % step, [left, relations, *index],
        prepared_shapes(depth, rows, index[0].shape[1], relations.shape[0]),
    )


def trained(parity, name, number, fixed, gives, left, lstate, right, rstate, rel, ready, keep=(), packs=False, after=()):
    depth, rows = left.shape
    edges = ready[0].shape[1]
    last = not gives
    blocks = [shape(depth, size) for _at, size in pieces_of(rows, gives or (8,))]
    if packs:
        blocks[STATE] = shape(depth + 8, blocks[STATE].shape[1])
    edge = shape(depth, edges)
    edge16 = shape(depth, edges, dtype=BF16)
    pair16 = shape(2 * depth, edges, dtype=BF16)
    slab = shape(depth, rows)
    inner = [edge, edge, slab, edge16, shape(edges, depth, dtype=BF16), edge, slab, pair16, pair16, shape(1, rows), shape(1, rows)]
    left_out, lstate_out, rel_out, *right_out, state_out = call(
        functools.partial(train, parity, number, last, fixed, len(keep) + len(after), len(right), gives or (8,), packs),
        name,
        [left, lstate, rstate, rel, *ready, *right, *keep, *after],
        [slab, shape(1, rows), shape(*rel.shape), *blocks, shape(1, rows)],
        out_large=(0, 3) if last else (),
        scratch_shapes=[*scratch(inner), pltpu.SemaphoreType.DMA((2, rows // 256))],
        aliases={15 + len(right) + i: 0 for i in range(len(keep))},
    )
    return left_out, lstate_out, right_out, rel_out, state_out


def only_on(parity, body):
    def kernel(*refs):
        @on_parity(parity)
        def _():
            body(*refs)

    return kernel


def last_piece(parity, name, number, at, piece, ready, after, held=()):
    (_weight, _source, query, query_rows, _left16, _oh_src, oh_dst, _count_l, count_r, _kind, _rows) = ready
    depth, edges = query.shape

    def body(piece, query, query_rows, oh_dst, count_r, *rest):
        take_piece(number, at, piece, query, query_rows, oh_dst, count_r, *rest[len(held) + 1 :], fixed=True)

    operands = [piece, query, query_rows, oh_dst, count_r, *held, after]
    return call(
        only_on(parity, body), name, operands,
        [shape(depth, edges), shape(depth, edges), shape(depth, piece.shape[1])],
        aliases={5: 0, 6: 1} if held else {},
    )


def source_scores(number, probe_rows, left16, count_l, gp, weights=None):
    rows = left16.shape[1]
    size = step_of(rows, 2048)
    total = None
    for i in range(rows // size):
        cut = lanes_at(i, size)
        rows16 = left16[:, cut]
        part = negative_weights(rows16, probe_rows[...], number)
        if weights is not None:
            weights[:, cut] = part
        more = mul(rows16, often(part, times_at(count_l, i, size)), NT)
        total = more if total is None else total + more
    gp[...] = total


def early_edges(parity, name, number, step, low, high, target, ready, dst):
    (weight, source, _query, _query_rows, left16, _oh_src, _oh_dst, count_l, _count_r, _kind, weight_rows) = ready
    depth = left16.shape[0]
    edges = weight.shape[1]

    def body(weight, source, target, left16, count_l, dst, weight_rows, to_dst, target_rows, gp, probe_rows):
        w, s, t = weight[...], source[...], target[...]
        target_rows[...] = t.T
        probe_rows[...] = half_product(weight_rows[...], target_rows[...])
        source_scores(number, probe_rows, left16, count_l, gp)
        at = dst[step : step + 1, :]
        here = jnp.logical_and(at >= low, at < high)
        coef = -jax.nn.sigmoid(-jnp.sum(s * w * t, axis=0, keepdims=True))
        to_dst[0:depth, :], to_dst[depth:, :] = split(jnp.where(here, coef * w * s + gp[...] * w, 0.0), 2)

    return call(
        only_on(parity, body), name, [weight, source, target, left16, count_l, dst, weight_rows],
        [shape(2 * depth, edges, dtype=BF16), shape(edges, depth)],
        scratch_shapes=scratch([shape(depth, edges), shape(edges, depth, dtype=BF16)]),
    )


def early_right(parity, name, at, piece, state, rgrad, to_dst, oh_dst, keep, order):
    depth, rows = keep.shape

    def body(piece, state, rgrad, to_dst, oh_dst, _order, _keep, out, _order_out, spare, sems):
        update_and_send([piece], state, [rgrad], to_dst, oh_dst, spare, out, sems, fixed=True, start=at)()

    return call(
        only_on(parity, body), name, [piece, state, rgrad, to_dst, oh_dst, order, keep], [shape(depth, rows), shape(*order.shape)],
        in_large=(6,), out_large=(0,),
        scratch_shapes=[*scratch([shape(1, rows)]), pltpu.SemaphoreType.DMA((rows // 256,))],
        aliases={5: 1, 6: 0},
    )


def late_edges(parity, number, step, at, piece, ready, dst, target_rows, gq, rel, after):
    (weight, source, query, query_rows, left16, _oh_src, oh_dst, count_l, count_r, kind, weight_rows) = ready
    depth, rows = left16.shape
    edges = weight.shape[1]
    pair16 = shape(2 * depth, edges, dtype=BF16)

    def body(piece, weight, source, query, query_rows, left16, oh_dst, count_l, count_r, kind, dst, weight_rows,
             held_rows, held_q, rel_in, _after,
             rgrad, to_src, to_dst, rel_out, probe, weights, gp, probe_rows):
        size = piece.shape[1]
        parts = split(piece[...], 3)
        hits = oh_dst[:, at : at + size]
        slab = jnp.concatenate(parts, axis=1)
        table = jnp.concatenate([hits] * 3, axis=1)
        t_rows = held_rows[...] + mul(table, slab, NT)
        probe_rows[...] = half_product(weight_rows[...], t_rows)
        rgrad[...], more = negatives(parts[0], query[...], query_rows[...], times_at(count_r, 0, size, at), number)
        w, s = weight[...], source[...]
        t = t_rows.T
        probe[...] = (w * t).astype(BF16)
        q = held_q[...] + more
        coef = -jax.nn.sigmoid(-jnp.sum(s * w * t, axis=0, keepdims=True))
        to_src[0:depth, :], to_src[depth:, :] = split(coef * w * t + q * w, 2)
        known = coef * s * t + q * s
        source_scores(number, probe_rows, left16, count_l, gp, weights)
        p = gp[...]
        rel_out[...] = rel_in[...] + sum(mul(kind[...], part, NT) for part in split(known + p * t, 2))
        here = dst[step : step + 1, :] >= at
        to_dst[0:depth, :], to_dst[depth:, :] = split(jnp.where(here, coef * w * s + p * w, 0.0), 2)

    return call(
        only_on(parity, body), "late_edges",
        [piece, weight, source, query, query_rows, left16, oh_dst, count_l, count_r, kind, dst, weight_rows,
         target_rows, gq, rel, after],
        [shape(depth, piece.shape[1]), pair16, pair16, shape(*rel.shape), shape(depth, edges, dtype=BF16), shape(edges, rows, dtype=BF16)],
        scratch_shapes=scratch([shape(depth, edges), shape(edges, depth, dtype=BF16)]),
        aliases={14: 3},
    )


def left_rows(cut, left, lstate, to_src, oh_src, probe, weights, count_l):
    depth = left.shape[0]
    size = cut.stop - cut.start
    g = mul(probe[...], weights[:, cut], NN) * times_at(count_l, 0, size, cut.start)
    g = g + mul_parts([to_src[0:depth, :], to_src[depth:, :]], oh_src[:, cut], NN)
    new = lstate[:, cut] + jnp.sum(g * g, axis=0, keepdims=True) * (1.0 / depth)
    return left[:, cut] - g * (rate * lax.rsqrt(new))


def ahead_rows(rows):
    return rows // 8 * 3


def first_along_rel():
    return lax.axis_index("rel") < lax.axis_size("rel") // 2


def ahead_left(parity, left, lstate, to_src, oh_src, probe, weights, count_l, rel):
    depth, rows = left.shape

    def body(left, lstate, to_src, oh_src, probe, weights, count_l, _rel, result, _rel_out):
        @pl.when(first_along_rel())
        def _():
            for i in range(ahead_rows(rows) // 256):
                cut = slice(i * 256, (i + 1) * 256)
                result[:, cut] = left_rows(cut, left, lstate, to_src, oh_src, probe, weights, count_l)

    return call(
        only_on(parity, body), "ahead_left", [left, lstate, to_src, oh_src, probe, weights, count_l, rel],
        [shape(depth, ahead_rows(rows)), shape(*rel.shape)], aliases={7: 1},
    )


def late_slabs(parity, at, left, lstate, to_src, oh_src, probe, weights, count_l, ahead,
               piece, state, rgrad, to_dst, oh_dst, keep_left, keep_right):
    depth, rows = left.shape

    def body(left, lstate, to_src, oh_src, probe, weights, count_l, ahead, piece, state, rgrad, to_dst, oh_dst,
             _keep_left, _keep_right, left_out, right_out, result, spare, sems):
        def made_ahead():
            return pltpu.make_async_copy(ahead, left_out.at[:, 0 : ahead_rows(rows)], sems.at[0, 0])

        def runs(start, stop):
            out = []
            while start < stop:
                size = 512 if start % 512 == 0 and start + 512 < rows and start + 512 <= stop else 256
                out.append(slice(start, start + size))
                start += size
            return out

        def copy(cut):
            return pltpu.make_async_copy(result.at[:, cut], left_out.at[:, cut], sems.at[0, cut.start // 256])

        def make(cut):
            result[:, cut] = left_rows(cut, left, lstate, to_src, oh_src, probe, weights, count_l)
            copy(cut).start()

        first, others = runs(0, ahead_rows(rows)), runs(ahead_rows(rows), rows)

        @pl.when(first_along_rel())
        def _():
            made_ahead().start()

        @pl.when(jnp.logical_not(first_along_rel()))
        def _():
            for cut in first:
                make(cut)

        wait = update_and_send([piece], state, [rgrad], to_dst, oh_dst, spare, right_out, sems.at[1], fixed=True, start=at)
        for cut in others:
            make(cut)
        wait()

        @pl.when(first_along_rel())
        def _():
            made_ahead().wait()

        @pl.when(jnp.logical_not(first_along_rel()))
        def _():
            for cut in first:
                copy(cut).wait()

        for cut in others:
            copy(cut).wait()

    operands = [left, lstate, to_src, oh_src, probe, weights, count_l, ahead, piece, state, rgrad, to_dst, oh_dst, keep_left, keep_right]
    return call(
        only_on(parity, body), "late_slabs", operands, [shape(depth, rows), shape(depth, rows)], in_large=(13, 14), out_large=(0, 1),
        scratch_shapes=[*scratch([shape(depth, rows), shape(1, rows)]), pltpu.SemaphoreType.DMA((2, rows // 256))],
        aliases={13: 0, 14: 1},
    )


def relation_update(relations, relation_state, rels):
    kinds, depth = relations.shape

    def body(relations, relation_state, *rest):
        grad = sum(ref[...] for ref in rest[:-1])
        first = lax.broadcasted_iota(jnp.int32, (kinds, kinds), 0)
        second = lax.broadcasted_iota(jnp.int32, (kinds, kinds), 1)
        old = jnp.sum(jnp.where(first == second, relation_state[...], 0.0), axis=1, keepdims=True)
        new = old + jnp.sum(grad * grad, axis=1, keepdims=True) * (1.0 / depth)
        rest[-1][...] = relations[...] - grad * (rate * lax.rsqrt(new))

    return call(body, "relation_update", [relations, relation_state, *rels], [shape(kinds, depth)])[0]


def local(
    left_slab, left_state, right_slab, right_state, relations, relation_state,
    src_index, dst_index, relation_id, neg_source, neg_target,
):
    peers = lax.axis_size("blk")
    inside = [(i, i + 1) for i in range(0, peers, 2)]
    across = [(i, (i + 1) % peers) for i in range(1, peers, 2)]
    back = [(i + 1, i) for i in range(0, peers, 2)]
    swap = inside + back
    skip = [(i, (i + 2) % peers) for i in range(0, peers, 2)]
    index = (src_index, dst_index, relation_id, neg_source, neg_target)
    left = left_slab.T
    right = right_slab.T
    rows = left.shape[1]
    lstate = left_state.reshape(1, rows)
    number = float(neg_source.shape[1])
    right_far = lax.ppermute(right, "blk", across)
    right_near = [lax.ppermute(right[:, at : at + size], "blk", inside) for at, size in pieces_of(rows, NEAR_FIRST)]
    state_near = lax.ppermute(right_state, "blk", swap)
    state_far = lax.ppermute(state_near, "blk", skip).reshape(1, rows)
    state_near = state_near.reshape(1, rows)
    rel = jnp.zeros(relations.shape, F32)
    ready = prepared(0, left, relations, index)
    left_a, lstate, far, rel, state = trained(1, "first_near", number, False, FAR, left, lstate, right_near, state_near, rel, ready)
    far = [lax.ppermute(piece, "blk", across) for piece in far]
    state = lax.ppermute(lax.ppermute(state, "blk", back), "blk", skip)
    left_a, lstate, near, rel, _ = trained(
        0, "first_far", number, True, NEAR, left, lstate, [right_far], state_far, rel, ready, (left_a,), True, (state,)
    )
    near = [lax.ppermute(piece, "blk", inside) for piece in near]
    ready = prepared(1, left_a, relations, index)
    first_lstate = lstate
    left_b, lstate, right_b, rel, _ = trained(1, "last_near", number, False, (), left_a, lstate, near, state_near, rel, ready)
    cuts = pieces_of(rows, FAR)
    right_b, = right_b
    held = ()
    order = lstate
    for i, (at, size) in enumerate(cuts[:-1]):
        target, gq, rgrad = last_piece(0, "last_piece%d" % i, number, at, far[i], ready, order, held)
        held = (target, gq)
        to_dst, target_rows = early_edges(0, "early_edges%d" % i, number, 1, at, at + size, target, ready, dst_index)
        right_b, order = early_right(0, "early_right%d" % i, at, far[i], state, rgrad, to_dst, ready[6], right_b, order)
    at = cuts[-1][0]
    rgrad, to_src, to_dst, rel, probe, weights = late_edges(0, number, 1, at, far[-1], ready, dst_index, target_rows, gq, rel, order)
    ahead, rel = ahead_left(0, left_a, first_lstate, to_src, ready[5], probe, weights, ready[7], rel)
    if lax.axis_size("rel") == 2:
        rels = [rel, lax.ppermute(rel, "rel", [(0, 1), (1, 0)])]
    else:
        rels = [lax.psum(rel, "rel")]
    left_b, right_b = late_slabs(
        0, at, left_a, first_lstate, to_src, ready[5], probe, weights, ready[7], ahead,
        far[-1], state, rgrad, to_dst, ready[6], left_b, right_b,
    )
    relations_out = relation_update(relations, relation_state.reshape(1, -1), rels)
    return (left_b.T, right_b.T, relations_out[None])


def solution(mesh):
    in_specs = (
        P(("blk", "rel"), None),
        P(("blk", "rel")),
        P(("blk", "rel"), None),
        P(("blk", "rel")),
        P(),
        P(),
        P(None, ("blk", "rel")),
        P(None, ("blk", "rel")),
        P(None, ("blk", "rel")),
        P(None, ("blk", "rel")),
        P(None, ("blk", "rel")),
    )
    out_specs = (P(("blk", "rel"), None), P(("blk", "rel"), None), P("blk", None, None))
    return jax.shard_map(local, mesh=mesh, in_specs=in_specs, out_specs=out_specs, check_vma=False)
```

```python
import functools

import jax
import jax.numpy as jnp
from jax import lax
from jax.experimental import pallas as pl
from jax.experimental.pallas import tpu as pltpu
from jax.sharding import PartitionSpec as P

rate = 0.1
F32 = jnp.float32
BF16 = jnp.bfloat16
LANES = 128
NEAR = (4, 4)
STATE = 0
NEAR_FIRST = (4, 4)
FAR = (5, 2, 1)
VMEM_LIMIT = 30 * 2**20

NN = (((1,), (0,)), ((), ()))
NT = (((1,), (1,)), ((), ()))
TN = (((0,), (0,)), ((), ()))


def mul(a, b, dims):
    return lax.dot_general(a, b, dims, preferred_element_type=F32)


def split(x, parts):
    out = []
    for _ in range(parts):
        part = x.astype(BF16)
        out.append(part)
        x = x - part.astype(F32)
    return out


def mul_parts(parts, table, dims):
    along = dims[0][1][0]
    return mul(jnp.concatenate(parts, axis=1), jnp.concatenate([table] * len(parts), axis=along), dims)


def lanes_at(i, size, start=0):
    if isinstance(i, int):
        return slice(start + i * size, start + (i + 1) * size)
    return pl.ds(pl.multiple_of(start + i * size, LANES), size)


def step_of(rows, most=512):
    return next(size for size in (2048, 1024, 512, 256) if size <= most and rows % size == 0)


def each(count, body, fixed=False):
    if fixed:
        for i in range(count):
            body(i)
        return

    def one(i, carry):
        body(i)
        return carry

    lax.fori_loop(0, count, one, 0)


def row_onehot(idx, table):
    count, rows = table.shape
    col = jnp.broadcast_to(idx, (LANES, count)).T
    lane = lax.broadcasted_iota(jnp.int32, (count, LANES), 1)

    def tile(t):
        hit = col == lane + t * LANES
        table[:, lanes_at(t, LANES)] = jnp.where(hit, 1.0, 0.0).astype(BF16)

    each(rows // LANES, tile)


def row_counts(idx, rows):
    count = idx.shape[1]
    high = lax.broadcasted_iota(jnp.int32, (rows // LANES, count), 0)
    low = lax.broadcasted_iota(jnp.int32, (LANES, count), 0)
    high_hit = jnp.where(idx // LANES == high, 1.0, 0.0).astype(BF16)
    low_hit = jnp.where(idx % LANES == low, 1.0, 0.0).astype(BF16)
    return mul(high_hit, low_hit, NT)


def times_at(counts, i, size, start=0):
    first = (start + i * size) // LANES
    return jnp.concatenate([counts[pl.ds(first + t, 1), :] for t in range(size // LANES)], axis=1)


def half_rows(x):
    return (0.5 * x).T.astype(BF16)


def half_product(a, b):
    return (0.5 * (a * b).astype(BF16).astype(F32)).astype(BF16)


def negative_weights(rows16, query_rows, number):
    half = 0.5 / number
    return (jnp.tanh(mul(query_rows, rows16, NN)) * half + half).astype(BF16)


def often(weight, times):
    return (weight.astype(F32) * times).astype(BF16)


def negatives(rows16, query, query_rows, times, number):
    weight = negative_weights(rows16, query_rows, number)
    return mul(query, weight, NN) * times, mul(rows16, often(weight, times), NT)


def prepare(step, left, relations, src, dst, rid, nsrc, ndst,
            weight, source, query, query_rows, left16, oh_src, oh_dst, count_l, count_r, kind, weight_rows):
    rows = left.shape[1]
    here = slice(step, step + 1)
    row_onehot(src[here, :], oh_src)
    row_onehot(dst[here, :], oh_dst)
    count_l[...] = row_counts(nsrc[here, :], rows)
    count_r[...] = row_counts(ndst[here, :], rows)
    kinds = lax.broadcasted_iota(jnp.int32, kind.shape, 0)
    kind[...] = jnp.where(rid[here, :] == kinds, 1.0, 0.0).astype(BF16)
    weight[...] = sum(mul(part, kind[...], TN) for part in split(relations[...], 3))
    weight_rows[...] = weight[...].T
    source[...] = jnp.zeros_like(source)

    size = step_of(rows)

    def part(i):
        cut = lanes_at(i, size)
        parts = split(left[:, cut], 3)
        left16[:, cut] = parts[0]
        source[...] += mul_parts(parts, oh_src[:, cut], NT)

    each(rows // size, part)
    product = source[...] * weight[...]
    query[...] = product.astype(BF16)
    query_rows[...] = half_rows(product.astype(BF16).astype(F32))


def take_piece(number, start, piece, query, query_rows, oh_dst, count_r, target, gq, rgrad, fixed=False):
    depth = target.shape[0]
    if start == 0:
        target[...] = jnp.zeros_like(target)
        gq[...] = jnp.zeros_like(gq)

    size = step_of(piece.shape[1], 256 if fixed else 512)

    def part(i):
        cut = lanes_at(i, size)
        parts = split(piece[0:depth, cut], 3)
        hits = oh_dst[:, lanes_at(i, size, start)]
        target[...] += mul_parts(parts, hits, NT)
        times = times_at(count_r, i, size, start)
        rgrad[:, cut], more = negatives(parts[0], query[...], query_rows[...], times, number)
        gq[...] += more

    each(piece.shape[1] // size, part, fixed)


def join(number, weight, source, target, gq, left16, count_l, kind, rel_in,
         probe, probe_rows, gp, lgrad, to_src, to_dst, rel_out, fixed=False):
    rows = left16.shape[1]
    product = weight[...] * target[...]
    probe[...] = product.astype(BF16)
    probe_rows[...] = half_rows(product.astype(BF16).astype(F32))
    gp[...] = jnp.zeros_like(gp)

    size = step_of(rows)

    def part(i):
        cut = lanes_at(i, size)
        lgrad[:, cut], more = negatives(left16[:, cut], probe[...], probe_rows[...], times_at(count_l, i, size), number)
        gp[...] += more

    each(rows // size, part, fixed)
    depth = weight.shape[0]
    w, s, t = weight[...], source[...], target[...]
    coef = -jax.nn.sigmoid(-jnp.sum(s * w * t, axis=0, keepdims=True))
    to_src[0:depth, :], to_src[depth:, :] = split(coef * w * t + gq[...] * w, 2)
    to_dst[0:depth, :], to_dst[depth:, :] = split(coef * w * s + gp[...] * w, 2)
    g_weight = coef * s * t + gq[...] * s + gp[...] * t
    rel_out[...] = rel_in[...] + sum(mul(kind[...], p, NT) for p in split(g_weight, 2))


def adagrad(slab, state, grad, edges, table, start, out, new_state, send=None, fixed=False, more=None):
    depth = grad.shape[0]
    size = step_of(grad.shape[1])

    def part(i):
        cut = lanes_at(i, size)
        hits = table[:, lanes_at(i, size, start)]
        g = grad[:, cut] + mul_parts([edges[0:depth, :], edges[depth:, :]], hits, NN)
        if more is not None:
            g = g + more(i, size)
        new = state[:, cut] + jnp.sum(g * g, axis=0, keepdims=True) * (1.0 / depth)
        new_state[:, cut] = new
        out[0:depth, cut] = slab[0:depth, cut] - g * (rate * lax.rsqrt(new))
        if send is not None:
            send(i).start()

    each(grad.shape[1] // size, part, fixed)


def sender(result, to, start, sems):
    size = step_of(result.shape[1])

    def copy(i):
        here = lanes_at(i, size)
        there = lanes_at(i, size, start)
        return pltpu.make_async_copy(result.at[:, here], to.at[:, there], sems.at[i + start // 256])

    return copy


def update_and_send(pieces, state, grads, edges, table, new_state, to, sems, fixed=False, start=0, more=None):
    sent = []
    for piece, grad in zip(pieces, grads):
        rows = grad.shape[1]
        copy = sender(grad, to, start, sems)
        cut = slice(start, start + rows)
        adagrad(piece, state.at[:, cut], grad, edges, table, start, grad, new_state.at[:, cut], copy, fixed, more)
        sent.append((copy, rows // step_of(rows)))
        start += rows

    def wait():
        for copy, count in sent:
            each(count, lambda i, copy=copy: copy(i).wait(), fixed)

    return wait


def pack_state(state, piece, depth):
    size = state.shape[1] // 8
    for k in range(8):
        piece[depth + k : depth + k + 1, 0:size] = state[:, k * size : (k + 1) * size]


def unpack_state(piece, depth, state):
    size = state.shape[1] // 8
    for k in range(8):
        state[:, k * size : (k + 1) * size] = piece[depth + k : depth + k + 1, 0:size]


def on_parity(parity):
    return pl.when(lax.axis_index("blk") % 2 == parity)


def pieces_of(rows, eighths):
    sizes = [rows // 8 * n for n in eighths]
    return [(sum(sizes[:i]), size) for i, size in enumerate(sizes)]


def rows_of(pieces, at, size):
    found = []
    start = 0
    for piece in pieces:
        begin, end = max(at, start), min(at + size, start + piece.shape[1])
        if begin < end:
            found.append((piece.at[:, begin - start : end - start], begin, end - begin))
        start += piece.shape[1]
    return found


def train(parity, number, last, fixed, kept, takes, gives, packs, *refs):
    refs = list(refs)
    (left, lstate, rstate_in, rel_in) = refs[:4]
    (weight, source, query, query_rows, left16, oh_src, oh_dst, count_l, count_r, kind, _rows) = refs[4:15]
    right = refs[15 : 15 + takes]
    refs = refs[15 + takes + kept :]
    left_out, lstate_out, rel_out = refs[:3]
    right_out = refs[3 : 3 + len(gives)]
    state_out = refs[3 + len(gives)]
    (target, gq, rgrad, probe, probe_rows, gp, lgrad, to_src, to_dst, rstate, spare, sems) = refs[4 + len(gives) :]
    depth, rows = left.shape
    lstate_out[...] = lstate[...]
    rel_out[...] = rel_in[...]

    @on_parity(parity)
    def _():
        grads = []
        at = 0
        for piece in right:
            grads.append(rgrad.at[:, at : at + piece.shape[1]])
            take_piece(number, at, piece, query, query_rows, oh_dst, count_r, target, gq, grads[-1], fixed)
            at += piece.shape[1]
        join(number, weight, source, target, gq, left16, count_l, kind, rel_in,
             probe, probe_rows, gp, lgrad, to_src, to_dst, rel_out, fixed)
        if last:
            unpack_state(right[STATE], depth, rstate)
            wait_right = update_and_send(right, rstate, grads, to_dst, oh_dst, spare, right_out[0], sems.at[0], fixed)
            wait_left = update_and_send([left], lstate, [lgrad], to_src, oh_src, spare, left_out, sems.at[1], fixed)
            wait_right()
            wait_left()
        else:
            for (at, size), out in zip(pieces_of(rows, gives), right_out):
                for old, begin, length in rows_of(right, at, size):
                    cut = slice(begin, begin + length)
                    here = slice(begin - at, begin - at + length)
                    adagrad(old, rstate_in.at[:, cut], rgrad.at[:, cut], to_dst, oh_dst, begin, out.at[:, here], spare.at[:, cut])
            if packs:
                pack_state(spare, right_out[STATE], depth)
            else:
                state_out[...] = spare[...]
            adagrad(left, lstate, lgrad, to_src, oh_src, 0, left_out, lstate_out)


def shape(*dims, dtype=F32):
    return jax.ShapeDtypeStruct(dims, dtype)


def prepared_shapes(depth, rows, edges, kinds):
    return (
        shape(depth, edges), shape(depth, edges), shape(depth, edges, dtype=BF16), shape(edges, depth, dtype=BF16),
        shape(depth, rows, dtype=BF16), shape(edges, rows, dtype=BF16), shape(edges, rows, dtype=BF16),
        shape(rows // LANES, LANES), shape(rows // LANES, LANES), shape(kinds, edges, dtype=BF16), shape(edges, depth),
    )


def scratch(shapes):
    return [pltpu.VMEM(s.shape, s.dtype) for s in shapes]


def call(kernel, name, operands, shapes, in_large=(), out_large=(), scratch_shapes=(), aliases=None):
    vmem = pl.BlockSpec(memory_space=pltpu.VMEM)
    large = pl.BlockSpec(memory_space=pl.ANY)
    return pl.pallas_call(
        kernel,
        out_shape=tuple(shapes),
        in_specs=[large if i in in_large else vmem for i in range(len(operands))],
        out_specs=tuple(large if i in out_large else vmem for i in range(len(shapes))),
        scratch_shapes=list(scratch_shapes),
        input_output_aliases=aliases or {},
        compiler_params=pltpu.CompilerParams(vmem_limit_bytes=VMEM_LIMIT),
        cost_estimate=pl.CostEstimate(flops=1_000_000, bytes_accessed=100_000, transcendentals=0),
        name=name,
    )(*operands)


def prepared(step, left, relations, index):
    depth, rows = left.shape
    return call(
        functools.partial(prepare, step), "prepare%d" % step, [left, relations, *index],
        prepared_shapes(depth, rows, index[0].shape[1], relations.shape[0]),
    )


def trained(parity, name, number, fixed, gives, left, lstate, right, rstate, rel, ready, keep=(), packs=False, after=()):
    depth, rows = left.shape
    edges = ready[0].shape[1]
    last = not gives
    blocks = [shape(depth, size) for _at, size in pieces_of(rows, gives or (8,))]
    if packs:
        blocks[STATE] = shape(depth + 8, blocks[STATE].shape[1])
    edge = shape(depth, edges)
    edge16 = shape(depth, edges, dtype=BF16)
    pair16 = shape(2 * depth, edges, dtype=BF16)
    slab = shape(depth, rows)
    inner = [edge, edge, slab, edge16, shape(edges, depth, dtype=BF16), edge, slab, pair16, pair16, shape(1, rows), shape(1, rows)]
    left_out, lstate_out, rel_out, *right_out, state_out = call(
        functools.partial(train, parity, number, last, fixed, len(keep) + len(after), len(right), gives or (8,), packs),
        name,
        [left, lstate, rstate, rel, *ready, *right, *keep, *after],
        [slab, shape(1, rows), shape(*rel.shape), *blocks, shape(1, rows)],
        out_large=(0, 3) if last else (),
        scratch_shapes=[*scratch(inner), pltpu.SemaphoreType.DMA((2, rows // 256))],
        aliases={15 + len(right) + i: 0 for i in range(len(keep))},
    )
    return left_out, lstate_out, right_out, rel_out, state_out


def only_on(parity, body):
    def kernel(*refs):
        @on_parity(parity)
        def _():
            body(*refs)

    return kernel


def last_piece(parity, name, number, at, piece, ready, after, held=()):
    (_weight, _source, query, query_rows, _left16, _oh_src, oh_dst, _count_l, count_r, _kind, _rows) = ready
    depth, edges = query.shape

    def body(piece, query, query_rows, oh_dst, count_r, *rest):
        take_piece(number, at, piece, query, query_rows, oh_dst, count_r, *rest[len(held) + 1 :], fixed=True)

    operands = [piece, query, query_rows, oh_dst, count_r, *held, after]
    return call(
        only_on(parity, body), name, operands,
        [shape(depth, edges), shape(depth, edges), shape(depth, piece.shape[1])],
        aliases={5: 0, 6: 1} if held else {},
    )


def source_scores(number, probe_rows, left16, count_l, gp, weights=None):
    rows = left16.shape[1]
    size = step_of(rows, 2048)
    total = None
    for i in range(rows // size):
        cut = lanes_at(i, size)
        rows16 = left16[:, cut]
        part = negative_weights(rows16, probe_rows[...], number)
        if weights is not None:
            weights[:, cut] = part
        more = mul(rows16, often(part, times_at(count_l, i, size)), NT)
        total = more if total is None else total + more
    gp[...] = total


def early_edges(parity, name, number, step, low, high, target, ready, dst):
    (weight, source, _query, _query_rows, left16, _oh_src, _oh_dst, count_l, _count_r, _kind, weight_rows) = ready
    depth = left16.shape[0]
    edges = weight.shape[1]

    def body(weight, source, target, left16, count_l, dst, weight_rows, to_dst, target_rows, gp, probe_rows):
        w, s, t = weight[...], source[...], target[...]
        target_rows[...] = t.T
        probe_rows[...] = half_product(weight_rows[...], target_rows[...])
        source_scores(number, probe_rows, left16, count_l, gp)
        at = dst[step : step + 1, :]
        here = jnp.logical_and(at >= low, at < high)
        coef = -jax.nn.sigmoid(-jnp.sum(s * w * t, axis=0, keepdims=True))
        to_dst[0:depth, :], to_dst[depth:, :] = split(jnp.where(here, coef * w * s + gp[...] * w, 0.0), 2)

    return call(
        only_on(parity, body), name, [weight, source, target, left16, count_l, dst, weight_rows],
        [shape(2 * depth, edges, dtype=BF16), shape(edges, depth)],
        scratch_shapes=scratch([shape(depth, edges), shape(edges, depth, dtype=BF16)]),
    )


def early_right(parity, name, at, piece, state, rgrad, to_dst, oh_dst, keep, order):
    depth, rows = keep.shape

    def body(piece, state, rgrad, to_dst, oh_dst, _order, _keep, out, _order_out, spare, sems):
        update_and_send([piece], state, [rgrad], to_dst, oh_dst, spare, out, sems, fixed=True, start=at)()

    return call(
        only_on(parity, body), name, [piece, state, rgrad, to_dst, oh_dst, order, keep], [shape(depth, rows), shape(*order.shape)],
        in_large=(6,), out_large=(0,),
        scratch_shapes=[*scratch([shape(1, rows)]), pltpu.SemaphoreType.DMA((rows // 256,))],
        aliases={5: 1, 6: 0},
    )


def late_edges(parity, number, step, at, piece, ready, dst, target_rows, gq, rel, after):
    (weight, source, query, query_rows, left16, _oh_src, oh_dst, count_l, count_r, kind, weight_rows) = ready
    depth, rows = left16.shape
    edges = weight.shape[1]
    pair16 = shape(2 * depth, edges, dtype=BF16)

    def body(piece, weight, source, query, query_rows, left16, oh_dst, count_l, count_r, kind, dst, weight_rows,
             held_rows, held_q, rel_in, _after,
             rgrad, to_src, to_dst, rel_out, probe, weights, gp, probe_rows):
        size = piece.shape[1]
        parts = split(piece[...], 3)
        hits = oh_dst[:, at : at + size]
        slab = jnp.concatenate(parts, axis=1)
        table = jnp.concatenate([hits] * 3, axis=1)
        t_rows = held_rows[...] + mul(table, slab, NT)
        probe_rows[...] = half_product(weight_rows[...], t_rows)
        source_scores(number, probe_rows, left16, count_l, gp, weights)
        w, s = weight[...], source[...]
        t = t_rows.T
        probe[...] = (w * t).astype(BF16)
        rgrad[...], more = negatives(parts[0], query[...], query_rows[...], times_at(count_r, 0, size, at), number)
        q = held_q[...] + more
        p = gp[...]
        coef = -jax.nn.sigmoid(-jnp.sum(s * w * t, axis=0, keepdims=True))
        g_weight = coef * s * t + q * s + p * t
        rel_out[...] = rel_in[...] + sum(mul(kind[...], part, NT) for part in split(g_weight, 2))
        to_src[0:depth, :], to_src[depth:, :] = split(coef * w * t + q * w, 2)
        here = dst[step : step + 1, :] >= at
        to_dst[0:depth, :], to_dst[depth:, :] = split(jnp.where(here, coef * w * s + p * w, 0.0), 2)

    return call(
        only_on(parity, body), "late_edges",
        [piece, weight, source, query, query_rows, left16, oh_dst, count_l, count_r, kind, dst, weight_rows,
         target_rows, gq, rel, after],
        [shape(depth, piece.shape[1]), pair16, pair16, shape(*rel.shape), shape(depth, edges, dtype=BF16), shape(edges, rows, dtype=BF16)],
        scratch_shapes=scratch([shape(depth, edges), shape(edges, depth, dtype=BF16)]),
        aliases={14: 3},
    )


def left_rows(cut, left, lstate, to_src, oh_src, probe, weights, count_l):
    depth = left.shape[0]
    size = cut.stop - cut.start
    g = mul(probe[...], weights[:, cut], NN) * times_at(count_l, 0, size, cut.start)
    g = g + mul_parts([to_src[0:depth, :], to_src[depth:, :]], oh_src[:, cut], NN)
    new = lstate[:, cut] + jnp.sum(g * g, axis=0, keepdims=True) * (1.0 / depth)
    return left[:, cut] - g * (rate * lax.rsqrt(new))


def ahead_rows(rows):
    return rows // 4


def first_along_rel():
    return lax.axis_index("rel") < lax.axis_size("rel") // 2


def ahead_left(parity, left, lstate, to_src, oh_src, probe, weights, count_l, rel):
    depth, rows = left.shape

    def body(left, lstate, to_src, oh_src, probe, weights, count_l, _rel, result, _rel_out):
        @pl.when(first_along_rel())
        def _():
            for i in range(ahead_rows(rows) // 256):
                cut = slice(i * 256, (i + 1) * 256)
                result[:, cut] = left_rows(cut, left, lstate, to_src, oh_src, probe, weights, count_l)

    return call(
        only_on(parity, body), "ahead_left", [left, lstate, to_src, oh_src, probe, weights, count_l, rel],
        [shape(depth, ahead_rows(rows)), shape(*rel.shape)], aliases={7: 1},
    )


def late_slabs(parity, at, left, lstate, to_src, oh_src, probe, weights, count_l, ahead,
               piece, state, rgrad, to_dst, oh_dst, keep_left, keep_right):
    depth, rows = left.shape

    def body(left, lstate, to_src, oh_src, probe, weights, count_l, ahead, piece, state, rgrad, to_dst, oh_dst,
             _keep_left, _keep_right, left_out, right_out, result, spare, sems):
        def made_ahead():
            return pltpu.make_async_copy(ahead, left_out.at[:, 0 : ahead_rows(rows)], sems.at[0, 0])

        def runs(start, stop):
            out = []
            while start < stop:
                size = 512 if start % 512 == 0 and start + 512 < rows and start + 512 <= stop else 256
                out.append(slice(start, start + size))
                start += size
            return out

        def copy(cut):
            return pltpu.make_async_copy(result.at[:, cut], left_out.at[:, cut], sems.at[0, cut.start // 256])

        def make(cut):
            result[:, cut] = left_rows(cut, left, lstate, to_src, oh_src, probe, weights, count_l)
            copy(cut).start()

        first, others = runs(0, ahead_rows(rows)), runs(ahead_rows(rows), rows)

        @pl.when(first_along_rel())
        def _():
            made_ahead().start()

        @pl.when(jnp.logical_not(first_along_rel()))
        def _():
            for cut in first:
                make(cut)

        wait = update_and_send([piece], state, [rgrad], to_dst, oh_dst, spare, right_out, sems.at[1], fixed=True, start=at)
        for cut in others:
            make(cut)
        wait()

        @pl.when(first_along_rel())
        def _():
            made_ahead().wait()

        @pl.when(jnp.logical_not(first_along_rel()))
        def _():
            for cut in first:
                copy(cut).wait()

        for cut in others:
            copy(cut).wait()

    operands = [left, lstate, to_src, oh_src, probe, weights, count_l, ahead, piece, state, rgrad, to_dst, oh_dst, keep_left, keep_right]
    return call(
        only_on(parity, body), "late_slabs", operands, [shape(depth, rows), shape(depth, rows)], in_large=(13, 14), out_large=(0, 1),
        scratch_shapes=[*scratch([shape(depth, rows), shape(1, rows)]), pltpu.SemaphoreType.DMA((2, rows // 256))],
        aliases={13: 0, 14: 1},
    )


def relation_update(relations, relation_state, rels):
    kinds, depth = relations.shape

    def body(relations, relation_state, *rest):
        grad = sum(ref[...] for ref in rest[:-1])
        first = lax.broadcasted_iota(jnp.int32, (kinds, kinds), 0)
        second = lax.broadcasted_iota(jnp.int32, (kinds, kinds), 1)
        old = jnp.sum(jnp.where(first == second, relation_state[...], 0.0), axis=1, keepdims=True)
        new = old + jnp.sum(grad * grad, axis=1, keepdims=True) * (1.0 / depth)
        rest[-1][...] = relations[...] - grad * (rate * lax.rsqrt(new))

    return call(body, "relation_update", [relations, relation_state, *rels], [shape(kinds, depth)])[0]


def local(
    left_slab, left_state, right_slab, right_state, relations, relation_state,
    src_index, dst_index, relation_id, neg_source, neg_target,
):
    peers = lax.axis_size("blk")
    inside = [(i, i + 1) for i in range(0, peers, 2)]
    across = [(i, (i + 1) % peers) for i in range(1, peers, 2)]
    back = [(i + 1, i) for i in range(0, peers, 2)]
    swap = inside + back
    skip = [(i, (i + 2) % peers) for i in range(0, peers, 2)]
    index = (src_index, dst_index, relation_id, neg_source, neg_target)
    left = left_slab.T
    right = right_slab.T
    rows = left.shape[1]
    lstate = left_state.reshape(1, rows)
    number = float(neg_source.shape[1])
    right_far = lax.ppermute(right, "blk", across)
    right_near = [lax.ppermute(right[:, at : at + size], "blk", inside) for at, size in pieces_of(rows, NEAR_FIRST)]
    state_near = lax.ppermute(right_state, "blk", swap)
    state_far = lax.ppermute(state_near, "blk", skip).reshape(1, rows)
    state_near = state_near.reshape(1, rows)
    rel = jnp.zeros(relations.shape, F32)
    ready = prepared(0, left, relations, index)
    left_a, lstate, far, rel, state = trained(1, "first_near", number, False, FAR, left, lstate, right_near, state_near, rel, ready)
    far = [lax.ppermute(piece, "blk", across) for piece in far]
    state = lax.ppermute(lax.ppermute(state, "blk", back), "blk", skip)
    left_a, lstate, near, rel, _ = trained(
        0, "first_far", number, True, NEAR, left, lstate, [right_far], state_far, rel, ready, (left_a,), True, (state,)
    )
    near = [lax.ppermute(piece, "blk", inside) for piece in near]
    ready = prepared(1, left_a, relations, index)
    first_lstate = lstate
    left_b, lstate, right_b, rel, _ = trained(1, "last_near", number, False, (), left_a, lstate, near, state_near, rel, ready)
    cuts = pieces_of(rows, FAR)
    right_b, = right_b
    held = ()
    order = lstate
    for i, (at, size) in enumerate(cuts[:-1]):
        target, gq, rgrad = last_piece(0, "last_piece%d" % i, number, at, far[i], ready, order, held)
        held = (target, gq)
        to_dst, target_rows = early_edges(0, "early_edges%d" % i, number, 1, at, at + size, target, ready, dst_index)
        right_b, order = early_right(0, "early_right%d" % i, at, far[i], state, rgrad, to_dst, ready[6], right_b, order)
    at = cuts[-1][0]
    rgrad, to_src, to_dst, rel, probe, weights = late_edges(0, number, 1, at, far[-1], ready, dst_index, target_rows, gq, rel, order)
    ahead, rel = ahead_left(0, left_a, first_lstate, to_src, ready[5], probe, weights, ready[7], rel)
    if lax.axis_size("rel") == 2:
        rels = [rel, lax.ppermute(rel, "rel", [(0, 1), (1, 0)])]
    else:
        rels = [lax.psum(rel, "rel")]
    left_b, right_b = late_slabs(
        0, at, left_a, first_lstate, to_src, ready[5], probe, weights, ready[7], ahead,
        far[-1], state, rgrad, to_dst, ready[6], left_b, right_b,
    )
    relations_out = relation_update(relations, relation_state.reshape(1, -1), rels)
    return (left_b.T, right_b.T, relations_out[None])


def solution(mesh):
    in_specs = (
        P(("blk", "rel"), None),
        P(("blk", "rel")),
        P(("blk", "rel"), None),
        P(("blk", "rel")),
        P(),
        P(),
        P(None, ("blk", "rel")),
        P(None, ("blk", "rel")),
        P(None, ("blk", "rel")),
        P(None, ("blk", "rel")),
        P(None, ("blk", "rel")),
    )
    out_specs = (P(("blk", "rel"), None), P(("blk", "rel"), None), P("blk", None, None))
    return jax.shard_map(local, mesh=mesh, in_specs=in_specs, out_specs=out_specs, check_vma=False)
```
